32 devices in a mesh: shot: 2 (over core), tx: 2 (over y), ty: 8 (over z, x).
Axes of the slice: x: 2, y: 2, z: 4, core: 2. Of those that a mesh axis runs over, the one named last changes fastest.
Arguments:
- forward_fields: float32 [2, 9, 32, 128, 128], P('shot', None, 'tx', 'ty'), may hold values from -6 to 6
- adjoint_fields: float32 [2, 9, 32, 128, 128], P('shot', None, 'tx', 'ty'), may hold values from -6 to 6
- lame_lambda: float32 [32, 128, 128], P('tx', 'ty'), may hold values from 1 to 4
- shear_modulus: float32 [32, 128, 128], P('tx', 'ty'), may hold values from 0.5 to 2
- density: float32 [32, 128, 128], P('tx', 'ty'), may hold values from 1 to 3
- source_cell: int32 [2], P('shot'), may hold values from 0 to 524287
- source_amp: float32 [2], P('shot'), may hold values from 4 to 12
- receiver_cell: int32 [2, 256], P('shot'), may hold values from 0 to 524287
- residual_amp: float32 [2, 256], P('shot'), may hold values from -16 to 16
Outputs:
- forward_next: float32 [2, 9, 32, 128, 128], P('shot', None, 'tx', 'ty')
- adjoint_next: float32 [2, 9, 32, 128, 128], P('shot', None, 'tx', 'ty')
- gradient: float32 [3, 32, 128, 128], P(None, 'tx', 'ty')
The draws below stay inside these ranges and needn't reach their ends.
Inputs may be any that keep to these rules, and one draw needn't show every extreme that they name: `source_cell`: each value is a flat index x * 128 * 128 + y * 128 + z of a grid cell. `receiver_cell`: each value is a flat index x * 128 * 128 + y * 128 + z of a grid cell; receivers may share cells.
All inputs are finite; a program needn't handle non-finite values.
Results may differ from the reference program's by a relative error of at most 0.0001.
Values sent between devices are 32-bit elements; how exact they have to be, the bound alone decides.
No kernel may reach another device: no remote copies, remote signals or barrier semaphores. Data moves between devices by JAX's collectives and lax.ppermute only.
A program may use at most 64 MiB of HBM per device.

```python
import jax
import jax.numpy as jnp
from jax import lax

NZ = 128
REC = 256
NX = 32
NY = 128
SHOTS = 2


def touch_ends(values, own_key, least, high):
    dims = values.shape
    spot = [jax.random.randint(jax.random.fold_in(own_key, axis), (), 0, dims[axis]) for axis in range(len(dims))]
    values = values.at[tuple(spot)].set(least)
    longest = dims.index(max(dims))
    spot[longest] = (spot[longest] + 1) % dims[longest]
    return values.at[tuple(spot)].set(high)


def steps_of(stream_key, extent, pieces, smallest, top_value):
    loudness, own = 1.0, jax.random.fold_in(stream_key, 6)
    for axis_at, blocks in pieces:
        draws = jnp.exp(jax.random.uniform(jax.random.fold_in(own, axis_at), (blocks,), jnp.float32, smallest / len(pieces), top_value / len(pieces)))
        loudness = loudness * jnp.repeat(draws, extent[axis_at] // blocks).reshape([-1 if axis == axis_at else 1 for axis in range(len(extent))])
    return loudness


def gaussian(key, extent, deviation, most, cuts=(), held_as=jnp.bfloat16):
    gain = steps_of(key, extent, cuts, -0.22, 0.18) if cuts else 1.0
    array = jax.random.normal(key, extent, jnp.float32) * deviation * gain
    return jnp.minimum(jnp.maximum(array, -most), most).astype(held_as)


def setup_inputs(seed: int = 0) -> dict:
    splits = jax.random.split(jax.random.key(seed), 10)
    return {
        "forward_fields": gaussian(splits[0], (SHOTS, 9, NX, NY, NZ), 1.0, 6.0, ((0, 2), (2, 2), (3, 8)), jnp.float32),
        "adjoint_fields": gaussian(splits[1], (SHOTS, 9, NX, NY, NZ), 1.0, 6.0, ((0, 2), (2, 2), (3, 8)), jnp.float32),
        "lame_lambda": jnp.clip(1.0 + 3.0 * jax.random.uniform(splits[2], (NX, NY, NZ), jnp.float32) ** steps_of(splits[2], (NX, NY, NZ), ((0, 2), (1, 8)), -0.2, 0.2), 1.0, 4.0),
        "shear_modulus": jnp.clip(0.5 + 1.5 * jax.random.uniform(splits[3], (NX, NY, NZ), jnp.float32) ** steps_of(splits[3], (NX, NY, NZ), ((0, 2), (1, 8)), -0.2, 0.2), 0.5, 2.0),
        "density": jnp.clip(1.0 + 2.0 * jax.random.uniform(splits[4], (NX, NY, NZ), jnp.float32) ** steps_of(splits[4], (NX, NY, NZ), ((0, 2), (1, 8)), -0.2, 0.2), 1.0, 3.0),
        "source_cell": jax.random.randint(splits[5], (SHOTS,), 0, NX * NY * NZ).astype(jnp.int32),
        "source_amp": jnp.clip(4.0 + 8.0 * jax.random.uniform(splits[6], (SHOTS,), jnp.float32) ** steps_of(splits[6], (SHOTS,), ((0, 2),), -0.2, 0.2), 4.0, 12.0),
        "receiver_cell": touch_ends(jax.random.randint(splits[7], (SHOTS, REC), 0, NX * NY * NZ), jax.random.fold_in(splits[7], 1), 0, (NX * NY * NZ) - 1).astype(jnp.int32),
        "residual_amp": gaussian(splits[8], (SHOTS, REC), 4.0, 16.0, ((0, 2),), jnp.float32),
    }


near_coef = 9.0 / 8.0
far_coef = -1.0 / 24.0
time_step = 0.15


def shifted(padded, margin, rim_width, direction, offset):
    rank_count = padded.ndim
    sliced = padded
    for which in range(3):
        length = padded.shape[rank_count - 3 + which] - 2 * margin[which] + 2 * rim_width[which]
        begin_at = margin[which] - rim_width[which] + (offset if which == direction else 0)
        sliced = lax.slice_in_dim(sliced, begin_at, begin_at + length, axis=rank_count - 3 + which)
    return sliced


def derive(padded, margin, rim_width, direction, upward):
    if upward:
        return near_coef * (shifted(padded, margin, rim_width, direction, 1) - shifted(padded, margin, rim_width, direction, 0)) + far_coef * (shifted(padded, margin, rim_width, direction, 2) - shifted(padded, margin, rim_width, direction, -1))
    return near_coef * (shifted(padded, margin, rim_width, direction, 0) - shifted(padded, margin, rim_width, direction, -1)) + far_coef * (shifted(padded, margin, rim_width, direction, 1) - shifted(padded, margin, rim_width, direction, -2))


def accelerate(stress_ext, buoyancy, margin, rim_width):
    comps = [stress_ext[..., which, :, :, :] for which in range(6)]
    accel_x = derive(comps[0], margin, rim_width, 0, True) + derive(comps[3], margin, rim_width, 1, False) + derive(comps[4], margin, rim_width, 2, False)
    accel_y = derive(comps[3], margin, rim_width, 0, False) + derive(comps[1], margin, rim_width, 1, True) + derive(comps[5], margin, rim_width, 2, False)
    accel_z = derive(comps[4], margin, rim_width, 0, False) + derive(comps[5], margin, rim_width, 1, False) + derive(comps[2], margin, rim_width, 2, True)
    return jnp.stack([accel_x, accel_y, accel_z], axis=-4) * buoyancy


def strain_rates(velocity_ext, margin):
    flat_rim = (0, 0, 0)
    comps = [velocity_ext[..., which, :, :, :] for which in range(3)]
    return jnp.stack([
        derive(comps[0], margin, flat_rim, 0, False),
        derive(comps[1], margin, flat_rim, 1, False),
        derive(comps[2], margin, flat_rim, 2, False),
        derive(comps[0], margin, flat_rim, 1, True) + derive(comps[1], margin, flat_rim, 0, True),
        derive(comps[0], margin, flat_rim, 2, True) + derive(comps[2], margin, flat_rim, 0, True),
        derive(comps[1], margin, flat_rim, 2, True) + derive(comps[2], margin, flat_rim, 1, True),
    ], axis=-4)


def new_stress(stress_now, strain, lame_lambda, shear_modulus):
    trace = strain[..., 0, :, :, :] + strain[..., 1, :, :, :] + strain[..., 2, :, :, :]
    normal = stress_now[..., :3, :, :, :] + time_step * (lame_lambda * trace[..., None, :, :, :] + 2.0 * shear_modulus * strain[..., :3, :, :, :])
    shear = stress_now[..., 3:, :, :, :] + time_step * shear_modulus * strain[..., 3:, :, :, :]
    return jnp.concatenate([normal, shear], axis=-4)


def image_terms(strain_fwd, stress_adj, accel_fwd, velocity_adj):
    trace_fwd = strain_fwd[..., 0, :, :, :] + strain_fwd[..., 1, :, :, :] + strain_fwd[..., 2, :, :, :]
    trace_adj = stress_adj[..., 0, :, :, :] + stress_adj[..., 1, :, :, :] + stress_adj[..., 2, :, :, :]
    grad_lambda = -time_step * trace_fwd * trace_adj
    grad_shear = -time_step * jnp.sum(strain_fwd * stress_adj, axis=-4)
    grad_density = -time_step * jnp.sum(accel_fwd * velocity_adj, axis=-4)
    return jnp.stack([grad_lambda, grad_shear, grad_density], axis=-4)


def pad_cells(values):
    return jnp.pad(values, [(0, 0)] * (values.ndim - 3) + [(2, 2), (2, 2), (2, 2)])


def reference(forward_fields, adjoint_fields, lame_lambda, shear_modulus, density, source_cell, source_amp, receiver_cell, residual_amp):
    buoyancy = 1.0 / density
    cell_count = NX * NY * NZ
    margin = (2, 2, 2)

    def one_shot(summed, inputs):
        forward, adjoint, source, amount, receivers, values = inputs
        forward = forward.reshape(9, cell_count).at[3:6, source].add(amount).reshape(9, NX, NY, NZ)
        adjoint = adjoint.reshape(9, cell_count).at[3:6, receivers].add(values[None, :]).reshape(9, NX, NY, NZ)
        wavefields = jnp.stack([forward, adjoint])
        acceleration = accelerate(pad_cells(wavefields[:, 3:]), buoyancy, margin, (0, 0, 0))
        velocity = wavefields[:, :3] + time_step * acceleration
        strain = strain_rates(pad_cells(velocity), margin)
        stress = new_stress(wavefields[:, 3:], strain, lame_lambda, shear_modulus)
        summed = summed + image_terms(strain[0], stress[1], acceleration[0], velocity[1])
        stepped = jnp.concatenate([velocity, stress], axis=1)
        return summed, (stepped[0], stepped[1])

    start = jnp.zeros((3, NX, NY, NZ), jnp.float32)
    summed, outputs = lax.scan(one_shot, start, (forward_fields, adjoint_fields, source_cell, source_amp, receiver_cell, residual_amp))
    return outputs[0], outputs[1], summed
```

```python
import functools

import jax
import jax.numpy as jnp
from jax import lax
from jax.experimental import pallas as pl
from jax.experimental.pallas import tpu as pltpu
from jax.sharding import PartitionSpec as P

near = 9.0 / 8.0
far = -1.0 / 24.0
time_step = 0.15

LAYERS = 2
ROWS = 8
SLOTS = 5

STRESS_ALONG = ((0, 3, 4), (1, 3, 5))
ACCEL_OF = ((0, 1, 2), (1, 0, 2))
VELOCITY_ALONG = ((0, 1, 2), (1, 0, 2))
STRAIN_OF = ((0, 3, 4), (1, 3, 5))

vmem = pl.BlockSpec(memory_space=pltpu.VMEM)
smem = pl.BlockSpec(memory_space=pltpu.SMEM)
anywhere = pl.BlockSpec(memory_space=pl.ANY)
params = pltpu.CompilerParams(vmem_limit_bytes=24 * 1024 * 1024)


def links_of(sizes):
    return [
        (name, dim, first)
        for dim, name in enumerate(("tx", "ty"))
        for first in (0, 1)
        if first + 1 < sizes[name]
    ]


def swap(value, axis, first):
    pairs = [(i, i + 1) for i in range(first, lax.axis_size(axis) - 1, 2)]
    return lax.ppermute(value, axis, pairs + [(j, i) for i, j in pairs])


def is_lower(axis, first):
    return lax.axis_index(axis) % 2 == first


def has_peer(axis, first):
    index = lax.axis_index(axis)
    partner = jnp.where(is_lower(axis, first), index + 1, index - 1)
    return (partner >= 0) & (partner < lax.axis_size(axis))


def pack_kernel(links, *refs):
    fields = refs[:2]
    sends = refs[2 : 2 + len(links)]
    edge, sems = refs[2 + len(links) :]
    _, tile_x, tile_y, _ = fields[0].shape
    copies = []

    def copy(source, target):
        started = pltpu.make_async_copy(source, target, sems.at[len(copies)])
        started.start()
        copies.append(started)

    for wave in range(2):
        for slot, part in enumerate(STRESS_ALONG[1]):
            for side, row in enumerate((0, tile_y - 8)):
                copy(fields[wave].at[3 + part, :, pl.ds(row, 8), :], edge.at[wave, slot, side])
    for (axis, dim, first), send in zip(links, sends):
        if dim == 1:
            continue
        lower = is_lower(axis, first)
        normal, one, two = (3 + part for part in STRESS_ALONG[0])
        last = tile_x - 1
        for wave in range(2):
            for slot, (upper_part, upper_layer, lower_part, lower_layer) in enumerate((
                (normal, 0, normal, last),
                (normal, 1, one, last - 1),
                (one, 0, one, last),
                (two, 0, two, last - 1),
                (two, 1, two, last),
            )):
                part = jnp.where(lower, lower_part, upper_part)
                layer = jnp.where(lower, lower_layer, upper_layer)
                copy(fields[wave].at[part, layer], send.at[wave, slot])
    for started in copies:
        started.wait()
    rows = edge.reshape(2, 3, 2, tile_x * 8, edge.shape[-1])

    def row_of(wave, part, row):
        side, at = (0, row) if row < 8 else (1, row - (tile_y - 8))
        return rows[wave, part, side, pl.ds(at, tile_x, stride=8), :]

    last = tile_y - 1
    for (axis, dim, first), send in zip(links, sends):
        if dim == 0:
            continue
        lower = is_lower(axis, first)
        for wave in range(2):
            for slot, (upper_part, upper_row, lower_part, lower_row) in enumerate((
                (0, 0, 0, last),
                (0, 1, 1, last - 1),
                (1, 0, 1, last),
                (2, 0, 2, last - 1),
                (2, 1, 2, last),
            )):
                send[wave, slot] = jnp.where(
                    lower, row_of(wave, lower_part, lower_row), row_of(wave, upper_part, upper_row)
                )


def column_ids(tile_x, tile_y, width_y, lanes):
    x_start = lax.axis_index("tx") * tile_x
    y_start = lax.axis_index("ty") * tile_y

    def column(x, y):
        inside = (y >= 0) & (y < width_y)
        return jnp.where(inside, x * width_y + y, -1)

    def iota(shape, dim):
        return lax.broadcasted_iota(jnp.int32, shape, dim)

    shape = (tile_x, tile_y, lanes)
    tile = column(x_start + iota(shape, 0), y_start + iota(shape, 1))
    shape = (3, tile_y, lanes)
    layer = iota(shape, 0)
    along_x = column(
        x_start + jnp.where(layer == 0, -1, tile_x - 1 + layer), y_start + iota(shape, 1)
    )
    shape = (3, tile_x, lanes)
    layer = iota(shape, 0)
    along_y = column(
        x_start + iota(shape, 1), y_start + jnp.where(layer == 0, -1, tile_y - 1 + layer)
    )
    return jnp.concatenate([part.reshape(-1, lanes) for part in (tile, along_x, along_y)], axis=0)


def differ(zero, one, two, minus):
    return near * (one - zero) + far * (two - minus)


def along_x(ref, part, x, tile_y, upward):
    def at(offset):
        return ref[part, x + (LAYERS + offset), pl.ds(ROWS, tile_y), :]

    return differ(at(0), at(1), at(2), at(-1)) if upward else differ(at(-1), at(0), at(1), at(-2))


def along_y(ref, part, x, tile_y, upward):
    def at(offset):
        return ref[part, x + LAYERS, pl.ds(ROWS + offset, tile_y), :]

    return differ(at(0), at(1), at(2), at(-1)) if upward else differ(at(-1), at(0), at(1), at(-2))


def along_z(ref, part, x, tile_y, upward):
    value = ref[part, x + LAYERS, pl.ds(ROWS, tile_y), :]
    depth = value.shape[-1]
    lane = lax.broadcasted_iota(jnp.int32, value.shape, 1)

    def at(offset):
        if offset == 0:
            return value
        moved = pltpu.roll(value, (-offset) % depth, 1)
        inside = lane < depth - offset if offset > 0 else lane >= -offset
        return jnp.where(inside, moved, 0.0)

    return differ(at(0), at(1), at(2), at(-1)) if upward else differ(at(-1), at(0), at(1), at(-2))


def clear_rim(ref, tile_x, tile_y):
    parts, layers, rows, depth = ref.shape
    for part in range(parts):
        for layer in (*range(LAYERS), *range(LAYERS + tile_x, layers)):
            ref[part, layer] = jnp.zeros((rows, depth), jnp.float32)
        for row in (0, ROWS + tile_y):
            ref[part, pl.ds(LAYERS, tile_x), pl.ds(row, ROWS), :] = jnp.zeros(
                (tile_x, ROWS, depth), jnp.float32
            )


def velocity_kernel(
    width_y,
    source_cell,
    source_amp,
    receiver_cell,
    residual_amp,
    forward,
    adjoint,
    lame,
    shear,
    density,
    stress,
    velocity,
    accel,
    rim_added,
    buoyancy,
    scaled_lame,
    scaled_shear,
    added,
):
    _, tile_x, tile_y, depth = forward.shape
    receivers = receiver_cell.shape[-1]
    cells = tile_x * tile_y
    columns = column_ids(tile_x, tile_y, width_y, depth)
    lane = lax.broadcasted_iota(jnp.int32, columns.shape, 1)
    added[0] = jnp.where(columns * depth + lane == source_cell[0], source_amp[0], 0.0)
    where = receiver_cell[...]
    column = lax.div(where, depth)
    depth_of = where - column * depth
    columns = column_ids(tile_x, tile_y, width_y, receivers)
    column_hot = (columns == column).astype(jnp.float32)
    level = lax.broadcasted_iota(jnp.int32, (depth, receivers), 0)
    depth_hot = jnp.where(level == depth_of, residual_amp[...], 0.0)
    added[1] = lax.dot_general(
        column_hot,
        depth_hot,
        (((1,), (1,)), ((), ())),
        precision=lax.Precision.HIGHEST,
        preferred_element_type=jnp.float32,
    )
    for wave in range(2):
        for layer in range(3):
            rim_added[wave, 0, layer] = added[wave, pl.ds(cells + layer * tile_y, tile_y), :]
            rim_added[wave, 1, layer] = added[
                wave, pl.ds(cells + 3 * tile_y + layer * tile_x, tile_x), :
            ]
    clear_rim(stress, tile_x, tile_y)
    clear_rim(velocity, tile_x, tile_y)
    middle = pl.ds(ROWS, tile_y)

    def fill(x, carry):
        for wave, fields in enumerate((forward, adjoint)):
            extra = added[wave, pl.ds(pl.multiple_of(x * tile_y, 8), tile_y), :]
            for part in range(6):
                value = fields[3 + part, x]
                stress[6 * wave + part, x + LAYERS, middle, :] = (
                    value + extra if part < 3 else value
                )
        buoyancy[x] = 1.0 / density[x]
        scaled_lame[x] = time_step * lame[x]
        scaled_shear[x] = time_step * shear[x]
        return carry

    lax.fori_loop(0, tile_x, fill, 0)

    def layer(x, carry):
        light = buoyancy[x]
        for wave, fields in enumerate((forward, adjoint)):
            xx, yy, zz, xy, xz, yz = range(6 * wave, 6 * wave + 6)
            values = (
                along_x(stress, xx, x, tile_y, True)
                + along_y(stress, xy, x, tile_y, False)
                + along_z(stress, xz, x, tile_y, False),
                along_x(stress, xy, x, tile_y, False)
                + along_y(stress, yy, x, tile_y, True)
                + along_z(stress, yz, x, tile_y, False),
                along_x(stress, xz, x, tile_y, False)
                + along_y(stress, yz, x, tile_y, False)
                + along_z(stress, zz, x, tile_y, True),
            )
            for part, value in enumerate(values):
                value = light * value
                if wave == 0:
                    accel[part, x] = value
                velocity[3 * wave + part, x + LAYERS, middle, :] = (
                    fields[part, x] + time_step * value
                )
        return carry

    lax.fori_loop(0, tile_x, layer, 0)


def stress_halo_terms(links, received, rim_added, waves, add):
    for (axis, dim, first), halo in zip(links, received):
        part_n, part_a, part_b = ACCEL_OF[dim]
        lower = is_lower(axis, first)
        real = has_peer(axis, first)

        @pl.when(real & lower)
        def after():
            for wave in waves:
                n0 = halo[wave, 0] + rim_added[wave, dim, 1]
                n1 = halo[wave, 1] + rim_added[wave, dim, 2]
                add(wave, part_n, dim, -1, near * n0 + far * n1)
                add(wave, part_n, dim, -2, far * n0)
                add(wave, part_a, dim, -1, far * halo[wave, 2])
                add(wave, part_b, dim, -1, far * halo[wave, 3])

        @pl.when(real & jnp.logical_not(lower))
        def before():
            for wave in waves:
                n0 = halo[wave, 0] + rim_added[wave, dim, 0]
                add(wave, part_n, dim, 0, -far * n0)
                for part, slot in ((part_a, 1), (part_b, 3)):
                    outer, inner = halo[wave, slot], halo[wave, slot + 1]
                    add(wave, part, dim, 0, -near * inner - far * outer)
                    add(wave, part, dim, 1, -far * inner)


def velocity_halo_terms(links, received, add):
    for (axis, dim, first), halo in zip(links, received):
        part_n, part_a, part_b = STRAIN_OF[dim]
        lower = is_lower(axis, first)
        real = has_peer(axis, first)

        @pl.when(real & lower)
        def after():
            for wave in range(2):
                add(wave, part_n, dim, -1, far * halo[wave, 0])
                for part, slot in ((part_a, 1), (part_b, 3)):
                    inner, outer = halo[wave, slot], halo[wave, slot + 1]
                    add(wave, part, dim, -1, near * inner + far * outer)
                    add(wave, part, dim, -2, far * inner)

        @pl.when(real & jnp.logical_not(lower))
        def before():
            for wave in range(2):
                outer, inner = halo[wave, 0], halo[wave, 1]
                add(wave, part_n, dim, 0, -near * inner - far * outer)
                add(wave, part_n, dim, 1, -far * inner)
                add(wave, part_a, dim, 0, -far * halo[wave, 2])
                add(wave, part_b, dim, 0, -far * halo[wave, 3])


def face(ref, part, dim, index, padded):
    layers, rows, depth = ref.shape[1:]
    tile_x = layers - 2 * LAYERS if padded else layers
    tile_y = rows - 2 * ROWS if padded else rows
    if dim == 0:
        at = index % tile_x
        if padded:
            return ref.at[part, at + LAYERS, pl.ds(ROWS, tile_y), :]
        return ref.at[part, at]
    at = index % tile_y
    flat = ref.reshape(ref.shape[0], layers * rows, depth)
    begin = LAYERS * rows + ROWS + at if padded else at
    return flat.at[part, pl.ds(begin, tile_x, stride=rows), :]


def light_face(buoyancy, dim, index):
    layers, rows, depth = buoyancy.shape
    if dim == 0:
        return buoyancy[index % layers]
    return buoyancy.reshape(layers * rows, depth)[pl.ds(index % rows, layers, stride=rows), :]


def boundary_kernel(links, *refs):
    count = len(links)
    received = refs[:count]
    rim_added, buoyancy, _ = refs[count : count + 3]
    velocity = refs[count + 3]
    sends = refs[count + 4 :]

    def add(wave, part, dim, index, term):
        target = face(velocity, 3 * wave + part, dim, index, True)
        target[...] += time_step * light_face(buoyancy, dim, index) * term

    stress_halo_terms(links, received, rim_added, (0, 1), add)
    for (axis, dim, first), send in zip(links, sends):
        lower = is_lower(axis, first)
        n, a, b = VELOCITY_ALONG[dim]

        def put(plan):
            for wave in range(2):
                for slot, (part, index) in enumerate(plan):
                    send[wave, slot] = face(velocity, 3 * wave + part, dim, index, True)[...]

        @pl.when(lower)
        def up():
            put(((n, -2), (n, -1), (a, -1), (b, -1), (b, -1)))

        @pl.when(jnp.logical_not(lower))
        def down():
            put(((n, 0), (a, 0), (a, 1), (b, 0), (b, 1)))


def strain_kernel(links, *refs):
    count = len(links)
    received = refs[:count]
    rim_added, buoyancy, velocity, accel, strain, gradient, accel_now = refs[count:]
    tile_x, tile_y, _ = buoyancy.shape
    middle = pl.ds(ROWS, tile_y)
    accel_now[...] = accel[...]

    def add(wave, part, dim, index, term):
        target = face(accel_now, part, dim, index, False)
        target[...] += light_face(buoyancy, dim, index) * term

    stress_halo_terms(links, received, rim_added, (0,), add)

    def layer(x, carry):
        for wave in range(2):
            vx, vy, vz = range(3 * wave, 3 * wave + 3)
            values = (
                along_x(velocity, vx, x, tile_y, False),
                along_y(velocity, vy, x, tile_y, False),
                along_z(velocity, vz, x, tile_y, False),
                along_y(velocity, vx, x, tile_y, True) + along_x(velocity, vy, x, tile_y, True),
                along_z(velocity, vx, x, tile_y, True) + along_x(velocity, vz, x, tile_y, True),
                along_z(velocity, vy, x, tile_y, True) + along_y(velocity, vz, x, tile_y, True),
            )
            for part, value in enumerate(values):
                strain[6 * wave + part, x] = value
        total = sum(
            accel_now[part, x] * velocity[3 + part, x + LAYERS, middle, :] for part in range(3)
        )
        gradient[2, x] = -time_step * total
        return carry

    lax.fori_loop(0, tile_x, layer, 0)


def new_stress(strain, stress, scaled_lame, scaled_shear, wave, x, tile_y):
    lame, shear = scaled_lame[x], scaled_shear[x]
    strains = [strain[6 * wave + part, x] for part in range(6)]
    volume = lame * (strains[0] + strains[1] + strains[2])
    values = []
    for part in range(6):
        old = stress[6 * wave + part, x + LAYERS, pl.ds(ROWS, tile_y), :]
        if part < 3:
            values.append(old + (volume + 2.0 * shear * strains[part]))
        else:
            values.append(old + shear * strains[part])
    return strains, values


def gradient_kernel(links, *refs):
    count = len(links)
    received = refs[:count]
    stress, scaled_lame, scaled_shear, _, _, strain, gradient = refs[count:]
    tile_x, tile_y, _ = scaled_lame.shape

    def add(wave, part, dim, index, term):
        target = face(strain, 6 * wave + part, dim, index, False)
        target[...] += term

    velocity_halo_terms(links, received, add)

    def layer(x, carry):
        strains = [strain[part, x] for part in range(6)]
        _, values = new_stress(strain, stress, scaled_lame, scaled_shear, 1, x, tile_y)
        trace = strains[0] + strains[1] + strains[2]
        gradient[0, x] = -time_step * trace * (values[0] + values[1] + values[2])
        total = sum(left * right for left, right in zip(strains, values))
        gradient[1, x] = -time_step * total
        return carry

    lax.fori_loop(0, tile_x, layer, 0)


def output_kernel(velocity, strain, stress, scaled_lame, scaled_shear, forward, adjoint):
    layers, tile_y = forward.shape[1:3]
    begin = pl.program_id(0) * layers
    for at in range(layers):
        x = begin + at
        for wave, out in enumerate((forward, adjoint)):
            for part in range(3):
                out[part, at] = velocity[3 * wave + part, x + LAYERS, pl.ds(ROWS, tile_y), :]
            _, values = new_stress(strain, stress, scaled_lame, scaled_shear, wave, x, tile_y)
            for part in range(6):
                out[3 + part, at] = values[part]


def cost(flops, size):
    return pl.CostEstimate(flops=flops, bytes_accessed=size, transcendentals=0)


def body(
    forward_fields,
    adjoint_fields,
    lame_lambda,
    shear_modulus,
    density,
    source_cell,
    source_amp,
    receiver_cell,
    residual_amp,
):
    _, _, tile_x, tile_y, depth = forward_fields.shape
    forward = forward_fields.reshape(forward_fields.shape[1:])
    adjoint = adjoint_fields.reshape(adjoint_fields.shape[1:])
    sizes = {name: lax.axis_size(name) for name in ("tx", "ty")}
    width_y = tile_y * sizes["ty"]
    links = links_of(sizes)
    cells = tile_x * tile_y * depth
    rims = 3 * tile_x + 3 * tile_y

    def buffers(dim):
        return pltpu.VMEM((2, SLOTS, tile_y if dim == 0 else tile_x, depth), jnp.float32)

    def tile(*lead):
        return pltpu.VMEM((*lead, tile_x, tile_y, depth), jnp.float32)

    def padded(parts):
        return pltpu.VMEM(
            (parts, tile_x + 2 * LAYERS, tile_y + 2 * ROWS, depth), jnp.float32
        )

    def exchange(sends):
        return [swap(send, axis, first) for (axis, _, first), send in zip(links, sends)]

    send_shapes = [buffers(dim) for _, dim, _ in links]
    sends = pl.pallas_call(
        functools.partial(pack_kernel, links),
        out_shape=send_shapes,
        in_specs=[anywhere] * 2,
        out_specs=[vmem] * len(links),
        scratch_shapes=[
            pltpu.VMEM((2, 3, 2, tile_x, 8, depth), jnp.float32),
            pltpu.SemaphoreType.DMA((12 + 10 * len(links),)),
        ],
        compiler_params=params,
        cost_estimate=cost(0, 10 * 2 * tile_x * depth * 4),
        name="pack",
    )(forward, adjoint)
    halos = exchange(sends)

    stress, velocity, accel, rim_added, buoyancy, scaled_lame, scaled_shear = pl.pallas_call(
        functools.partial(velocity_kernel, width_y),
        out_shape=[
            padded(12),
            padded(6),
            tile(3),
            pltpu.VMEM((2, 2, 3, max(tile_x, tile_y), depth), jnp.float32),
            tile(),
            tile(),
            tile(),
        ],
        in_specs=[smem] * 2 + [vmem] * 7,
        out_specs=[vmem] * 7,
        scratch_shapes=[pltpu.VMEM((2, tile_x * tile_y + rims, depth), jnp.float32)],
        compiler_params=params,
        cost_estimate=cost(200 * cells, 18 * 4 * cells),
        name="velocity",
    )(
        source_cell,
        source_amp,
        receiver_cell,
        residual_amp,
        forward,
        adjoint,
        lame_lambda,
        shear_modulus,
        density,
    )

    count = len(links)
    velocity, *sends = pl.pallas_call(
        functools.partial(boundary_kernel, links),
        out_shape=[padded(6)] + send_shapes,
        in_specs=[vmem] * (count + 3),
        out_specs=[vmem] * (count + 1),
        input_output_aliases={count + 2: 0},
        compiler_params=params,
        cost_estimate=cost(cells, 10 * 2 * tile_x * depth * 4),
        name="boundary",
    )(*halos, rim_added, buoyancy, velocity)
    velocity_halos = exchange(sends)

    strain, gradient = pl.pallas_call(
        functools.partial(strain_kernel, links),
        out_shape=[tile(12), tile(3)],
        in_specs=[vmem] * (count + 4),
        out_specs=[vmem] * 2,
        scratch_shapes=[tile(3)],
        compiler_params=params,
        cost_estimate=cost(200 * cells, 18 * 4 * cells),
        name="strain",
    )(*halos, rim_added, buoyancy, velocity, accel)

    strain, gradient = pl.pallas_call(
        functools.partial(gradient_kernel, links),
        out_shape=[tile(12), tile(3)],
        in_specs=[vmem] * (count + 5),
        out_specs=[vmem] * 2,
        input_output_aliases={count + 3: 0, count + 4: 1},
        compiler_params=params,
        cost_estimate=cost(30 * cells, 2 * 4 * cells),
        name="gradient",
    )(*velocity_halos, stress, scaled_lame, scaled_shear, strain, gradient)
    other = lax.ppermute(gradient, "shot", [(0, 1), (1, 0)])

    step = 4 if tile_x % 4 == 0 else 1
    out_block = pl.BlockSpec((9, step, tile_y, depth), lambda i: (0, i, 0, 0))
    forward_next, adjoint_next = pl.pallas_call(
        output_kernel,
        grid=(tile_x // step,),
        out_shape=[jax.ShapeDtypeStruct(forward.shape, jnp.float32)] * 2,
        in_specs=[vmem] * 5,
        out_specs=[out_block] * 2,
        compiler_params=params,
        cost_estimate=cost(60 * cells, 18 * 4 * cells),
        name="outputs",
    )(velocity, strain, stress, scaled_lame, scaled_shear)
    return forward_next[None], adjoint_next[None], gradient + other


def solution(mesh):
    return jax.shard_map(
        body,
        mesh=mesh,
        in_specs=(
            P("shot", None, "tx", "ty", None),
            P("shot", None, "tx", "ty", None),
            P("tx", "ty", None),
            P("tx", "ty", None),
            P("tx", "ty", None),
            P("shot"),
            P("shot"),
            P("shot", None),
            P("shot", None),
        ),
        out_specs=(
            P("shot", None, "tx", "ty", None),
            P("shot", None, "tx", "ty", None),
            P(None, "tx", "ty", None),
        ),
        check_vma=False,
    )
```

```python
import functools

import jax
import jax.numpy as jnp
from jax import lax
from jax.experimental import pallas as pl
from jax.experimental.pallas import tpu as pltpu
from jax.sharding import PartitionSpec as P

near = 9.0 / 8.0
far = -1.0 / 24.0
time_step = 0.15

LAYERS = 2
ROWS = 8
SLOTS = 5

STRESS_ALONG = ((0, 3, 4), (1, 3, 5))
ACCEL_OF = ((0, 1, 2), (1, 0, 2))
VELOCITY_ALONG = ((0, 1, 2), (1, 0, 2))
STRAIN_OF = ((0, 3, 4), (1, 3, 5))

vmem = pl.BlockSpec(memory_space=pltpu.VMEM)
smem = pl.BlockSpec(memory_space=pltpu.SMEM)
hbm = pl.BlockSpec(memory_space=pltpu.HBM)
params = pltpu.CompilerParams(vmem_limit_bytes=24 * 1024 * 1024)


def links_of(sizes):
    order = (("ty", 1, 1), ("tx", 0, 1), ("tx", 0, 0), ("ty", 1, 0))
    return [(name, dim, first) for name, dim, first in order if first + 1 < sizes[name]]


def swap(value, axis, first):
    pairs = [(i, i + 1) for i in range(first, lax.axis_size(axis) - 1, 2)]
    return lax.ppermute(value, axis, pairs + [(j, i) for i, j in pairs])


def is_lower(axis, first):
    return lax.axis_index(axis) % 2 == first


def has_peer(axis, first):
    index = lax.axis_index(axis)
    partner = jnp.where(is_lower(axis, first), index + 1, index - 1)
    return (partner >= 0) & (partner < lax.axis_size(axis))


def pack_kernel(links, *refs):
    fields = refs[:2]
    sends = refs[2 : 2 + len(links)]
    edge, sems = refs[2 + len(links) :]
    _, tile_x, tile_y, _ = fields[0].shape
    copies = []

    def copy(source, target):
        started = pltpu.make_async_copy(source, target, sems.at[len(copies)])
        started.start()
        copies.append(started)

    for wave in range(2):
        for slot, part in enumerate(STRESS_ALONG[1]):
            for side, row in enumerate((0, tile_y - 8)):
                copy(fields[wave].at[3 + part, :, pl.ds(row, 8), :], edge.at[wave, slot, side])
    for (axis, dim, first), send in zip(links, sends):
        if dim == 1:
            continue
        lower = is_lower(axis, first)
        normal, one, two = (3 + part for part in STRESS_ALONG[0])
        last = tile_x - 1
        for wave in range(2):
            for slot, (upper_part, upper_layer, lower_part, lower_layer) in enumerate((
                (normal, 0, normal, last),
                (normal, 1, one, last - 1),
                (one, 0, one, last),
                (two, 0, two, last - 1),
                (two, 1, two, last),
            )):
                part = jnp.where(lower, lower_part, upper_part)
                layer = jnp.where(lower, lower_layer, upper_layer)
                copy(fields[wave].at[part, layer], send.at[wave, slot])
    for started in copies:
        started.wait()
    rows = edge.reshape(2, 3, 2, tile_x * 8, edge.shape[-1])

    def row_of(wave, part, row):
        side, at = (0, row) if row < 8 else (1, row - (tile_y - 8))
        return rows[wave, part, side, pl.ds(at, tile_x, stride=8), :]

    last = tile_y - 1
    for (axis, dim, first), send in zip(links, sends):
        if dim == 0:
            continue
        lower = is_lower(axis, first)
        for wave in range(2):
            for slot, (upper_part, upper_row, lower_part, lower_row) in enumerate((
                (0, 0, 0, last),
                (0, 1, 1, last - 1),
                (1, 0, 1, last),
                (2, 0, 2, last - 1),
                (2, 1, 2, last),
            )):
                send[wave, slot] = jnp.where(
                    lower, row_of(wave, lower_part, lower_row), row_of(wave, upper_part, upper_row)
                )


def column_ids(tile_x, tile_y, width_y, lanes):
    x_start = lax.axis_index("tx") * tile_x
    y_start = lax.axis_index("ty") * tile_y

    def column(x, y):
        inside = (y >= 0) & (y < width_y)
        return jnp.where(inside, x * width_y + y, -1)

    def iota(shape, dim):
        return lax.broadcasted_iota(jnp.int32, shape, dim)

    shape = (tile_x, tile_y, lanes)
    tile = column(x_start + iota(shape, 0), y_start + iota(shape, 1))
    shape = (3, tile_y, lanes)
    layer = iota(shape, 0)
    along_x = column(
        x_start + jnp.where(layer == 0, -1, tile_x - 1 + layer), y_start + iota(shape, 1)
    )
    shape = (3, tile_x, lanes)
    layer = iota(shape, 0)
    along_y = column(
        x_start + iota(shape, 1), y_start + jnp.where(layer == 0, -1, tile_y - 1 + layer)
    )
    return jnp.concatenate([part.reshape(-1, lanes) for part in (tile, along_x, along_y)], axis=0)


def differ(zero, one, two, minus):
    return near * (one - zero) + far * (two - minus)


def along_x(ref, part, x, tile_y, upward):
    def at(offset):
        return ref[part, x + (LAYERS + offset), pl.ds(ROWS, tile_y), :]

    return differ(at(0), at(1), at(2), at(-1)) if upward else differ(at(-1), at(0), at(1), at(-2))


def along_y(ref, part, x, tile_y, upward):
    def at(offset):
        return ref[part, x + LAYERS, pl.ds(ROWS + offset, tile_y), :]

    return differ(at(0), at(1), at(2), at(-1)) if upward else differ(at(-1), at(0), at(1), at(-2))


def along_z(ref, part, x, tile_y, upward):
    value = ref[part, x + LAYERS, pl.ds(ROWS, tile_y), :]
    depth = value.shape[-1]
    lane = lax.broadcasted_iota(jnp.int32, value.shape, 1)

    def at(offset):
        if offset == 0:
            return value
        moved = pltpu.roll(value, (-offset) % depth, 1)
        inside = lane < depth - offset if offset > 0 else lane >= -offset
        return jnp.where(inside, moved, 0.0)

    return differ(at(0), at(1), at(2), at(-1)) if upward else differ(at(-1), at(0), at(1), at(-2))


def clear_rim(ref, tile_x, tile_y):
    parts, layers, rows, depth = ref.shape
    for part in range(parts):
        for layer in (*range(LAYERS), *range(LAYERS + tile_x, layers)):
            ref[part, layer] = jnp.zeros((rows, depth), jnp.float32)
        for row in (0, ROWS + tile_y):
            ref[part, pl.ds(LAYERS, tile_x), pl.ds(row, ROWS), :] = jnp.zeros(
                (tile_x, ROWS, depth), jnp.float32
            )


def velocity_kernel(
    width_y,
    lame,
    shear,
    density,
    source_cell,
    source_amp,
    receiver_cell,
    residual_amp,
    forward,
    adjoint,
    stress,
    velocity,
    accel,
    rim_added,
    buoyancy,
    scaled_lame,
    scaled_shear,
    added,
    lame_now,
    shear_now,
    density_now,
    sems,
):
    _, tile_x, tile_y, depth = forward.shape
    receivers = receiver_cell.shape[-1]
    cells = tile_x * tile_y
    copies = [
        pltpu.make_async_copy(source, target, sems.at[at])
        for at, (source, target) in enumerate((
            (density, density_now),
            (lame, lame_now),
            (shear, shear_now),
        ))
    ]
    for copy in copies:
        copy.start()
    where = receiver_cell[...]
    column = lax.div(where, depth)
    depth_of = where - column * depth
    columns = column_ids(tile_x, tile_y, width_y, depth)
    column_hot = jnp.concatenate(
        [
            (columns == column[:, begin : begin + depth]).astype(jnp.bfloat16)
            for begin in range(0, receivers, depth)
        ],
        axis=1,
    )
    level = lax.broadcasted_iota(jnp.int32, (depth, receivers), 0)
    rest = jnp.where(level == depth_of, residual_amp[...], 0.0)
    total = jnp.zeros(columns.shape, jnp.float32)
    for _ in range(3):
        part = rest.astype(jnp.bfloat16)
        rest = rest - part.astype(jnp.float32)
        total = total + lax.dot_general(
            column_hot,
            part,
            (((1,), (1,)), ((), ())),
            preferred_element_type=jnp.float32,
        )
    added[1] = total
    lane = lax.broadcasted_iota(jnp.int32, columns.shape, 1)
    added[0] = jnp.where(columns * depth + lane == source_cell[0], source_amp[0], 0.0)
    for copy in copies:
        copy.wait()
    for wave in range(2):
        for layer in range(3):
            rim_added[wave, 0, layer] = added[wave, pl.ds(cells + layer * tile_y, tile_y), :]
            rim_added[wave, 1, layer] = added[
                wave, pl.ds(cells + 3 * tile_y + layer * tile_x, tile_x), :
            ]
    clear_rim(stress, tile_x, tile_y)
    clear_rim(velocity, tile_x, tile_y)
    middle = pl.ds(ROWS, tile_y)

    def fill(x, carry):
        for wave, fields in enumerate((forward, adjoint)):
            extra = added[wave, pl.ds(pl.multiple_of(x * tile_y, 8), tile_y), :]
            for part in range(6):
                value = fields[3 + part, x]
                stress[6 * wave + part, x + LAYERS, middle, :] = (
                    value + extra if part < 3 else value
                )
        buoyancy[x] = 1.0 / density_now[x]
        scaled_lame[x] = time_step * lame_now[x]
        scaled_shear[x] = time_step * shear_now[x]
        return carry

    lax.fori_loop(0, tile_x, fill, 0, unroll=4)

    def layer(x, carry):
        light = buoyancy[x]
        for wave, fields in enumerate((forward, adjoint)):
            xx, yy, zz, xy, xz, yz = range(6 * wave, 6 * wave + 6)
            values = (
                along_x(stress, xx, x, tile_y, True)
                + along_y(stress, xy, x, tile_y, False)
                + along_z(stress, xz, x, tile_y, False),
                along_x(stress, xy, x, tile_y, False)
                + along_y(stress, yy, x, tile_y, True)
                + along_z(stress, yz, x, tile_y, False),
                along_x(stress, xz, x, tile_y, False)
                + along_y(stress, yz, x, tile_y, False)
                + along_z(stress, zz, x, tile_y, True),
            )
            for part, value in enumerate(values):
                value = light * value
                if wave == 0:
                    accel[part, x] = value
                velocity[3 * wave + part, x + LAYERS, middle, :] = (
                    fields[part, x] + time_step * value
                )
        return carry

    lax.fori_loop(0, tile_x, layer, 0, unroll=4)


def stress_halo_terms(links, received, rim_added, waves, add):
    for (axis, dim, first), halo in zip(links, received):
        part_n, part_a, part_b = ACCEL_OF[dim]
        lower = is_lower(axis, first)
        real = has_peer(axis, first)

        @pl.when(real & lower)
        def after():
            for wave in waves:
                n0 = halo[wave, 0] + rim_added[wave, dim, 1]
                n1 = halo[wave, 1] + rim_added[wave, dim, 2]
                add(wave, part_n, dim, -1, near * n0 + far * n1)
                add(wave, part_n, dim, -2, far * n0)
                add(wave, part_a, dim, -1, far * halo[wave, 2])
                add(wave, part_b, dim, -1, far * halo[wave, 3])

        @pl.when(real & jnp.logical_not(lower))
        def before():
            for wave in waves:
                n0 = halo[wave, 0] + rim_added[wave, dim, 0]
                add(wave, part_n, dim, 0, -far * n0)
                for part, slot in ((part_a, 1), (part_b, 3)):
                    outer, inner = halo[wave, slot], halo[wave, slot + 1]
                    add(wave, part, dim, 0, -near * inner - far * outer)
                    add(wave, part, dim, 1, -far * inner)


def velocity_halo_terms(links, received, add):
    for (axis, dim, first), halo in zip(links, received):
        part_n, part_a, part_b = STRAIN_OF[dim]
        lower = is_lower(axis, first)
        real = has_peer(axis, first)

        @pl.when(real & lower)
        def after():
            for wave in range(2):
                add(wave, part_n, dim, -1, far * halo[wave, 0])
                for part, slot in ((part_a, 1), (part_b, 3)):
                    inner, outer = halo[wave, slot], halo[wave, slot + 1]
                    add(wave, part, dim, -1, near * inner + far * outer)
                    add(wave, part, dim, -2, far * inner)

        @pl.when(real & jnp.logical_not(lower))
        def before():
            for wave in range(2):
                outer, inner = halo[wave, 0], halo[wave, 1]
                add(wave, part_n, dim, 0, -near * inner - far * outer)
                add(wave, part_n, dim, 1, -far * inner)
                add(wave, part_a, dim, 0, -far * halo[wave, 2])
                add(wave, part_b, dim, 0, -far * halo[wave, 3])


def face(ref, part, dim, index, padded):
    layers, rows, depth = ref.shape[1:]
    tile_x = layers - 2 * LAYERS if padded else layers
    tile_y = rows - 2 * ROWS if padded else rows
    if dim == 0:
        at = index % tile_x
        if padded:
            return ref.at[part, at + LAYERS, pl.ds(ROWS, tile_y), :]
        return ref.at[part, at]
    at = index % tile_y
    flat = ref.reshape(ref.shape[0], layers * rows, depth)
    begin = LAYERS * rows + ROWS + at if padded else at
    return flat.at[part, pl.ds(begin, tile_x, stride=rows), :]


def light_face(buoyancy, dim, index):
    layers, rows, depth = buoyancy.shape
    if dim == 0:
        return buoyancy[index % layers]
    return buoyancy.reshape(layers * rows, depth)[pl.ds(index % rows, layers, stride=rows), :]


def boundary_kernel(links, *refs):
    count = len(links)
    received = refs[:count]
    rim_added, buoyancy, _ = refs[count : count + 3]
    velocity = refs[count + 3]
    sends = refs[count + 4 :]

    def add(wave, part, dim, index, term):
        target = face(velocity, 3 * wave + part, dim, index, True)
        target[...] += time_step * light_face(buoyancy, dim, index) * term

    stress_halo_terms(links, received, rim_added, (0, 1), add)
    for (axis, dim, first), send in zip(links, sends):
        lower = is_lower(axis, first)
        n, a, b = VELOCITY_ALONG[dim]

        def put(plan):
            for wave in range(2):
                for slot, (part, index) in enumerate(plan):
                    send[wave, slot] = face(velocity, 3 * wave + part, dim, index, True)[...]

        @pl.when(lower)
        def up():
            put(((n, -2), (n, -1), (a, -1), (b, -1), (b, -1)))

        @pl.when(jnp.logical_not(lower))
        def down():
            put(((n, 0), (a, 0), (a, 1), (b, 0), (b, 1)))


def strain_kernel(links, *refs):
    count = len(links)
    received = refs[:count]
    rim_added, buoyancy, velocity, accel, strain, gradient, accel_now = refs[count:]
    tile_x, tile_y, _ = buoyancy.shape
    middle = pl.ds(ROWS, tile_y)
    accel_now[...] = accel[...]

    def add(wave, part, dim, index, term):
        target = face(accel_now, part, dim, index, False)
        target[...] += light_face(buoyancy, dim, index) * term

    stress_halo_terms(links, received, rim_added, (0,), add)

    def layer(x, carry):
        for wave in range(2):
            vx, vy, vz = range(3 * wave, 3 * wave + 3)
            values = (
                along_x(velocity, vx, x, tile_y, False),
                along_y(velocity, vy, x, tile_y, False),
                along_z(velocity, vz, x, tile_y, False),
                along_y(velocity, vx, x, tile_y, True) + along_x(velocity, vy, x, tile_y, True),
                along_z(velocity, vx, x, tile_y, True) + along_x(velocity, vz, x, tile_y, True),
                along_z(velocity, vy, x, tile_y, True) + along_y(velocity, vz, x, tile_y, True),
            )
            for part, value in enumerate(values):
                strain[6 * wave + part, x] = value
        total = sum(
            accel_now[part, x] * velocity[3 + part, x + LAYERS, middle, :] for part in range(3)
        )
        gradient[2, x] = -time_step * total
        return carry

    lax.fori_loop(0, tile_x, layer, 0, unroll=4)


def new_stress(strain, stress, scaled_lame, scaled_shear, wave, x, tile_y):
    lame, shear = scaled_lame[x], scaled_shear[x]
    strains = [strain[6 * wave + part, x] for part in range(6)]
    volume = lame * (strains[0] + strains[1] + strains[2])
    values = []
    for part in range(6):
        old = stress[6 * wave + part, x + LAYERS, pl.ds(ROWS, tile_y), :]
        if part < 3:
            values.append(old + (volume + 2.0 * shear * strains[part]))
        else:
            values.append(old + shear * strains[part])
    return strains, values


def gradient_kernel(links, *refs):
    count = len(links)
    received = refs[:count]
    stress, scaled_lame, scaled_shear, _, _, strain, gradient = refs[count:]
    tile_x, tile_y, _ = scaled_lame.shape

    def add(wave, part, dim, index, term):
        target = face(strain, 6 * wave + part, dim, index, False)
        target[...] += term

    velocity_halo_terms(links, received, add)

    def layer(x, carry):
        strains = [strain[part, x] for part in range(6)]
        _, values = new_stress(strain, stress, scaled_lame, scaled_shear, 1, x, tile_y)
        trace = strains[0] + strains[1] + strains[2]
        gradient[0, x] = -time_step * trace * (values[0] + values[1] + values[2])
        total = sum(left * right for left, right in zip(strains, values))
        gradient[1, x] = -time_step * total
        return carry

    lax.fori_loop(0, tile_x, layer, 0, unroll=4)


def output_kernel(velocity, strain, stress, scaled_lame, scaled_shear, forward, adjoint):
    layers, tile_y = forward.shape[1:3]
    begin = pl.program_id(0) * layers
    for at in range(layers):
        x = begin + at
        for wave, out in enumerate((forward, adjoint)):
            for part in range(3):
                out[part, at] = velocity[3 * wave + part, x + LAYERS, pl.ds(ROWS, tile_y), :]
            _, values = new_stress(strain, stress, scaled_lame, scaled_shear, wave, x, tile_y)
            for part in range(6):
                out[3 + part, at] = values[part]


def in_hbm(value):
    return pltpu.with_memory_space_constraint(value, pltpu.HBM)


def cost(flops, size):
    return pl.CostEstimate(flops=flops, bytes_accessed=size, transcendentals=0)


def body(
    forward_fields,
    adjoint_fields,
    lame_lambda,
    shear_modulus,
    density,
    source_cell,
    source_amp,
    receiver_cell,
    residual_amp,
):
    _, _, tile_x, tile_y, depth = forward_fields.shape
    forward = forward_fields.reshape(forward_fields.shape[1:])
    adjoint = adjoint_fields.reshape(adjoint_fields.shape[1:])
    sizes = {name: lax.axis_size(name) for name in ("tx", "ty")}
    width_y = tile_y * sizes["ty"]
    links = links_of(sizes)
    cells = tile_x * tile_y * depth
    rims = 3 * tile_x + 3 * tile_y

    def buffers(dim):
        return pltpu.VMEM((2, SLOTS, tile_y if dim == 0 else tile_x, depth), jnp.float32)

    def tile(*lead):
        return pltpu.VMEM((*lead, tile_x, tile_y, depth), jnp.float32)

    def padded(parts):
        return pltpu.VMEM(
            (parts, tile_x + 2 * LAYERS, tile_y + 2 * ROWS, depth), jnp.float32
        )

    def exchange(sends):
        return [swap(send, axis, first) for (axis, _, first), send in zip(links, sends)]

    send_shapes = [buffers(dim) for _, dim, _ in links]
    sends = pl.pallas_call(
        functools.partial(pack_kernel, links),
        out_shape=send_shapes,
        in_specs=[hbm] * 2,
        out_specs=[vmem] * len(links),
        scratch_shapes=[
            pltpu.VMEM((2, 3, 2, tile_x, 8, depth), jnp.float32),
            pltpu.SemaphoreType.DMA((12 + 10 * len(links),)),
        ],
        compiler_params=params,
        cost_estimate=cost(0, 10 * 2 * tile_x * depth * 4),
        name="pack",
    )(in_hbm(forward), in_hbm(adjoint))
    halos = exchange(sends)

    stress, velocity, accel, rim_added, buoyancy, scaled_lame, scaled_shear = pl.pallas_call(
        functools.partial(velocity_kernel, width_y),
        out_shape=[
            padded(12),
            padded(6),
            tile(3),
            pltpu.VMEM((2, 2, 3, max(tile_x, tile_y), depth), jnp.float32),
            tile(),
            tile(),
            tile(),
        ],
        in_specs=[hbm] * 3 + [smem] * 2 + [vmem] * 4,
        out_specs=[vmem] * 7,
        scratch_shapes=[
            pltpu.VMEM((2, tile_x * tile_y + rims, depth), jnp.float32),
            tile(),
            tile(),
            tile(),
            pltpu.SemaphoreType.DMA((3,)),
        ],
        compiler_params=params,
        cost_estimate=cost(200 * cells, 18 * 4 * cells),
        name="velocity",
    )(
        *(in_hbm(x) for x in (lame_lambda, shear_modulus, density)),
        source_cell,
        source_amp,
        receiver_cell,
        residual_amp,
        forward,
        adjoint,
    )

    count = len(links)
    velocity, *sends = pl.pallas_call(
        functools.partial(boundary_kernel, links),
        out_shape=[padded(6)] + send_shapes,
        in_specs=[vmem] * (count + 3),
        out_specs=[vmem] * (count + 1),
        input_output_aliases={count + 2: 0},
        compiler_params=params,
        cost_estimate=cost(cells, 10 * 2 * tile_x * depth * 4),
        name="boundary",
    )(*halos, rim_added, buoyancy, velocity)
    velocity_halos = exchange(sends)

    strain, gradient = pl.pallas_call(
        functools.partial(strain_kernel, links),
        out_shape=[tile(12), tile(3)],
        in_specs=[vmem] * (count + 4),
        out_specs=[vmem] * 2,
        scratch_shapes=[tile(3)],
        compiler_params=params,
        cost_estimate=cost(200 * cells, 18 * 4 * cells),
        name="strain",
    )(*halos, rim_added, buoyancy, velocity, accel)

    strain, gradient = pl.pallas_call(
        functools.partial(gradient_kernel, links),
        out_shape=[tile(12), tile(3)],
        in_specs=[vmem] * (count + 5),
        out_specs=[vmem] * 2,
        input_output_aliases={count + 3: 0, count + 4: 1},
        compiler_params=params,
        cost_estimate=cost(30 * cells, 2 * 4 * cells),
        name="gradient",
    )(*velocity_halos, stress, scaled_lame, scaled_shear, strain, gradient)
    other = lax.ppermute(gradient, "shot", [(0, 1), (1, 0)])

    step = 4 if tile_x % 4 == 0 else 1
    out_block = pl.BlockSpec((9, step, tile_y, depth), lambda i: (0, i, 0, 0))
    forward_next, adjoint_next = pl.pallas_call(
        output_kernel,
        grid=(tile_x // step,),
        out_shape=[jax.ShapeDtypeStruct(forward.shape, jnp.float32)] * 2,
        in_specs=[vmem] * 5,
        out_specs=[out_block] * 2,
        compiler_params=params,
        cost_estimate=cost(60 * cells, 18 * 4 * cells),
        name="outputs",
    )(velocity, strain, stress, scaled_lame, scaled_shear)
    return forward_next[None], adjoint_next[None], gradient + other


def solution(mesh):
    return jax.shard_map(
        body,
        mesh=mesh,
        in_specs=(
            P("shot", None, "tx", "ty", None),
            P("shot", None, "tx", "ty", None),
            P("tx", "ty", None),
            P("tx", "ty", None),
            P("tx", "ty", None),
            P("shot"),
            P("shot"),
            P("shot", None),
            P("shot", None),
        ),
        out_specs=(
            P("shot", None, "tx", "ty", None),
            P("shot", None, "tx", "ty", None),
            P(None, "tx", "ty", None),
        ),
        check_vma=False,
    )
```

```python
import functools

import jax
import jax.numpy as jnp
from jax import lax
from jax.experimental import pallas as pl
from jax.experimental.pallas import tpu as pltpu
from jax.sharding import PartitionSpec as P

near = 9.0 / 8.0
far = -1.0 / 24.0
time_step = 0.15

LAYERS = 2
ROWS = 8
SLOTS = 5

STRESS_ALONG = ((0, 3, 4), (1, 3, 5))
ACCEL_OF = ((0, 1, 2), (1, 0, 2))
VELOCITY_ALONG = ((0, 1, 2), (1, 0, 2))
STRAIN_OF = ((0, 3, 4), (1, 3, 5))

vmem = pl.BlockSpec(memory_space=pltpu.VMEM)
smem = pl.BlockSpec(memory_space=pltpu.SMEM)
hbm = pl.BlockSpec(memory_space=pltpu.HBM)
params = pltpu.CompilerParams(vmem_limit_bytes=24 * 1024 * 1024)


def links_of(sizes):
    order = (("ty", 1, 1), ("tx", 0, 1), ("tx", 0, 0), ("ty", 1, 0))
    return [(name, dim, first) for name, dim, first in order if first + 1 < sizes[name]]


def swap(value, axis, first):
    pairs = [(i, i + 1) for i in range(first, lax.axis_size(axis) - 1, 2)]
    return lax.ppermute(value, axis, pairs + [(j, i) for i, j in pairs])


def is_lower(axis, first):
    return lax.axis_index(axis) % 2 == first


def has_peer(axis, first):
    index = lax.axis_index(axis)
    partner = jnp.where(is_lower(axis, first), index + 1, index - 1)
    return (partner >= 0) & (partner < lax.axis_size(axis))


def send_faces(field, count, links, sends, plans):
    for (axis, dim, first), send in zip(links, sends):
        lower = is_lower(axis, first)
        upper_plan, lower_plan = plans[dim]

        def put(plan):
            for wave in range(2):
                for slot, (part, index) in enumerate(plan):
                    send[wave, slot] = face(field, count * wave + part, dim, index, True)[...]

        pl.when(lower)(functools.partial(put, lower_plan))
        pl.when(jnp.logical_not(lower))(functools.partial(put, upper_plan))


def stress_plan(dim):
    n, a, b = STRESS_ALONG[dim]
    return (
        ((n, 0), (n, 1), (a, 0), (b, 0), (b, 0)),
        ((n, -1), (a, -2), (a, -1), (b, -2), (b, -1)),
    )


def velocity_plan(dim):
    n, a, b = VELOCITY_ALONG[dim]
    return (
        ((n, 0), (a, 0), (a, 1), (b, 0), (b, 1)),
        ((n, -2), (n, -1), (a, -1), (b, -1), (b, -1)),
    )


def pack_kernel(links, width_y, *refs):
    fields, (receiver_cell, residual_amp) = refs[:2], refs[2:4]
    sends = refs[4 : 4 + len(links)]
    stress, velocity, added, cells_now, amps_now, sems = refs[4 + len(links) :]
    _, tile_x, tile_y, depth = fields[0].shape
    small = [
        pltpu.make_async_copy(receiver_cell, cells_now, sems.at[0]),
        pltpu.make_async_copy(residual_amp, amps_now, sems.at[1]),
    ]
    large = [
        pltpu.make_async_copy(
            fields[wave].at[3 + part],
            stress.at[6 * wave + part, pl.ds(LAYERS, tile_x), pl.ds(ROWS, tile_y), :],
            sems.at[2 + 6 * wave + part],
        )
        for wave in range(2)
        for part in range(6)
    ]
    for copy in small + large:
        copy.start()
    clear_rim(stress, tile_x, tile_y)
    clear_rim(velocity, tile_x, tile_y)
    columns = column_ids(tile_x, tile_y, width_y, depth)
    for copy in small:
        copy.wait()
    where = cells_now[...]
    receivers = where.shape[-1]
    column = lax.div(where, depth)
    depth_of = where - column * depth
    column_hot = jnp.concatenate(
        [
            (columns == column[:, begin : begin + depth]).astype(jnp.bfloat16)
            for begin in range(0, receivers, depth)
        ],
        axis=1,
    )
    level = lax.broadcasted_iota(jnp.int32, (depth, receivers), 0)
    rest = jnp.where(level == depth_of, amps_now[...], 0.0)
    total = jnp.zeros(columns.shape, jnp.float32)
    for _ in range(3):
        part = rest.astype(jnp.bfloat16)
        rest = rest - part.astype(jnp.float32)
        total = total + lax.dot_general(
            column_hot,
            part,
            (((1,), (1,)), ((), ())),
            preferred_element_type=jnp.float32,
        )
    added[...] = total
    for copy in large:
        copy.wait()
    send_faces(stress, 6, links, sends, [stress_plan(dim) for dim in range(2)])


def column_ids(tile_x, tile_y, width_y, lanes):
    x_start = lax.axis_index("tx") * tile_x
    y_start = lax.axis_index("ty") * tile_y

    def column(x, y):
        inside = (y >= 0) & (y < width_y)
        return jnp.where(inside, x * width_y + y, -1)

    def iota(shape, dim):
        return lax.broadcasted_iota(jnp.int32, shape, dim)

    shape = (tile_x, tile_y, lanes)
    tile = column(x_start + iota(shape, 0), y_start + iota(shape, 1))
    shape = (3, tile_y, lanes)
    layer = iota(shape, 0)
    along_x = column(
        x_start + jnp.where(layer == 0, -1, tile_x - 1 + layer), y_start + iota(shape, 1)
    )
    shape = (3, tile_x, lanes)
    layer = iota(shape, 0)
    along_y = column(
        x_start + iota(shape, 1), y_start + jnp.where(layer == 0, -1, tile_y - 1 + layer)
    )
    return jnp.concatenate([part.reshape(-1, lanes) for part in (tile, along_x, along_y)], axis=0)


def differ(zero, one, two, minus):
    return near * (one - zero) + far * (two - minus)


def along_x(ref, part, x, tile_y, upward):
    def at(offset):
        return ref[part, x + (LAYERS + offset), pl.ds(ROWS, tile_y), :]

    return differ(at(0), at(1), at(2), at(-1)) if upward else differ(at(-1), at(0), at(1), at(-2))


def along_y(ref, part, x, tile_y, upward):
    def at(offset):
        return ref[part, x + LAYERS, pl.ds(ROWS + offset, tile_y), :]

    return differ(at(0), at(1), at(2), at(-1)) if upward else differ(at(-1), at(0), at(1), at(-2))


def along_z(ref, part, x, tile_y, upward):
    value = ref[part, x + LAYERS, pl.ds(ROWS, tile_y), :]
    depth = value.shape[-1]
    lane = lax.broadcasted_iota(jnp.int32, value.shape, 1)

    def at(offset):
        if offset == 0:
            return value
        moved = pltpu.roll(value, (-offset) % depth, 1)
        inside = lane < depth - offset if offset > 0 else lane >= -offset
        return jnp.where(inside, moved, 0.0)

    return differ(at(0), at(1), at(2), at(-1)) if upward else differ(at(-1), at(0), at(1), at(-2))


def clear_rim(ref, tile_x, tile_y):
    parts, layers, rows, depth = ref.shape
    for part in range(parts):
        for layer in (*range(LAYERS), *range(LAYERS + tile_x, layers)):
            ref[part, layer] = jnp.zeros((rows, depth), jnp.float32)
        for row in (0, ROWS + tile_y):
            ref[part, pl.ds(LAYERS, tile_x), pl.ds(row, ROWS), :] = jnp.zeros(
                (tile_x, ROWS, depth), jnp.float32
            )


def velocity_kernel(width_y, *refs):
    forward, adjoint, lame, shear, density, source_cell, source_amp, received, _, _ = refs[:10]
    stress, velocity, accel, rim_added, buoyancy, scaled_lame, scaled_shear = refs[10:17]
    gained, lame_now, shear_now, density_now, sems = refs[17:]
    tile_x, tile_y, depth = density.shape
    cells = tile_x * tile_y
    middle = pl.ds(ROWS, tile_y)
    copies = [
        pltpu.make_async_copy(source, target, sems.at[at])
        for at, (source, target) in enumerate((
            (density, density_now),
            (lame, lame_now),
            (shear, shear_now),
            (forward.at[pl.ds(0, 3)], velocity.at[pl.ds(0, 3), pl.ds(LAYERS, tile_x), middle, :]),
            (adjoint.at[pl.ds(0, 3)], velocity.at[pl.ds(3, 3), pl.ds(LAYERS, tile_x), middle, :]),
        ))
    ]
    for copy in copies:
        copy.start()
    columns = column_ids(tile_x, tile_y, width_y, depth)
    lane = lax.broadcasted_iota(jnp.int32, columns.shape, 1)
    sourced = jnp.where(columns * depth + lane == source_cell[0], source_amp[0], 0.0)
    for wave, added in enumerate((sourced, received[...])):
        for layer in range(3):
            begin = cells + layer * tile_y
            rim_added[wave, 0, layer] = added[begin : begin + tile_y]
            begin = cells + 3 * tile_y + layer * tile_x
            rim_added[wave, 1, layer] = added[begin : begin + tile_x]
        for x in range(tile_x):
            extra = added[x * tile_y : (x + 1) * tile_y]
            for part in range(3):
                stress[6 * wave + part, x + LAYERS, middle, :] += extra

    def layer(x, carry):
        for wave in range(2):
            xx, yy, zz, xy, xz, yz = range(6 * wave, 6 * wave + 6)
            values = (
                along_x(stress, xx, x, tile_y, True)
                + along_y(stress, xy, x, tile_y, False)
                + along_z(stress, xz, x, tile_y, False),
                along_x(stress, xy, x, tile_y, False)
                + along_y(stress, yy, x, tile_y, True)
                + along_z(stress, yz, x, tile_y, False),
                along_x(stress, xz, x, tile_y, False)
                + along_y(stress, yz, x, tile_y, False)
                + along_z(stress, zz, x, tile_y, True),
            )
            for part, value in enumerate(values):
                gained[3 * wave + part, x] = value
        return carry

    lax.fori_loop(0, tile_x, layer, 0, unroll=4)
    for copy in copies:
        copy.wait()

    def finish(x, carry):
        light = 1.0 / density_now[x]
        buoyancy[x] = light
        scaled_lame[x] = time_step * lame_now[x]
        scaled_shear[x] = time_step * shear_now[x]
        for part in range(6):
            value = light * gained[part, x]
            if part < 3:
                accel[part, x] = value
            velocity[part, x + LAYERS, middle, :] += time_step * value
        return carry

    lax.fori_loop(0, tile_x, finish, 0, unroll=4)


def stress_halo_terms(links, received, rim_added, waves, add):
    for (axis, dim, first), halo in zip(links, received):
        part_n, part_a, part_b = ACCEL_OF[dim]
        lower = is_lower(axis, first)
        real = has_peer(axis, first)

        @pl.when(real & lower)
        def after():
            for wave in waves:
                n0 = halo[wave, 0] + rim_added[wave, dim, 1]
                n1 = halo[wave, 1] + rim_added[wave, dim, 2]
                add(wave, part_n, dim, -1, near * n0 + far * n1)
                add(wave, part_n, dim, -2, far * n0)
                add(wave, part_a, dim, -1, far * halo[wave, 2])
                add(wave, part_b, dim, -1, far * halo[wave, 3])

        @pl.when(real & jnp.logical_not(lower))
        def before():
            for wave in waves:
                n0 = halo[wave, 0] + rim_added[wave, dim, 0]
                add(wave, part_n, dim, 0, -far * n0)
                for part, slot in ((part_a, 1), (part_b, 3)):
                    outer, inner = halo[wave, slot], halo[wave, slot + 1]
                    add(wave, part, dim, 0, -near * inner - far * outer)
                    add(wave, part, dim, 1, -far * inner)


def velocity_halo_terms(links, received, add):
    for (axis, dim, first), halo in zip(links, received):
        part_n, part_a, part_b = STRAIN_OF[dim]
        lower = is_lower(axis, first)
        real = has_peer(axis, first)

        @pl.when(real & lower)
        def after():
            for wave in range(2):
                add(wave, part_n, dim, -1, far * halo[wave, 0])
                for part, slot in ((part_a, 1), (part_b, 3)):
                    inner, outer = halo[wave, slot], halo[wave, slot + 1]
                    add(wave, part, dim, -1, near * inner + far * outer)
                    add(wave, part, dim, -2, far * inner)

        @pl.when(real & jnp.logical_not(lower))
        def before():
            for wave in range(2):
                outer, inner = halo[wave, 0], halo[wave, 1]
                add(wave, part_n, dim, 0, -near * inner - far * outer)
                add(wave, part_n, dim, 1, -far * inner)
                add(wave, part_a, dim, 0, -far * halo[wave, 2])
                add(wave, part_b, dim, 0, -far * halo[wave, 3])


def face(ref, part, dim, index, padded):
    layers, rows, depth = ref.shape[1:]
    tile_x = layers - 2 * LAYERS if padded else layers
    tile_y = rows - 2 * ROWS if padded else rows
    if dim == 0:
        at = index % tile_x
        if padded:
            return ref.at[part, at + LAYERS, pl.ds(ROWS, tile_y), :]
        return ref.at[part, at]
    at = index % tile_y
    flat = ref.reshape(ref.shape[0], layers * rows, depth)
    begin = LAYERS * rows + ROWS + at if padded else at
    return flat.at[part, pl.ds(begin, tile_x, stride=rows), :]


def light_face(buoyancy, dim, index):
    layers, rows, depth = buoyancy.shape
    if dim == 0:
        return buoyancy[index % layers]
    return buoyancy.reshape(layers * rows, depth)[pl.ds(index % rows, layers, stride=rows), :]


def boundary_kernel(links, *refs):
    count = len(links)
    received = refs[:count]
    rim_added, buoyancy, _ = refs[count : count + 3]
    velocity = refs[count + 3]
    sends = refs[count + 4 :]

    def add(wave, part, dim, index, term):
        target = face(velocity, 3 * wave + part, dim, index, True)
        target[...] += time_step * light_face(buoyancy, dim, index) * term

    stress_halo_terms(links, received, rim_added, (0, 1), add)
    send_faces(velocity, 3, links, sends, [velocity_plan(dim) for dim in range(2)])


def strain_kernel(links, *refs):
    count = len(links)
    received = refs[:count]
    rim_added, buoyancy, velocity, accel, strain, gradient = refs[count : count + 6]
    outputs, (accel_now, sems) = refs[count + 6 : count + 8], refs[count + 8 :]
    tile_x, tile_y, _ = buoyancy.shape
    middle = pl.ds(ROWS, tile_y)
    copies = [
        pltpu.make_async_copy(
            velocity.at[3 * wave + part, pl.ds(LAYERS, tile_x), middle, :],
            outputs[wave].at[part],
            sems.at[3 * wave + part],
        )
        for wave in range(2)
        for part in range(3)
    ]
    for copy in copies:
        copy.start()
    accel_now[...] = accel[...]

    def add(wave, part, dim, index, term):
        target = face(accel_now, part, dim, index, False)
        target[...] += light_face(buoyancy, dim, index) * term

    stress_halo_terms(links, received, rim_added, (0,), add)

    def layer(x, carry):
        for wave in range(2):
            vx, vy, vz = range(3 * wave, 3 * wave + 3)
            values = (
                along_x(velocity, vx, x, tile_y, False),
                along_y(velocity, vy, x, tile_y, False),
                along_z(velocity, vz, x, tile_y, False),
                along_y(velocity, vx, x, tile_y, True) + along_x(velocity, vy, x, tile_y, True),
                along_z(velocity, vx, x, tile_y, True) + along_x(velocity, vz, x, tile_y, True),
                along_z(velocity, vy, x, tile_y, True) + along_y(velocity, vz, x, tile_y, True),
            )
            for part, value in enumerate(values):
                strain[6 * wave + part, x] = value
        total = sum(
            accel_now[part, x] * velocity[3 + part, x + LAYERS, middle, :] for part in range(3)
        )
        gradient[2, x] = -time_step * total
        return carry

    lax.fori_loop(0, tile_x, layer, 0, unroll=4)
    for copy in copies:
        copy.wait()


def new_stress(strain, stress, scaled_lame, scaled_shear, wave, x, tile_y):
    lame, shear = scaled_lame[x], scaled_shear[x]
    strains = [strain[6 * wave + part, x] for part in range(6)]
    volume = lame * (strains[0] + strains[1] + strains[2])
    values = []
    for part in range(6):
        old = stress[6 * wave + part, x + LAYERS, pl.ds(ROWS, tile_y), :]
        if part < 3:
            values.append(old + (volume + 2.0 * shear * strains[part]))
        else:
            values.append(old + shear * strains[part])
    return strains, values


def gradient_kernel(links, *refs):
    count = len(links)
    received = refs[:count]
    stress, scaled_lame, scaled_shear, _, _, strain, gradient = refs[count:]
    tile_x, tile_y, _ = scaled_lame.shape

    def add(wave, part, dim, index, term):
        target = face(strain, 6 * wave + part, dim, index, False)
        target[...] += term

    velocity_halo_terms(links, received, add)

    def layer(x, carry):
        strains = [strain[part, x] for part in range(6)]
        _, values = new_stress(strain, stress, scaled_lame, scaled_shear, 1, x, tile_y)
        trace = strains[0] + strains[1] + strains[2]
        gradient[0, x] = -time_step * trace * (values[0] + values[1] + values[2])
        total = sum(left * right for left, right in zip(strains, values))
        gradient[1, x] = -time_step * total
        return carry

    lax.fori_loop(0, tile_x, layer, 0, unroll=4)


def output_kernel(chunk, strain, stress, scaled_lame, scaled_shear, *refs):
    outputs, (values_now, sems) = refs[2:4], refs[4:]
    tile_x, tile_y, _ = scaled_lame.shape
    copies = []
    for begin in range(0, tile_x, chunk):
        for wave in range(2):
            for x in range(begin, begin + chunk):
                _, values = new_stress(strain, stress, scaled_lame, scaled_shear, wave, x, tile_y)
                for part in range(6):
                    values_now[6 * wave + part, x] = values[part]
            layers = pl.ds(begin, chunk)
            copy = pltpu.make_async_copy(
                values_now.at[pl.ds(6 * wave, 6), layers],
                outputs[wave].at[pl.ds(3, 6), layers],
                sems.at[len(copies)],
            )
            copy.start()
            copies.append(copy)
    for copy in copies:
        copy.wait()


def sum_kernel(mine, other, total, total_now, sems):
    copies = []
    for part in range(mine.shape[0]):
        total_now[part] = mine[part] + other[part]
        copy = pltpu.make_async_copy(total_now.at[part], total.at[part], sems.at[part])
        copy.start()
        copies.append(copy)
    for copy in copies:
        copy.wait()


def in_hbm(value):
    return pltpu.with_memory_space_constraint(value, pltpu.HBM)


def cost(flops, size):
    return pl.CostEstimate(flops=flops, bytes_accessed=size, transcendentals=0)


def body(
    forward_fields,
    adjoint_fields,
    lame_lambda,
    shear_modulus,
    density,
    source_cell,
    source_amp,
    receiver_cell,
    residual_amp,
):
    _, _, tile_x, tile_y, depth = forward_fields.shape
    forward = forward_fields.reshape(forward_fields.shape[1:])
    adjoint = adjoint_fields.reshape(adjoint_fields.shape[1:])
    sizes = {name: lax.axis_size(name) for name in ("tx", "ty")}
    width_y = tile_y * sizes["ty"]
    links = links_of(sizes)
    cells = tile_x * tile_y * depth
    rims = 3 * tile_x + 3 * tile_y

    def buffers(dim):
        return pltpu.VMEM((2, SLOTS, tile_y if dim == 0 else tile_x, depth), jnp.float32)

    def tile(*lead):
        return pltpu.VMEM((*lead, tile_x, tile_y, depth), jnp.float32)

    def padded(parts):
        return pltpu.VMEM(
            (parts, tile_x + 2 * LAYERS, tile_y + 2 * ROWS, depth), jnp.float32
        )

    def exchange(sends):
        return [swap(send, axis, first) for (axis, _, first), send in zip(links, sends)]

    send_shapes = [buffers(dim) for _, dim, _ in links]
    count = len(links)
    receivers = receiver_cell.shape[-1]
    *sends, stress, velocity, added = pl.pallas_call(
        functools.partial(pack_kernel, links, width_y),
        out_shape=send_shapes
        + [padded(12), padded(6), pltpu.VMEM((tile_x * tile_y + rims, depth), jnp.float32)],
        in_specs=[hbm] * 4,
        out_specs=[vmem] * (count + 3),
        scratch_shapes=[
            pltpu.VMEM((1, receivers), jnp.int32),
            pltpu.VMEM((1, receivers), jnp.float32),
            pltpu.SemaphoreType.DMA((14,)),
        ],
        compiler_params=params,
        cost_estimate=cost(6 * 400 * 256 * 128, 12 * 4 * cells),
        name="pack",
    )(*(in_hbm(x) for x in (forward, adjoint, receiver_cell, residual_amp)))
    halos = exchange(sends)

    stress, velocity, accel, rim_added, buoyancy, scaled_lame, scaled_shear = pl.pallas_call(
        functools.partial(velocity_kernel, width_y),
        out_shape=[
            padded(12),
            padded(6),
            tile(3),
            pltpu.VMEM((2, 2, 3, max(tile_x, tile_y), depth), jnp.float32),
            tile(),
            tile(),
            tile(),
        ],
        in_specs=[hbm] * 5 + [smem] * 2 + [vmem] * 3,
        out_specs=[vmem] * 7,
        input_output_aliases={8: 0, 9: 1},
        scratch_shapes=[tile(6), tile(), tile(), tile(), pltpu.SemaphoreType.DMA((5,))],
        compiler_params=params,
        cost_estimate=cost(200 * cells, 9 * 4 * cells),
        name="velocity",
    )(
        *(in_hbm(x) for x in (forward, adjoint, lame_lambda, shear_modulus, density)),
        source_cell,
        source_amp,
        added,
        stress,
        velocity,
    )

    velocity, *sends = pl.pallas_call(
        functools.partial(boundary_kernel, links),
        out_shape=[padded(6)] + send_shapes,
        in_specs=[vmem] * (count + 3),
        out_specs=[vmem] * (count + 1),
        input_output_aliases={count + 2: 0},
        compiler_params=params,
        cost_estimate=cost(cells, 10 * 2 * tile_x * depth * 4),
        name="boundary",
    )(*halos, rim_added, buoyancy, velocity)
    velocity_halos = exchange(sends)

    out_shape = jax.ShapeDtypeStruct(forward.shape, jnp.float32)
    strain, gradient, forward_next, adjoint_next = pl.pallas_call(
        functools.partial(strain_kernel, links),
        out_shape=[tile(12), tile(3), out_shape, out_shape],
        in_specs=[vmem] * (count + 4),
        out_specs=[vmem] * 2 + [hbm] * 2,
        scratch_shapes=[tile(3), pltpu.SemaphoreType.DMA((6,))],
        compiler_params=params,
        cost_estimate=cost(200 * cells, 18 * 4 * cells),
        name="strain",
    )(*halos, rim_added, buoyancy, velocity, accel)

    strain, gradient = pl.pallas_call(
        functools.partial(gradient_kernel, links),
        out_shape=[tile(12), tile(3)],
        in_specs=[vmem] * (count + 5),
        out_specs=[vmem] * 2,
        input_output_aliases={count + 3: 0, count + 4: 1},
        compiler_params=params,
        cost_estimate=cost(30 * cells, 2 * 4 * cells),
        name="gradient",
    )(*velocity_halos, stress, scaled_lame, scaled_shear, strain, gradient)
    other = lax.ppermute(gradient, "shot", [(0, 1), (1, 0)])

    chunk = 4 if tile_x % 4 == 0 else 1
    forward_next, adjoint_next = pl.pallas_call(
        functools.partial(output_kernel, chunk),
        out_shape=[out_shape, out_shape],
        in_specs=[vmem] * 4 + [hbm] * 2,
        out_specs=[hbm] * 2,
        input_output_aliases={4: 0, 5: 1},
        scratch_shapes=[tile(12), pltpu.SemaphoreType.DMA((2 * tile_x // chunk,))],
        compiler_params=params,
        cost_estimate=cost(60 * cells, 18 * 4 * cells),
        name="outputs",
    )(strain, stress, scaled_lame, scaled_shear, forward_next, adjoint_next)
    total = pl.pallas_call(
        sum_kernel,
        out_shape=jax.ShapeDtypeStruct((3, tile_x, tile_y, depth), jnp.float32),
        in_specs=[vmem] * 2,
        out_specs=hbm,
        scratch_shapes=[tile(3), pltpu.SemaphoreType.DMA((3,))],
        compiler_params=params,
        cost_estimate=cost(3 * cells, 9 * 4 * cells),
        name="sum",
    )(gradient, other)
    return forward_next[None], adjoint_next[None], total


def solution(mesh):
    return jax.shard_map(
        body,
        mesh=mesh,
        in_specs=(
            P("shot", None, "tx", "ty", None),
            P("shot", None, "tx", "ty", None),
            P("tx", "ty", None),
            P("tx", "ty", None),
            P("tx", "ty", None),
            P("shot"),
            P("shot"),
            P("shot", None),
            P("shot", None),
        ),
        out_specs=(
            P("shot", None, "tx", "ty", None),
            P("shot", None, "tx", "ty", None),
            P(None, "tx", "ty", None),
        ),
        check_vma=False,
    )
```

```python
import functools

import jax
import jax.numpy as jnp
from jax import lax
from jax.experimental import pallas as pl
from jax.experimental.pallas import tpu as pltpu
from jax.sharding import PartitionSpec as P

near = 9.0 / 8.0
far = -1.0 / 24.0
time_step = 0.15

LAYERS = 2
ROWS = 8
SLOTS = 5

STRESS_ALONG = ((0, 3, 4), (1, 3, 5))
ACCEL_OF = ((0, 1, 2), (1, 0, 2))
VELOCITY_ALONG = ((0, 1, 2), (1, 0, 2))
STRAIN_OF = ((0, 3, 4), (1, 3, 5))

vmem = pl.BlockSpec(memory_space=pltpu.VMEM)
smem = pl.BlockSpec(memory_space=pltpu.SMEM)
hbm = pl.BlockSpec(memory_space=pltpu.HBM)
params = pltpu.CompilerParams(vmem_limit_bytes=24 * 1024 * 1024)


def links_of(sizes):
    order = (("ty", 1, 1), ("tx", 0, 1), ("tx", 0, 0), ("ty", 1, 0))
    return [(name, dim, first) for name, dim, first in order if first + 1 < sizes[name]]


def swap(value, axis, first):
    pairs = [(i, i + 1) for i in range(first, lax.axis_size(axis) - 1, 2)]
    return lax.ppermute(value, axis, pairs + [(j, i) for i, j in pairs])


def is_lower(axis, first):
    return lax.axis_index(axis) % 2 == first


def has_peer(axis, first):
    index = lax.axis_index(axis)
    partner = jnp.where(is_lower(axis, first), index + 1, index - 1)
    return (partner >= 0) & (partner < lax.axis_size(axis))


def send_faces(field, count, links, sends, plans):
    for (axis, dim, first), send in zip(links, sends):
        lower = is_lower(axis, first)
        upper_plan, lower_plan = plans[dim]

        def put(plan):
            for wave in range(2):
                for slot, (part, index) in enumerate(plan):
                    send[wave, slot] = face(field, count * wave + part, dim, index, True)[...]

        pl.when(lower)(functools.partial(put, lower_plan))
        pl.when(jnp.logical_not(lower))(functools.partial(put, upper_plan))


def stress_plan(dim):
    n, a, b = STRESS_ALONG[dim]
    return (
        ((n, 0), (n, 1), (a, 0), (b, 0), (b, 0)),
        ((n, -1), (a, -2), (a, -1), (b, -2), (b, -1)),
    )


def velocity_plan(dim):
    n, a, b = VELOCITY_ALONG[dim]
    return (
        ((n, 0), (a, 0), (a, 1), (b, 0), (b, 1)),
        ((n, -2), (n, -1), (a, -1), (b, -1), (b, -1)),
    )


def pack_kernel(links, forward, adjoint, *refs):
    sends, sems = refs[: len(links)], refs[-1]
    tile = forward.shape[1:3]
    copies = []
    for (axis, dim, first), send in zip(links, sends):
        lower = is_lower(axis, first)
        for slot, ((up_part, up_at), (low_part, low_at)) in enumerate(zip(*stress_plan(dim))):
            part = 3 + jnp.where(lower, low_part, up_part)
            at = jnp.where(lower, low_at % tile[dim], up_at % tile[dim])
            for wave, fields in enumerate((forward, adjoint)):
                source = fields.at[part, at] if dim == 0 else fields.at[part, :, at, :]
                copy = pltpu.make_async_copy(source, send.at[wave, slot], sems.at[len(copies)])
                copy.start()
                copies.append(copy)
    for copy in copies:
        copy.wait()


def column_ids(tile_x, tile_y, width_y, lanes):
    x_start = lax.axis_index("tx") * tile_x
    y_start = lax.axis_index("ty") * tile_y

    def column(x, y):
        inside = (y >= 0) & (y < width_y)
        return jnp.where(inside, x * width_y + y, -1)

    def iota(shape, dim):
        return lax.broadcasted_iota(jnp.int32, shape, dim)

    shape = (tile_x, tile_y, lanes)
    tile = column(x_start + iota(shape, 0), y_start + iota(shape, 1))
    shape = (3, tile_y, lanes)
    layer = iota(shape, 0)
    along_x = column(
        x_start + jnp.where(layer == 0, -1, tile_x - 1 + layer), y_start + iota(shape, 1)
    )
    shape = (3, tile_x, lanes)
    layer = iota(shape, 0)
    along_y = column(
        x_start + iota(shape, 1), y_start + jnp.where(layer == 0, -1, tile_y - 1 + layer)
    )
    return jnp.concatenate([part.reshape(-1, lanes) for part in (tile, along_x, along_y)], axis=0)


def differ(zero, one, two, minus):
    return near * (one - zero) + far * (two - minus)


def along_x(ref, part, x, tile_y, upward):
    def at(offset):
        return ref[part, x + (LAYERS + offset), pl.ds(ROWS, tile_y), :]

    return differ(at(0), at(1), at(2), at(-1)) if upward else differ(at(-1), at(0), at(1), at(-2))


def along_y(ref, part, x, tile_y, upward):
    def at(offset):
        return ref[part, x + LAYERS, pl.ds(ROWS + offset, tile_y), :]

    return differ(at(0), at(1), at(2), at(-1)) if upward else differ(at(-1), at(0), at(1), at(-2))


def along_z(ref, part, x, tile_y, upward):
    value = ref[part, x + LAYERS, pl.ds(ROWS, tile_y), :]
    depth = value.shape[-1]
    lane = lax.broadcasted_iota(jnp.int32, value.shape, 1)

    def at(offset):
        if offset == 0:
            return value
        moved = pltpu.roll(value, (-offset) % depth, 1)
        inside = lane < depth - offset if offset > 0 else lane >= -offset
        return jnp.where(inside, moved, 0.0)

    return differ(at(0), at(1), at(2), at(-1)) if upward else differ(at(-1), at(0), at(1), at(-2))


def clear_rim(ref, parts_x, parts_y):
    _, layers, rows, depth = ref.shape
    tile_x, tile_y = layers - 2 * LAYERS, rows - 2 * ROWS
    for part in parts_x:
        for begin in (0, LAYERS + tile_x):
            ref[part, pl.ds(begin, LAYERS), pl.ds(ROWS, tile_y), :] = jnp.zeros(
                (LAYERS, tile_y, depth), jnp.float32
            )
    for part in parts_y:
        for begin in (0, ROWS + tile_y):
            ref[part, pl.ds(LAYERS, tile_x), pl.ds(begin, ROWS), :] = jnp.zeros(
                (tile_x, ROWS, depth), jnp.float32
            )


def receiver_sum(cells, amps, columns):
    depth, receivers = columns.shape[-1], cells.shape[-1]
    column = lax.div(cells, depth)
    level = cells - column * depth
    column_hot = jnp.concatenate(
        [
            (columns == column[:, begin : begin + depth]).astype(jnp.bfloat16)
            for begin in range(0, receivers, depth)
        ],
        axis=1,
    )
    levels = lax.broadcasted_iota(jnp.int32, (depth, receivers), 0)
    rest = jnp.where(levels == level, amps, 0.0)
    total = jnp.zeros(columns.shape, jnp.float32)
    for _ in range(3):
        part = rest.astype(jnp.bfloat16)
        rest = rest - part.astype(jnp.float32)
        total = total + lax.dot_general(
            column_hot,
            part,
            (((1,), (1,)), ((), ())),
            preferred_element_type=jnp.float32,
        )
    return total


def velocity_kernel(
    width_y,
    lame,
    shear,
    density,
    source_cell,
    source_amp,
    receiver_cell,
    residual_amp,
    forward,
    adjoint,
    stress,
    velocity,
    accel,
    rim_added,
    buoyancy,
    scaled_lame,
    scaled_shear,
    added,
    lame_now,
    shear_now,
    density_now,
    sems,
):
    tile_x, tile_y, depth = density.shape
    copies = [
        pltpu.make_async_copy(source, target, sems.at[at])
        for at, (source, target) in enumerate((
            (density, density_now),
            (lame, lame_now),
            (shear, shear_now),
        ))
    ]
    for copy in copies:
        copy.start()
    cells = tile_x * tile_y
    middle = pl.ds(ROWS, tile_y)
    columns = column_ids(tile_x, tile_y, width_y, depth)
    lane = lax.broadcasted_iota(jnp.int32, columns.shape, 1)
    added[0] = jnp.where(columns * depth + lane == source_cell[0], source_amp[0], 0.0)
    added[1] = receiver_sum(receiver_cell[...], residual_amp[...], columns)
    for wave in range(2):
        clear_rim(
            stress, *([6 * wave + part for part in STRESS_ALONG[dim]] for dim in range(2))
        )
        for layer in range(3):
            rim_added[wave, 0, layer] = added[wave, pl.ds(cells + layer * tile_y, tile_y), :]
            begin = cells + 3 * tile_y + layer * tile_x
            rim_added[wave, 1, layer] = added[wave, pl.ds(begin, tile_x), :]

    for copy in copies:
        copy.wait()

    def fill(x, carry):
        for wave, fields in enumerate((forward, adjoint)):
            extra = added[wave, pl.ds(pl.multiple_of(x * tile_y, 8), tile_y), :]
            for part in range(6):
                value = fields[3 + part, x]
                stress[6 * wave + part, x + LAYERS, middle, :] = (
                    value + extra if part < 3 else value
                )
        buoyancy[x] = 1.0 / density_now[x]
        scaled_lame[x] = time_step * lame_now[x]
        scaled_shear[x] = time_step * shear_now[x]
        return carry

    lax.fori_loop(0, tile_x, fill, 0, unroll=4)

    def layer(x, carry):
        light = buoyancy[x]
        for wave, fields in enumerate((forward, adjoint)):
            xx, yy, zz, xy, xz, yz = range(6 * wave, 6 * wave + 6)
            values = (
                along_x(stress, xx, x, tile_y, True)
                + along_y(stress, xy, x, tile_y, False)
                + along_z(stress, xz, x, tile_y, False),
                along_x(stress, xy, x, tile_y, False)
                + along_y(stress, yy, x, tile_y, True)
                + along_z(stress, yz, x, tile_y, False),
                along_x(stress, xz, x, tile_y, False)
                + along_y(stress, yz, x, tile_y, False)
                + along_z(stress, zz, x, tile_y, True),
            )
            for part, value in enumerate(values):
                value = light * value
                if wave == 0:
                    accel[part, x] = value
                velocity[3 * wave + part, x + LAYERS, middle, :] = (
                    fields[part, x] + time_step * value
                )
        return carry

    lax.fori_loop(0, tile_x, layer, 0, unroll=4)


def stress_halo_terms(links, received, rim_added, waves, add):
    for (axis, dim, first), halo in zip(links, received):
        part_n, part_a, part_b = ACCEL_OF[dim]
        lower = is_lower(axis, first)
        real = has_peer(axis, first)

        @pl.when(real & lower)
        def after():
            for wave in waves:
                n0 = halo[wave, 0] + rim_added[wave, dim, 1]
                n1 = halo[wave, 1] + rim_added[wave, dim, 2]
                add(wave, part_n, dim, -1, near * n0 + far * n1)
                add(wave, part_n, dim, -2, far * n0)
                add(wave, part_a, dim, -1, far * halo[wave, 2])
                add(wave, part_b, dim, -1, far * halo[wave, 3])

        @pl.when(real & jnp.logical_not(lower))
        def before():
            for wave in waves:
                n0 = halo[wave, 0] + rim_added[wave, dim, 0]
                add(wave, part_n, dim, 0, -far * n0)
                for part, slot in ((part_a, 1), (part_b, 3)):
                    outer, inner = halo[wave, slot], halo[wave, slot + 1]
                    add(wave, part, dim, 0, -near * inner - far * outer)
                    add(wave, part, dim, 1, -far * inner)


def velocity_halo_terms(links, received, add):
    for (axis, dim, first), halo in zip(links, received):
        part_n, part_a, part_b = STRAIN_OF[dim]
        lower = is_lower(axis, first)
        real = has_peer(axis, first)

        @pl.when(real & lower)
        def after():
            for wave in range(2):
                add(wave, part_n, dim, -1, far * halo[wave, 0])
                for part, slot in ((part_a, 1), (part_b, 3)):
                    inner, outer = halo[wave, slot], halo[wave, slot + 1]
                    add(wave, part, dim, -1, near * inner + far * outer)
                    add(wave, part, dim, -2, far * inner)

        @pl.when(real & jnp.logical_not(lower))
        def before():
            for wave in range(2):
                outer, inner = halo[wave, 0], halo[wave, 1]
                add(wave, part_n, dim, 0, -near * inner - far * outer)
                add(wave, part_n, dim, 1, -far * inner)
                add(wave, part_a, dim, 0, -far * halo[wave, 2])
                add(wave, part_b, dim, 0, -far * halo[wave, 3])


def face(ref, part, dim, index, padded):
    layers, rows, depth = ref.shape[1:]
    tile_x = layers - 2 * LAYERS if padded else layers
    tile_y = rows - 2 * ROWS if padded else rows
    if dim == 0:
        at = index % tile_x
        if padded:
            return ref.at[part, at + LAYERS, pl.ds(ROWS, tile_y), :]
        return ref.at[part, at]
    at = index % tile_y
    flat = ref.reshape(ref.shape[0], layers * rows, depth)
    begin = LAYERS * rows + ROWS + at if padded else at
    return flat.at[part, pl.ds(begin, tile_x, stride=rows), :]


def light_face(buoyancy, dim, index):
    layers, rows, depth = buoyancy.shape
    if dim == 0:
        return buoyancy[index % layers]
    return buoyancy.reshape(layers * rows, depth)[pl.ds(index % rows, layers, stride=rows), :]


def boundary_kernel(links, *refs):
    count = len(links)
    received = refs[:count]
    rim_added, buoyancy, _ = refs[count : count + 3]
    velocity = refs[count + 3]
    sends = refs[count + 4 :]

    def add(wave, part, dim, index, term):
        target = face(velocity, 3 * wave + part, dim, index, True)
        target[...] += time_step * light_face(buoyancy, dim, index) * term

    stress_halo_terms(links, received, rim_added, (0, 1), add)
    send_faces(velocity, 3, links, sends, [velocity_plan(dim) for dim in range(2)])


def strain_kernel(links, *refs):
    count = len(links)
    received = refs[:count]
    rim_added, buoyancy, _, accel, strain, gradient, velocity = refs[count : count + 7]
    outputs, (accel_now, sems) = refs[count + 7 : count + 9], refs[count + 9 :]
    tile_x, tile_y, _ = buoyancy.shape
    middle = pl.ds(ROWS, tile_y)
    copies = [
        pltpu.make_async_copy(
            velocity.at[3 * wave + part, pl.ds(LAYERS, tile_x), middle, :],
            outputs[wave].at[part],
            sems.at[3 * wave + part],
        )
        for wave in range(2)
        for part in range(3)
    ]
    for copy in copies:
        copy.start()
    clear_rim(velocity, range(6), range(6))
    accel_now[...] = accel[...]

    def add(wave, part, dim, index, term):
        target = face(accel_now, part, dim, index, False)
        target[...] += light_face(buoyancy, dim, index) * term

    stress_halo_terms(links, received, rim_added, (0,), add)

    def layer(x, carry):
        for wave in range(2):
            vx, vy, vz = range(3 * wave, 3 * wave + 3)
            values = (
                along_x(velocity, vx, x, tile_y, False),
                along_y(velocity, vy, x, tile_y, False),
                along_z(velocity, vz, x, tile_y, False),
                along_y(velocity, vx, x, tile_y, True) + along_x(velocity, vy, x, tile_y, True),
                along_z(velocity, vx, x, tile_y, True) + along_x(velocity, vz, x, tile_y, True),
                along_z(velocity, vy, x, tile_y, True) + along_y(velocity, vz, x, tile_y, True),
            )
            for part, value in enumerate(values):
                strain[6 * wave + part, x] = value
        total = sum(
            accel_now[part, x] * velocity[3 + part, x + LAYERS, middle, :] for part in range(3)
        )
        gradient[2, x] = -time_step * total
        return carry

    lax.fori_loop(0, tile_x, layer, 0, unroll=4)
    for copy in copies:
        copy.wait()


def new_stress(strain, stress, scaled_lame, scaled_shear, wave, x, tile_y):
    lame, shear = scaled_lame[x], scaled_shear[x]
    strains = [strain[6 * wave + part, x] for part in range(6)]
    volume = lame * (strains[0] + strains[1] + strains[2])
    values = []
    for part in range(6):
        old = stress[6 * wave + part, x + LAYERS, pl.ds(ROWS, tile_y), :]
        if part < 3:
            values.append(old + (volume + 2.0 * shear * strains[part]))
        else:
            values.append(old + shear * strains[part])
    return strains, values


def gradient_kernel(links, *refs):
    count = len(links)
    received = refs[:count]
    stress, scaled_lame, scaled_shear, _, _, strain, gradient = refs[count:]
    tile_x, tile_y, _ = scaled_lame.shape

    def add(wave, part, dim, index, term):
        target = face(strain, 6 * wave + part, dim, index, False)
        target[...] += term

    velocity_halo_terms(links, received, add)

    def layer(x, carry):
        strains = [strain[part, x] for part in range(6)]
        _, values = new_stress(strain, stress, scaled_lame, scaled_shear, 1, x, tile_y)
        trace = strains[0] + strains[1] + strains[2]
        gradient[0, x] = -time_step * trace * (values[0] + values[1] + values[2])
        total = sum(left * right for left, right in zip(strains, values))
        gradient[1, x] = -time_step * total
        return carry

    lax.fori_loop(0, tile_x, layer, 0, unroll=4)


def output_kernel(chunk, strain, stress, scaled_lame, scaled_shear, *refs):
    outputs, (values_now, sems) = refs[2:4], refs[4:]
    tile_x, tile_y, _ = scaled_lame.shape
    copies = []
    for begin in range(0, tile_x, chunk):
        for wave in range(2):
            for x in range(begin, begin + chunk):
                _, values = new_stress(strain, stress, scaled_lame, scaled_shear, wave, x, tile_y)
                for part in range(6):
                    values_now[6 * wave + part, x] = values[part]
            layers = pl.ds(begin, chunk)
            copy = pltpu.make_async_copy(
                values_now.at[pl.ds(6 * wave, 6), layers],
                outputs[wave].at[pl.ds(3, 6), layers],
                sems.at[len(copies)],
            )
            copy.start()
            copies.append(copy)
    for copy in copies:
        copy.wait()


def sum_kernel(mine, other, total, total_now, sems):
    copies = []
    for part in range(mine.shape[0]):
        total_now[part] = mine[part] + other[part]
        copy = pltpu.make_async_copy(total_now.at[part], total.at[part], sems.at[part])
        copy.start()
        copies.append(copy)
    for copy in copies:
        copy.wait()


def in_hbm(value):
    return pltpu.with_memory_space_constraint(value, pltpu.HBM)


def cost(flops, size):
    return pl.CostEstimate(flops=flops, bytes_accessed=size, transcendentals=0)


def body(
    forward_fields,
    adjoint_fields,
    lame_lambda,
    shear_modulus,
    density,
    source_cell,
    source_amp,
    receiver_cell,
    residual_amp,
):
    _, _, tile_x, tile_y, depth = forward_fields.shape
    forward = forward_fields.reshape(forward_fields.shape[1:])
    adjoint = adjoint_fields.reshape(adjoint_fields.shape[1:])
    sizes = {name: lax.axis_size(name) for name in ("tx", "ty")}
    width_y = tile_y * sizes["ty"]
    links = links_of(sizes)
    cells = tile_x * tile_y * depth

    def buffers(dim):
        return pltpu.VMEM((2, SLOTS, tile_y if dim == 0 else tile_x, depth), jnp.float32)

    def tile(*lead):
        return pltpu.VMEM((*lead, tile_x, tile_y, depth), jnp.float32)

    def padded(parts):
        return pltpu.VMEM(
            (parts, tile_x + 2 * LAYERS, tile_y + 2 * ROWS, depth), jnp.float32
        )

    def exchange(sends):
        return [swap(send, axis, first) for (axis, _, first), send in zip(links, sends)]

    send_shapes = [buffers(dim) for _, dim, _ in links]
    count = len(links)
    sends = pl.pallas_call(
        functools.partial(pack_kernel, links),
        out_shape=send_shapes,
        in_specs=[hbm] * 2,
        out_specs=[vmem] * count,
        scratch_shapes=[pltpu.SemaphoreType.DMA((2 * SLOTS * count,))],
        compiler_params=params,
        cost_estimate=cost(0, 2 * SLOTS * count * tile_x * depth * 4),
        name="pack",
    )(in_hbm(forward), in_hbm(adjoint))
    halos = exchange(sends)

    stress, velocity, accel, rim_added, buoyancy, scaled_lame, scaled_shear = pl.pallas_call(
        functools.partial(velocity_kernel, width_y),
        out_shape=[
            padded(12),
            padded(6),
            tile(3),
            pltpu.VMEM((2, 2, 3, max(tile_x, tile_y), depth), jnp.float32),
            tile(),
            tile(),
            tile(),
        ],
        in_specs=[hbm] * 3 + [smem] * 2 + [vmem] * 4,
        out_specs=[vmem] * 7,
        scratch_shapes=[
            pltpu.VMEM((2, tile_x * tile_y + 3 * (tile_x + tile_y), depth), jnp.float32),
            tile(),
            tile(),
            tile(),
            pltpu.SemaphoreType.DMA((3,)),
        ],
        compiler_params=params,
        cost_estimate=cost(200 * cells, 18 * 4 * cells),
        name="velocity",
    )(
        *(in_hbm(x) for x in (lame_lambda, shear_modulus, density)),
        source_cell,
        source_amp,
        receiver_cell,
        residual_amp,
        forward,
        adjoint,
    )

    velocity, *sends = pl.pallas_call(
        functools.partial(boundary_kernel, links),
        out_shape=[padded(6)] + send_shapes,
        in_specs=[vmem] * (count + 3),
        out_specs=[vmem] * (count + 1),
        input_output_aliases={count + 2: 0},
        compiler_params=params,
        cost_estimate=cost(cells, 10 * 2 * tile_x * depth * 4),
        name="boundary",
    )(*halos, rim_added, buoyancy, velocity)
    velocity_halos = exchange(sends)

    out_shape = jax.ShapeDtypeStruct(forward.shape, jnp.float32)
    strain, gradient, _, forward_next, adjoint_next = pl.pallas_call(
        functools.partial(strain_kernel, links),
        out_shape=[tile(12), tile(3), padded(6), out_shape, out_shape],
        in_specs=[vmem] * (count + 4),
        out_specs=[vmem] * 3 + [hbm] * 2,
        input_output_aliases={count + 2: 2},
        scratch_shapes=[tile(3), pltpu.SemaphoreType.DMA((6,))],
        compiler_params=params,
        cost_estimate=cost(200 * cells, 18 * 4 * cells),
        name="strain",
    )(*halos, rim_added, buoyancy, velocity, accel)

    strain, gradient = pl.pallas_call(
        functools.partial(gradient_kernel, links),
        out_shape=[tile(12), tile(3)],
        in_specs=[vmem] * (count + 5),
        out_specs=[vmem] * 2,
        input_output_aliases={count + 3: 0, count + 4: 1},
        compiler_params=params,
        cost_estimate=cost(30 * cells, 2 * 4 * cells),
        name="gradient",
    )(*velocity_halos, stress, scaled_lame, scaled_shear, strain, gradient)
    other = lax.ppermute(gradient, "shot", [(0, 1), (1, 0)])

    chunk = 4 if tile_x % 4 == 0 else 1
    forward_next, adjoint_next = pl.pallas_call(
        functools.partial(output_kernel, chunk),
        out_shape=[out_shape, out_shape],
        in_specs=[vmem] * 4 + [hbm] * 2,
        out_specs=[hbm] * 2,
        input_output_aliases={4: 0, 5: 1},
        scratch_shapes=[tile(12), pltpu.SemaphoreType.DMA((2 * tile_x // chunk,))],
        compiler_params=params,
        cost_estimate=cost(60 * cells, 18 * 4 * cells),
        name="outputs",
    )(strain, stress, scaled_lame, scaled_shear, forward_next, adjoint_next)
    total = pl.pallas_call(
        sum_kernel,
        out_shape=jax.ShapeDtypeStruct((3, tile_x, tile_y, depth), jnp.float32),
        in_specs=[vmem] * 2,
        out_specs=hbm,
        scratch_shapes=[tile(3), pltpu.SemaphoreType.DMA((3,))],
        compiler_params=params,
        cost_estimate=cost(3 * cells, 9 * 4 * cells),
        name="sum",
    )(gradient, other)
    return forward_next[None], adjoint_next[None], total


def solution(mesh):
    return jax.shard_map(
        body,
        mesh=mesh,
        in_specs=(
            P("shot", None, "tx", "ty", None),
            P("shot", None, "tx", "ty", None),
            P("tx", "ty", None),
            P("tx", "ty", None),
            P("tx", "ty", None),
            P("shot"),
            P("shot"),
            P("shot", None),
            P("shot", None),
        ),
        out_specs=(
            P("shot", None, "tx", "ty", None),
            P("shot", None, "tx", "ty", None),
            P(None, "tx", "ty", None),
        ),
        check_vma=False,
    )
```

```python
import functools

import jax
import jax.numpy as jnp
from jax import lax
from jax.experimental import pallas as pl
from jax.experimental.pallas import tpu as pltpu
from jax.sharding import PartitionSpec as P

near = 9.0 / 8.0
far = -1.0 / 24.0
time_step = 0.15

LAYERS = 2
ROWS = 8
SLOTS = 5

STRESS_ALONG = ((0, 3, 4), (1, 3, 5))
ACCEL_OF = ((0, 1, 2), (1, 0, 2))
VELOCITY_ALONG = ((0, 1, 2), (1, 0, 2))
STRAIN_OF = ((0, 3, 4), (1, 3, 5))

vmem = pl.BlockSpec(memory_space=pltpu.VMEM)
smem = pl.BlockSpec(memory_space=pltpu.SMEM)
hbm = pl.BlockSpec(memory_space=pltpu.HBM)
params = pltpu.CompilerParams(vmem_limit_bytes=24 * 1024 * 1024)


def links_of(sizes):
    far_y, near_y, *along = ("ty", 1, 1), ("ty", 1, 0), ("tx", 0, 1), ("tx", 0, 0)
    return [
        [link for link in order if link[2] + 1 < sizes[link[0]]]
        for order in ((far_y, near_y, *along), (far_y, *along, near_y))
    ]


def swap(value, axis, first):
    pairs = [(i, i + 1) for i in range(first, lax.axis_size(axis) - 1, 2)]
    return lax.ppermute(value, axis, pairs + [(j, i) for i, j in pairs])


def is_lower(axis, first):
    return lax.axis_index(axis) % 2 == first


def has_peer(axis, first):
    index = lax.axis_index(axis)
    partner = jnp.where(is_lower(axis, first), index + 1, index - 1)
    return (partner >= 0) & (partner < lax.axis_size(axis))


def send_faces(field, count, links, sends, plans):
    for (axis, dim, first), send in zip(links, sends):
        lower = is_lower(axis, first)
        upper_plan, lower_plan = plans[dim]

        def put(plan):
            for wave in range(2):
                for slot, (part, index) in enumerate(plan):
                    send[wave, slot] = face(field, count * wave + part, dim, index, True)[...]

        pl.when(lower)(functools.partial(put, lower_plan))
        pl.when(jnp.logical_not(lower))(functools.partial(put, upper_plan))


def stress_plan(dim):
    n, a, b = STRESS_ALONG[dim]
    return (
        ((n, 0), (n, 1), (a, 0), (b, 0), (b, 0)),
        ((n, -1), (a, -2), (a, -1), (b, -2), (b, -1)),
    )


def velocity_plan(dim):
    n, a, b = VELOCITY_ALONG[dim]
    return (
        ((n, 0), (a, 0), (a, 1), (b, 0), (b, 1)),
        ((n, -2), (n, -1), (a, -1), (b, -1), (b, -1)),
    )


def pack_kernel(links, width_y, forward, adjoint, receiver_cell, residual_amp, *refs):
    sends, (added, stress, cells_now, amps_now, sems) = refs[: len(links)], refs[len(links) :]
    tile = forward.shape[1:3]
    copies = [
        pltpu.make_async_copy(receiver_cell, cells_now, sems.at[0]),
        pltpu.make_async_copy(residual_amp, amps_now, sems.at[1]),
    ]
    for copy in copies:
        copy.start()
    for (axis, dim, first), send in zip(links, sends):
        lower = is_lower(axis, first)
        for slot, ((up_part, up_at), (low_part, low_at)) in enumerate(zip(*stress_plan(dim))):
            part = 3 + jnp.where(lower, low_part, up_part)
            at = jnp.where(lower, low_at % tile[dim], up_at % tile[dim])
            for wave, fields in enumerate((forward, adjoint)):
                source = fields.at[part, at] if dim == 0 else fields.at[part, :, at, :]
                copy = pltpu.make_async_copy(source, send.at[wave, slot], sems.at[len(copies)])
                copy.start()
                copies.append(copy)
    for wave in range(2):
        clear_rim(
            stress, *([6 * wave + part for part in STRESS_ALONG[dim]] for dim in range(2))
        )
    columns = column_ids(*tile, width_y, forward.shape[-1])
    for copy in copies[:2]:
        copy.wait()
    added[...] = receiver_sum(cells_now[...], amps_now[...], columns)
    for copy in copies[2:]:
        copy.wait()


def column_ids(tile_x, tile_y, width_y, lanes):
    x_start = lax.axis_index("tx") * tile_x
    y_start = lax.axis_index("ty") * tile_y

    def column(x, y):
        inside = (y >= 0) & (y < width_y)
        return jnp.where(inside, x * width_y + y, -1)

    def iota(shape, dim):
        return lax.broadcasted_iota(jnp.int32, shape, dim)

    shape = (tile_x, tile_y, lanes)
    tile = column(x_start + iota(shape, 0), y_start + iota(shape, 1))
    shape = (3, tile_y, lanes)
    layer = iota(shape, 0)
    along_x = column(
        x_start + jnp.where(layer == 0, -1, tile_x - 1 + layer), y_start + iota(shape, 1)
    )
    shape = (3, tile_x, lanes)
    layer = iota(shape, 0)
    along_y = column(
        x_start + iota(shape, 1), y_start + jnp.where(layer == 0, -1, tile_y - 1 + layer)
    )
    return jnp.concatenate([part.reshape(-1, lanes) for part in (tile, along_x, along_y)], axis=0)


def differ(zero, one, two, minus):
    return near * (one - zero) + far * (two - minus)


def along_x(ref, part, x, tile_y, upward):
    def at(offset):
        return ref[part, x + (LAYERS + offset), pl.ds(ROWS, tile_y), :]

    return differ(at(0), at(1), at(2), at(-1)) if upward else differ(at(-1), at(0), at(1), at(-2))


def along_y(ref, part, x, tile_y, upward):
    def at(offset):
        return ref[part, x + LAYERS, pl.ds(ROWS + offset, tile_y), :]

    return differ(at(0), at(1), at(2), at(-1)) if upward else differ(at(-1), at(0), at(1), at(-2))


def along_z(ref, part, x, tile_y, upward):
    value = ref[part, x + LAYERS, pl.ds(ROWS, tile_y), :]
    depth = value.shape[-1]
    lane = lax.broadcasted_iota(jnp.int32, value.shape, 1)

    def at(offset):
        if offset == 0:
            return value
        moved = pltpu.roll(value, (-offset) % depth, 1)
        inside = lane < depth - offset if offset > 0 else lane >= -offset
        return jnp.where(inside, moved, 0.0)

    return differ(at(0), at(1), at(2), at(-1)) if upward else differ(at(-1), at(0), at(1), at(-2))


def clear_rim(ref, parts_x, parts_y):
    _, layers, rows, depth = ref.shape
    tile_x, tile_y = layers - 2 * LAYERS, rows - 2 * ROWS
    for part in parts_x:
        for begin in (0, LAYERS + tile_x):
            ref[part, pl.ds(begin, LAYERS), pl.ds(ROWS, tile_y), :] = jnp.zeros(
                (LAYERS, tile_y, depth), jnp.float32
            )
    for part in parts_y:
        for begin in (0, ROWS + tile_y):
            ref[part, pl.ds(LAYERS, tile_x), pl.ds(begin, ROWS), :] = jnp.zeros(
                (tile_x, ROWS, depth), jnp.float32
            )


def receiver_sum(cells, amps, columns):
    depth, receivers = columns.shape[-1], cells.shape[-1]
    column = lax.div(cells, depth)
    level = cells - column * depth
    column_hot = jnp.concatenate(
        [
            (columns == column[:, begin : begin + depth]).astype(jnp.bfloat16)
            for begin in range(0, receivers, depth)
        ],
        axis=1,
    )
    levels = lax.broadcasted_iota(jnp.int32, (depth, receivers), 0)
    rest = jnp.where(levels == level, amps, 0.0)
    total = jnp.zeros(columns.shape, jnp.float32)
    for _ in range(3):
        part = rest.astype(jnp.bfloat16)
        rest = rest - part.astype(jnp.float32)
        total = total + lax.dot_general(
            column_hot,
            part,
            (((1,), (1,)), ((), ())),
            preferred_element_type=jnp.float32,
        )
    return total


def velocity_kernel(
    width_y,
    lame,
    shear,
    density,
    source_cell,
    source_amp,
    received,
    forward,
    adjoint,
    _,
    stress,
    velocity,
    accel,
    rim_added,
    buoyancy,
    scaled_lame,
    scaled_shear,
    sourced,
    lame_now,
    shear_now,
    density_now,
    sems,
):
    tile_x, tile_y, depth = density.shape
    copies = [
        pltpu.make_async_copy(source, target, sems.at[at])
        for at, (source, target) in enumerate((
            (density, density_now),
            (lame, lame_now),
            (shear, shear_now),
        ))
    ]
    for copy in copies:
        copy.start()
    cells = tile_x * tile_y
    middle = pl.ds(ROWS, tile_y)
    columns = column_ids(tile_x, tile_y, width_y, depth)
    lane = lax.broadcasted_iota(jnp.int32, columns.shape, 1)
    sourced[...] = jnp.where(columns * depth + lane == source_cell[0], source_amp[0], 0.0)
    for wave, added in enumerate((sourced, received)):
        for layer in range(3):
            rim_added[wave, 0, layer] = added[pl.ds(cells + layer * tile_y, tile_y), :]
            begin = cells + 3 * tile_y + layer * tile_x
            rim_added[wave, 1, layer] = added[pl.ds(begin, tile_x), :]
    for copy in copies:
        copy.wait()

    def fill(x, carry):
        for wave, (fields, added) in enumerate(((forward, sourced), (adjoint, received))):
            extra = added[pl.ds(pl.multiple_of(x * tile_y, 8), tile_y), :]
            for part in range(6):
                value = fields[3 + part, x]
                stress[6 * wave + part, x + LAYERS, middle, :] = (
                    value + extra if part < 3 else value
                )
        buoyancy[x] = 1.0 / density_now[x]
        scaled_lame[x] = time_step * lame_now[x]
        scaled_shear[x] = time_step * shear_now[x]
        return carry

    lax.fori_loop(0, tile_x, fill, 0, unroll=4)

    def layer(x, carry):
        light = buoyancy[x]
        for wave, fields in enumerate((forward, adjoint)):
            xx, yy, zz, xy, xz, yz = range(6 * wave, 6 * wave + 6)
            values = (
                along_x(stress, xx, x, tile_y, True)
                + along_y(stress, xy, x, tile_y, False)
                + along_z(stress, xz, x, tile_y, False),
                along_x(stress, xy, x, tile_y, False)
                + along_y(stress, yy, x, tile_y, True)
                + along_z(stress, yz, x, tile_y, False),
                along_x(stress, xz, x, tile_y, False)
                + along_y(stress, yz, x, tile_y, False)
                + along_z(stress, zz, x, tile_y, True),
            )
            for part, value in enumerate(values):
                value = light * value
                if wave == 0:
                    accel[part, x] = value
                velocity[3 * wave + part, x + LAYERS, middle, :] = (
                    fields[part, x] + time_step * value
                )
        return carry

    lax.fori_loop(0, tile_x, layer, 0, unroll=4)


def stress_halo_terms(links, received, rim_added, waves, add):
    for (axis, dim, first), halo in zip(links, received):
        part_n, part_a, part_b = ACCEL_OF[dim]
        lower = is_lower(axis, first)
        real = has_peer(axis, first)

        @pl.when(real & lower)
        def after():
            for wave in waves:
                n0 = halo[wave, 0] + rim_added[wave, dim, 1]
                n1 = halo[wave, 1] + rim_added[wave, dim, 2]
                add(wave, part_n, dim, -1, near * n0 + far * n1)
                add(wave, part_n, dim, -2, far * n0)
                add(wave, part_a, dim, -1, far * halo[wave, 2])
                add(wave, part_b, dim, -1, far * halo[wave, 3])

        @pl.when(real & jnp.logical_not(lower))
        def before():
            for wave in waves:
                n0 = halo[wave, 0] + rim_added[wave, dim, 0]
                add(wave, part_n, dim, 0, -far * n0)
                for part, slot in ((part_a, 1), (part_b, 3)):
                    outer, inner = halo[wave, slot], halo[wave, slot + 1]
                    add(wave, part, dim, 0, -near * inner - far * outer)
                    add(wave, part, dim, 1, -far * inner)


def velocity_halo_terms(links, received, add):
    for (axis, dim, first), halo in zip(links, received):
        part_n, part_a, part_b = STRAIN_OF[dim]
        lower = is_lower(axis, first)
        real = has_peer(axis, first)

        @pl.when(real & lower)
        def after():
            for wave in range(2):
                add(wave, part_n, dim, -1, far * halo[wave, 0])
                for part, slot in ((part_a, 1), (part_b, 3)):
                    inner, outer = halo[wave, slot], halo[wave, slot + 1]
                    add(wave, part, dim, -1, near * inner + far * outer)
                    add(wave, part, dim, -2, far * inner)

        @pl.when(real & jnp.logical_not(lower))
        def before():
            for wave in range(2):
                outer, inner = halo[wave, 0], halo[wave, 1]
                add(wave, part_n, dim, 0, -near * inner - far * outer)
                add(wave, part_n, dim, 1, -far * inner)
                add(wave, part_a, dim, 0, -far * halo[wave, 2])
                add(wave, part_b, dim, 0, -far * halo[wave, 3])


def face(ref, part, dim, index, padded):
    layers, rows, depth = ref.shape[1:]
    tile_x = layers - 2 * LAYERS if padded else layers
    tile_y = rows - 2 * ROWS if padded else rows
    if dim == 0:
        at = index % tile_x
        if padded:
            return ref.at[part, at + LAYERS, pl.ds(ROWS, tile_y), :]
        return ref.at[part, at]
    at = index % tile_y
    flat = ref.reshape(ref.shape[0], layers * rows, depth)
    begin = LAYERS * rows + ROWS + at if padded else at
    return flat.at[part, pl.ds(begin, tile_x, stride=rows), :]


def light_face(buoyancy, dim, index):
    layers, rows, depth = buoyancy.shape
    if dim == 0:
        return buoyancy[index % layers]
    return buoyancy.reshape(layers * rows, depth)[pl.ds(index % rows, layers, stride=rows), :]


def boundary_kernel(links, later_links, *refs):
    count = len(links)
    received = refs[:count]
    rim_added, buoyancy, _ = refs[count : count + 3]
    velocity = refs[count + 3]
    sends = refs[count + 4 :]

    def add(wave, part, dim, index, term):
        target = face(velocity, 3 * wave + part, dim, index, True)
        target[...] += time_step * light_face(buoyancy, dim, index) * term

    stress_halo_terms(links, received, rim_added, (0, 1), add)
    send_faces(velocity, 3, later_links, sends, [velocity_plan(dim) for dim in range(2)])


def strain_kernel(links, *refs):
    count = len(links)
    received = refs[:count]
    rim_added, buoyancy, _, accel, strain, gradient, velocity = refs[count : count + 7]
    outputs, (accel_now, sems) = refs[count + 7 : count + 9], refs[count + 9 :]
    tile_x, tile_y, _ = buoyancy.shape
    middle = pl.ds(ROWS, tile_y)
    copies = [
        pltpu.make_async_copy(
            velocity.at[3 * wave + part, pl.ds(LAYERS, tile_x), middle, :],
            outputs[wave].at[part],
            sems.at[3 * wave + part],
        )
        for wave in range(2)
        for part in range(3)
    ]
    for copy in copies:
        copy.start()
    clear_rim(velocity, range(6), range(6))
    accel_now[...] = accel[...]

    def add(wave, part, dim, index, term):
        target = face(accel_now, part, dim, index, False)
        target[...] += light_face(buoyancy, dim, index) * term

    stress_halo_terms(links, received, rim_added, (0,), add)

    def layer(x, carry):
        for wave in range(2):
            vx, vy, vz = range(3 * wave, 3 * wave + 3)
            values = (
                along_x(velocity, vx, x, tile_y, False),
                along_y(velocity, vy, x, tile_y, False),
                along_z(velocity, vz, x, tile_y, False),
                along_y(velocity, vx, x, tile_y, True) + along_x(velocity, vy, x, tile_y, True),
                along_z(velocity, vx, x, tile_y, True) + along_x(velocity, vz, x, tile_y, True),
                along_z(velocity, vy, x, tile_y, True) + along_y(velocity, vz, x, tile_y, True),
            )
            for part, value in enumerate(values):
                strain[6 * wave + part, x] = value
        total = sum(
            accel_now[part, x] * velocity[3 + part, x + LAYERS, middle, :] for part in range(3)
        )
        gradient[2, x] = -time_step * total
        return carry

    lax.fori_loop(0, tile_x, layer, 0, unroll=4)
    for copy in copies:
        copy.wait()


def new_stress(strain, stress, scaled_lame, scaled_shear, wave, x, tile_y):
    lame, shear = scaled_lame[x], scaled_shear[x]
    strains = [strain[6 * wave + part, x] for part in range(6)]
    volume = lame * (strains[0] + strains[1] + strains[2])
    values = []
    for part in range(6):
        old = stress[6 * wave + part, x + LAYERS, pl.ds(ROWS, tile_y), :]
        if part < 3:
            values.append(old + (volume + 2.0 * shear * strains[part]))
        else:
            values.append(old + shear * strains[part])
    return strains, values


def gradient_kernel(links, *refs):
    count = len(links)
    received = refs[:count]
    stress, scaled_lame, scaled_shear, _, _, strain, gradient = refs[count:]
    tile_x, tile_y, _ = scaled_lame.shape

    def add(wave, part, dim, index, term):
        target = face(strain, 6 * wave + part, dim, index, False)
        target[...] += term

    velocity_halo_terms(links, received, add)

    def layer(x, carry):
        strains = [strain[part, x] for part in range(6)]
        _, values = new_stress(strain, stress, scaled_lame, scaled_shear, 1, x, tile_y)
        trace = strains[0] + strains[1] + strains[2]
        gradient[0, x] = -time_step * trace * (values[0] + values[1] + values[2])
        total = sum(left * right for left, right in zip(strains, values))
        gradient[1, x] = -time_step * total
        return carry

    lax.fori_loop(0, tile_x, layer, 0, unroll=4)


def output_kernel(chunk, strain, stress, scaled_lame, scaled_shear, *refs):
    outputs, (values_now, sems) = refs[2:4], refs[4:]
    tile_x, tile_y, _ = scaled_lame.shape
    copies = []
    for begin in range(0, tile_x, chunk):
        for wave in range(2):
            for x in range(begin, begin + chunk):
                _, values = new_stress(strain, stress, scaled_lame, scaled_shear, wave, x, tile_y)
                for part in range(6):
                    values_now[6 * wave + part, x] = values[part]
            layers = pl.ds(begin, chunk)
            copy = pltpu.make_async_copy(
                values_now.at[pl.ds(6 * wave, 6), layers],
                outputs[wave].at[pl.ds(3, 6), layers],
                sems.at[len(copies)],
            )
            copy.start()
            copies.append(copy)
    for copy in copies:
        copy.wait()


def sum_kernel(mine, other, total, total_now, sems):
    copies = []
    for part in range(mine.shape[0]):
        total_now[part] = mine[part] + other[part]
        copy = pltpu.make_async_copy(total_now.at[part], total.at[part], sems.at[part])
        copy.start()
        copies.append(copy)
    for copy in copies:
        copy.wait()


def in_hbm(value):
    return pltpu.with_memory_space_constraint(value, pltpu.HBM)


def cost(flops, size):
    return pl.CostEstimate(flops=flops, bytes_accessed=size, transcendentals=0)


def body(
    forward_fields,
    adjoint_fields,
    lame_lambda,
    shear_modulus,
    density,
    source_cell,
    source_amp,
    receiver_cell,
    residual_amp,
):
    _, _, tile_x, tile_y, depth = forward_fields.shape
    forward = forward_fields.reshape(forward_fields.shape[1:])
    adjoint = adjoint_fields.reshape(adjoint_fields.shape[1:])
    sizes = {name: lax.axis_size(name) for name in ("tx", "ty")}
    width_y = tile_y * sizes["ty"]
    links, later_links = links_of(sizes)
    cells = tile_x * tile_y * depth

    def buffers(dim):
        return pltpu.VMEM((2, SLOTS, tile_y if dim == 0 else tile_x, depth), jnp.float32)

    def tile(*lead):
        return pltpu.VMEM((*lead, tile_x, tile_y, depth), jnp.float32)

    def padded(parts):
        return pltpu.VMEM(
            (parts, tile_x + 2 * LAYERS, tile_y + 2 * ROWS, depth), jnp.float32
        )

    def exchange(links, sends):
        return [swap(send, axis, first) for (axis, _, first), send in zip(links, sends)]

    send_shapes = [buffers(dim) for _, dim, _ in links]
    count = len(links)
    receivers = receiver_cell.shape[-1]
    rows = tile_x * tile_y + 3 * (tile_x + tile_y)
    *sends, added, stress = pl.pallas_call(
        functools.partial(pack_kernel, links, width_y),
        out_shape=send_shapes + [pltpu.VMEM((rows, depth), jnp.float32), padded(12)],
        in_specs=[hbm] * 4,
        out_specs=[vmem] * (count + 2),
        scratch_shapes=[
            pltpu.VMEM((1, receivers), jnp.int32),
            pltpu.VMEM((1, receivers), jnp.float32),
            pltpu.SemaphoreType.DMA((2 + 2 * SLOTS * count,)),
        ],
        compiler_params=params,
        cost_estimate=cost(6 * rows * receivers * depth, 2 * SLOTS * count * tile_x * depth * 4),
        name="pack",
    )(*(in_hbm(x) for x in (forward, adjoint, receiver_cell, residual_amp)))
    halos = exchange(links, sends)

    stress, velocity, accel, rim_added, buoyancy, scaled_lame, scaled_shear = pl.pallas_call(
        functools.partial(velocity_kernel, width_y),
        out_shape=[
            padded(12),
            padded(6),
            tile(3),
            pltpu.VMEM((2, 2, 3, max(tile_x, tile_y), depth), jnp.float32),
            tile(),
            tile(),
            tile(),
        ],
        in_specs=[hbm] * 3 + [smem] * 2 + [vmem] * 4,
        out_specs=[vmem] * 7,
        input_output_aliases={8: 0},
        scratch_shapes=[
            pltpu.VMEM((rows, depth), jnp.float32),
            tile(),
            tile(),
            tile(),
            pltpu.SemaphoreType.DMA((3,)),
        ],
        compiler_params=params,
        cost_estimate=cost(200 * cells, 18 * 4 * cells),
        name="velocity",
    )(
        *(in_hbm(x) for x in (lame_lambda, shear_modulus, density)),
        source_cell,
        source_amp,
        added,
        forward,
        adjoint,
        stress,
    )

    velocity, *sends = pl.pallas_call(
        functools.partial(boundary_kernel, links, later_links),
        out_shape=[padded(6)] + [buffers(dim) for _, dim, _ in later_links],
        in_specs=[vmem] * (count + 3),
        out_specs=[vmem] * (count + 1),
        input_output_aliases={count + 2: 0},
        compiler_params=params,
        cost_estimate=cost(cells, 10 * 2 * tile_x * depth * 4),
        name="boundary",
    )(*halos, rim_added, buoyancy, velocity)
    velocity_halos = exchange(later_links, sends)

    out_shape = jax.ShapeDtypeStruct(forward.shape, jnp.float32)
    strain, gradient, _, forward_next, adjoint_next = pl.pallas_call(
        functools.partial(strain_kernel, links),
        out_shape=[tile(12), tile(3), padded(6), out_shape, out_shape],
        in_specs=[vmem] * (count + 4),
        out_specs=[vmem] * 3 + [hbm] * 2,
        input_output_aliases={count + 2: 2},
        scratch_shapes=[tile(3), pltpu.SemaphoreType.DMA((6,))],
        compiler_params=params,
        cost_estimate=cost(200 * cells, 18 * 4 * cells),
        name="strain",
    )(*halos, rim_added, buoyancy, velocity, accel)

    strain, gradient = pl.pallas_call(
        functools.partial(gradient_kernel, later_links),
        out_shape=[tile(12), tile(3)],
        in_specs=[vmem] * (count + 5),
        out_specs=[vmem] * 2,
        input_output_aliases={count + 3: 0, count + 4: 1},
        compiler_params=params,
        cost_estimate=cost(30 * cells, 2 * 4 * cells),
        name="gradient",
    )(*velocity_halos, stress, scaled_lame, scaled_shear, strain, gradient)
    other = lax.ppermute(gradient, "shot", [(0, 1), (1, 0)])

    chunk = 4 if tile_x % 4 == 0 else 1
    forward_next, adjoint_next = pl.pallas_call(
        functools.partial(output_kernel, chunk),
        out_shape=[out_shape, out_shape],
        in_specs=[vmem] * 4 + [hbm] * 2,
        out_specs=[hbm] * 2,
        input_output_aliases={4: 0, 5: 1},
        scratch_shapes=[tile(12), pltpu.SemaphoreType.DMA((2 * tile_x // chunk,))],
        compiler_params=params,
        cost_estimate=cost(60 * cells, 18 * 4 * cells),
        name="outputs",
    )(strain, stress, scaled_lame, scaled_shear, forward_next, adjoint_next)
    total = pl.pallas_call(
        sum_kernel,
        out_shape=jax.ShapeDtypeStruct((3, tile_x, tile_y, depth), jnp.float32),
        in_specs=[vmem] * 2,
        out_specs=hbm,
        scratch_shapes=[tile(3), pltpu.SemaphoreType.DMA((3,))],
        compiler_params=params,
        cost_estimate=cost(3 * cells, 9 * 4 * cells),
        name="sum",
    )(gradient, other)
    return forward_next[None], adjoint_next[None], total


def solution(mesh):
    return jax.shard_map(
        body,
        mesh=mesh,
        in_specs=(
            P("shot", None, "tx", "ty", None),
            P("shot", None, "tx", "ty", None),
            P("tx", "ty", None),
            P("tx", "ty", None),
            P("tx", "ty", None),
            P("shot"),
            P("shot"),
            P("shot", None),
            P("shot", None),
        ),
        out_specs=(
            P("shot", None, "tx", "ty", None),
            P("shot", None, "tx", "ty", None),
            P(None, "tx", "ty", None),
        ),
        check_vma=False,
    )
```

```python
import functools

import jax
import jax.numpy as jnp
from jax import lax
from jax.experimental import pallas as pl
from jax.experimental.pallas import tpu as pltpu
from jax.sharding import PartitionSpec as P

near = 9.0 / 8.0
far = -1.0 / 24.0
time_step = 0.15

LAYERS = 2
ROWS = 8
SLOTS = 5

STRESS_ALONG = ((0, 3, 4), (1, 3, 5))
ACCEL_OF = ((0, 1, 2), (1, 0, 2))
VELOCITY_ALONG = ((0, 1, 2), (1, 0, 2))
STRAIN_OF = ((0, 3, 4), (1, 3, 5))

vmem = pl.BlockSpec(memory_space=pltpu.VMEM)
smem = pl.BlockSpec(memory_space=pltpu.SMEM)
hbm = pl.BlockSpec(memory_space=pltpu.HBM)
params = pltpu.CompilerParams(vmem_limit_bytes=24 * 1024 * 1024)


def links_of(sizes):
    far_y, near_y, *along = ("ty", 1, 1), ("ty", 1, 0), ("tx", 0, 1), ("tx", 0, 0)
    return [
        [link for link in order if link[2] + 1 < sizes[link[0]]]
        for order in ((far_y, *along, near_y), (far_y, *along, near_y))
    ]


def swap(value, axis, first):
    pairs = [(i, i + 1) for i in range(first, lax.axis_size(axis) - 1, 2)]
    return lax.ppermute(value, axis, pairs + [(j, i) for i, j in pairs])


def is_lower(axis, first):
    return lax.axis_index(axis) % 2 == first


def has_peer(axis, first):
    index = lax.axis_index(axis)
    partner = jnp.where(is_lower(axis, first), index + 1, index - 1)
    return (partner >= 0) & (partner < lax.axis_size(axis))


def send_faces(field, count, links, sends, plans):
    for (axis, dim, first), send in zip(links, sends):
        lower = is_lower(axis, first)
        upper_plan, lower_plan = plans[dim]

        def put(plan):
            for wave in range(2):
                for slot, (part, index) in enumerate(plan):
                    send[wave, slot] = face(field, count * wave + part, dim, index, True)[...]

        pl.when(lower)(functools.partial(put, lower_plan))
        pl.when(jnp.logical_not(lower))(functools.partial(put, upper_plan))


def stress_plan(dim):
    n, a, b = STRESS_ALONG[dim]
    return (
        ((n, 0), (n, 1), (a, 0), (b, 0), (b, 0)),
        ((n, -1), (a, -2), (a, -1), (b, -2), (b, -1)),
    )


def velocity_plan(dim):
    n, a, b = VELOCITY_ALONG[dim]
    return (
        ((n, 0), (a, 0), (a, 1), (b, 0), (b, 1)),
        ((n, -2), (n, -1), (a, -1), (b, -1), (b, -1)),
    )


def pack_kernel(links, width_y, forward, adjoint, receiver_cell, residual_amp, *refs):
    sends, (added, stress, cells_now, amps_now, sems) = refs[: len(links)], refs[len(links) :]
    tile = forward.shape[1:3]
    copies = [
        pltpu.make_async_copy(receiver_cell, cells_now, sems.at[0]),
        pltpu.make_async_copy(residual_amp, amps_now, sems.at[1]),
    ]
    for copy in copies:
        copy.start()
    for (axis, dim, first), send in zip(links, sends):
        lower = is_lower(axis, first)
        for slot, ((up_part, up_at), (low_part, low_at)) in enumerate(zip(*stress_plan(dim))):
            part = 3 + jnp.where(lower, low_part, up_part)
            at = jnp.where(lower, low_at % tile[dim], up_at % tile[dim])
            for wave, fields in enumerate((forward, adjoint)):
                source = fields.at[part, at] if dim == 0 else fields.at[part, :, at, :]
                copy = pltpu.make_async_copy(source, send.at[wave, slot], sems.at[len(copies)])
                copy.start()
                copies.append(copy)
    for wave in range(2):
        clear_rim(
            stress, *([6 * wave + part for part in STRESS_ALONG[dim]] for dim in range(2))
        )
    columns = column_ids(*tile, width_y, forward.shape[-1])
    for copy in copies[:2]:
        copy.wait()
    added[...] = receiver_sum(cells_now[...], amps_now[...], columns)
    for copy in copies[2:]:
        copy.wait()


def column_ids(tile_x, tile_y, width_y, lanes):
    x_start = lax.axis_index("tx") * tile_x
    y_start = lax.axis_index("ty") * tile_y

    def column(x, y):
        inside = (y >= 0) & (y < width_y)
        return jnp.where(inside, x * width_y + y, -1)

    def iota(shape, dim):
        return lax.broadcasted_iota(jnp.int32, shape, dim)

    shape = (tile_x, tile_y, lanes)
    tile = column(x_start + iota(shape, 0), y_start + iota(shape, 1))
    shape = (3, tile_y, lanes)
    layer = iota(shape, 0)
    along_x = column(
        x_start + jnp.where(layer == 0, -1, tile_x - 1 + layer), y_start + iota(shape, 1)
    )
    shape = (3, tile_x, lanes)
    layer = iota(shape, 0)
    along_y = column(
        x_start + iota(shape, 1), y_start + jnp.where(layer == 0, -1, tile_y - 1 + layer)
    )
    return jnp.concatenate([part.reshape(-1, lanes) for part in (tile, along_x, along_y)], axis=0)


def differ(zero, one, two, minus):
    return near * (one - zero) + far * (two - minus)


def along_x(ref, part, x, tile_y, upward):
    def at(offset):
        return ref[part, x + (LAYERS + offset), pl.ds(ROWS, tile_y), :]

    return differ(at(0), at(1), at(2), at(-1)) if upward else differ(at(-1), at(0), at(1), at(-2))


def along_y(ref, part, x, tile_y, upward):
    def at(offset):
        return ref[part, x + LAYERS, pl.ds(ROWS + offset, tile_y), :]

    return differ(at(0), at(1), at(2), at(-1)) if upward else differ(at(-1), at(0), at(1), at(-2))


def along_z(ref, part, x, tile_y, upward):
    value = ref[part, x + LAYERS, pl.ds(ROWS, tile_y), :]
    depth = value.shape[-1]
    lane = lax.broadcasted_iota(jnp.int32, value.shape, 1)

    def at(offset):
        if offset == 0:
            return value
        moved = pltpu.roll(value, (-offset) % depth, 1)
        inside = lane < depth - offset if offset > 0 else lane >= -offset
        return jnp.where(inside, moved, 0.0)

    return differ(at(0), at(1), at(2), at(-1)) if upward else differ(at(-1), at(0), at(1), at(-2))


def clear_rim(ref, parts_x, parts_y):
    _, layers, rows, depth = ref.shape
    tile_x, tile_y = layers - 2 * LAYERS, rows - 2 * ROWS
    for part in parts_x:
        for begin in (0, LAYERS + tile_x):
            ref[part, pl.ds(begin, LAYERS), pl.ds(ROWS, tile_y), :] = jnp.zeros(
                (LAYERS, tile_y, depth), jnp.float32
            )
    for part in parts_y:
        for begin in (0, ROWS + tile_y):
            ref[part, pl.ds(LAYERS, tile_x), pl.ds(begin, ROWS), :] = jnp.zeros(
                (tile_x, ROWS, depth), jnp.float32
            )


def receiver_sum(cells, amps, columns):
    depth, receivers = columns.shape[-1], cells.shape[-1]
    column = lax.div(cells, depth)
    level = cells - column * depth
    column_hot = jnp.concatenate(
        [
            (columns == column[:, begin : begin + depth]).astype(jnp.bfloat16)
            for begin in range(0, receivers, depth)
        ],
        axis=1,
    )
    levels = lax.broadcasted_iota(jnp.int32, (depth, receivers), 0)
    rest = jnp.where(levels == level, amps, 0.0)
    total = jnp.zeros(columns.shape, jnp.float32)
    for _ in range(3):
        part = rest.astype(jnp.bfloat16)
        rest = rest - part.astype(jnp.float32)
        total = total + lax.dot_general(
            column_hot,
            part,
            (((1,), (1,)), ((), ())),
            preferred_element_type=jnp.float32,
        )
    return total


def velocity_kernel(
    width_y,
    lame,
    shear,
    density,
    source_cell,
    source_amp,
    received,
    forward,
    adjoint,
    _,
    stress,
    velocity,
    accel,
    rim_added,
    buoyancy,
    scaled_lame,
    scaled_shear,
    sourced,
    gained,
    lame_now,
    shear_now,
    density_now,
    sems,
):
    tile_x, tile_y, depth = density.shape
    copies = [
        pltpu.make_async_copy(source, target, sems.at[at])
        for at, (source, target) in enumerate((
            (density, density_now),
            (lame, lame_now),
            (shear, shear_now),
        ))
    ]
    for copy in copies:
        copy.start()
    cells = tile_x * tile_y
    middle = pl.ds(ROWS, tile_y)
    columns = column_ids(tile_x, tile_y, width_y, depth)
    lane = lax.broadcasted_iota(jnp.int32, columns.shape, 1)
    sourced[...] = jnp.where(columns * depth + lane == source_cell[0], source_amp[0], 0.0)
    for wave, added in enumerate((sourced, received)):
        for layer in range(3):
            rim_added[wave, 0, layer] = added[pl.ds(cells + layer * tile_y, tile_y), :]
            begin = cells + 3 * tile_y + layer * tile_x
            rim_added[wave, 1, layer] = added[pl.ds(begin, tile_x), :]

    def fill(x, carry):
        for wave, (fields, added) in enumerate(((forward, sourced), (adjoint, received))):
            extra = added[pl.ds(pl.multiple_of(x * tile_y, 8), tile_y), :]
            for part in range(6):
                value = fields[3 + part, x]
                stress[6 * wave + part, x + LAYERS, middle, :] = (
                    value + extra if part < 3 else value
                )
        return carry

    lax.fori_loop(0, tile_x, fill, 0, unroll=4)

    def layer(x, carry):
        for wave in range(2):
            xx, yy, zz, xy, xz, yz = range(6 * wave, 6 * wave + 6)
            values = (
                along_x(stress, xx, x, tile_y, True)
                + along_y(stress, xy, x, tile_y, False)
                + along_z(stress, xz, x, tile_y, False),
                along_x(stress, xy, x, tile_y, False)
                + along_y(stress, yy, x, tile_y, True)
                + along_z(stress, yz, x, tile_y, False),
                along_x(stress, xz, x, tile_y, False)
                + along_y(stress, yz, x, tile_y, False)
                + along_z(stress, zz, x, tile_y, True),
            )
            for part, value in enumerate(values):
                gained[3 * wave + part, x] = value
        return carry

    lax.fori_loop(0, tile_x, layer, 0, unroll=4)
    for copy in copies:
        copy.wait()

    def finish(x, carry):
        light = 1.0 / density_now[x]
        buoyancy[x] = light
        scaled_lame[x] = time_step * lame_now[x]
        scaled_shear[x] = time_step * shear_now[x]
        for wave, fields in enumerate((forward, adjoint)):
            for part in range(3):
                value = light * gained[3 * wave + part, x]
                if wave == 0:
                    accel[part, x] = value
                velocity[3 * wave + part, x + LAYERS, middle, :] = (
                    fields[part, x] + time_step * value
                )
        return carry

    lax.fori_loop(0, tile_x, finish, 0, unroll=4)


def stress_halo_terms(links, received, rim_added, waves, add):
    for (axis, dim, first), halo in zip(links, received):
        part_n, part_a, part_b = ACCEL_OF[dim]
        lower = is_lower(axis, first)
        real = has_peer(axis, first)

        @pl.when(real & lower)
        def after():
            for wave in waves:
                n0 = halo[wave, 0] + rim_added[wave, dim, 1]
                n1 = halo[wave, 1] + rim_added[wave, dim, 2]
                add(wave, part_n, dim, -1, near * n0 + far * n1)
                add(wave, part_n, dim, -2, far * n0)
                add(wave, part_a, dim, -1, far * halo[wave, 2])
                add(wave, part_b, dim, -1, far * halo[wave, 3])

        @pl.when(real & jnp.logical_not(lower))
        def before():
            for wave in waves:
                n0 = halo[wave, 0] + rim_added[wave, dim, 0]
                add(wave, part_n, dim, 0, -far * n0)
                for part, slot in ((part_a, 1), (part_b, 3)):
                    outer, inner = halo[wave, slot], halo[wave, slot + 1]
                    add(wave, part, dim, 0, -near * inner - far * outer)
                    add(wave, part, dim, 1, -far * inner)


def velocity_halo_terms(links, received, add):
    for (axis, dim, first), halo in zip(links, received):
        part_n, part_a, part_b = STRAIN_OF[dim]
        lower = is_lower(axis, first)
        real = has_peer(axis, first)

        @pl.when(real & lower)
        def after():
            for wave in range(2):
                add(wave, part_n, dim, -1, far * halo[wave, 0])
                for part, slot in ((part_a, 1), (part_b, 3)):
                    inner, outer = halo[wave, slot], halo[wave, slot + 1]
                    add(wave, part, dim, -1, near * inner + far * outer)
                    add(wave, part, dim, -2, far * inner)

        @pl.when(real & jnp.logical_not(lower))
        def before():
            for wave in range(2):
                outer, inner = halo[wave, 0], halo[wave, 1]
                add(wave, part_n, dim, 0, -near * inner - far * outer)
                add(wave, part_n, dim, 1, -far * inner)
                add(wave, part_a, dim, 0, -far * halo[wave, 2])
                add(wave, part_b, dim, 0, -far * halo[wave, 3])


def face(ref, part, dim, index, padded):
    layers, rows, depth = ref.shape[1:]
    tile_x = layers - 2 * LAYERS if padded else layers
    tile_y = rows - 2 * ROWS if padded else rows
    if dim == 0:
        at = index % tile_x
        if padded:
            return ref.at[part, at + LAYERS, pl.ds(ROWS, tile_y), :]
        return ref.at[part, at]
    at = index % tile_y
    flat = ref.reshape(ref.shape[0], layers * rows, depth)
    begin = LAYERS * rows + ROWS + at if padded else at
    return flat.at[part, pl.ds(begin, tile_x, stride=rows), :]


def light_face(buoyancy, dim, index):
    layers, rows, depth = buoyancy.shape
    if dim == 0:
        return buoyancy[index % layers]
    return buoyancy.reshape(layers * rows, depth)[pl.ds(index % rows, layers, stride=rows), :]


def boundary_kernel(links, later_links, *refs):
    count = len(links)
    received = refs[:count]
    rim_added, buoyancy, _ = refs[count : count + 3]
    velocity = refs[count + 3]
    sends = refs[count + 4 :]

    def add(wave, part, dim, index, term):
        target = face(velocity, 3 * wave + part, dim, index, True)
        target[...] += time_step * light_face(buoyancy, dim, index) * term

    stress_halo_terms(links, received, rim_added, (0, 1), add)
    send_faces(velocity, 3, later_links, sends, [velocity_plan(dim) for dim in range(2)])


def strain_kernel(links, *refs):
    count = len(links)
    received = refs[:count]
    rim_added, buoyancy, _, accel, strain, gradient, velocity = refs[count : count + 7]
    outputs, (accel_now, sems) = refs[count + 7 : count + 9], refs[count + 9 :]
    tile_x, tile_y, _ = buoyancy.shape
    middle = pl.ds(ROWS, tile_y)
    copies = [
        pltpu.make_async_copy(
            velocity.at[3 * wave + part, pl.ds(LAYERS, tile_x), middle, :],
            outputs[wave].at[part],
            sems.at[3 * wave + part],
        )
        for wave in range(2)
        for part in range(3)
    ]
    for copy in copies:
        copy.start()
    clear_rim(velocity, range(6), range(6))
    accel_now[...] = accel[...]

    def add(wave, part, dim, index, term):
        target = face(accel_now, part, dim, index, False)
        target[...] += light_face(buoyancy, dim, index) * term

    stress_halo_terms(links, received, rim_added, (0,), add)

    def layer(x, carry):
        for wave in range(2):
            vx, vy, vz = range(3 * wave, 3 * wave + 3)
            values = (
                along_x(velocity, vx, x, tile_y, False),
                along_y(velocity, vy, x, tile_y, False),
                along_z(velocity, vz, x, tile_y, False),
                along_y(velocity, vx, x, tile_y, True) + along_x(velocity, vy, x, tile_y, True),
                along_z(velocity, vx, x, tile_y, True) + along_x(velocity, vz, x, tile_y, True),
                along_z(velocity, vy, x, tile_y, True) + along_y(velocity, vz, x, tile_y, True),
            )
            for part, value in enumerate(values):
                strain[6 * wave + part, x] = value
        total = sum(
            accel_now[part, x] * velocity[3 + part, x + LAYERS, middle, :] for part in range(3)
        )
        gradient[2, x] = -time_step * total
        return carry

    lax.fori_loop(0, tile_x, layer, 0, unroll=4)
    for copy in copies:
        copy.wait()


def new_stress(strain, stress, scaled_lame, scaled_shear, wave, x, tile_y):
    lame, shear = scaled_lame[x], scaled_shear[x]
    strains = [strain[6 * wave + part, x] for part in range(6)]
    volume = lame * (strains[0] + strains[1] + strains[2])
    values = []
    for part in range(6):
        old = stress[6 * wave + part, x + LAYERS, pl.ds(ROWS, tile_y), :]
        if part < 3:
            values.append(old + (volume + 2.0 * shear * strains[part]))
        else:
            values.append(old + shear * strains[part])
    return strains, values


def gradient_kernel(links, *refs):
    count = len(links)
    received = refs[:count]
    stress, scaled_lame, scaled_shear, _, _, strain, gradient = refs[count:]
    tile_x, tile_y, _ = scaled_lame.shape

    def add(wave, part, dim, index, term):
        target = face(strain, 6 * wave + part, dim, index, False)
        target[...] += term

    velocity_halo_terms(links, received, add)

    def layer(x, carry):
        strains = [strain[part, x] for part in range(6)]
        _, values = new_stress(strain, stress, scaled_lame, scaled_shear, 1, x, tile_y)
        trace = strains[0] + strains[1] + strains[2]
        gradient[0, x] = -time_step * trace * (values[0] + values[1] + values[2])
        total = sum(left * right for left, right in zip(strains, values))
        gradient[1, x] = -time_step * total
        return carry

    lax.fori_loop(0, tile_x, layer, 0, unroll=4)


def output_kernel(chunk, strain, stress, scaled_lame, scaled_shear, *refs):
    outputs, (values_now, sems) = refs[2:4], refs[4:]
    tile_x, tile_y, _ = scaled_lame.shape
    copies = []
    for begin in range(0, tile_x, chunk):
        for wave in range(2):
            for x in range(begin, begin + chunk):
                _, values = new_stress(strain, stress, scaled_lame, scaled_shear, wave, x, tile_y)
                for part in range(6):
                    values_now[6 * wave + part, x] = values[part]
            layers = pl.ds(begin, chunk)
            copy = pltpu.make_async_copy(
                values_now.at[pl.ds(6 * wave, 6), layers],
                outputs[wave].at[pl.ds(3, 6), layers],
                sems.at[len(copies)],
            )
            copy.start()
            copies.append(copy)
    for copy in copies:
        copy.wait()


def sum_kernel(mine, other, total, total_now, sems):
    copies = []
    for part in range(mine.shape[0]):
        total_now[part] = mine[part] + other[part]
        copy = pltpu.make_async_copy(total_now.at[part], total.at[part], sems.at[part])
        copy.start()
        copies.append(copy)
    for copy in copies:
        copy.wait()


def in_hbm(value):
    return pltpu.with_memory_space_constraint(value, pltpu.HBM)


def cost(flops, size):
    return pl.CostEstimate(flops=flops, bytes_accessed=size, transcendentals=0)


def body(
    forward_fields,
    adjoint_fields,
    lame_lambda,
    shear_modulus,
    density,
    source_cell,
    source_amp,
    receiver_cell,
    residual_amp,
):
    _, _, tile_x, tile_y, depth = forward_fields.shape
    forward = forward_fields.reshape(forward_fields.shape[1:])
    adjoint = adjoint_fields.reshape(adjoint_fields.shape[1:])
    sizes = {name: lax.axis_size(name) for name in ("tx", "ty")}
    width_y = tile_y * sizes["ty"]
    links, later_links = links_of(sizes)
    cells = tile_x * tile_y * depth

    def buffers(dim):
        return pltpu.VMEM((2, SLOTS, tile_y if dim == 0 else tile_x, depth), jnp.float32)

    def tile(*lead):
        return pltpu.VMEM((*lead, tile_x, tile_y, depth), jnp.float32)

    def padded(parts):
        return pltpu.VMEM(
            (parts, tile_x + 2 * LAYERS, tile_y + 2 * ROWS, depth), jnp.float32
        )

    def exchange(links, sends):
        return [swap(send, axis, first) for (axis, _, first), send in zip(links, sends)]

    send_shapes = [buffers(dim) for _, dim, _ in links]
    count = len(links)
    receivers = receiver_cell.shape[-1]
    rows = tile_x * tile_y + 3 * (tile_x + tile_y)
    *sends, added, stress = pl.pallas_call(
        functools.partial(pack_kernel, links, width_y),
        out_shape=send_shapes + [pltpu.VMEM((rows, depth), jnp.float32), padded(12)],
        in_specs=[hbm] * 4,
        out_specs=[vmem] * (count + 2),
        scratch_shapes=[
            pltpu.VMEM((1, receivers), jnp.int32),
            pltpu.VMEM((1, receivers), jnp.float32),
            pltpu.SemaphoreType.DMA((2 + 2 * SLOTS * count,)),
        ],
        compiler_params=params,
        cost_estimate=cost(6 * rows * receivers * depth, 2 * SLOTS * count * tile_x * depth * 4),
        name="pack",
    )(*(in_hbm(x) for x in (forward, adjoint, receiver_cell, residual_amp)))
    halos = exchange(links, sends)

    stress, velocity, accel, rim_added, buoyancy, scaled_lame, scaled_shear = pl.pallas_call(
        functools.partial(velocity_kernel, width_y),
        out_shape=[
            padded(12),
            padded(6),
            tile(3),
            pltpu.VMEM((2, 2, 3, max(tile_x, tile_y), depth), jnp.float32),
            tile(),
            tile(),
            tile(),
        ],
        in_specs=[hbm] * 3 + [smem] * 2 + [vmem] * 4,
        out_specs=[vmem] * 7,
        input_output_aliases={8: 0},
        scratch_shapes=[
            pltpu.VMEM((rows, depth), jnp.float32),
            tile(6),
            tile(),
            tile(),
            tile(),
            pltpu.SemaphoreType.DMA((3,)),
        ],
        compiler_params=params,
        cost_estimate=cost(200 * cells, 18 * 4 * cells),
        name="velocity",
    )(
        *(in_hbm(x) for x in (lame_lambda, shear_modulus, density)),
        source_cell,
        source_amp,
        added,
        forward,
        adjoint,
        stress,
    )

    velocity, *sends = pl.pallas_call(
        functools.partial(boundary_kernel, links, later_links),
        out_shape=[padded(6)] + [buffers(dim) for _, dim, _ in later_links],
        in_specs=[vmem] * (count + 3),
        out_specs=[vmem] * (count + 1),
        input_output_aliases={count + 2: 0},
        compiler_params=params,
        cost_estimate=cost(cells, 10 * 2 * tile_x * depth * 4),
        name="boundary",
    )(*halos, rim_added, buoyancy, velocity)
    velocity_halos = exchange(later_links, sends)

    out_shape = jax.ShapeDtypeStruct(forward.shape, jnp.float32)
    strain, gradient, _, forward_next, adjoint_next = pl.pallas_call(
        functools.partial(strain_kernel, links),
        out_shape=[tile(12), tile(3), padded(6), out_shape, out_shape],
        in_specs=[vmem] * (count + 4),
        out_specs=[vmem] * 3 + [hbm] * 2,
        input_output_aliases={count + 2: 2},
        scratch_shapes=[tile(3), pltpu.SemaphoreType.DMA((6,))],
        compiler_params=params,
        cost_estimate=cost(200 * cells, 18 * 4 * cells),
        name="strain",
    )(*halos, rim_added, buoyancy, velocity, accel)

    strain, gradient = pl.pallas_call(
        functools.partial(gradient_kernel, later_links),
        out_shape=[tile(12), tile(3)],
        in_specs=[vmem] * (count + 5),
        out_specs=[vmem] * 2,
        input_output_aliases={count + 3: 0, count + 4: 1},
        compiler_params=params,
        cost_estimate=cost(30 * cells, 2 * 4 * cells),
        name="gradient",
    )(*velocity_halos, stress, scaled_lame, scaled_shear, strain, gradient)
    other = lax.ppermute(gradient, "shot", [(0, 1), (1, 0)])

    chunk = 4 if tile_x % 4 == 0 else 1
    forward_next, adjoint_next = pl.pallas_call(
        functools.partial(output_kernel, chunk),
        out_shape=[out_shape, out_shape],
        in_specs=[vmem] * 4 + [hbm] * 2,
        out_specs=[hbm] * 2,
        input_output_aliases={4: 0, 5: 1},
        scratch_shapes=[tile(12), pltpu.SemaphoreType.DMA((2 * tile_x // chunk,))],
        compiler_params=params,
        cost_estimate=cost(60 * cells, 18 * 4 * cells),
        name="outputs",
    )(strain, stress, scaled_lame, scaled_shear, forward_next, adjoint_next)
    total = pl.pallas_call(
        sum_kernel,
        out_shape=jax.ShapeDtypeStruct((3, tile_x, tile_y, depth), jnp.float32),
        in_specs=[vmem] * 2,
        out_specs=hbm,
        scratch_shapes=[tile(3), pltpu.SemaphoreType.DMA((3,))],
        compiler_params=params,
        cost_estimate=cost(3 * cells, 9 * 4 * cells),
        name="sum",
    )(gradient, other)
    return forward_next[None], adjoint_next[None], total


def solution(mesh):
    return jax.shard_map(
        body,
        mesh=mesh,
        in_specs=(
            P("shot", None, "tx", "ty", None),
            P("shot", None, "tx", "ty", None),
            P("tx", "ty", None),
            P("tx", "ty", None),
            P("tx", "ty", None),
            P("shot"),
            P("shot"),
            P("shot", None),
            P("shot", None),
        ),
        out_specs=(
            P("shot", None, "tx", "ty", None),
            P("shot", None, "tx", "ty", None),
            P(None, "tx", "ty", None),
        ),
        check_vma=False,
    )
```

```python
import functools

import jax
import jax.numpy as jnp
from jax import lax
from jax.experimental import pallas as pl
from jax.experimental.pallas import tpu as pltpu
from jax.sharding import PartitionSpec as P

near = 9.0 / 8.0
far = -1.0 / 24.0
time_step = 0.15

LAYERS = 2
ROWS = 8
SLOTS = 5

STRESS_ALONG = ((0, 3, 4), (1, 3, 5))
ACCEL_OF = ((0, 1, 2), (1, 0, 2))
VELOCITY_ALONG = ((0, 1, 2), (1, 0, 2))
STRAIN_OF = ((0, 3, 4), (1, 3, 5))

vmem = pl.BlockSpec(memory_space=pltpu.VMEM)
smem = pl.BlockSpec(memory_space=pltpu.SMEM)
hbm = pl.BlockSpec(memory_space=pltpu.HBM)
params = pltpu.CompilerParams(vmem_limit_bytes=24 * 1024 * 1024)


def links_of(sizes):
    far_y, near_y, *along = ("ty", 1, 1), ("ty", 1, 0), ("tx", 0, 1), ("tx", 0, 0)
    return [
        [link for link in order if link[2] + 1 < sizes[link[0]]]
        for order in ((far_y, *along, near_y), (far_y, *along, near_y))
    ]


def swap(value, axis, first):
    pairs = [(i, i + 1) for i in range(first, lax.axis_size(axis) - 1, 2)]
    return lax.ppermute(value, axis, pairs + [(j, i) for i, j in pairs])


def is_lower(axis, first):
    return lax.axis_index(axis) % 2 == first


def has_peer(axis, first):
    index = lax.axis_index(axis)
    partner = jnp.where(is_lower(axis, first), index + 1, index - 1)
    return (partner >= 0) & (partner < lax.axis_size(axis))


def send_faces(field, count, links, sends, plans):
    for (axis, dim, first), send in zip(links, sends):
        lower = is_lower(axis, first)
        upper_plan, lower_plan = plans[dim]

        def put(plan):
            for wave in range(2):
                for slot, (part, index) in enumerate(plan):
                    send[wave, slot] = face(field, count * wave + part, dim, index, True)[...]

        pl.when(lower)(functools.partial(put, lower_plan))
        pl.when(jnp.logical_not(lower))(functools.partial(put, upper_plan))


def stress_plan(dim):
    n, a, b = STRESS_ALONG[dim]
    return (
        ((n, 0), (n, 1), (a, 0), (b, 0), (b, 0)),
        ((n, -1), (a, -2), (a, -1), (b, -2), (b, -1)),
    )


def velocity_plan(dim):
    n, a, b = VELOCITY_ALONG[dim]
    return (
        ((n, 0), (a, 0), (a, 1), (b, 0), (b, 1)),
        ((n, -2), (n, -1), (a, -1), (b, -1), (b, -1)),
    )


def early_pack_kernel(links, forward, adjoint, *refs):
    sends, sems = refs[: len(links)], refs[-1]
    tile = forward.shape[1:3]
    copies = []
    for (axis, dim, first), send in zip(links, sends):
        lower = is_lower(axis, first)
        for slot, ((up_part, up_at), (low_part, low_at)) in enumerate(zip(*stress_plan(dim))):
            part = 3 + jnp.where(lower, low_part, up_part)
            at = jnp.where(lower, low_at % tile[dim], up_at % tile[dim])
            for wave, fields in enumerate((forward, adjoint)):
                source = fields.at[part, at] if dim == 0 else fields.at[part, :, at, :]
                copy = pltpu.make_async_copy(source, send.at[wave, slot], sems.at[len(copies)])
                copy.start()
                copies.append(copy)
    for copy in copies:
        copy.wait()


def pack_kernel(links, forward, adjoint, *sends):
    for (axis, dim, first), send in zip(links, sends):
        lower = is_lower(axis, first)

        def put(plan):
            for wave, fields in enumerate((forward, adjoint)):
                for slot, (part, index) in enumerate(plan):
                    send[wave, slot] = face(fields, 3 + part, dim, index, False)[...]

        upper_plan, lower_plan = stress_plan(dim)
        pl.when(lower)(functools.partial(put, lower_plan))
        pl.when(jnp.logical_not(lower))(functools.partial(put, upper_plan))


def column_ids(tile_x, tile_y, width_y, lanes):
    x_start = lax.axis_index("tx") * tile_x
    y_start = lax.axis_index("ty") * tile_y

    def column(x, y):
        inside = (y >= 0) & (y < width_y)
        return jnp.where(inside, x * width_y + y, -1)

    def iota(shape, dim):
        return lax.broadcasted_iota(jnp.int32, shape, dim)

    shape = (tile_x, tile_y, lanes)
    tile = column(x_start + iota(shape, 0), y_start + iota(shape, 1))
    shape = (3, tile_y, lanes)
    layer = iota(shape, 0)
    along_x = column(
        x_start + jnp.where(layer == 0, -1, tile_x - 1 + layer), y_start + iota(shape, 1)
    )
    shape = (3, tile_x, lanes)
    layer = iota(shape, 0)
    along_y = column(
        x_start + iota(shape, 1), y_start + jnp.where(layer == 0, -1, tile_y - 1 + layer)
    )
    return jnp.concatenate([part.reshape(-1, lanes) for part in (tile, along_x, along_y)], axis=0)


def differ(zero, one, two, minus):
    return near * (one - zero) + far * (two - minus)


def along_x(ref, part, x, tile_y, upward):
    def at(offset):
        return ref[part, x + (LAYERS + offset), pl.ds(ROWS, tile_y), :]

    return differ(at(0), at(1), at(2), at(-1)) if upward else differ(at(-1), at(0), at(1), at(-2))


def along_y(ref, part, x, tile_y, upward):
    def at(offset):
        return ref[part, x + LAYERS, pl.ds(ROWS + offset, tile_y), :]

    return differ(at(0), at(1), at(2), at(-1)) if upward else differ(at(-1), at(0), at(1), at(-2))


def along_z(ref, part, x, tile_y, upward):
    value = ref[part, x + LAYERS, pl.ds(ROWS, tile_y), :]
    depth = value.shape[-1]
    lane = lax.broadcasted_iota(jnp.int32, value.shape, 1)

    def at(offset):
        if offset == 0:
            return value
        moved = pltpu.roll(value, (-offset) % depth, 1)
        inside = lane < depth - offset if offset > 0 else lane >= -offset
        return jnp.where(inside, moved, 0.0)

    return differ(at(0), at(1), at(2), at(-1)) if upward else differ(at(-1), at(0), at(1), at(-2))


def clear_rim(ref, parts_x, parts_y):
    _, layers, rows, depth = ref.shape
    tile_x, tile_y = layers - 2 * LAYERS, rows - 2 * ROWS
    for part in parts_x:
        for begin in (0, LAYERS + tile_x):
            ref[part, pl.ds(begin, LAYERS), pl.ds(ROWS, tile_y), :] = jnp.zeros(
                (LAYERS, tile_y, depth), jnp.float32
            )
    for part in parts_y:
        for begin in (0, ROWS + tile_y):
            ref[part, pl.ds(LAYERS, tile_x), pl.ds(begin, ROWS), :] = jnp.zeros(
                (tile_x, ROWS, depth), jnp.float32
            )


def receiver_sum(cells, amps, columns):
    depth, receivers = columns.shape[-1], cells.shape[-1]
    column = lax.div(cells, depth)
    level = cells - column * depth
    column_hot = jnp.concatenate(
        [
            (columns == column[:, begin : begin + depth]).astype(jnp.bfloat16)
            for begin in range(0, receivers, depth)
        ],
        axis=1,
    )
    levels = lax.broadcasted_iota(jnp.int32, (depth, receivers), 0)
    rest = jnp.where(levels == level, amps, 0.0)
    total = jnp.zeros(columns.shape, jnp.float32)
    for _ in range(3):
        part = rest.astype(jnp.bfloat16)
        rest = rest - part.astype(jnp.float32)
        total = total + lax.dot_general(
            column_hot,
            part,
            (((1,), (1,)), ((), ())),
            preferred_element_type=jnp.float32,
        )
    return total


def velocity_kernel(
    width_y,
    lame,
    shear,
    density,
    source_cell,
    source_amp,
    receiver_cell,
    residual_amp,
    forward,
    adjoint,
    stress,
    velocity,
    accel,
    rim_added,
    buoyancy,
    scaled_lame,
    scaled_shear,
    sourced,
    received,
    gained,
    lame_now,
    shear_now,
    density_now,
    sems,
):
    tile_x, tile_y, depth = density.shape
    copies = [
        pltpu.make_async_copy(source, target, sems.at[at])
        for at, (source, target) in enumerate((
            (density, density_now),
            (lame, lame_now),
            (shear, shear_now),
        ))
    ]
    for copy in copies:
        copy.start()
    cells = tile_x * tile_y
    middle = pl.ds(ROWS, tile_y)
    columns = column_ids(tile_x, tile_y, width_y, depth)
    lane = lax.broadcasted_iota(jnp.int32, columns.shape, 1)
    sourced[...] = jnp.where(columns * depth + lane == source_cell[0], source_amp[0], 0.0)
    received[...] = receiver_sum(receiver_cell[...], residual_amp[...], columns)
    for wave, added in enumerate((sourced, received)):
        clear_rim(
            stress, *([6 * wave + part for part in STRESS_ALONG[dim]] for dim in range(2))
        )
        for layer in range(3):
            rim_added[wave, 0, layer] = added[pl.ds(cells + layer * tile_y, tile_y), :]
            begin = cells + 3 * tile_y + layer * tile_x
            rim_added[wave, 1, layer] = added[pl.ds(begin, tile_x), :]

    def fill(x, carry):
        for wave, (fields, added) in enumerate(((forward, sourced), (adjoint, received))):
            extra = added[pl.ds(pl.multiple_of(x * tile_y, 8), tile_y), :]
            for part in range(6):
                value = fields[3 + part, x]
                stress[6 * wave + part, x + LAYERS, middle, :] = (
                    value + extra if part < 3 else value
                )
        return carry

    lax.fori_loop(0, tile_x, fill, 0, unroll=4)

    def layer(x, carry):
        for wave in range(2):
            xx, yy, zz, xy, xz, yz = range(6 * wave, 6 * wave + 6)
            values = (
                along_x(stress, xx, x, tile_y, True)
                + along_y(stress, xy, x, tile_y, False)
                + along_z(stress, xz, x, tile_y, False),
                along_x(stress, xy, x, tile_y, False)
                + along_y(stress, yy, x, tile_y, True)
                + along_z(stress, yz, x, tile_y, False),
                along_x(stress, xz, x, tile_y, False)
                + along_y(stress, yz, x, tile_y, False)
                + along_z(stress, zz, x, tile_y, True),
            )
            for part, value in enumerate(values):
                gained[3 * wave + part, x] = value
        return carry

    lax.fori_loop(0, tile_x, layer, 0, unroll=4)
    for copy in copies:
        copy.wait()

    def finish(x, carry):
        light = 1.0 / density_now[x]
        buoyancy[x] = light
        scaled_lame[x] = time_step * lame_now[x]
        scaled_shear[x] = time_step * shear_now[x]
        for wave, fields in enumerate((forward, adjoint)):
            for part in range(3):
                value = light * gained[3 * wave + part, x]
                if wave == 0:
                    accel[part, x] = value
                velocity[3 * wave + part, x + LAYERS, middle, :] = (
                    fields[part, x] + time_step * value
                )
        return carry

    lax.fori_loop(0, tile_x, finish, 0, unroll=4)


def stress_halo_terms(links, received, rim_added, waves, add):
    for (axis, dim, first), halo in zip(links, received):
        part_n, part_a, part_b = ACCEL_OF[dim]
        lower = is_lower(axis, first)
        real = has_peer(axis, first)

        @pl.when(real & lower)
        def after():
            for wave in waves:
                n0 = halo[wave, 0] + rim_added[wave, dim, 1]
                n1 = halo[wave, 1] + rim_added[wave, dim, 2]
                add(wave, part_n, dim, -1, near * n0 + far * n1)
                add(wave, part_n, dim, -2, far * n0)
                add(wave, part_a, dim, -1, far * halo[wave, 2])
                add(wave, part_b, dim, -1, far * halo[wave, 3])

        @pl.when(real & jnp.logical_not(lower))
        def before():
            for wave in waves:
                n0 = halo[wave, 0] + rim_added[wave, dim, 0]
                add(wave, part_n, dim, 0, -far * n0)
                for part, slot in ((part_a, 1), (part_b, 3)):
                    outer, inner = halo[wave, slot], halo[wave, slot + 1]
                    add(wave, part, dim, 0, -near * inner - far * outer)
                    add(wave, part, dim, 1, -far * inner)


def velocity_halo_terms(links, received, add):
    for (axis, dim, first), halo in zip(links, received):
        part_n, part_a, part_b = STRAIN_OF[dim]
        lower = is_lower(axis, first)
        real = has_peer(axis, first)

        @pl.when(real & lower)
        def after():
            for wave in range(2):
                add(wave, part_n, dim, -1, far * halo[wave, 0])
                for part, slot in ((part_a, 1), (part_b, 3)):
                    inner, outer = halo[wave, slot], halo[wave, slot + 1]
                    add(wave, part, dim, -1, near * inner + far * outer)
                    add(wave, part, dim, -2, far * inner)

        @pl.when(real & jnp.logical_not(lower))
        def before():
            for wave in range(2):
                outer, inner = halo[wave, 0], halo[wave, 1]
                add(wave, part_n, dim, 0, -near * inner - far * outer)
                add(wave, part_n, dim, 1, -far * inner)
                add(wave, part_a, dim, 0, -far * halo[wave, 2])
                add(wave, part_b, dim, 0, -far * halo[wave, 3])


def face(ref, part, dim, index, padded):
    layers, rows, depth = ref.shape[1:]
    tile_x = layers - 2 * LAYERS if padded else layers
    tile_y = rows - 2 * ROWS if padded else rows
    if dim == 0:
        at = index % tile_x
        if padded:
            return ref.at[part, at + LAYERS, pl.ds(ROWS, tile_y), :]
        return ref.at[part, at]
    at = index % tile_y
    flat = ref.reshape(ref.shape[0], layers * rows, depth)
    begin = LAYERS * rows + ROWS + at if padded else at
    return flat.at[part, pl.ds(begin, tile_x, stride=rows), :]


def light_face(buoyancy, dim, index):
    layers, rows, depth = buoyancy.shape
    if dim == 0:
        return buoyancy[index % layers]
    return buoyancy.reshape(layers * rows, depth)[pl.ds(index % rows, layers, stride=rows), :]


def boundary_kernel(links, later_links, *refs):
    count = len(links)
    received = refs[:count]
    rim_added, buoyancy, _ = refs[count : count + 3]
    velocity = refs[count + 3]
    sends = refs[count + 4 :]

    def add(wave, part, dim, index, term):
        target = face(velocity, 3 * wave + part, dim, index, True)
        target[...] += time_step * light_face(buoyancy, dim, index) * term

    stress_halo_terms(links, received, rim_added, (0, 1), add)
    send_faces(velocity, 3, later_links, sends, [velocity_plan(dim) for dim in range(2)])


def strain_kernel(links, *refs):
    count = len(links)
    received = refs[:count]
    rim_added, buoyancy, _, accel, strain, gradient, velocity = refs[count : count + 7]
    outputs, (accel_now, sems) = refs[count + 7 : count + 9], refs[count + 9 :]
    tile_x, tile_y, _ = buoyancy.shape
    middle = pl.ds(ROWS, tile_y)
    copies = [
        pltpu.make_async_copy(
            velocity.at[3 * wave + part, pl.ds(LAYERS, tile_x), middle, :],
            outputs[wave].at[part],
            sems.at[3 * wave + part],
        )
        for wave in range(2)
        for part in range(3)
    ]
    for copy in copies:
        copy.start()
    clear_rim(velocity, range(6), range(6))
    accel_now[...] = accel[...]

    def add(wave, part, dim, index, term):
        target = face(accel_now, part, dim, index, False)
        target[...] += light_face(buoyancy, dim, index) * term

    stress_halo_terms(links, received, rim_added, (0,), add)

    def layer(x, carry):
        for wave in range(2):
            vx, vy, vz = range(3 * wave, 3 * wave + 3)
            values = (
                along_x(velocity, vx, x, tile_y, False),
                along_y(velocity, vy, x, tile_y, False),
                along_z(velocity, vz, x, tile_y, False),
                along_y(velocity, vx, x, tile_y, True) + along_x(velocity, vy, x, tile_y, True),
                along_z(velocity, vx, x, tile_y, True) + along_x(velocity, vz, x, tile_y, True),
                along_z(velocity, vy, x, tile_y, True) + along_y(velocity, vz, x, tile_y, True),
            )
            for part, value in enumerate(values):
                strain[6 * wave + part, x] = value
        total = sum(
            accel_now[part, x] * velocity[3 + part, x + LAYERS, middle, :] for part in range(3)
        )
        gradient[2, x] = -time_step * total
        return carry

    lax.fori_loop(0, tile_x, layer, 0, unroll=4)
    for copy in copies:
        copy.wait()


def new_stress(strain, stress, scaled_lame, scaled_shear, wave, x, tile_y):
    lame, shear = scaled_lame[x], scaled_shear[x]
    strains = [strain[6 * wave + part, x] for part in range(6)]
    volume = lame * (strains[0] + strains[1] + strains[2])
    values = []
    for part in range(6):
        old = stress[6 * wave + part, x + LAYERS, pl.ds(ROWS, tile_y), :]
        if part < 3:
            values.append(old + (volume + 2.0 * shear * strains[part]))
        else:
            values.append(old + shear * strains[part])
    return strains, values


def gradient_kernel(links, *refs):
    count = len(links)
    received = refs[:count]
    stress, scaled_lame, scaled_shear, _, _, strain, gradient = refs[count:]
    tile_x, tile_y, _ = scaled_lame.shape

    def add(wave, part, dim, index, term):
        target = face(strain, 6 * wave + part, dim, index, False)
        target[...] += term

    velocity_halo_terms(links, received, add)

    def layer(x, carry):
        strains = [strain[part, x] for part in range(6)]
        _, values = new_stress(strain, stress, scaled_lame, scaled_shear, 1, x, tile_y)
        trace = strains[0] + strains[1] + strains[2]
        gradient[0, x] = -time_step * trace * (values[0] + values[1] + values[2])
        total = sum(left * right for left, right in zip(strains, values))
        gradient[1, x] = -time_step * total
        return carry

    lax.fori_loop(0, tile_x, layer, 0, unroll=4)


def output_kernel(chunk, strain, stress, scaled_lame, scaled_shear, *refs):
    outputs, (values_now, sems) = refs[2:4], refs[4:]
    tile_x, tile_y, _ = scaled_lame.shape
    copies = []
    for begin in range(0, tile_x, chunk):
        for wave in range(2):
            for x in range(begin, begin + chunk):
                _, values = new_stress(strain, stress, scaled_lame, scaled_shear, wave, x, tile_y)
                for part in range(6):
                    values_now[6 * wave + part, x] = values[part]
            layers = pl.ds(begin, chunk)
            copy = pltpu.make_async_copy(
                values_now.at[pl.ds(6 * wave, 6), layers],
                outputs[wave].at[pl.ds(3, 6), layers],
                sems.at[len(copies)],
            )
            copy.start()
            copies.append(copy)
    for copy in copies:
        copy.wait()


def sum_kernel(mine, other, total, total_now, sems):
    copies = []
    for part in range(mine.shape[0]):
        total_now[part] = mine[part] + other[part]
        copy = pltpu.make_async_copy(total_now.at[part], total.at[part], sems.at[part])
        copy.start()
        copies.append(copy)
    for copy in copies:
        copy.wait()


def in_hbm(value):
    return pltpu.with_memory_space_constraint(value, pltpu.HBM)


def cost(flops, size):
    return pl.CostEstimate(flops=flops, bytes_accessed=size, transcendentals=0)


def body(
    forward_fields,
    adjoint_fields,
    lame_lambda,
    shear_modulus,
    density,
    source_cell,
    source_amp,
    receiver_cell,
    residual_amp,
):
    _, _, tile_x, tile_y, depth = forward_fields.shape
    forward = forward_fields.reshape(forward_fields.shape[1:])
    adjoint = adjoint_fields.reshape(adjoint_fields.shape[1:])
    sizes = {name: lax.axis_size(name) for name in ("tx", "ty")}
    width_y = tile_y * sizes["ty"]
    links, later_links = links_of(sizes)
    cells = tile_x * tile_y * depth

    def buffers(dim):
        return pltpu.VMEM((2, SLOTS, tile_y if dim == 0 else tile_x, depth), jnp.float32)

    def tile(*lead):
        return pltpu.VMEM((*lead, tile_x, tile_y, depth), jnp.float32)

    def padded(parts):
        return pltpu.VMEM(
            (parts, tile_x + 2 * LAYERS, tile_y + 2 * ROWS, depth), jnp.float32
        )

    def exchange(links, sends):
        return [swap(send, axis, first) for (axis, _, first), send in zip(links, sends)]

    send_shapes = [buffers(dim) for _, dim, _ in links]
    count = len(links)
    rows = tile_x * tile_y + 3 * (tile_x + tile_y)
    sends = pl.pallas_call(
        functools.partial(early_pack_kernel, links[:1]),
        out_shape=send_shapes[:1],
        in_specs=[hbm] * 2,
        out_specs=[vmem],
        scratch_shapes=[pltpu.SemaphoreType.DMA((2 * SLOTS,))],
        compiler_params=params,
        cost_estimate=cost(0, 2 * 2 * SLOTS * tile_x * depth * 4),
        name="early_pack",
    )(in_hbm(forward), in_hbm(adjoint))
    halos = exchange(links[:1], sends)
    if count > 1:
        sends = pl.pallas_call(
            functools.partial(pack_kernel, links[1:]),
            out_shape=send_shapes[1:],
            in_specs=[vmem] * 2,
            out_specs=[vmem] * (count - 1),
            compiler_params=params,
            cost_estimate=cost(0, 2 * 2 * SLOTS * (count - 1) * tile_x * depth * 4),
            name="pack",
        )(forward, adjoint)
        halos += exchange(links[1:], sends)

    stress, velocity, accel, rim_added, buoyancy, scaled_lame, scaled_shear = pl.pallas_call(
        functools.partial(velocity_kernel, width_y),
        out_shape=[
            padded(12),
            padded(6),
            tile(3),
            pltpu.VMEM((2, 2, 3, max(tile_x, tile_y), depth), jnp.float32),
            tile(),
            tile(),
            tile(),
        ],
        in_specs=[hbm] * 3 + [smem] * 2 + [vmem] * 4,
        out_specs=[vmem] * 7,
        scratch_shapes=[
            pltpu.VMEM((rows, depth), jnp.float32),
            pltpu.VMEM((rows, depth), jnp.float32),
            tile(6),
            tile(),
            tile(),
            tile(),
            pltpu.SemaphoreType.DMA((3,)),
        ],
        compiler_params=params,
        cost_estimate=cost(200 * cells, 18 * 4 * cells),
        name="velocity",
    )(
        *(in_hbm(x) for x in (lame_lambda, shear_modulus, density)),
        source_cell,
        source_amp,
        receiver_cell,
        residual_amp,
        forward,
        adjoint,
    )

    velocity, *sends = pl.pallas_call(
        functools.partial(boundary_kernel, links, later_links),
        out_shape=[padded(6)] + [buffers(dim) for _, dim, _ in later_links],
        in_specs=[vmem] * (count + 3),
        out_specs=[vmem] * (count + 1),
        input_output_aliases={count + 2: 0},
        compiler_params=params,
        cost_estimate=cost(cells, 10 * 2 * tile_x * depth * 4),
        name="boundary",
    )(*halos, rim_added, buoyancy, velocity)
    velocity_halos = exchange(later_links, sends)

    out_shape = jax.ShapeDtypeStruct(forward.shape, jnp.float32)
    strain, gradient, _, forward_next, adjoint_next = pl.pallas_call(
        functools.partial(strain_kernel, links),
        out_shape=[tile(12), tile(3), padded(6), out_shape, out_shape],
        in_specs=[vmem] * (count + 4),
        out_specs=[vmem] * 3 + [hbm] * 2,
        input_output_aliases={count + 2: 2},
        scratch_shapes=[tile(3), pltpu.SemaphoreType.DMA((6,))],
        compiler_params=params,
        cost_estimate=cost(200 * cells, 18 * 4 * cells),
        name="strain",
    )(*halos, rim_added, buoyancy, velocity, accel)

    strain, gradient = pl.pallas_call(
        functools.partial(gradient_kernel, later_links),
        out_shape=[tile(12), tile(3)],
        in_specs=[vmem] * (count + 5),
        out_specs=[vmem] * 2,
        input_output_aliases={count + 3: 0, count + 4: 1},
        compiler_params=params,
        cost_estimate=cost(30 * cells, 2 * 4 * cells),
        name="gradient",
    )(*velocity_halos, stress, scaled_lame, scaled_shear, strain, gradient)
    other = lax.ppermute(gradient, "shot", [(0, 1), (1, 0)])

    chunk = 4 if tile_x % 4 == 0 else 1
    forward_next, adjoint_next = pl.pallas_call(
        functools.partial(output_kernel, chunk),
        out_shape=[out_shape, out_shape],
        in_specs=[vmem] * 4 + [hbm] * 2,
        out_specs=[hbm] * 2,
        input_output_aliases={4: 0, 5: 1},
        scratch_shapes=[tile(12), pltpu.SemaphoreType.DMA((2 * tile_x // chunk,))],
        compiler_params=params,
        cost_estimate=cost(60 * cells, 18 * 4 * cells),
        name="outputs",
    )(strain, stress, scaled_lame, scaled_shear, forward_next, adjoint_next)
    total = pl.pallas_call(
        sum_kernel,
        out_shape=jax.ShapeDtypeStruct((3, tile_x, tile_y, depth), jnp.float32),
        in_specs=[vmem] * 2,
        out_specs=hbm,
        scratch_shapes=[tile(3), pltpu.SemaphoreType.DMA((3,))],
        compiler_params=params,
        cost_estimate=cost(3 * cells, 9 * 4 * cells),
        name="sum",
    )(gradient, other)
    return forward_next[None], adjoint_next[None], total


def solution(mesh):
    return jax.shard_map(
        body,
        mesh=mesh,
        in_specs=(
            P("shot", None, "tx", "ty", None),
            P("shot", None, "tx", "ty", None),
            P("tx", "ty", None),
            P("tx", "ty", None),
            P("tx", "ty", None),
            P("shot"),
            P("shot"),
            P("shot", None),
            P("shot", None),
        ),
        out_specs=(
            P("shot", None, "tx", "ty", None),
            P("shot", None, "tx", "ty", None),
            P(None, "tx", "ty", None),
        ),
        check_vma=False,
    )
```

```python
import functools

import jax
import jax.numpy as jnp
from jax import lax
from jax.experimental import pallas as pl
from jax.experimental.pallas import tpu as pltpu
from jax.sharding import PartitionSpec as P

near = 9.0 / 8.0
far = -1.0 / 24.0
time_step = 0.15

LAYERS = 2
ROWS = 8
SLOTS = 5

STRESS_ALONG = ((0, 3, 4), (1, 3, 5))
ACCEL_OF = ((0, 1, 2), (1, 0, 2))
VELOCITY_ALONG = ((0, 1, 2), (1, 0, 2))
STRAIN_OF = ((0, 3, 4), (1, 3, 5))

vmem = pl.BlockSpec(memory_space=pltpu.VMEM)
smem = pl.BlockSpec(memory_space=pltpu.SMEM)
hbm = pl.BlockSpec(memory_space=pltpu.HBM)
params = pltpu.CompilerParams(vmem_limit_bytes=24 * 1024 * 1024)


def links_of(sizes):
    along_x = (("tx", 0, 1), ("tx", 0, 0))
    along_y = (("ty", 1, 1), ("ty", 1, 0))
    return [[link for link in order if link[2] + 1 < sizes[link[0]]] for order in (along_x, along_y)]


def swap(value, axis, first):
    pairs = [(i, i + 1) for i in range(first, lax.axis_size(axis) - 1, 2)]
    return lax.ppermute(value, axis, pairs + [(j, i) for i, j in pairs])


def is_lower(axis, first):
    return lax.axis_index(axis) % 2 == first


def has_peer(axis, first):
    index = lax.axis_index(axis)
    partner = jnp.where(is_lower(axis, first), index + 1, index - 1)
    return (partner >= 0) & (partner < lax.axis_size(axis))


def by_role(link, act, upper, lower):
    lower_here = is_lower(link[0], link[2])
    pl.when(lower_here)(lambda: act(lower, True))
    pl.when(jnp.logical_not(lower_here))(lambda: act(upper, False))


SPARE = SLOTS - 1


def stress_plan(dim):
    n, a, b = STRESS_ALONG[dim]
    return ((n, 0), (n, 1), (a, 0), (b, 0)), ((n, -1), (a, -2), (a, -1), (b, -2), (b, -1))


def velocity_plan(dim):
    n, a, b = VELOCITY_ALONG[dim]
    return ((n, 0), (a, 0), (a, 1), (b, 0), (b, 1)), ((n, -2), (n, -1), (a, -1), (b, -1))


def early_pack_kernel(links, forward, adjoint, density, *refs):
    sends, (density_now, sems) = refs[: len(links)], refs[len(links) :]
    tile_x = forward.shape[1]
    whole = pltpu.make_async_copy(density, density_now, sems.at[0])
    whole.start()
    waits = []
    for at, (link, send) in enumerate(zip(links, sends)):

        def sources(plan, lower, wave):
            fields = (forward, adjoint)[wave]
            found = [fields.at[3 + part, index % tile_x] for part, index in plan]
            return found if lower else found + [density.at[wave]]

        def start(plan, lower):
            for wave in range(2):
                for slot, source in enumerate(sources(plan, lower, wave)):
                    pltpu.make_async_copy(
                        source, send.at[wave, slot], sems.at[1 + (2 * at + wave) * SLOTS + slot]
                    ).start()

        by_role(link, start, *stress_plan(link[1]))
        for wave in range(2):
            for slot in range(SLOTS):
                waits.append(
                    pltpu.make_async_copy(
                        density.at[0],
                        send.at[wave, slot],
                        sems.at[1 + (2 * at + wave) * SLOTS + slot],
                    )
                )
    for copy in waits:
        copy.wait()
    whole.wait()


def pack_kernel(links, forward, adjoint, density, *sends):
    for link, send in zip(links, sends):
        dim = link[1]

        def put(plan, lower):
            for wave, fields in enumerate((forward, adjoint)):
                for slot, (part, index) in enumerate(plan):
                    send[wave, slot] = face(fields, 3 + part, dim, index, False)[...]
                if not lower:
                    send[wave, SPARE] = light_face(density, dim, wave)

        by_role(link, put, *stress_plan(dim))


def send_velocities(links, velocity, buoyancy, sends):
    for link, send in zip(links, sends):
        dim = link[1]

        def put(plan, lower):
            for wave in range(2):
                for slot, (part, index) in enumerate(plan):
                    send[wave, slot] = face(velocity, 3 * wave + part, dim, index, True)[...]
                if lower:
                    send[wave, SPARE] = light_face(buoyancy, dim, -1 - wave)

        by_role(link, put, *velocity_plan(dim))


def column_ids(tile_x, tile_y, width_y, lanes):
    x_start = lax.axis_index("tx") * tile_x
    y_start = lax.axis_index("ty") * tile_y

    def column(x, y):
        inside = (y >= 0) & (y < width_y)
        return jnp.where(inside, x * width_y + y, -1)

    def iota(shape, dim):
        return lax.broadcasted_iota(jnp.int32, shape, dim)

    shape = (tile_x, tile_y, lanes)
    tile = column(x_start + iota(shape, 0), y_start + iota(shape, 1))
    shape = (3, tile_y, lanes)
    layer = iota(shape, 0)
    along_x = column(
        x_start + jnp.where(layer == 0, -1, tile_x - 1 + layer), y_start + iota(shape, 1)
    )
    shape = (3, tile_x, lanes)
    layer = iota(shape, 0)
    along_y = column(
        x_start + iota(shape, 1), y_start + jnp.where(layer == 0, -1, tile_y - 1 + layer)
    )
    return jnp.concatenate([part.reshape(-1, lanes) for part in (tile, along_x, along_y)], axis=0)


def differ(zero, one, two, minus):
    return near * (one - zero) + far * (two - minus)


def along_x(ref, part, x, tile_y, upward):
    def at(offset):
        return ref[part, x + (LAYERS + offset), pl.ds(ROWS, tile_y), :]

    return differ(at(0), at(1), at(2), at(-1)) if upward else differ(at(-1), at(0), at(1), at(-2))


def along_y(ref, part, x, tile_y, upward):
    def at(offset):
        return ref[part, x + LAYERS, pl.ds(ROWS + offset, tile_y), :]

    return differ(at(0), at(1), at(2), at(-1)) if upward else differ(at(-1), at(0), at(1), at(-2))


def along_z(ref, part, x, tile_y, upward):
    value = ref[part, x + LAYERS, pl.ds(ROWS, tile_y), :]
    depth = value.shape[-1]
    lane = lax.broadcasted_iota(jnp.int32, value.shape, 1)

    def at(offset):
        if offset == 0:
            return value
        moved = pltpu.roll(value, (-offset) % depth, 1)
        inside = lane < depth - offset if offset > 0 else lane >= -offset
        return jnp.where(inside, moved, 0.0)

    return differ(at(0), at(1), at(2), at(-1)) if upward else differ(at(-1), at(0), at(1), at(-2))


def clear_rim(ref, parts_x, parts_y):
    _, layers, rows, depth = ref.shape
    tile_x, tile_y = layers - 2 * LAYERS, rows - 2 * ROWS
    for part in parts_x:
        for begin in (0, LAYERS + tile_x):
            ref[part, pl.ds(begin, LAYERS), pl.ds(ROWS, tile_y), :] = jnp.zeros(
                (LAYERS, tile_y, depth), jnp.float32
            )
    for part in parts_y:
        for begin in (0, ROWS + tile_y):
            ref[part, pl.ds(LAYERS, tile_x), pl.ds(begin, ROWS), :] = jnp.zeros(
                (tile_x, ROWS, depth), jnp.float32
            )


def receiver_sum(cells, amps, columns):
    depth, receivers = columns.shape[-1], cells.shape[-1]
    column = lax.div(cells, depth)
    level = cells - column * depth
    column_hot = jnp.concatenate(
        [
            (columns == column[:, begin : begin + depth]).astype(jnp.bfloat16)
            for begin in range(0, receivers, depth)
        ],
        axis=1,
    )
    levels = lax.broadcasted_iota(jnp.int32, (depth, receivers), 0)
    rest = jnp.where(levels == level, amps, 0.0)
    total = jnp.zeros(columns.shape, jnp.float32)
    for _ in range(3):
        part = rest.astype(jnp.bfloat16)
        rest = rest - part.astype(jnp.float32)
        total = total + lax.dot_general(
            column_hot,
            part,
            (((1,), (1,)), ((), ())),
            preferred_element_type=jnp.float32,
        )
    return total


def velocity_kernel(
    width_y,
    lame,
    shear,
    receiver_cell,
    residual_amp,
    forward,
    adjoint,
    density,
    stress,
    velocity,
    accel,
    rim_added,
    buoyancy,
    scaled_lame,
    scaled_shear,
    received,
    gained,
    lame_now,
    shear_now,
    sems,
):
    tile_x, tile_y, depth = density.shape
    copies = [
        pltpu.make_async_copy(lame, lame_now, sems.at[0]),
        pltpu.make_async_copy(shear, shear_now, sems.at[1]),
    ]
    for copy in copies:
        copy.start()
    cells = tile_x * tile_y
    middle = pl.ds(ROWS, tile_y)
    columns = column_ids(tile_x, tile_y, width_y, depth)
    received[...] = receiver_sum(receiver_cell[...], residual_amp[...], columns)
    for layer in range(3):
        rim_added[0, layer] = received[pl.ds(cells + layer * tile_y, tile_y), :]
        rim_added[1, layer] = received[pl.ds(cells + 3 * tile_y + layer * tile_x, tile_x), :]
    for wave in range(2):
        clear_rim(
            stress, *([6 * wave + part for part in STRESS_ALONG[dim]] for dim in range(2))
        )

    def fill(x, carry):
        extra = received[pl.ds(pl.multiple_of(x * tile_y, 8), tile_y), :]
        for wave, fields in enumerate((forward, adjoint)):
            for part in range(6):
                value = fields[3 + part, x]
                stress[6 * wave + part, x + LAYERS, middle, :] = (
                    value + extra if wave == 1 and part < 3 else value
                )
        return carry

    lax.fori_loop(0, tile_x, fill, 0, unroll=4)

    def layer(x, carry):
        for wave in range(2):
            xx, yy, zz, xy, xz, yz = range(6 * wave, 6 * wave + 6)
            values = (
                along_x(stress, xx, x, tile_y, True)
                + along_y(stress, xy, x, tile_y, False)
                + along_z(stress, xz, x, tile_y, False),
                along_x(stress, xy, x, tile_y, False)
                + along_y(stress, yy, x, tile_y, True)
                + along_z(stress, yz, x, tile_y, False),
                along_x(stress, xz, x, tile_y, False)
                + along_y(stress, yz, x, tile_y, False)
                + along_z(stress, zz, x, tile_y, True),
            )
            for part, value in enumerate(values):
                gained[3 * wave + part, x] = value
        return carry

    lax.fori_loop(0, tile_x, layer, 0, unroll=4)
    for copy in copies:
        copy.wait()

    def finish(x, carry):
        light = 1.0 / density[x]
        buoyancy[x] = light
        scaled_lame[x] = time_step * lame_now[x]
        scaled_shear[x] = time_step * shear_now[x]
        for wave, fields in enumerate((forward, adjoint)):
            for part in range(3):
                value = light * gained[3 * wave + part, x]
                if wave == 0:
                    accel[part, x] = value
                velocity[3 * wave + part, x + LAYERS, middle, :] = (
                    fields[part, x] + time_step * value
                )
        return carry

    lax.fori_loop(0, tile_x, finish, 0, unroll=4)


def stress_halo_terms(links, received, rim_added, waves, add):
    for link, halo in zip(links, received):
        dim = link[1]
        part_n, part_a, part_b = ACCEL_OF[dim]

        def normal(wave, slot, layer):
            value = halo[wave, slot]
            return value + rim_added[dim, layer] if wave == 1 else value

        def after():
            for wave in waves:
                n0, n1 = normal(wave, 0, 1), normal(wave, 1, 2)
                add(wave, part_n, dim, -1, near * n0 + far * n1)
                add(wave, part_n, dim, -2, far * n0)
                add(wave, part_a, dim, -1, far * halo[wave, 2])
                add(wave, part_b, dim, -1, far * halo[wave, 3])

        def before():
            for wave in waves:
                add(wave, part_n, dim, 0, -far * normal(wave, 0, 0))
                for part, slot in ((part_a, 1), (part_b, 3)):
                    outer, inner = halo[wave, slot], halo[wave, slot + 1]
                    add(wave, part, dim, 0, -near * inner - far * outer)
                    add(wave, part, dim, 1, -far * inner)

        real = has_peer(link[0], link[2])
        lower = is_lower(link[0], link[2])
        pl.when(real & lower)(after)
        pl.when(real & jnp.logical_not(lower))(before)


def source_gain(cell, part, x, y, z, width_y):
    depth = z.shape[-1]
    column = lax.div(cell, depth)
    source_x = lax.div(column, width_y)
    away = [source_x - x, column - source_x * width_y - y, cell - column * depth - z]
    along = away.pop(part)
    gain = jnp.where(along == 0, -near, 0.0)
    for offset, value in ((1, near), (2, far), (-1, -far)):
        gain = jnp.where(along == offset, value, gain)
    return jnp.where((away[0] == 0) & (away[1] == 0), gain, 0.0)


def start_of(tile_x, tile_y):
    return lax.axis_index("tx") * tile_x, lax.axis_index("ty") * tile_y


def velocity_halo_terms(links, received, stresses, stress, source, width_y, add):
    cell, amp = source
    layers, rows, depth = stress.shape[1:]
    tile = layers - 2 * LAYERS, rows - 2 * ROWS
    starts = start_of(*tile)
    for link, halo, stress_halo in zip(links, received, stresses):
        dim = link[1]
        part_n, part_a, part_b = STRAIN_OF[dim]
        shape = halo.shape[2:]
        cross = starts[1 - dim] + lax.broadcasted_iota(jnp.int32, shape, 0)
        level = lax.broadcasted_iota(jnp.int32, shape, 1)

        def own(wave, part, index):
            return face(stress, 6 * wave + STRESS_ALONG[dim][part], dim, index, True)[...]

        def whole(wave, slot, part, layer, light, terms):
            value = halo[wave, slot]
            if dim == 1:
                value += time_step * light * terms()
            if wave == 0:
                here = jnp.full(shape, starts[dim] + layer, jnp.int32)
                x, y = (here, cross) if dim == 0 else (cross, here)
                gain = source_gain(cell, VELOCITY_ALONG[dim][part], x, y, level, width_y)
                value += time_step * amp * light * gain
            return value

        def after():
            count = tile[dim]
            lights = [1.0 / stress_halo[layer, SPARE] for layer in range(2)]
            for wave in range(2):
                n = whole(wave, 0, 0, count, lights[0], lambda: -far * own(wave, 0, -1))
                add(wave, part_n, dim, -1, far * n)
                for part, name, slot in ((part_a, 1, 1), (part_b, 2, 3)):
                    inner = whole(
                        wave, slot, name, count, lights[0],
                        lambda: -near * own(wave, name, -1) - far * own(wave, name, -2),
                    )
                    outer = whole(
                        wave, slot + 1, name, count + 1, lights[1],
                        lambda: -far * own(wave, name, -1),
                    )
                    add(wave, part, dim, -1, near * inner + far * outer)
                    add(wave, part, dim, -2, far * inner)

        def before():
            lights = [halo[layer, SPARE] for layer in range(2)]
            for wave in range(2):
                outer = whole(wave, 0, 0, -2, lights[1], lambda: far * own(wave, 0, 0))
                inner = whole(
                    wave, 1, 0, -1, lights[0],
                    lambda: near * own(wave, 0, 0) + far * own(wave, 0, 1),
                )
                add(wave, part_n, dim, 0, -near * inner - far * outer)
                add(wave, part_n, dim, 1, -far * inner)
                for part, name, slot in ((part_a, 1, 2), (part_b, 2, 3)):
                    value = whole(
                        wave, slot, name, -1, lights[0], lambda: far * own(wave, name, 0)
                    )
                    add(wave, part, dim, 0, -far * value)

        real = has_peer(link[0], link[2])
        lower = is_lower(link[0], link[2])
        pl.when(real & lower)(after)
        pl.when(real & jnp.logical_not(lower))(before)


def face(ref, part, dim, index, padded):
    layers, rows, depth = ref.shape[1:]
    tile_x = layers - 2 * LAYERS if padded else layers
    tile_y = rows - 2 * ROWS if padded else rows
    if dim == 0:
        at = index % tile_x
        if padded:
            return ref.at[part, at + LAYERS, pl.ds(ROWS, tile_y), :]
        return ref.at[part, at]
    at = index % tile_y
    flat = ref.reshape(ref.shape[0], layers * rows, depth)
    begin = LAYERS * rows + ROWS + at if padded else at
    return flat.at[part, pl.ds(begin, tile_x, stride=rows), :]


def light_face(buoyancy, dim, index):
    layers, rows, depth = buoyancy.shape
    if dim == 0:
        return buoyancy[index % layers]
    return buoyancy.reshape(layers * rows, depth)[pl.ds(index % rows, layers, stride=rows), :]


def boundary_kernel(links, send_links, *refs):
    count = len(links)
    received = refs[:count]
    rim_added, buoyancy, _, velocity = refs[count : count + 4]
    sends = refs[count + 4 :]

    def add(wave, part, dim, index, term):
        target = face(velocity, 3 * wave + part, dim, index, True)
        target[...] += time_step * light_face(buoyancy, dim, index) * term

    stress_halo_terms(links, received, rim_added, (0, 1), add)
    send_velocities(send_links, velocity, buoyancy, sends)


def strain_kernel(links, width_y, *refs):
    count = len(links)
    received = refs[:count]
    source_cell, source_amp, rim_added, buoyancy, accel = refs[count : count + 5]
    strain, gradient, velocity = refs[count + 6 : count + 9]
    outputs, (accel_now, sems) = refs[count + 9 : count + 11], refs[count + 11 :]
    tile_x, tile_y, depth = buoyancy.shape
    middle = pl.ds(ROWS, tile_y)
    clear_rim(velocity, range(6), range(6))
    accel_now[...] = accel[...]

    def add(wave, part, dim, index, term):
        target = face(accel_now, part, dim, index, False)
        target[...] += light_face(buoyancy, dim, index) * term

    stress_halo_terms(links, received, rim_added, (0,), add)
    x_start, y_start = start_of(tile_x, tile_y)
    cell, amp = source_cell[0], source_amp[0]
    source_x = lax.div(cell, width_y * depth)
    y = y_start + lax.broadcasted_iota(jnp.int32, (tile_y, depth), 0)
    level = lax.broadcasted_iota(jnp.int32, (tile_y, depth), 1)
    for offset in (-2, -1, 0, 1):
        x = source_x + offset - x_start

        @pl.when((x >= 0) & (x < tile_x))
        def add_source():
            here = jnp.full((tile_y, depth), source_x + offset, jnp.int32)
            for part in range(3):
                gain = source_gain(cell, part, here, y, level, width_y)
                value = amp * buoyancy[x] * gain
                accel_now[part, x] += value
                velocity[part, x + LAYERS, middle, :] += time_step * value

    copies = [
        pltpu.make_async_copy(
            velocity.at[3 * wave + part, pl.ds(LAYERS, tile_x), middle, :],
            outputs[wave].at[part],
            sems.at[3 * wave + part],
        )
        for wave in range(2)
        for part in range(3)
    ]
    for copy in copies:
        copy.start()
    def layer(x, carry):
        for wave in range(2):
            vx, vy, vz = range(3 * wave, 3 * wave + 3)
            values = (
                along_x(velocity, vx, x, tile_y, False),
                along_y(velocity, vy, x, tile_y, False),
                along_z(velocity, vz, x, tile_y, False),
                along_y(velocity, vx, x, tile_y, True) + along_x(velocity, vy, x, tile_y, True),
                along_z(velocity, vx, x, tile_y, True) + along_x(velocity, vz, x, tile_y, True),
                along_z(velocity, vy, x, tile_y, True) + along_y(velocity, vz, x, tile_y, True),
            )
            for part, value in enumerate(values):
                strain[6 * wave + part, x] = value
        total = sum(
            accel_now[part, x] * velocity[3 + part, x + LAYERS, middle, :] for part in range(3)
        )
        gradient[2, x] = -time_step * total
        return carry

    lax.fori_loop(0, tile_x, layer, 0, unroll=4)
    for copy in copies:
        copy.wait()


def new_stress(strain, stress, scaled_lame, scaled_shear, wave, x, tile_y):
    lame, shear = scaled_lame[x], scaled_shear[x]
    strains = [strain[6 * wave + part, x] for part in range(6)]
    volume = lame * (strains[0] + strains[1] + strains[2])
    values = []
    for part in range(6):
        old = stress[6 * wave + part, x + LAYERS, pl.ds(ROWS, tile_y), :]
        if part < 3:
            values.append(old + (volume + 2.0 * shear * strains[part]))
        else:
            values.append(old + shear * strains[part])
    return strains, values


def gradient_kernel(links, width_y, *refs):
    count = len(links)
    received, stresses = refs[:count], refs[count : 2 * count]
    source_cell, source_amp, stress, scaled_lame, scaled_shear = refs[2 * count : 2 * count + 5]
    strain, gradient = refs[2 * count + 7 :]
    tile_x, tile_y, _ = scaled_lame.shape

    def add(wave, part, dim, index, term):
        target = face(strain, 6 * wave + part, dim, index, False)
        target[...] += term

    source = source_cell[0], source_amp[0]
    velocity_halo_terms(links, received, stresses, stress, source, width_y, add)

    def layer(x, carry):
        strains = [strain[part, x] for part in range(6)]
        _, values = new_stress(strain, stress, scaled_lame, scaled_shear, 1, x, tile_y)
        trace = strains[0] + strains[1] + strains[2]
        gradient[0, x] = -time_step * trace * (values[0] + values[1] + values[2])
        total = sum(left * right for left, right in zip(strains, values))
        gradient[1, x] = -time_step * total
        return carry

    lax.fori_loop(0, tile_x, layer, 0, unroll=4)


def output_kernel(
    chunk, width_y, source_cell, source_amp, strain, stress, scaled_lame, scaled_shear, *refs
):
    outputs, (values_now, sems) = refs[2:4], refs[4:]
    tile_x, tile_y, depth = scaled_lame.shape
    x_start, y_start = start_of(tile_x, tile_y)
    y = y_start + lax.broadcasted_iota(jnp.int32, (tile_y, depth), 0)
    level = lax.broadcasted_iota(jnp.int32, (tile_y, depth), 1)
    in_layer = y * depth + level - source_cell[0]
    copies = []
    for begin in range(0, tile_x, chunk):
        for wave in range(2):
            for x in range(begin, begin + chunk):
                _, values = new_stress(strain, stress, scaled_lame, scaled_shear, wave, x, tile_y)
                if wave == 0:
                    first = (x_start + x) * (width_y * depth)
                    added = jnp.where(in_layer == -first, source_amp[0], 0.0)
                    values[:3] = [value + added for value in values[:3]]
                for part in range(6):
                    values_now[6 * wave + part, x] = values[part]
            layers = pl.ds(begin, chunk)
            copy = pltpu.make_async_copy(
                values_now.at[pl.ds(6 * wave, 6), layers],
                outputs[wave].at[pl.ds(3, 6), layers],
                sems.at[len(copies)],
            )
            copy.start()
            copies.append(copy)
    for copy in copies:
        copy.wait()


def sum_kernel(mine, other, total, total_now, sems):
    copies = []
    for part in range(mine.shape[0]):
        total_now[part] = mine[part] + other[part]
        copy = pltpu.make_async_copy(total_now.at[part], total.at[part], sems.at[part])
        copy.start()
        copies.append(copy)
    for copy in copies:
        copy.wait()


def in_hbm(value):
    return pltpu.with_memory_space_constraint(value, pltpu.HBM)


def cost(flops, size):
    return pl.CostEstimate(flops=flops, bytes_accessed=size, transcendentals=0)


def body(
    forward_fields,
    adjoint_fields,
    lame_lambda,
    shear_modulus,
    density,
    source_cell,
    source_amp,
    receiver_cell,
    residual_amp,
):
    _, _, tile_x, tile_y, depth = forward_fields.shape
    forward = forward_fields.reshape(forward_fields.shape[1:])
    adjoint = adjoint_fields.reshape(adjoint_fields.shape[1:])
    sizes = {name: lax.axis_size(name) for name in ("tx", "ty")}
    width_y = tile_y * sizes["ty"]
    links_x, links_y = links_of(sizes)
    cells = tile_x * tile_y * depth

    def buffers(dim):
        return pltpu.VMEM((2, SLOTS, tile_y if dim == 0 else tile_x, depth), jnp.float32)

    def tile(*lead):
        return pltpu.VMEM((*lead, tile_x, tile_y, depth), jnp.float32)

    def padded(parts):
        return pltpu.VMEM(
            (parts, tile_x + 2 * LAYERS, tile_y + 2 * ROWS, depth), jnp.float32
        )

    def exchange(links, sends):
        return [swap(send, axis, first) for (axis, _, first), send in zip(links, sends)]

    def shapes(links):
        return [buffers(dim) for _, dim, _ in links]

    links = links_x + links_y
    count, count_x, count_y = len(links), len(links_x), len(links_y)
    rows = tile_x * tile_y + 3 * (tile_x + tile_y)
    source = source_cell, source_amp

    *sends, density_now = pl.pallas_call(
        functools.partial(early_pack_kernel, links_x),
        out_shape=shapes(links_x) + [tile()],
        in_specs=[hbm] * 3,
        out_specs=[vmem] * (count_x + 1),
        scratch_shapes=[pltpu.SemaphoreType.DMA((1 + 2 * SLOTS * count_x,))],
        compiler_params=params,
        cost_estimate=cost(0, 4 * cells),
        name="early_pack",
    )(*(in_hbm(x) for x in (forward, adjoint, density)))
    halos_x = exchange(links_x, sends)
    halos_y = []
    if links_y:
        sends = pl.pallas_call(
            functools.partial(pack_kernel, links_y),
            out_shape=shapes(links_y),
            in_specs=[vmem] * 3,
            out_specs=[vmem] * count_y,
            compiler_params=params,
            cost_estimate=cost(0, 2 * 2 * SLOTS * count_y * tile_x * depth * 4),
            name="pack",
        )(forward, adjoint, density_now)
        halos_y = exchange(links_y, sends)

    stress, velocity, accel, rim_added, buoyancy, scaled_lame, scaled_shear = pl.pallas_call(
        functools.partial(velocity_kernel, width_y),
        out_shape=[
            padded(12),
            padded(6),
            tile(3),
            pltpu.VMEM((2, 3, max(tile_x, tile_y), depth), jnp.float32),
            tile(),
            tile(),
            tile(),
        ],
        in_specs=[hbm] * 2 + [vmem] * 5,
        out_specs=[vmem] * 7,
        scratch_shapes=[
            pltpu.VMEM((rows, depth), jnp.float32),
            tile(6),
            tile(),
            tile(),
            pltpu.SemaphoreType.DMA((2,)),
        ],
        compiler_params=params,
        cost_estimate=cost(200 * cells, 18 * 4 * cells),
        name="velocity",
    )(
        in_hbm(lame_lambda),
        in_hbm(shear_modulus),
        receiver_cell,
        residual_amp,
        forward,
        adjoint,
        density_now,
    )

    def boundary(links, send_links, halos, velocity, name):
        velocity, *sends = pl.pallas_call(
            functools.partial(boundary_kernel, links, send_links),
            out_shape=[padded(6)] + shapes(send_links),
            in_specs=[vmem] * (len(links) + 3),
            out_specs=[vmem] * (1 + len(send_links)),
            input_output_aliases={len(links) + 2: 0},
            compiler_params=params,
            cost_estimate=cost(cells, 10 * 2 * tile_x * depth * 4),
            name=name,
        )(*halos, rim_added, buoyancy, velocity)
        return velocity, exchange(send_links, sends)

    velocity, velocity_halos_y = boundary(links_x, links_y, halos_x, velocity, "boundary_x")
    velocity, velocity_halos_x = boundary(links_y, links_x, halos_y, velocity, "boundary_y")
    halos = halos_x + halos_y
    velocity_halos = velocity_halos_x + velocity_halos_y

    out_shape = jax.ShapeDtypeStruct(forward.shape, jnp.float32)
    strain, gradient, _, forward_next, adjoint_next = pl.pallas_call(
        functools.partial(strain_kernel, links, width_y),
        out_shape=[tile(12), tile(3), padded(6), out_shape, out_shape],
        in_specs=[vmem] * count + [smem] * 2 + [vmem] * 4,
        out_specs=[vmem] * 3 + [hbm] * 2,
        input_output_aliases={count + 5: 2},
        scratch_shapes=[tile(3), pltpu.SemaphoreType.DMA((6,))],
        compiler_params=params,
        cost_estimate=cost(200 * cells, 18 * 4 * cells),
        name="strain",
    )(*halos, *source, rim_added, buoyancy, accel, velocity)

    strain, gradient = pl.pallas_call(
        functools.partial(gradient_kernel, links, width_y),
        out_shape=[tile(12), tile(3)],
        in_specs=[vmem] * (2 * count) + [smem] * 2 + [vmem] * 5,
        out_specs=[vmem] * 2,
        input_output_aliases={2 * count + 5: 0, 2 * count + 6: 1},
        compiler_params=params,
        cost_estimate=cost(30 * cells, 2 * 4 * cells),
        name="gradient",
    )(*velocity_halos, *halos, *source, stress, scaled_lame, scaled_shear, strain, gradient)
    other = lax.ppermute(gradient, "shot", [(0, 1), (1, 0)])

    chunk = 4 if tile_x % 4 == 0 else 1
    forward_next, adjoint_next = pl.pallas_call(
        functools.partial(output_kernel, chunk, width_y),
        out_shape=[out_shape, out_shape],
        in_specs=[smem] * 2 + [vmem] * 4 + [hbm] * 2,
        out_specs=[hbm] * 2,
        input_output_aliases={6: 0, 7: 1},
        scratch_shapes=[tile(12), pltpu.SemaphoreType.DMA((2 * tile_x // chunk,))],
        compiler_params=params,
        cost_estimate=cost(60 * cells, 18 * 4 * cells),
        name="outputs",
    )(*source, strain, stress, scaled_lame, scaled_shear, forward_next, adjoint_next)
    total = pl.pallas_call(
        sum_kernel,
        out_shape=jax.ShapeDtypeStruct((3, tile_x, tile_y, depth), jnp.float32),
        in_specs=[vmem] * 2,
        out_specs=hbm,
        scratch_shapes=[tile(3), pltpu.SemaphoreType.DMA((3,))],
        compiler_params=params,
        cost_estimate=cost(3 * cells, 9 * 4 * cells),
        name="sum",
    )(gradient, other)
    return forward_next[None], adjoint_next[None], total


def solution(mesh):
    return jax.shard_map(
        body,
        mesh=mesh,
        in_specs=(
            P("shot", None, "tx", "ty", None),
            P("shot", None, "tx", "ty", None),
            P("tx", "ty", None),
            P("tx", "ty", None),
            P("tx", "ty", None),
            P("shot"),
            P("shot"),
            P("shot", None),
            P("shot", None),
        ),
        out_specs=(
            P("shot", None, "tx", "ty", None),
            P("shot", None, "tx", "ty", None),
            P(None, "tx", "ty", None),
        ),
        check_vma=False,
    )
```

```python
import functools

import jax
import jax.numpy as jnp
from jax import lax
from jax.experimental import pallas as pl
from jax.experimental.pallas import tpu as pltpu
from jax.sharding import PartitionSpec as P

near = 9.0 / 8.0
far = -1.0 / 24.0
time_step = 0.15

LAYERS = 2
ROWS = 8
SLOTS = 5

STRESS_ALONG = ((0, 3, 4), (1, 3, 5))
ACCEL_OF = ((0, 1, 2), (1, 0, 2))
VELOCITY_ALONG = ((0, 1, 2), (1, 0, 2))
STRAIN_OF = ((0, 3, 4), (1, 3, 5))

vmem = pl.BlockSpec(memory_space=pltpu.VMEM)
smem = pl.BlockSpec(memory_space=pltpu.SMEM)
hbm = pl.BlockSpec(memory_space=pltpu.HBM)
params = pltpu.CompilerParams(vmem_limit_bytes=24 * 1024 * 1024)


def links_of(sizes):
    along_x = (("tx", 0, 1), ("tx", 0, 0))
    along_y = (("ty", 1, 1), ("ty", 1, 0))
    return [[link for link in order if link[2] + 1 < sizes[link[0]]] for order in (along_x, along_y)]


def swap(value, axis, first):
    pairs = [(i, i + 1) for i in range(first, lax.axis_size(axis) - 1, 2)]
    return lax.ppermute(value, axis, pairs + [(j, i) for i, j in pairs])


def is_lower(axis, first):
    return lax.axis_index(axis) % 2 == first


def has_peer(axis, first):
    index = lax.axis_index(axis)
    partner = jnp.where(is_lower(axis, first), index + 1, index - 1)
    return (partner >= 0) & (partner < lax.axis_size(axis))


def by_role(link, act, upper, lower):
    lower_here = is_lower(link[0], link[2])
    pl.when(lower_here)(lambda: act(lower, True))
    pl.when(jnp.logical_not(lower_here))(lambda: act(upper, False))


SPARE = SLOTS - 1


def stress_plan(dim):
    n, a, b = STRESS_ALONG[dim]
    return ((n, 0), (n, 1), (a, 0), (b, 0)), ((n, -1), (a, -2), (a, -1), (b, -2), (b, -1))


def velocity_plan(dim):
    n, a, b = VELOCITY_ALONG[dim]
    return ((n, 0), (a, 0), (a, 1), (b, 0), (b, 1)), ((n, -2), (n, -1), (a, -1), (b, -1))


def early_pack_kernel(links, forward, adjoint, density, *refs):
    sends, (density_now, sems) = refs[: len(links)], refs[len(links) :]
    tile_x = forward.shape[1]
    whole = pltpu.make_async_copy(density, density_now, sems.at[0])
    whole.start()
    waits = []
    for at, (link, send) in enumerate(zip(links, sends)):

        def sources(plan, lower, wave):
            fields = (forward, adjoint)[wave]
            found = [fields.at[3 + part, index % tile_x] for part, index in plan]
            return found if lower else found + [density.at[wave]]

        def start(plan, lower):
            for wave in range(2):
                for slot, source in enumerate(sources(plan, lower, wave)):
                    pltpu.make_async_copy(
                        source, send.at[wave, slot], sems.at[1 + (2 * at + wave) * SLOTS + slot]
                    ).start()

        by_role(link, start, *stress_plan(link[1]))
        for wave in range(2):
            for slot in range(SLOTS):
                waits.append(
                    pltpu.make_async_copy(
                        density.at[0],
                        send.at[wave, slot],
                        sems.at[1 + (2 * at + wave) * SLOTS + slot],
                    )
                )
    for copy in waits:
        copy.wait()
    whole.wait()


def pack_kernel(links, forward, adjoint, density, *sends):
    for link, send in zip(links, sends):
        dim = link[1]

        def put(plan, lower):
            for wave, fields in enumerate((forward, adjoint)):
                for slot, (part, index) in enumerate(plan):
                    send[wave, slot] = face(fields, 3 + part, dim, index, False)[...]
                if not lower:
                    send[wave, SPARE] = light_face(density, dim, wave)

        by_role(link, put, *stress_plan(dim))


def send_velocities(links, velocity, buoyancy, sends):
    for link, send in zip(links, sends):
        dim = link[1]

        def put(plan, lower):
            for wave in range(2):
                for slot, (part, index) in enumerate(plan):
                    send[wave, slot] = face(velocity, 3 * wave + part, dim, index, True)[...]
                if lower:
                    send[wave, SPARE] = light_face(buoyancy, dim, -1 - wave)

        by_role(link, put, *velocity_plan(dim))


def column_ids(tile_x, tile_y, width_y, lanes):
    x_start = lax.axis_index("tx") * tile_x
    y_start = lax.axis_index("ty") * tile_y

    def column(x, y):
        inside = (y >= 0) & (y < width_y)
        return jnp.where(inside, x * width_y + y, -1)

    def iota(shape, dim):
        return lax.broadcasted_iota(jnp.int32, shape, dim)

    shape = (tile_x, tile_y, lanes)
    tile = column(x_start + iota(shape, 0), y_start + iota(shape, 1))
    shape = (3, tile_y, lanes)
    layer = iota(shape, 0)
    along_x = column(
        x_start + jnp.where(layer == 0, -1, tile_x - 1 + layer), y_start + iota(shape, 1)
    )
    shape = (3, tile_x, lanes)
    layer = iota(shape, 0)
    along_y = column(
        x_start + iota(shape, 1), y_start + jnp.where(layer == 0, -1, tile_y - 1 + layer)
    )
    return jnp.concatenate([part.reshape(-1, lanes) for part in (tile, along_x, along_y)], axis=0)


def differ(zero, one, two, minus):
    return near * (one - zero) + far * (two - minus)


def along_x(ref, part, x, tile_y, upward):
    def at(offset):
        return ref[part, x + (LAYERS + offset), pl.ds(ROWS, tile_y), :]

    return differ(at(0), at(1), at(2), at(-1)) if upward else differ(at(-1), at(0), at(1), at(-2))


def along_y(ref, part, x, tile_y, upward):
    def at(offset):
        return ref[part, x + LAYERS, pl.ds(ROWS + offset, tile_y), :]

    return differ(at(0), at(1), at(2), at(-1)) if upward else differ(at(-1), at(0), at(1), at(-2))


def along_z(ref, part, x, tile_y, upward):
    value = ref[part, x + LAYERS, pl.ds(ROWS, tile_y), :]
    depth = value.shape[-1]
    lane = lax.broadcasted_iota(jnp.int32, value.shape, 1)

    def at(offset):
        if offset == 0:
            return value
        moved = pltpu.roll(value, (-offset) % depth, 1)
        inside = lane < depth - offset if offset > 0 else lane >= -offset
        return jnp.where(inside, moved, 0.0)

    return differ(at(0), at(1), at(2), at(-1)) if upward else differ(at(-1), at(0), at(1), at(-2))


def clear_rim(ref, parts_x, parts_y):
    _, layers, rows, depth = ref.shape
    tile_x, tile_y = layers - 2 * LAYERS, rows - 2 * ROWS
    for part in parts_x:
        for begin in (0, LAYERS + tile_x):
            ref[part, pl.ds(begin, LAYERS), pl.ds(ROWS, tile_y), :] = jnp.zeros(
                (LAYERS, tile_y, depth), jnp.float32
            )
    for part in parts_y:
        for begin in (0, ROWS + tile_y):
            ref[part, pl.ds(LAYERS, tile_x), pl.ds(begin, ROWS), :] = jnp.zeros(
                (tile_x, ROWS, depth), jnp.float32
            )


def receiver_sum(cells, amps, columns):
    depth, receivers = columns.shape[-1], cells.shape[-1]
    column = lax.div(cells, depth)
    level = cells - column * depth
    column_hot = jnp.concatenate(
        [
            (columns == column[:, begin : begin + depth]).astype(jnp.bfloat16)
            for begin in range(0, receivers, depth)
        ],
        axis=1,
    )
    levels = lax.broadcasted_iota(jnp.int32, (depth, receivers), 0)
    rest = jnp.where(levels == level, amps, 0.0)
    total = jnp.zeros(columns.shape, jnp.float32)
    for _ in range(3):
        part = rest.astype(jnp.bfloat16)
        rest = rest - part.astype(jnp.float32)
        total = total + lax.dot_general(
            column_hot,
            part,
            (((1,), (1,)), ((), ())),
            preferred_element_type=jnp.float32,
        )
    return total


def velocity_kernel(
    width_y,
    lame,
    shear,
    receiver_cell,
    residual_amp,
    forward,
    adjoint,
    density,
    stress,
    velocity,
    accel,
    rim_added,
    buoyancy,
    scaled_lame,
    scaled_shear,
    received,
    gained,
    lame_now,
    shear_now,
    sems,
):
    tile_x, tile_y, depth = density.shape
    copies = [
        pltpu.make_async_copy(lame, lame_now, sems.at[0]),
        pltpu.make_async_copy(shear, shear_now, sems.at[1]),
    ]
    for copy in copies:
        copy.start()
    cells = tile_x * tile_y
    middle = pl.ds(ROWS, tile_y)
    columns = column_ids(tile_x, tile_y, width_y, depth)
    received[...] = receiver_sum(receiver_cell[...], residual_amp[...], columns)
    for layer in range(3):
        rim_added[0, layer] = received[pl.ds(cells + layer * tile_y, tile_y), :]
        rim_added[1, layer] = received[pl.ds(cells + 3 * tile_y + layer * tile_x, tile_x), :]
    for wave in range(2):
        clear_rim(
            stress, *([6 * wave + part for part in STRESS_ALONG[dim]] for dim in range(2))
        )

    def fill(x, carry):
        extra = received[pl.ds(pl.multiple_of(x * tile_y, 8), tile_y), :]
        for wave, fields in enumerate((forward, adjoint)):
            for part in range(6):
                value = fields[3 + part, x]
                stress[6 * wave + part, x + LAYERS, middle, :] = (
                    value + extra if wave == 1 and part < 3 else value
                )
        return carry

    lax.fori_loop(0, tile_x, fill, 0, unroll=4)

    def layer(x, carry):
        for wave in range(2):
            xx, yy, zz, xy, xz, yz = range(6 * wave, 6 * wave + 6)
            values = (
                along_x(stress, xx, x, tile_y, True)
                + along_y(stress, xy, x, tile_y, False)
                + along_z(stress, xz, x, tile_y, False),
                along_x(stress, xy, x, tile_y, False)
                + along_y(stress, yy, x, tile_y, True)
                + along_z(stress, yz, x, tile_y, False),
                along_x(stress, xz, x, tile_y, False)
                + along_y(stress, yz, x, tile_y, False)
                + along_z(stress, zz, x, tile_y, True),
            )
            for part, value in enumerate(values):
                gained[3 * wave + part, x] = value
        return carry

    lax.fori_loop(0, tile_x, layer, 0, unroll=4)
    for copy in copies:
        copy.wait()

    def finish(x, carry):
        light = 1.0 / density[x]
        buoyancy[x] = light
        scaled_lame[x] = time_step * lame_now[x]
        scaled_shear[x] = time_step * shear_now[x]
        for wave, fields in enumerate((forward, adjoint)):
            for part in range(3):
                value = light * gained[3 * wave + part, x]
                if wave == 0:
                    accel[part, x] = value
                velocity[3 * wave + part, x + LAYERS, middle, :] = (
                    fields[part, x] + time_step * value
                )
        return carry

    lax.fori_loop(0, tile_x, finish, 0, unroll=4)


def stress_halo_terms(links, received, rim_added, waves, add):
    for link, halo in zip(links, received):
        dim = link[1]
        part_n, part_a, part_b = ACCEL_OF[dim]

        def normal(wave, slot, layer):
            value = halo[wave, slot]
            return value + rim_added[dim, layer] if wave == 1 else value

        def after():
            for wave in waves:
                n0, n1 = normal(wave, 0, 1), normal(wave, 1, 2)
                add(wave, part_n, dim, -1, near * n0 + far * n1)
                add(wave, part_n, dim, -2, far * n0)
                add(wave, part_a, dim, -1, far * halo[wave, 2])
                add(wave, part_b, dim, -1, far * halo[wave, 3])

        def before():
            for wave in waves:
                add(wave, part_n, dim, 0, -far * normal(wave, 0, 0))
                for part, slot in ((part_a, 1), (part_b, 3)):
                    outer, inner = halo[wave, slot], halo[wave, slot + 1]
                    add(wave, part, dim, 0, -near * inner - far * outer)
                    add(wave, part, dim, 1, -far * inner)

        real = has_peer(link[0], link[2])
        lower = is_lower(link[0], link[2])
        pl.when(real & lower)(after)
        pl.when(real & jnp.logical_not(lower))(before)


def source_gain(cell, part, x, y, z, width_y):
    depth = z.shape[-1]
    column = lax.div(cell, depth)
    source_x = lax.div(column, width_y)
    away = [source_x - x, column - source_x * width_y - y, cell - column * depth - z]
    along = away.pop(part)
    gain = jnp.where(along == 0, -near, 0.0)
    for offset, value in ((1, near), (2, far), (-1, -far)):
        gain = jnp.where(along == offset, value, gain)
    return jnp.where((away[0] == 0) & (away[1] == 0), gain, 0.0)


def start_of(tile_x, tile_y):
    return lax.axis_index("tx") * tile_x, lax.axis_index("ty") * tile_y


def velocity_halo_terms(links, received, stresses, stress, source, width_y, add):
    cell, amp = source
    layers, rows, depth = stress.shape[1:]
    tile = layers - 2 * LAYERS, rows - 2 * ROWS
    starts = start_of(*tile)
    for link, halo, stress_halo in zip(links, received, stresses):
        dim = link[1]
        part_n, part_a, part_b = STRAIN_OF[dim]
        shape = halo.shape[2:]
        cross = starts[1 - dim] + lax.broadcasted_iota(jnp.int32, shape, 0)
        level = lax.broadcasted_iota(jnp.int32, shape, 1)

        def own(wave, part, index):
            return face(stress, 6 * wave + STRESS_ALONG[dim][part], dim, index, True)[...]

        def whole(wave, slot, part, layer, light, terms):
            value = halo[wave, slot]
            if dim == 1:
                value += time_step * light * terms()
            if wave == 0:
                here = jnp.full(shape, starts[dim] + layer, jnp.int32)
                x, y = (here, cross) if dim == 0 else (cross, here)
                gain = source_gain(cell, VELOCITY_ALONG[dim][part], x, y, level, width_y)
                value += time_step * amp * light * gain
            return value

        def after():
            count = tile[dim]
            lights = [1.0 / stress_halo[layer, SPARE] for layer in range(2)]
            for wave in range(2):
                n = whole(wave, 0, 0, count, lights[0], lambda: -far * own(wave, 0, -1))
                add(wave, part_n, dim, -1, far * n)
                for part, name, slot in ((part_a, 1, 1), (part_b, 2, 3)):
                    inner = whole(
                        wave, slot, name, count, lights[0],
                        lambda: -near * own(wave, name, -1) - far * own(wave, name, -2),
                    )
                    outer = whole(
                        wave, slot + 1, name, count + 1, lights[1],
                        lambda: -far * own(wave, name, -1),
                    )
                    add(wave, part, dim, -1, near * inner + far * outer)
                    add(wave, part, dim, -2, far * inner)

        def before():
            lights = [halo[layer, SPARE] for layer in range(2)]
            for wave in range(2):
                outer = whole(wave, 0, 0, -2, lights[1], lambda: far * own(wave, 0, 0))
                inner = whole(
                    wave, 1, 0, -1, lights[0],
                    lambda: near * own(wave, 0, 0) + far * own(wave, 0, 1),
                )
                add(wave, part_n, dim, 0, -near * inner - far * outer)
                add(wave, part_n, dim, 1, -far * inner)
                for part, name, slot in ((part_a, 1, 2), (part_b, 2, 3)):
                    value = whole(
                        wave, slot, name, -1, lights[0], lambda: far * own(wave, name, 0)
                    )
                    add(wave, part, dim, 0, -far * value)

        real = has_peer(link[0], link[2])
        lower = is_lower(link[0], link[2])
        pl.when(real & lower)(after)
        pl.when(real & jnp.logical_not(lower))(before)


def face(ref, part, dim, index, padded):
    layers, rows, depth = ref.shape[1:]
    tile_x = layers - 2 * LAYERS if padded else layers
    tile_y = rows - 2 * ROWS if padded else rows
    if dim == 0:
        at = index % tile_x
        if padded:
            return ref.at[part, at + LAYERS, pl.ds(ROWS, tile_y), :]
        return ref.at[part, at]
    at = index % tile_y
    flat = ref.reshape(ref.shape[0], layers * rows, depth)
    begin = LAYERS * rows + ROWS + at if padded else at
    return flat.at[part, pl.ds(begin, tile_x, stride=rows), :]


def light_face(buoyancy, dim, index):
    layers, rows, depth = buoyancy.shape
    if dim == 0:
        return buoyancy[index % layers]
    return buoyancy.reshape(layers * rows, depth)[pl.ds(index % rows, layers, stride=rows), :]


def boundary_kernel(links, send_links, *refs):
    count = len(links)
    received = refs[:count]
    rim_added, buoyancy, _, velocity = refs[count : count + 4]
    sends = refs[count + 4 :]

    def add(wave, part, dim, index, term):
        target = face(velocity, 3 * wave + part, dim, index, True)
        target[...] += time_step * light_face(buoyancy, dim, index) * term

    stress_halo_terms(links, received, rim_added, (0, 1), add)
    send_velocities(send_links, velocity, buoyancy, sends)


def strain_kernel(links, width_y, *refs):
    count = len(links)
    received = refs[:count]
    source_cell, source_amp, rim_added, buoyancy, accel = refs[count : count + 5]
    strain, gradient, velocity = refs[count + 6 : count + 9]
    outputs, (accel_now, sems) = refs[count + 9 : count + 11], refs[count + 11 :]
    tile_x, tile_y, depth = buoyancy.shape
    middle = pl.ds(ROWS, tile_y)
    clear_rim(velocity, range(6), range(6))
    accel_now[...] = accel[...]

    def add(wave, part, dim, index, term):
        target = face(accel_now, part, dim, index, False)
        target[...] += light_face(buoyancy, dim, index) * term

    stress_halo_terms(links, received, rim_added, (0,), add)
    x_start, y_start = start_of(tile_x, tile_y)
    cell, amp = source_cell[0], source_amp[0]
    source_x = lax.div(cell, width_y * depth)
    y = y_start + lax.broadcasted_iota(jnp.int32, (tile_y, depth), 0)
    level = lax.broadcasted_iota(jnp.int32, (tile_y, depth), 1)
    for offset in (-2, -1, 0, 1):
        x = source_x + offset - x_start

        @pl.when((x >= 0) & (x < tile_x))
        def add_source():
            here = jnp.full((tile_y, depth), source_x + offset, jnp.int32)
            for part in range(3):
                gain = source_gain(cell, part, here, y, level, width_y)
                value = amp * buoyancy[x] * gain
                accel_now[part, x] += value
                velocity[part, x + LAYERS, middle, :] += time_step * value

    copies = [
        pltpu.make_async_copy(
            velocity.at[3 * wave + part, pl.ds(LAYERS, tile_x), middle, :],
            outputs[wave].at[part],
            sems.at[3 * wave + part],
        )
        for wave in range(2)
        for part in range(3)
    ]
    for copy in copies:
        copy.start()
    def layer(x, carry):
        for wave in range(2):
            vx, vy, vz = range(3 * wave, 3 * wave + 3)
            values = (
                along_x(velocity, vx, x, tile_y, False),
                along_y(velocity, vy, x, tile_y, False),
                along_z(velocity, vz, x, tile_y, False),
                along_y(velocity, vx, x, tile_y, True) + along_x(velocity, vy, x, tile_y, True),
                along_z(velocity, vx, x, tile_y, True) + along_x(velocity, vz, x, tile_y, True),
                along_z(velocity, vy, x, tile_y, True) + along_y(velocity, vz, x, tile_y, True),
            )
            for part, value in enumerate(values):
                strain[6 * wave + part, x] = value
        total = sum(
            accel_now[part, x] * velocity[3 + part, x + LAYERS, middle, :] for part in range(3)
        )
        gradient[2, x] = -time_step * total
        return carry

    lax.fori_loop(0, tile_x, layer, 0, unroll=4)
    for copy in copies:
        copy.wait()


def new_stress(strain, stress, scaled_lame, scaled_shear, wave, x, tile_y):
    lame, shear = scaled_lame[x], scaled_shear[x]
    strains = [strain[6 * wave + part, x] for part in range(6)]
    volume = lame * (strains[0] + strains[1] + strains[2])
    values = []
    for part in range(6):
        old = stress[6 * wave + part, x + LAYERS, pl.ds(ROWS, tile_y), :]
        if part < 3:
            values.append(old + (volume + 2.0 * shear * strains[part]))
        else:
            values.append(old + shear * strains[part])
    return strains, values


def gradient_kernel(links, width_y, *refs):
    count = len(links)
    received, stresses = refs[:count], refs[count : 2 * count]
    source_cell, source_amp, stress, scaled_lame, scaled_shear = refs[2 * count : 2 * count + 5]
    strain, gradient = refs[2 * count + 7 :]
    tile_x, tile_y, _ = scaled_lame.shape

    def add(wave, part, dim, index, term):
        target = face(strain, 6 * wave + part, dim, index, False)
        target[...] += term

    source = source_cell[0], source_amp[0]
    velocity_halo_terms(links, received, stresses, stress, source, width_y, add)

    def layer(x, carry):
        strains = [strain[part, x] for part in range(6)]
        _, values = new_stress(strain, stress, scaled_lame, scaled_shear, 1, x, tile_y)
        trace = strains[0] + strains[1] + strains[2]
        gradient[0, x] = -time_step * trace * (values[0] + values[1] + values[2])
        total = sum(left * right for left, right in zip(strains, values))
        gradient[1, x] = -time_step * total
        return carry

    lax.fori_loop(0, tile_x, layer, 0, unroll=4)


def output_kernel(
    chunk, width_y, source_cell, source_amp, strain, stress, scaled_lame, scaled_shear, *refs
):
    outputs, (values_now, sems) = refs[2:4], refs[4:]
    tile_x, tile_y, depth = scaled_lame.shape
    x_start, y_start = start_of(tile_x, tile_y)
    y = y_start + lax.broadcasted_iota(jnp.int32, (tile_y, depth), 0)
    level = lax.broadcasted_iota(jnp.int32, (tile_y, depth), 1)
    in_layer = y * depth + level - source_cell[0]
    copies = []
    for begin in range(0, tile_x, chunk):
        for wave in range(2):
            for x in range(begin, begin + chunk):
                _, values = new_stress(strain, stress, scaled_lame, scaled_shear, wave, x, tile_y)
                if wave == 0:
                    first = (x_start + x) * (width_y * depth)
                    added = jnp.where(in_layer == -first, source_amp[0], 0.0)
                    values[:3] = [value + added for value in values[:3]]
                for part in range(6):
                    values_now[6 * wave + part, x] = values[part]
            layers = pl.ds(begin, chunk)
            copy = pltpu.make_async_copy(
                values_now.at[pl.ds(6 * wave, 6), layers],
                outputs[wave].at[pl.ds(3, 6), layers],
                sems.at[len(copies)],
            )
            copy.start()
            copies.append(copy)
    for copy in copies:
        copy.wait()


def sum_kernel(mine, other, total, total_now, sems):
    copies = []
    for part in range(mine.shape[0]):
        total_now[part] = mine[part] + other[part]
        copy = pltpu.make_async_copy(total_now.at[part], total.at[part], sems.at[part])
        copy.start()
        copies.append(copy)
    for copy in copies:
        copy.wait()


def in_hbm(value):
    return pltpu.with_memory_space_constraint(value, pltpu.HBM)


def cost(flops, size):
    return pl.CostEstimate(flops=flops, bytes_accessed=size, transcendentals=0)


def body(
    forward_fields,
    adjoint_fields,
    lame_lambda,
    shear_modulus,
    density,
    source_cell,
    source_amp,
    receiver_cell,
    residual_amp,
):
    _, _, tile_x, tile_y, depth = forward_fields.shape
    forward = forward_fields.reshape(forward_fields.shape[1:])
    adjoint = adjoint_fields.reshape(adjoint_fields.shape[1:])
    sizes = {name: lax.axis_size(name) for name in ("tx", "ty")}
    width_y = tile_y * sizes["ty"]
    links_x, links_y = links_of(sizes)
    cells = tile_x * tile_y * depth

    def buffers(dim):
        return pltpu.VMEM((2, SLOTS, tile_y if dim == 0 else tile_x, depth), jnp.float32)

    def tile(*lead):
        return pltpu.VMEM((*lead, tile_x, tile_y, depth), jnp.float32)

    def padded(parts):
        return pltpu.VMEM(
            (parts, tile_x + 2 * LAYERS, tile_y + 2 * ROWS, depth), jnp.float32
        )

    def exchange(links, sends):
        return [swap(send, axis, first) for (axis, _, first), send in zip(links, sends)]

    def shapes(links):
        return [buffers(dim) for _, dim, _ in links]

    links = links_y + links_x
    count, count_x, count_y = len(links), len(links_x), len(links_y)
    rows = tile_x * tile_y + 3 * (tile_x + tile_y)
    source = source_cell, source_amp

    *sends, density_now = pl.pallas_call(
        functools.partial(early_pack_kernel, links_x),
        out_shape=shapes(links_x) + [tile()],
        in_specs=[hbm] * 3,
        out_specs=[vmem] * (count_x + 1),
        scratch_shapes=[pltpu.SemaphoreType.DMA((1 + 2 * SLOTS * count_x,))],
        compiler_params=params,
        cost_estimate=cost(0, 4 * cells),
        name="early_pack",
    )(*(in_hbm(x) for x in (forward, adjoint, density)))
    halos_x = exchange(links_x, sends)
    halos_y = []
    if links_y:
        sends = pl.pallas_call(
            functools.partial(pack_kernel, links_y),
            out_shape=shapes(links_y),
            in_specs=[vmem] * 3,
            out_specs=[vmem] * count_y,
            compiler_params=params,
            cost_estimate=cost(0, 2 * 2 * SLOTS * count_y * tile_x * depth * 4),
            name="pack",
        )(forward, adjoint, density_now)
        halos_y = exchange(links_y, sends)

    stress, velocity, accel, rim_added, buoyancy, scaled_lame, scaled_shear = pl.pallas_call(
        functools.partial(velocity_kernel, width_y),
        out_shape=[
            padded(12),
            padded(6),
            tile(3),
            pltpu.VMEM((2, 3, max(tile_x, tile_y), depth), jnp.float32),
            tile(),
            tile(),
            tile(),
        ],
        in_specs=[hbm] * 2 + [vmem] * 5,
        out_specs=[vmem] * 7,
        scratch_shapes=[
            pltpu.VMEM((rows, depth), jnp.float32),
            tile(6),
            tile(),
            tile(),
            pltpu.SemaphoreType.DMA((2,)),
        ],
        compiler_params=params,
        cost_estimate=cost(200 * cells, 18 * 4 * cells),
        name="velocity",
    )(
        in_hbm(lame_lambda),
        in_hbm(shear_modulus),
        receiver_cell,
        residual_amp,
        forward,
        adjoint,
        density_now,
    )

    def boundary(links, send_links, halos, velocity, name):
        velocity, *sends = pl.pallas_call(
            functools.partial(boundary_kernel, links, send_links),
            out_shape=[padded(6)] + shapes(send_links),
            in_specs=[vmem] * (len(links) + 3),
            out_specs=[vmem] * (1 + len(send_links)),
            input_output_aliases={len(links) + 2: 0},
            compiler_params=params,
            cost_estimate=cost(cells, 10 * 2 * tile_x * depth * 4),
            name=name,
        )(*halos, rim_added, buoyancy, velocity)
        return velocity, exchange(send_links, sends)

    velocity, velocity_halos_y = boundary(links_x, links_y, halos_x, velocity, "boundary_x")
    velocity, velocity_halos_x = boundary(links_y, links_x, halos_y, velocity, "boundary_y")
    halos = halos_y + halos_x
    velocity_halos = velocity_halos_y + velocity_halos_x

    out_shape = jax.ShapeDtypeStruct(forward.shape, jnp.float32)
    strain, gradient, _, forward_next, adjoint_next = pl.pallas_call(
        functools.partial(strain_kernel, links, width_y),
        out_shape=[tile(12), tile(3), padded(6), out_shape, out_shape],
        in_specs=[vmem] * count + [smem] * 2 + [vmem] * 4,
        out_specs=[vmem] * 3 + [hbm] * 2,
        input_output_aliases={count + 5: 2},
        scratch_shapes=[tile(3), pltpu.SemaphoreType.DMA((6,))],
        compiler_params=params,
        cost_estimate=cost(200 * cells, 18 * 4 * cells),
        name="strain",
    )(*halos, *source, rim_added, buoyancy, accel, velocity)

    strain, gradient = pl.pallas_call(
        functools.partial(gradient_kernel, links, width_y),
        out_shape=[tile(12), tile(3)],
        in_specs=[vmem] * (2 * count) + [smem] * 2 + [vmem] * 5,
        out_specs=[vmem] * 2,
        input_output_aliases={2 * count + 5: 0, 2 * count + 6: 1},
        compiler_params=params,
        cost_estimate=cost(30 * cells, 2 * 4 * cells),
        name="gradient",
    )(*velocity_halos, *halos, *source, stress, scaled_lame, scaled_shear, strain, gradient)
    other = lax.ppermute(gradient, "shot", [(0, 1), (1, 0)])

    chunk = 4 if tile_x % 4 == 0 else 1
    forward_next, adjoint_next = pl.pallas_call(
        functools.partial(output_kernel, chunk, width_y),
        out_shape=[out_shape, out_shape],
        in_specs=[smem] * 2 + [vmem] * 4 + [hbm] * 2,
        out_specs=[hbm] * 2,
        input_output_aliases={6: 0, 7: 1},
        scratch_shapes=[tile(12), pltpu.SemaphoreType.DMA((2 * tile_x // chunk,))],
        compiler_params=params,
        cost_estimate=cost(60 * cells, 18 * 4 * cells),
        name="outputs",
    )(*source, strain, stress, scaled_lame, scaled_shear, forward_next, adjoint_next)
    total = pl.pallas_call(
        sum_kernel,
        out_shape=jax.ShapeDtypeStruct((3, tile_x, tile_y, depth), jnp.float32),
        in_specs=[vmem] * 2,
        out_specs=hbm,
        scratch_shapes=[tile(3), pltpu.SemaphoreType.DMA((3,))],
        compiler_params=params,
        cost_estimate=cost(3 * cells, 9 * 4 * cells),
        name="sum",
    )(gradient, other)
    return forward_next[None], adjoint_next[None], total


def solution(mesh):
    return jax.shard_map(
        body,
        mesh=mesh,
        in_specs=(
            P("shot", None, "tx", "ty", None),
            P("shot", None, "tx", "ty", None),
            P("tx", "ty", None),
            P("tx", "ty", None),
            P("tx", "ty", None),
            P("shot"),
            P("shot"),
            P("shot", None),
            P("shot", None),
        ),
        out_specs=(
            P("shot", None, "tx", "ty", None),
            P("shot", None, "tx", "ty", None),
            P(None, "tx", "ty", None),
        ),
        check_vma=False,
    )
```

```python
import functools

import jax
import jax.numpy as jnp
from jax import lax
from jax.experimental import pallas as pl
from jax.experimental.pallas import tpu as pltpu
from jax.sharding import PartitionSpec as P

near = 9.0 / 8.0
far = -1.0 / 24.0
time_step = 0.15

LAYERS = 2
ROWS = 8
SLOTS = 5

STRESS_ALONG = ((0, 3, 4), (1, 3, 5))
ACCEL_OF = ((0, 1, 2), (1, 0, 2))
VELOCITY_ALONG = ((0, 1, 2), (1, 0, 2))
STRAIN_OF = ((0, 3, 4), (1, 3, 5))

vmem = pl.BlockSpec(memory_space=pltpu.VMEM)
smem = pl.BlockSpec(memory_space=pltpu.SMEM)
hbm = pl.BlockSpec(memory_space=pltpu.HBM)
params = pltpu.CompilerParams(vmem_limit_bytes=24 * 1024 * 1024)


def links_of(sizes):
    along_x = (("tx", 0, 1), ("tx", 0, 0))
    along_y = (("ty", 1, 1), ("ty", 1, 0))
    return [[link for link in order if link[2] + 1 < sizes[link[0]]] for order in (along_x, along_y)]


def swap(value, axis, first):
    pairs = [(i, i + 1) for i in range(first, lax.axis_size(axis) - 1, 2)]
    return lax.ppermute(value, axis, pairs + [(j, i) for i, j in pairs])


def is_lower(axis, first):
    return lax.axis_index(axis) % 2 == first


def has_peer(axis, first):
    index = lax.axis_index(axis)
    partner = jnp.where(is_lower(axis, first), index + 1, index - 1)
    return (partner >= 0) & (partner < lax.axis_size(axis))


def by_role(link, act, upper, lower):
    lower_here = is_lower(link[0], link[2])
    pl.when(lower_here)(lambda: act(lower, True))
    pl.when(jnp.logical_not(lower_here))(lambda: act(upper, False))


SPARE = SLOTS - 1


def stress_plan(dim):
    n, a, b = STRESS_ALONG[dim]
    return ((n, 0), (n, 1), (a, 0), (b, 0)), ((n, -1), (a, -2), (a, -1), (b, -2), (b, -1))


def velocity_plan(dim):
    n, a, b = VELOCITY_ALONG[dim]
    return ((n, 0), (a, 0), (a, 1), (b, 0), (b, 1)), ((n, -2), (n, -1), (a, -1), (b, -1))


def early_pack_kernel(links, forward, adjoint, density, *refs):
    sends, (density_now, sems) = refs[: len(links)], refs[len(links) :]
    tile_x = forward.shape[1]
    whole = pltpu.make_async_copy(density, density_now, sems.at[0])
    whole.start()
    waits = []
    for at, (link, send) in enumerate(zip(links, sends)):

        def sources(plan, lower, wave):
            fields = (forward, adjoint)[wave]
            found = [fields.at[3 + part, index % tile_x] for part, index in plan]
            return found if lower else found + [density.at[wave]]

        def start(plan, lower):
            for wave in range(2):
                for slot, source in enumerate(sources(plan, lower, wave)):
                    pltpu.make_async_copy(
                        source, send.at[wave, slot], sems.at[1 + (2 * at + wave) * SLOTS + slot]
                    ).start()

        by_role(link, start, *stress_plan(link[1]))
        for wave in range(2):
            for slot in range(SLOTS):
                waits.append(
                    pltpu.make_async_copy(
                        density.at[0],
                        send.at[wave, slot],
                        sems.at[1 + (2 * at + wave) * SLOTS + slot],
                    )
                )
    for copy in waits:
        copy.wait()
    whole.wait()


def pack_kernel(links, forward, adjoint, density, *sends):
    for link, send in zip(links, sends):
        dim = link[1]

        def put(plan, lower):
            for wave, fields in enumerate((forward, adjoint)):
                for slot, (part, index) in enumerate(plan):
                    send[wave, slot] = face(fields, 3 + part, dim, index, False)[...]
                if not lower:
                    send[wave, SPARE] = light_face(density, dim, wave)

        by_role(link, put, *stress_plan(dim))


def send_velocities(links, velocity, buoyancy, sends):
    for link, send in zip(links, sends):
        dim = link[1]

        def put(plan, lower):
            for wave in range(2):
                for slot, (part, index) in enumerate(plan):
                    send[wave, slot] = face(velocity, 3 * wave + part, dim, index, True)[...]
                if lower:
                    send[wave, SPARE] = light_face(buoyancy, dim, -1 - wave)

        by_role(link, put, *velocity_plan(dim))


def column_ids(tile_x, tile_y, width_y, lanes):
    x_start = lax.axis_index("tx") * tile_x
    y_start = lax.axis_index("ty") * tile_y

    def column(x, y):
        inside = (y >= 0) & (y < width_y)
        return jnp.where(inside, x * width_y + y, -1)

    def iota(shape, dim):
        return lax.broadcasted_iota(jnp.int32, shape, dim)

    shape = (tile_x, tile_y, lanes)
    tile = column(x_start + iota(shape, 0), y_start + iota(shape, 1))
    shape = (3, tile_y, lanes)
    layer = iota(shape, 0)
    along_x = column(
        x_start + jnp.where(layer == 0, -1, tile_x - 1 + layer), y_start + iota(shape, 1)
    )
    shape = (3, tile_x, lanes)
    layer = iota(shape, 0)
    along_y = column(
        x_start + iota(shape, 1), y_start + jnp.where(layer == 0, -1, tile_y - 1 + layer)
    )
    return jnp.concatenate([part.reshape(-1, lanes) for part in (tile, along_x, along_y)], axis=0)


def differ(zero, one, two, minus):
    return near * (one - zero) + far * (two - minus)


def along_x(ref, part, x, tile_y, upward):
    def at(offset):
        return ref[part, x + (LAYERS + offset), pl.ds(ROWS, tile_y), :]

    return differ(at(0), at(1), at(2), at(-1)) if upward else differ(at(-1), at(0), at(1), at(-2))


def along_y(ref, part, x, tile_y, upward):
    def at(offset):
        return ref[part, x + LAYERS, pl.ds(ROWS + offset, tile_y), :]

    return differ(at(0), at(1), at(2), at(-1)) if upward else differ(at(-1), at(0), at(1), at(-2))


def along_z(ref, part, x, tile_y, upward):
    value = ref[part, x + LAYERS, pl.ds(ROWS, tile_y), :]
    depth = value.shape[-1]
    lane = lax.broadcasted_iota(jnp.int32, value.shape, 1)

    def at(offset):
        if offset == 0:
            return value
        moved = pltpu.roll(value, (-offset) % depth, 1)
        inside = lane < depth - offset if offset > 0 else lane >= -offset
        return jnp.where(inside, moved, 0.0)

    return differ(at(0), at(1), at(2), at(-1)) if upward else differ(at(-1), at(0), at(1), at(-2))


def clear_rim(ref, parts_x, parts_y):
    _, layers, rows, depth = ref.shape
    tile_x, tile_y = layers - 2 * LAYERS, rows - 2 * ROWS
    for part in parts_x:
        for begin in (0, LAYERS + tile_x):
            ref[part, pl.ds(begin, LAYERS), pl.ds(ROWS, tile_y), :] = jnp.zeros(
                (LAYERS, tile_y, depth), jnp.float32
            )
    for part in parts_y:
        for begin in (0, ROWS + tile_y):
            ref[part, pl.ds(LAYERS, tile_x), pl.ds(begin, ROWS), :] = jnp.zeros(
                (tile_x, ROWS, depth), jnp.float32
            )


def receiver_sum(cells, amps, columns):
    depth, receivers = columns.shape[-1], cells.shape[-1]
    column = lax.div(cells, depth)
    level = cells - column * depth
    column_hot = jnp.concatenate(
        [
            (columns == column[:, begin : begin + depth]).astype(jnp.bfloat16)
            for begin in range(0, receivers, depth)
        ],
        axis=1,
    )
    levels = lax.broadcasted_iota(jnp.int32, (depth, receivers), 0)
    rest = jnp.where(levels == level, amps, 0.0)
    total = jnp.zeros(columns.shape, jnp.float32)
    for _ in range(3):
        part = rest.astype(jnp.bfloat16)
        rest = rest - part.astype(jnp.float32)
        total = total + lax.dot_general(
            column_hot,
            part,
            (((1,), (1,)), ((), ())),
            preferred_element_type=jnp.float32,
        )
    return total


def velocity_kernel(
    width_y,
    lame,
    shear,
    receiver_cell,
    residual_amp,
    forward,
    adjoint,
    density,
    stress,
    velocity,
    accel,
    rim_added,
    buoyancy,
    scaled_lame,
    scaled_shear,
    received,
    gained,
    lame_now,
    shear_now,
    sems,
):
    tile_x, tile_y, depth = density.shape
    copies = [
        pltpu.make_async_copy(lame, lame_now, sems.at[0]),
        pltpu.make_async_copy(shear, shear_now, sems.at[1]),
    ]
    for copy in copies:
        copy.start()
    cells = tile_x * tile_y
    middle = pl.ds(ROWS, tile_y)
    columns = column_ids(tile_x, tile_y, width_y, depth)
    received[...] = receiver_sum(receiver_cell[...], residual_amp[...], columns)
    for layer in range(3):
        rim_added[0, layer] = received[pl.ds(cells + layer * tile_y, tile_y), :]
        rim_added[1, layer] = received[pl.ds(cells + 3 * tile_y + layer * tile_x, tile_x), :]
    for wave in range(2):
        clear_rim(
            stress, *([6 * wave + part for part in STRESS_ALONG[dim]] for dim in range(2))
        )

    def fill(x, carry):
        extra = received[pl.ds(pl.multiple_of(x * tile_y, 8), tile_y), :]
        for wave, fields in enumerate((forward, adjoint)):
            for part in range(6):
                value = fields[3 + part, x]
                stress[6 * wave + part, x + LAYERS, middle, :] = (
                    value + extra if wave == 1 and part < 3 else value
                )
        return carry

    lax.fori_loop(0, tile_x, fill, 0, unroll=4)

    def layer(x, carry):
        for wave in range(2):
            xx, yy, zz, xy, xz, yz = range(6 * wave, 6 * wave + 6)
            values = (
                along_x(stress, xx, x, tile_y, True)
                + along_y(stress, xy, x, tile_y, False)
                + along_z(stress, xz, x, tile_y, False),
                along_x(stress, xy, x, tile_y, False)
                + along_y(stress, yy, x, tile_y, True)
                + along_z(stress, yz, x, tile_y, False),
                along_x(stress, xz, x, tile_y, False)
                + along_y(stress, yz, x, tile_y, False)
                + along_z(stress, zz, x, tile_y, True),
            )
            for part, value in enumerate(values):
                gained[3 * wave + part, x] = value
        return carry

    lax.fori_loop(0, tile_x, layer, 0, unroll=4)
    for copy in copies:
        copy.wait()

    def finish(x, carry):
        light = 1.0 / density[x]
        buoyancy[x] = light
        scaled_lame[x] = time_step * lame_now[x]
        scaled_shear[x] = time_step * shear_now[x]
        for wave, fields in enumerate((forward, adjoint)):
            for part in range(3):
                value = light * gained[3 * wave + part, x]
                if wave == 0:
                    accel[part, x] = value
                velocity[3 * wave + part, x + LAYERS, middle, :] = (
                    fields[part, x] + time_step * value
                )
        return carry

    lax.fori_loop(0, tile_x, finish, 0, unroll=4)


def stress_halo_terms(links, received, rim_added, waves, add):
    for link, halo in zip(links, received):
        dim = link[1]
        part_n, part_a, part_b = ACCEL_OF[dim]

        def normal(wave, slot, layer):
            value = halo[wave, slot]
            return value + rim_added[dim, layer] if wave == 1 else value

        def after():
            for wave in waves:
                n0, n1 = normal(wave, 0, 1), normal(wave, 1, 2)
                add(wave, part_n, dim, -1, near * n0 + far * n1)
                add(wave, part_n, dim, -2, far * n0)
                add(wave, part_a, dim, -1, far * halo[wave, 2])
                add(wave, part_b, dim, -1, far * halo[wave, 3])

        def before():
            for wave in waves:
                add(wave, part_n, dim, 0, -far * normal(wave, 0, 0))
                for part, slot in ((part_a, 1), (part_b, 3)):
                    outer, inner = halo[wave, slot], halo[wave, slot + 1]
                    add(wave, part, dim, 0, -near * inner - far * outer)
                    add(wave, part, dim, 1, -far * inner)

        real = has_peer(link[0], link[2])
        lower = is_lower(link[0], link[2])
        pl.when(real & lower)(after)
        pl.when(real & jnp.logical_not(lower))(before)


def source_gain(cell, part, x, y, z, width_y):
    depth = z.shape[-1]
    column = lax.div(cell, depth)
    source_x = lax.div(column, width_y)
    away = [source_x - x, column - source_x * width_y - y, cell - column * depth - z]
    along = away.pop(part)
    gain = jnp.where(along == 0, -near, 0.0)
    for offset, value in ((1, near), (2, far), (-1, -far)):
        gain = jnp.where(along == offset, value, gain)
    return jnp.where((away[0] == 0) & (away[1] == 0), gain, 0.0)


def start_of(tile_x, tile_y):
    return lax.axis_index("tx") * tile_x, lax.axis_index("ty") * tile_y


def velocity_halo_terms(links, received, stresses, stress, source, width_y, add):
    cell, amp = source
    layers, rows, depth = stress.shape[1:]
    tile = layers - 2 * LAYERS, rows - 2 * ROWS
    starts = start_of(*tile)
    for link, halo, stress_halo in zip(links, received, stresses):
        dim = link[1]
        part_n, part_a, part_b = STRAIN_OF[dim]
        shape = halo.shape[2:]
        cross = starts[1 - dim] + lax.broadcasted_iota(jnp.int32, shape, 0)
        level = lax.broadcasted_iota(jnp.int32, shape, 1)

        def own(wave, part, index):
            return face(stress, 6 * wave + STRESS_ALONG[dim][part], dim, index, True)[...]

        def whole(wave, slot, part, layer, light, terms):
            value = halo[wave, slot]
            if dim == 1:
                value += time_step * light * terms()
            if wave == 0:
                here = jnp.full(shape, starts[dim] + layer, jnp.int32)
                x, y = (here, cross) if dim == 0 else (cross, here)
                gain = source_gain(cell, VELOCITY_ALONG[dim][part], x, y, level, width_y)
                value += time_step * amp * light * gain
            return value

        def after():
            count = tile[dim]
            lights = [1.0 / stress_halo[layer, SPARE] for layer in range(2)]
            for wave in range(2):
                n = whole(wave, 0, 0, count, lights[0], lambda: -far * own(wave, 0, -1))
                add(wave, part_n, dim, -1, far * n)
                for part, name, slot in ((part_a, 1, 1), (part_b, 2, 3)):
                    inner = whole(
                        wave, slot, name, count, lights[0],
                        lambda: -near * own(wave, name, -1) - far * own(wave, name, -2),
                    )
                    outer = whole(
                        wave, slot + 1, name, count + 1, lights[1],
                        lambda: -far * own(wave, name, -1),
                    )
                    add(wave, part, dim, -1, near * inner + far * outer)
                    add(wave, part, dim, -2, far * inner)

        def before():
            lights = [halo[layer, SPARE] for layer in range(2)]
            for wave in range(2):
                outer = whole(wave, 0, 0, -2, lights[1], lambda: far * own(wave, 0, 0))
                inner = whole(
                    wave, 1, 0, -1, lights[0],
                    lambda: near * own(wave, 0, 0) + far * own(wave, 0, 1),
                )
                add(wave, part_n, dim, 0, -near * inner - far * outer)
                add(wave, part_n, dim, 1, -far * inner)
                for part, name, slot in ((part_a, 1, 2), (part_b, 2, 3)):
                    value = whole(
                        wave, slot, name, -1, lights[0], lambda: far * own(wave, name, 0)
                    )
                    add(wave, part, dim, 0, -far * value)

        real = has_peer(link[0], link[2])
        lower = is_lower(link[0], link[2])
        pl.when(real & lower)(after)
        pl.when(real & jnp.logical_not(lower))(before)


def face(ref, part, dim, index, padded):
    layers, rows, depth = ref.shape[1:]
    tile_x = layers - 2 * LAYERS if padded else layers
    tile_y = rows - 2 * ROWS if padded else rows
    if dim == 0:
        at = index % tile_x
        if padded:
            return ref.at[part, at + LAYERS, pl.ds(ROWS, tile_y), :]
        return ref.at[part, at]
    at = index % tile_y
    flat = ref.reshape(ref.shape[0], layers * rows, depth)
    begin = LAYERS * rows + ROWS + at if padded else at
    return flat.at[part, pl.ds(begin, tile_x, stride=rows), :]


def light_face(buoyancy, dim, index):
    layers, rows, depth = buoyancy.shape
    if dim == 0:
        return buoyancy[index % layers]
    return buoyancy.reshape(layers * rows, depth)[pl.ds(index % rows, layers, stride=rows), :]


def boundary_kernel(links, send_links, *refs):
    count = len(links)
    received = refs[:count]
    rim_added, buoyancy, _, velocity = refs[count : count + 4]
    sends = refs[count + 4 :]

    def add(wave, part, dim, index, term):
        target = face(velocity, 3 * wave + part, dim, index, True)
        target[...] += time_step * light_face(buoyancy, dim, index) * term

    stress_halo_terms(links, received, rim_added, (0, 1), add)
    send_velocities(send_links, velocity, buoyancy, sends)


def strain_kernel(links, width_y, *refs):
    count = len(links)
    received = refs[:count]
    source_cell, source_amp, rim_added, buoyancy, accel = refs[count : count + 5]
    strain, gradient, velocity = refs[count + 6 : count + 9]
    outputs, (accel_now, sems) = refs[count + 9 : count + 11], refs[count + 11 :]
    tile_x, tile_y, depth = buoyancy.shape
    middle = pl.ds(ROWS, tile_y)
    clear_rim(velocity, range(6), range(6))
    accel_now[...] = accel[...]

    def add(wave, part, dim, index, term):
        target = face(accel_now, part, dim, index, False)
        target[...] += light_face(buoyancy, dim, index) * term

    stress_halo_terms(links, received, rim_added, (0,), add)
    x_start, y_start = start_of(tile_x, tile_y)
    cell, amp = source_cell[0], source_amp[0]
    source_x = lax.div(cell, width_y * depth)
    y = y_start + lax.broadcasted_iota(jnp.int32, (tile_y, depth), 0)
    level = lax.broadcasted_iota(jnp.int32, (tile_y, depth), 1)
    for offset in (-2, -1, 0, 1):
        x = source_x + offset - x_start

        @pl.when((x >= 0) & (x < tile_x))
        def add_source():
            here = jnp.full((tile_y, depth), source_x + offset, jnp.int32)
            for part in range(3):
                gain = source_gain(cell, part, here, y, level, width_y)
                value = amp * buoyancy[x] * gain
                accel_now[part, x] += value
                velocity[part, x + LAYERS, middle, :] += time_step * value

    copies = [
        pltpu.make_async_copy(
            velocity.at[3 * wave + part, pl.ds(LAYERS, tile_x), middle, :],
            outputs[wave].at[part],
            sems.at[3 * wave + part],
        )
        for wave in range(2)
        for part in range(3)
    ]
    for copy in copies:
        copy.start()
    def layer(x, carry):
        for wave in range(2):
            vx, vy, vz = range(3 * wave, 3 * wave + 3)
            values = (
                along_x(velocity, vx, x, tile_y, False),
                along_y(velocity, vy, x, tile_y, False),
                along_z(velocity, vz, x, tile_y, False),
                along_y(velocity, vx, x, tile_y, True) + along_x(velocity, vy, x, tile_y, True),
                along_z(velocity, vx, x, tile_y, True) + along_x(velocity, vz, x, tile_y, True),
                along_z(velocity, vy, x, tile_y, True) + along_y(velocity, vz, x, tile_y, True),
            )
            for part, value in enumerate(values):
                strain[6 * wave + part, x] = value
        total = sum(
            accel_now[part, x] * velocity[3 + part, x + LAYERS, middle, :] for part in range(3)
        )
        gradient[2, x] = -time_step * total
        return carry

    lax.fori_loop(0, tile_x, layer, 0, unroll=4)
    for copy in copies:
        copy.wait()


def new_stress(strain, stress, scaled_lame, scaled_shear, wave, x, tile_y):
    lame, shear = scaled_lame[x], scaled_shear[x]
    strains = [strain[6 * wave + part, x] for part in range(6)]
    volume = lame * (strains[0] + strains[1] + strains[2])
    values = []
    for part in range(6):
        old = stress[6 * wave + part, x + LAYERS, pl.ds(ROWS, tile_y), :]
        if part < 3:
            values.append(old + (volume + 2.0 * shear * strains[part]))
        else:
            values.append(old + shear * strains[part])
    return strains, values


def gradient_kernel(links, width_y, *refs):
    count = len(links)
    received, stresses = refs[:count], refs[count : 2 * count]
    source_cell, source_amp, stress, scaled_lame, scaled_shear = refs[2 * count : 2 * count + 5]
    strain, gradient = refs[2 * count + 7 :]
    tile_x, tile_y, _ = scaled_lame.shape

    def add(wave, part, dim, index, term):
        target = face(strain, 6 * wave + part, dim, index, False)
        target[...] += term

    source = source_cell[0], source_amp[0]
    velocity_halo_terms(links, received, stresses, stress, source, width_y, add)

    def layer(x, carry):
        strains = [strain[part, x] for part in range(6)]
        _, values = new_stress(strain, stress, scaled_lame, scaled_shear, 1, x, tile_y)
        trace = strains[0] + strains[1] + strains[2]
        gradient[0, x] = -time_step * trace * (values[0] + values[1] + values[2])
        total = sum(left * right for left, right in zip(strains, values))
        gradient[1, x] = -time_step * total
        return carry

    lax.fori_loop(0, tile_x, layer, 0, unroll=4)


def output_kernel(
    chunk, width_y, source_cell, source_amp, strain, stress, scaled_lame, scaled_shear, *refs
):
    outputs, (values_now, sems) = refs[2:4], refs[4:]
    tile_x, tile_y, depth = scaled_lame.shape
    x_start, y_start = start_of(tile_x, tile_y)
    y = y_start + lax.broadcasted_iota(jnp.int32, (tile_y, depth), 0)
    level = lax.broadcasted_iota(jnp.int32, (tile_y, depth), 1)
    in_layer = y * depth + level - source_cell[0]
    copies = []
    for begin in range(0, tile_x, chunk):
        for wave in range(2):
            for x in range(begin, begin + chunk):
                _, values = new_stress(strain, stress, scaled_lame, scaled_shear, wave, x, tile_y)
                if wave == 0:
                    first = (x_start + x) * (width_y * depth)
                    added = jnp.where(in_layer == -first, source_amp[0], 0.0)
                    values[:3] = [value + added for value in values[:3]]
                for part in range(6):
                    values_now[6 * wave + part, x] = values[part]
            layers = pl.ds(begin, chunk)
            copy = pltpu.make_async_copy(
                values_now.at[pl.ds(6 * wave, 6), layers],
                outputs[wave].at[pl.ds(3, 6), layers],
                sems.at[len(copies)],
            )
            copy.start()
            copies.append(copy)
    for copy in copies:
        copy.wait()


def sum_kernel(mine, other, total, total_now, sems):
    copies = []
    for part in range(mine.shape[0]):
        total_now[part] = mine[part] + other[part]
        copy = pltpu.make_async_copy(total_now.at[part], total.at[part], sems.at[part])
        copy.start()
        copies.append(copy)
    for copy in copies:
        copy.wait()


def in_hbm(value):
    return pltpu.with_memory_space_constraint(value, pltpu.HBM)


def cost(flops, size):
    return pl.CostEstimate(flops=flops, bytes_accessed=size, transcendentals=0)


def body(
    forward_fields,
    adjoint_fields,
    lame_lambda,
    shear_modulus,
    density,
    source_cell,
    source_amp,
    receiver_cell,
    residual_amp,
):
    _, _, tile_x, tile_y, depth = forward_fields.shape
    forward = forward_fields.reshape(forward_fields.shape[1:])
    adjoint = adjoint_fields.reshape(adjoint_fields.shape[1:])
    sizes = {name: lax.axis_size(name) for name in ("tx", "ty")}
    width_y = tile_y * sizes["ty"]
    links_x, links_y = links_of(sizes)
    cells = tile_x * tile_y * depth

    def buffers(dim):
        return pltpu.VMEM((2, SLOTS, tile_y if dim == 0 else tile_x, depth), jnp.float32)

    def tile(*lead):
        return pltpu.VMEM((*lead, tile_x, tile_y, depth), jnp.float32)

    def padded(parts):
        return pltpu.VMEM(
            (parts, tile_x + 2 * LAYERS, tile_y + 2 * ROWS, depth), jnp.float32
        )

    def exchange(links, sends):
        return [swap(send, axis, first) for (axis, _, first), send in zip(links, sends)]

    def shapes(links):
        return [buffers(dim) for _, dim, _ in links]

    links = links_y + links_x
    count, count_x, count_y = len(links), len(links_x), len(links_y)
    rows = tile_x * tile_y + 3 * (tile_x + tile_y)
    source = source_cell, source_amp

    *sends, density_now = pl.pallas_call(
        functools.partial(early_pack_kernel, links_x),
        out_shape=shapes(links_x) + [tile()],
        in_specs=[hbm] * 3,
        out_specs=[vmem] * (count_x + 1),
        scratch_shapes=[pltpu.SemaphoreType.DMA((1 + 2 * SLOTS * count_x,))],
        compiler_params=params,
        cost_estimate=cost(0, 4 * cells),
        name="early_pack",
    )(*(in_hbm(x) for x in (forward, adjoint, density)))
    halos_x = exchange(links_x, sends)
    halos_y = []
    if links_y:
        sends = pl.pallas_call(
            functools.partial(pack_kernel, links_y),
            out_shape=shapes(links_y),
            in_specs=[vmem] * 3,
            out_specs=[vmem] * count_y,
            compiler_params=params,
            cost_estimate=cost(0, 2 * 2 * SLOTS * count_y * tile_x * depth * 4),
            name="pack",
        )(forward, adjoint, density_now)
        halos_y = exchange(links_y, sends)

    stress, velocity, accel, rim_added, buoyancy, scaled_lame, scaled_shear = pl.pallas_call(
        functools.partial(velocity_kernel, width_y),
        out_shape=[
            padded(12),
            padded(6),
            tile(3),
            pltpu.VMEM((2, 3, max(tile_x, tile_y), depth), jnp.float32),
            tile(),
            tile(),
            tile(),
        ],
        in_specs=[hbm] * 2 + [vmem] * 5,
        out_specs=[vmem] * 7,
        scratch_shapes=[
            pltpu.VMEM((rows, depth), jnp.float32),
            tile(6),
            tile(),
            tile(),
            pltpu.SemaphoreType.DMA((2,)),
        ],
        compiler_params=params,
        cost_estimate=cost(200 * cells, 18 * 4 * cells),
        name="velocity",
    )(
        in_hbm(lame_lambda),
        in_hbm(shear_modulus),
        receiver_cell,
        residual_amp,
        forward,
        adjoint,
        density_now,
    )

    def boundary(links, send_links, halos, velocity, name):
        velocity, *sends = pl.pallas_call(
            functools.partial(boundary_kernel, links, send_links),
            out_shape=[padded(6)] + shapes(send_links),
            in_specs=[vmem] * (len(links) + 3),
            out_specs=[vmem] * (1 + len(send_links)),
            input_output_aliases={len(links) + 2: 0},
            compiler_params=params,
            cost_estimate=cost(cells, 10 * 2 * tile_x * depth * 4),
            name=name,
        )(*halos, rim_added, buoyancy, velocity)
        return velocity, exchange(send_links, sends)

    later_y = links_y[::-1]
    velocity, velocity_halos_y = boundary(links_x, later_y, halos_x, velocity, "boundary_x")
    velocity, velocity_halos_x = boundary(links_y, links_x, halos_y, velocity, "boundary_y")
    halos = halos_y + halos_x
    later_links = later_y + links_x
    later_halos = halos_y[::-1] + halos_x
    velocity_halos = velocity_halos_y + velocity_halos_x

    out_shape = jax.ShapeDtypeStruct(forward.shape, jnp.float32)
    strain, gradient, _, forward_next, adjoint_next = pl.pallas_call(
        functools.partial(strain_kernel, links, width_y),
        out_shape=[tile(12), tile(3), padded(6), out_shape, out_shape],
        in_specs=[vmem] * count + [smem] * 2 + [vmem] * 4,
        out_specs=[vmem] * 3 + [hbm] * 2,
        input_output_aliases={count + 5: 2},
        scratch_shapes=[tile(3), pltpu.SemaphoreType.DMA((6,))],
        compiler_params=params,
        cost_estimate=cost(200 * cells, 18 * 4 * cells),
        name="strain",
    )(*halos, *source, rim_added, buoyancy, accel, velocity)

    strain, gradient = pl.pallas_call(
        functools.partial(gradient_kernel, later_links, width_y),
        out_shape=[tile(12), tile(3)],
        in_specs=[vmem] * (2 * count) + [smem] * 2 + [vmem] * 5,
        out_specs=[vmem] * 2,
        input_output_aliases={2 * count + 5: 0, 2 * count + 6: 1},
        compiler_params=params,
        cost_estimate=cost(30 * cells, 2 * 4 * cells),
        name="gradient",
    )(*velocity_halos, *later_halos, *source, stress, scaled_lame, scaled_shear, strain, gradient)
    other = lax.ppermute(gradient, "shot", [(0, 1), (1, 0)])

    chunk = 4 if tile_x % 4 == 0 else 1
    forward_next, adjoint_next = pl.pallas_call(
        functools.partial(output_kernel, chunk, width_y),
        out_shape=[out_shape, out_shape],
        in_specs=[smem] * 2 + [vmem] * 4 + [hbm] * 2,
        out_specs=[hbm] * 2,
        input_output_aliases={6: 0, 7: 1},
        scratch_shapes=[tile(12), pltpu.SemaphoreType.DMA((2 * tile_x // chunk,))],
        compiler_params=params,
        cost_estimate=cost(60 * cells, 18 * 4 * cells),
        name="outputs",
    )(*source, strain, stress, scaled_lame, scaled_shear, forward_next, adjoint_next)
    total = pl.pallas_call(
        sum_kernel,
        out_shape=jax.ShapeDtypeStruct((3, tile_x, tile_y, depth), jnp.float32),
        in_specs=[vmem] * 2,
        out_specs=hbm,
        scratch_shapes=[tile(3), pltpu.SemaphoreType.DMA((3,))],
        compiler_params=params,
        cost_estimate=cost(3 * cells, 9 * 4 * cells),
        name="sum",
    )(gradient, other)
    return forward_next[None], adjoint_next[None], total


def solution(mesh):
    return jax.shard_map(
        body,
        mesh=mesh,
        in_specs=(
            P("shot", None, "tx", "ty", None),
            P("shot", None, "tx", "ty", None),
            P("tx", "ty", None),
            P("tx", "ty", None),
            P("tx", "ty", None),
            P("shot"),
            P("shot"),
            P("shot", None),
            P("shot", None),
        ),
        out_specs=(
            P("shot", None, "tx", "ty", None),
            P("shot", None, "tx", "ty", None),
            P(None, "tx", "ty", None),
        ),
        check_vma=False,
    )
```

```python
import functools

import jax
import jax.numpy as jnp
from jax import lax
from jax.experimental import pallas as pl
from jax.experimental.pallas import tpu as pltpu
from jax.sharding import PartitionSpec as P

near = 9.0 / 8.0
far = -1.0 / 24.0
time_step = 0.15

LAYERS = 2
ROWS = 8
SLOTS = 5

STRESS_ALONG = ((0, 3, 4), (1, 3, 5))
ACCEL_OF = ((0, 1, 2), (1, 0, 2))
VELOCITY_ALONG = ((0, 1, 2), (1, 0, 2))
STRAIN_OF = ((0, 3, 4), (1, 3, 5))

vmem = pl.BlockSpec(memory_space=pltpu.VMEM)
smem = pl.BlockSpec(memory_space=pltpu.SMEM)
hbm = pl.BlockSpec(memory_space=pltpu.HBM)
params = pltpu.CompilerParams(vmem_limit_bytes=24 * 1024 * 1024)


def links_of(sizes):
    along_x = (("tx", 0, 1), ("tx", 0, 0))
    along_y = (("ty", 1, 1), ("ty", 1, 0))
    return [[link for link in order if link[2] + 1 < sizes[link[0]]] for order in (along_x, along_y)]


def swap(value, axis, first):
    pairs = [(i, i + 1) for i in range(first, lax.axis_size(axis) - 1, 2)]
    return lax.ppermute(value, axis, pairs + [(j, i) for i, j in pairs])


def is_lower(axis, first):
    return lax.axis_index(axis) % 2 == first


def has_peer(axis, first):
    index = lax.axis_index(axis)
    partner = jnp.where(is_lower(axis, first), index + 1, index - 1)
    return (partner >= 0) & (partner < lax.axis_size(axis))


def by_role(link, act, upper, lower):
    lower_here = is_lower(link[0], link[2])
    pl.when(lower_here)(lambda: act(lower, True))
    pl.when(jnp.logical_not(lower_here))(lambda: act(upper, False))


SPARE = SLOTS - 1


def stress_plan(dim):
    n, a, b = STRESS_ALONG[dim]
    return ((n, 0), (n, 1), (a, 0), (b, 0)), ((n, -1), (a, -2), (a, -1), (b, -2), (b, -1))


def velocity_plan(dim):
    n, a, b = VELOCITY_ALONG[dim]
    return ((n, 0), (a, 0), (a, 1), (b, 0), (b, 1)), ((n, -2), (n, -1), (a, -1), (b, -1))


def early_pack_kernel(links, forward, adjoint, density, *refs):
    sends, (density_now, sems) = refs[: len(links)], refs[len(links) :]
    tile_x = forward.shape[1]
    whole = pltpu.make_async_copy(density, density_now, sems.at[0])
    whole.start()
    waits = []
    for at, (link, send) in enumerate(zip(links, sends)):

        def sources(plan, lower, wave):
            fields = (forward, adjoint)[wave]
            found = [fields.at[3 + part, index % tile_x] for part, index in plan]
            return found if lower else found + [density.at[wave]]

        def start(plan, lower):
            for wave in range(2):
                for slot, source in enumerate(sources(plan, lower, wave)):
                    pltpu.make_async_copy(
                        source, send.at[wave, slot], sems.at[1 + (2 * at + wave) * SLOTS + slot]
                    ).start()

        by_role(link, start, *stress_plan(link[1]))
        for wave in range(2):
            for slot in range(SLOTS):
                waits.append(
                    pltpu.make_async_copy(
                        density.at[0],
                        send.at[wave, slot],
                        sems.at[1 + (2 * at + wave) * SLOTS + slot],
                    )
                )
    for copy in waits:
        copy.wait()
    whole.wait()


def pack_kernel(links, forward, adjoint, density, *sends):
    for link, send in zip(links, sends):
        dim = link[1]

        def put(plan, lower):
            for wave, fields in enumerate((forward, adjoint)):
                for slot, (part, index) in enumerate(plan):
                    send[wave, slot] = face(fields, 3 + part, dim, index, False)[...]
                if not lower:
                    send[wave, SPARE] = light_face(density, dim, wave)

        by_role(link, put, *stress_plan(dim))


def send_velocities(links, velocity, buoyancy, sends):
    for link, send in zip(links, sends):
        dim = link[1]

        def put(plan, lower):
            for wave in range(2):
                for slot, (part, index) in enumerate(plan):
                    send[wave, slot] = face(velocity, 3 * wave + part, dim, index, True)[...]
                if lower:
                    send[wave, SPARE] = light_face(buoyancy, dim, -1 - wave)

        by_role(link, put, *velocity_plan(dim))


def column_ids(tile_x, tile_y, width_y, lanes):
    x_start = lax.axis_index("tx") * tile_x
    y_start = lax.axis_index("ty") * tile_y

    def column(x, y):
        inside = (y >= 0) & (y < width_y)
        return jnp.where(inside, x * width_y + y, -1)

    def iota(shape, dim):
        return lax.broadcasted_iota(jnp.int32, shape, dim)

    shape = (tile_x, tile_y, lanes)
    tile = column(x_start + iota(shape, 0), y_start + iota(shape, 1))
    shape = (3, tile_y, lanes)
    layer = iota(shape, 0)
    along_x = column(
        x_start + jnp.where(layer == 0, -1, tile_x - 1 + layer), y_start + iota(shape, 1)
    )
    shape = (3, tile_x, lanes)
    layer = iota(shape, 0)
    along_y = column(
        x_start + iota(shape, 1), y_start + jnp.where(layer == 0, -1, tile_y - 1 + layer)
    )
    return jnp.concatenate([part.reshape(-1, lanes) for part in (tile, along_x, along_y)], axis=0)


def differ(zero, one, two, minus):
    return near * (one - zero) + far * (two - minus)


def along_x(ref, part, x, tile_y, upward):
    def at(offset):
        return ref[part, x + (LAYERS + offset), pl.ds(ROWS, tile_y), :]

    return differ(at(0), at(1), at(2), at(-1)) if upward else differ(at(-1), at(0), at(1), at(-2))


def along_y(ref, part, x, tile_y, upward):
    def at(offset):
        return ref[part, x + LAYERS, pl.ds(ROWS + offset, tile_y), :]

    return differ(at(0), at(1), at(2), at(-1)) if upward else differ(at(-1), at(0), at(1), at(-2))


def along_z(ref, part, x, tile_y, upward):
    value = ref[part, x + LAYERS, pl.ds(ROWS, tile_y), :]
    depth = value.shape[-1]
    lane = lax.broadcasted_iota(jnp.int32, value.shape, 1)

    def at(offset):
        if offset == 0:
            return value
        moved = pltpu.roll(value, (-offset) % depth, 1)
        inside = lane < depth - offset if offset > 0 else lane >= -offset
        return jnp.where(inside, moved, 0.0)

    return differ(at(0), at(1), at(2), at(-1)) if upward else differ(at(-1), at(0), at(1), at(-2))


def clear_rim(ref, parts_x, parts_y):
    _, layers, rows, depth = ref.shape
    tile_x, tile_y = layers - 2 * LAYERS, rows - 2 * ROWS
    for part in parts_x:
        for begin in (0, LAYERS + tile_x):
            ref[part, pl.ds(begin, LAYERS), pl.ds(ROWS, tile_y), :] = jnp.zeros(
                (LAYERS, tile_y, depth), jnp.float32
            )
    for part in parts_y:
        for begin in (0, ROWS + tile_y):
            ref[part, pl.ds(LAYERS, tile_x), pl.ds(begin, ROWS), :] = jnp.zeros(
                (tile_x, ROWS, depth), jnp.float32
            )


def receiver_sum(cells, amps, columns):
    depth, receivers = columns.shape[-1], cells.shape[-1]
    column = lax.div(cells, depth)
    level = cells - column * depth
    column_hot = jnp.concatenate(
        [
            (columns == column[:, begin : begin + depth]).astype(jnp.bfloat16)
            for begin in range(0, receivers, depth)
        ],
        axis=1,
    )
    levels = lax.broadcasted_iota(jnp.int32, (depth, receivers), 0)
    rest = jnp.where(levels == level, amps, 0.0)
    total = jnp.zeros(columns.shape, jnp.float32)
    for _ in range(3):
        part = rest.astype(jnp.bfloat16)
        rest = rest - part.astype(jnp.float32)
        total = total + lax.dot_general(
            column_hot,
            part,
            (((1,), (1,)), ((), ())),
            preferred_element_type=jnp.float32,
        )
    return total


def velocity_kernel(
    width_y,
    lame,
    shear,
    receiver_cell,
    residual_amp,
    forward,
    adjoint,
    density,
    stress,
    velocity,
    accel,
    rim_added,
    buoyancy,
    scaled_lame,
    scaled_shear,
    received,
    gained,
    lame_now,
    shear_now,
    sems,
):
    tile_x, tile_y, depth = density.shape
    copies = [
        pltpu.make_async_copy(lame, lame_now, sems.at[0]),
        pltpu.make_async_copy(shear, shear_now, sems.at[1]),
    ]
    for copy in copies:
        copy.start()
    cells = tile_x * tile_y
    middle = pl.ds(ROWS, tile_y)
    columns = column_ids(tile_x, tile_y, width_y, depth)
    received[...] = receiver_sum(receiver_cell[...], residual_amp[...], columns)
    for layer in range(3):
        rim_added[0, layer] = received[pl.ds(cells + layer * tile_y, tile_y), :]
        rim_added[1, layer] = received[pl.ds(cells + 3 * tile_y + layer * tile_x, tile_x), :]
    for wave in range(2):
        clear_rim(
            stress, *([6 * wave + part for part in STRESS_ALONG[dim]] for dim in range(2))
        )

    def fill(x, carry):
        extra = received[pl.ds(pl.multiple_of(x * tile_y, 8), tile_y), :]
        for wave, fields in enumerate((forward, adjoint)):
            for part in range(6):
                value = fields[3 + part, x]
                stress[6 * wave + part, x + LAYERS, middle, :] = (
                    value + extra if wave == 1 and part < 3 else value
                )
        return carry

    lax.fori_loop(0, tile_x, fill, 0, unroll=4)

    def layer(x, carry):
        for wave in range(2):
            xx, yy, zz, xy, xz, yz = range(6 * wave, 6 * wave + 6)
            values = (
                along_x(stress, xx, x, tile_y, True)
                + along_y(stress, xy, x, tile_y, False)
                + along_z(stress, xz, x, tile_y, False),
                along_x(stress, xy, x, tile_y, False)
                + along_y(stress, yy, x, tile_y, True)
                + along_z(stress, yz, x, tile_y, False),
                along_x(stress, xz, x, tile_y, False)
                + along_y(stress, yz, x, tile_y, False)
                + along_z(stress, zz, x, tile_y, True),
            )
            for part, value in enumerate(values):
                gained[3 * wave + part, x] = value
        return carry

    lax.fori_loop(0, tile_x, layer, 0, unroll=4)
    for copy in copies:
        copy.wait()

    def finish(x, carry):
        light = 1.0 / density[x]
        buoyancy[x] = light
        scaled_lame[x] = time_step * lame_now[x]
        scaled_shear[x] = time_step * shear_now[x]
        for wave, fields in enumerate((forward, adjoint)):
            for part in range(3):
                value = light * gained[3 * wave + part, x]
                if wave == 0:
                    accel[part, x] = value
                velocity[3 * wave + part, x + LAYERS, middle, :] = (
                    fields[part, x] + time_step * value
                )
        return carry

    lax.fori_loop(0, tile_x, finish, 0, unroll=4)


def stress_halo_terms(links, received, rim_added, waves, add):
    for link, halo in zip(links, received):
        dim = link[1]
        part_n, part_a, part_b = ACCEL_OF[dim]

        def normal(wave, slot, layer):
            value = halo[wave, slot]
            return value + rim_added[dim, layer] if wave == 1 else value

        def after():
            for wave in waves:
                n0, n1 = normal(wave, 0, 1), normal(wave, 1, 2)
                add(wave, part_n, dim, -1, near * n0 + far * n1)
                add(wave, part_n, dim, -2, far * n0)
                add(wave, part_a, dim, -1, far * halo[wave, 2])
                add(wave, part_b, dim, -1, far * halo[wave, 3])

        def before():
            for wave in waves:
                add(wave, part_n, dim, 0, -far * normal(wave, 0, 0))
                for part, slot in ((part_a, 1), (part_b, 3)):
                    outer, inner = halo[wave, slot], halo[wave, slot + 1]
                    add(wave, part, dim, 0, -near * inner - far * outer)
                    add(wave, part, dim, 1, -far * inner)

        real = has_peer(link[0], link[2])
        lower = is_lower(link[0], link[2])
        pl.when(real & lower)(after)
        pl.when(real & jnp.logical_not(lower))(before)


def source_gain(cell, part, x, y, z, width_y):
    depth = z.shape[-1]
    column = lax.div(cell, depth)
    source_x = lax.div(column, width_y)
    away = [source_x - x, column - source_x * width_y - y, cell - column * depth - z]
    along = away.pop(part)
    gain = jnp.where(along == 0, -near, 0.0)
    for offset, value in ((1, near), (2, far), (-1, -far)):
        gain = jnp.where(along == offset, value, gain)
    return jnp.where((away[0] == 0) & (away[1] == 0), gain, 0.0)


def start_of(tile_x, tile_y):
    return lax.axis_index("tx") * tile_x, lax.axis_index("ty") * tile_y


def missing_terms(links, stress, source, width_y, missing):
    cell, amp = source
    layers, rows, depth = stress.shape[1:]
    tile = layers - 2 * LAYERS, rows - 2 * ROWS
    starts = start_of(*tile)
    for link, out in zip(links, missing):
        dim = link[1]
        shape = out.shape[2:]
        cross = starts[1 - dim] + lax.broadcasted_iota(jnp.int32, shape, 0)
        level = lax.broadcasted_iota(jnp.int32, shape, 1)

        def own(wave, part, index):
            return face(stress, 6 * wave + STRESS_ALONG[dim][part], dim, index, True)[...]

        def put(slots):
            for wave in range(2):
                for slot, (part, layer, terms) in enumerate(slots):
                    value = terms(wave) if dim == 1 else jnp.zeros(shape, jnp.float32)
                    if wave == 0:
                        here = jnp.full(shape, starts[dim] + layer, jnp.int32)
                        x, y = (here, cross) if dim == 0 else (cross, here)
                        value += amp * source_gain(
                            cell, VELOCITY_ALONG[dim][part], x, y, level, width_y
                        )
                    out[wave, slot] = value

        def after():
            count = tile[dim]
            slots = [(0, count, lambda wave: -far * own(wave, 0, -1))]
            for part in (1, 2):
                slots += [
                    (
                        part,
                        count,
                        lambda wave, part=part: -near * own(wave, part, -1)
                        - far * own(wave, part, -2),
                    ),
                    (part, count + 1, lambda wave, part=part: -far * own(wave, part, -1)),
                ]
            put(slots)

        def before():
            put([
                (0, -2, lambda wave: far * own(wave, 0, 0)),
                (0, -1, lambda wave: near * own(wave, 0, 0) + far * own(wave, 0, 1)),
                (1, -1, lambda wave: far * own(wave, 1, 0)),
                (2, -1, lambda wave: far * own(wave, 2, 0)),
            ])

        lower = is_lower(link[0], link[2])
        pl.when(lower)(after)
        pl.when(jnp.logical_not(lower))(before)


def velocity_halo_terms(links, received, stresses, missing, add):
    for link, halo, stress_halo, lack in zip(links, received, stresses, missing):
        dim = link[1]
        part_n, part_a, part_b = STRAIN_OF[dim]

        def after():
            lights = [time_step / stress_halo[layer, SPARE] for layer in range(2)]
            for wave in range(2):

                def whole(slot, layer):
                    return halo[wave, slot] + lights[layer] * lack[wave, slot]

                add(wave, part_n, dim, -1, far * whole(0, 0))
                for part, slot in ((part_a, 1), (part_b, 3)):
                    inner, outer = whole(slot, 0), whole(slot + 1, 1)
                    add(wave, part, dim, -1, near * inner + far * outer)
                    add(wave, part, dim, -2, far * inner)

        def before():
            lights = [time_step * halo[layer, SPARE] for layer in range(2)]
            for wave in range(2):

                def whole(slot, layer):
                    return halo[wave, slot] + lights[layer] * lack[wave, slot]

                outer, inner = whole(0, 1), whole(1, 0)
                add(wave, part_n, dim, 0, -near * inner - far * outer)
                add(wave, part_n, dim, 1, -far * inner)
                add(wave, part_a, dim, 0, -far * whole(2, 0))
                add(wave, part_b, dim, 0, -far * whole(3, 0))

        real = has_peer(link[0], link[2])
        lower = is_lower(link[0], link[2])
        pl.when(real & lower)(after)
        pl.when(real & jnp.logical_not(lower))(before)


def face(ref, part, dim, index, padded):
    layers, rows, depth = ref.shape[1:]
    tile_x = layers - 2 * LAYERS if padded else layers
    tile_y = rows - 2 * ROWS if padded else rows
    if dim == 0:
        at = index % tile_x
        if padded:
            return ref.at[part, at + LAYERS, pl.ds(ROWS, tile_y), :]
        return ref.at[part, at]
    at = index % tile_y
    flat = ref.reshape(ref.shape[0], layers * rows, depth)
    begin = LAYERS * rows + ROWS + at if padded else at
    return flat.at[part, pl.ds(begin, tile_x, stride=rows), :]


def light_face(buoyancy, dim, index):
    layers, rows, depth = buoyancy.shape
    if dim == 0:
        return buoyancy[index % layers]
    return buoyancy.reshape(layers * rows, depth)[pl.ds(index % rows, layers, stride=rows), :]


def boundary_kernel(links, send_links, *refs):
    count = len(links)
    received = refs[:count]
    rim_added, buoyancy, _, velocity = refs[count : count + 4]
    sends = refs[count + 4 :]

    def add(wave, part, dim, index, term):
        target = face(velocity, 3 * wave + part, dim, index, True)
        target[...] += time_step * light_face(buoyancy, dim, index) * term

    stress_halo_terms(links, received, rim_added, (0, 1), add)
    send_velocities(send_links, velocity, buoyancy, sends)


def strain_kernel(links, width_y, *refs):
    count = len(links)
    received = refs[:count]
    source_cell, source_amp, rim_added, buoyancy, accel = refs[count : count + 5]
    stress = refs[count + 6]
    strain, low_part, high_part, velocity = refs[count + 7 : count + 11]
    outputs, missing = refs[count + 11 : count + 13], refs[count + 13 : 2 * count + 13]
    accel_now, sems = refs[2 * count + 13 :]
    tile_x, tile_y, depth = buoyancy.shape
    middle = pl.ds(ROWS, tile_y)
    clear_rim(velocity, range(6), range(6))
    accel_now[...] = accel[...]

    def add(wave, part, dim, index, term):
        target = face(accel_now, part, dim, index, False)
        target[...] += light_face(buoyancy, dim, index) * term

    stress_halo_terms(links, received, rim_added, (0,), add)
    x_start, y_start = start_of(tile_x, tile_y)
    cell, amp = source_cell[0], source_amp[0]
    source_x = lax.div(cell, width_y * depth)
    y = y_start + lax.broadcasted_iota(jnp.int32, (tile_y, depth), 0)
    level = lax.broadcasted_iota(jnp.int32, (tile_y, depth), 1)
    for offset in (-2, -1, 0, 1):
        x = source_x + offset - x_start

        @pl.when((x >= 0) & (x < tile_x))
        def add_source():
            here = jnp.full((tile_y, depth), source_x + offset, jnp.int32)
            for part in range(3):
                gain = source_gain(cell, part, here, y, level, width_y)
                value = amp * buoyancy[x] * gain
                accel_now[part, x] += value
                velocity[part, x + LAYERS, middle, :] += time_step * value

    copies = [
        pltpu.make_async_copy(
            velocity.at[3 * wave + part, pl.ds(LAYERS, tile_x), middle, :],
            outputs[wave].at[part],
            sems.at[3 * wave + part],
        )
        for wave in range(2)
        for part in range(3)
    ]
    for copy in copies:
        copy.start()
    def layer(begin, half, x, carry):
        for wave in range(2):
            vx, vy, vz = range(3 * wave, 3 * wave + 3)
            values = (
                along_x(velocity, vx, x, tile_y, False),
                along_y(velocity, vy, x, tile_y, False),
                along_z(velocity, vz, x, tile_y, False),
                along_y(velocity, vx, x, tile_y, True) + along_x(velocity, vy, x, tile_y, True),
                along_z(velocity, vx, x, tile_y, True) + along_x(velocity, vz, x, tile_y, True),
                along_z(velocity, vy, x, tile_y, True) + along_y(velocity, vz, x, tile_y, True),
            )
            for part, value in enumerate(values):
                strain[6 * wave + part, x] = value
        total = sum(
            accel_now[part, x] * velocity[3 + part, x + LAYERS, middle, :] for part in range(3)
        )
        half[x - begin] = -time_step * total
        return carry

    for begin, half in ((0, low_part), (tile_x // 2, high_part)):
        lax.fori_loop(
            begin,
            begin + half.shape[0],
            functools.partial(layer, begin, half),
            0,
            unroll=4,
        )
    missing_terms(links, stress, (cell, amp), width_y, missing)
    for copy in copies:
        copy.wait()


def new_stress(strain, stress, scaled_lame, scaled_shear, wave, x, tile_y):
    lame, shear = scaled_lame[x], scaled_shear[x]
    strains = [strain[6 * wave + part, x] for part in range(6)]
    volume = lame * (strains[0] + strains[1] + strains[2])
    values = []
    for part in range(6):
        old = stress[6 * wave + part, x + LAYERS, pl.ds(ROWS, tile_y), :]
        if part < 3:
            values.append(old + (volume + 2.0 * shear * strains[part]))
        else:
            values.append(old + shear * strains[part])
    return strains, values


def gradient_kernel(links, *refs):
    count = len(links)
    received, stresses, missing = (refs[at : at + count] for at in range(0, 3 * count, count))
    stress, scaled_lame, scaled_shear, *halves, _ = refs[3 * count : 3 * count + 8]
    strain, gradient, density_total = refs[3 * count + 8 :]
    tile_x, tile_y, _ = scaled_lame.shape
    for at, (mine, other) in enumerate(zip(halves[:2], halves[2:])):
        density_total[pl.ds(at * (tile_x // 2), mine.shape[0])] = mine[...] + other[...]

    def add(wave, part, dim, index, term):
        target = face(strain, 6 * wave + part, dim, index, False)
        target[...] += term

    velocity_halo_terms(links, received, stresses, missing, add)

    def layer(x, carry):
        strains = [strain[part, x] for part in range(6)]
        _, values = new_stress(strain, stress, scaled_lame, scaled_shear, 1, x, tile_y)
        trace = strains[0] + strains[1] + strains[2]
        gradient[0, x] = -time_step * trace * (values[0] + values[1] + values[2])
        total = sum(left * right for left, right in zip(strains, values))
        gradient[1, x] = -time_step * total
        return carry

    lax.fori_loop(0, tile_x, layer, 0, unroll=4)


def output_kernel(
    chunk,
    width_y,
    source_cell,
    source_amp,
    strain,
    stress,
    scaled_lame,
    scaled_shear,
    density_total,
    *refs,
):
    outputs, total = refs[2:4], refs[4]
    values_now, sems = refs[5:]
    tile_x, tile_y, depth = scaled_lame.shape
    x_start, y_start = start_of(tile_x, tile_y)
    y = y_start + lax.broadcasted_iota(jnp.int32, (tile_y, depth), 0)
    level = lax.broadcasted_iota(jnp.int32, (tile_y, depth), 1)
    in_layer = y * depth + level - source_cell[0]
    copies = [pltpu.make_async_copy(density_total, total.at[2], sems.at[0])]
    copies[0].start()
    for begin in range(0, tile_x, chunk):
        for wave in range(2):
            for x in range(begin, begin + chunk):
                _, values = new_stress(strain, stress, scaled_lame, scaled_shear, wave, x, tile_y)
                if wave == 0:
                    first = (x_start + x) * (width_y * depth)
                    added = jnp.where(in_layer == -first, source_amp[0], 0.0)
                    values[:3] = [value + added for value in values[:3]]
                for part in range(6):
                    values_now[6 * wave + part, x] = values[part]
            layers = pl.ds(begin, chunk)
            copy = pltpu.make_async_copy(
                values_now.at[pl.ds(6 * wave, 6), layers],
                outputs[wave].at[pl.ds(3, 6), layers],
                sems.at[len(copies)],
            )
            copy.start()
            copies.append(copy)
    for copy in copies:
        copy.wait()


def sum_kernel(mine, other, _, total, total_now, sems):
    copies = []
    for part in range(mine.shape[0]):
        total_now[part] = mine[part] + other[part]
        copy = pltpu.make_async_copy(total_now.at[part], total.at[part], sems.at[part])
        copy.start()
        copies.append(copy)
    for copy in copies:
        copy.wait()


def in_hbm(value):
    return pltpu.with_memory_space_constraint(value, pltpu.HBM)


def cost(flops, size):
    return pl.CostEstimate(flops=flops, bytes_accessed=size, transcendentals=0)


def body(
    forward_fields,
    adjoint_fields,
    lame_lambda,
    shear_modulus,
    density,
    source_cell,
    source_amp,
    receiver_cell,
    residual_amp,
):
    _, _, tile_x, tile_y, depth = forward_fields.shape
    forward = forward_fields.reshape(forward_fields.shape[1:])
    adjoint = adjoint_fields.reshape(adjoint_fields.shape[1:])
    sizes = {name: lax.axis_size(name) for name in ("tx", "ty")}
    width_y = tile_y * sizes["ty"]
    links_x, links_y = links_of(sizes)
    cells = tile_x * tile_y * depth

    def buffers(dim):
        return pltpu.VMEM((2, SLOTS, tile_y if dim == 0 else tile_x, depth), jnp.float32)

    def tile(*lead):
        return pltpu.VMEM((*lead, tile_x, tile_y, depth), jnp.float32)

    def padded(parts):
        return pltpu.VMEM(
            (parts, tile_x + 2 * LAYERS, tile_y + 2 * ROWS, depth), jnp.float32
        )

    def exchange(links, sends):
        return [swap(send, axis, first) for (axis, _, first), send in zip(links, sends)]

    def shapes(links):
        return [buffers(dim) for _, dim, _ in links]

    links = links_y + links_x
    count, count_x, count_y = len(links), len(links_x), len(links_y)
    rows = tile_x * tile_y + 3 * (tile_x + tile_y)
    source = source_cell, source_amp

    *sends, density_now = pl.pallas_call(
        functools.partial(early_pack_kernel, links_x),
        out_shape=shapes(links_x) + [tile()],
        in_specs=[hbm] * 3,
        out_specs=[vmem] * (count_x + 1),
        scratch_shapes=[pltpu.SemaphoreType.DMA((1 + 2 * SLOTS * count_x,))],
        compiler_params=params,
        cost_estimate=cost(0, 4 * cells),
        name="early_pack",
    )(*(in_hbm(x) for x in (forward, adjoint, density)))
    halos_x = exchange(links_x, sends)
    halos_y = []
    if links_y:
        sends = pl.pallas_call(
            functools.partial(pack_kernel, links_y),
            out_shape=shapes(links_y),
            in_specs=[vmem] * 3,
            out_specs=[vmem] * count_y,
            compiler_params=params,
            cost_estimate=cost(0, 2 * 2 * SLOTS * count_y * tile_x * depth * 4),
            name="pack",
        )(forward, adjoint, density_now)
        halos_y = exchange(links_y, sends)

    stress, velocity, accel, rim_added, buoyancy, scaled_lame, scaled_shear = pl.pallas_call(
        functools.partial(velocity_kernel, width_y),
        out_shape=[
            padded(12),
            padded(6),
            tile(3),
            pltpu.VMEM((2, 3, max(tile_x, tile_y), depth), jnp.float32),
            tile(),
            tile(),
            tile(),
        ],
        in_specs=[hbm] * 2 + [vmem] * 5,
        out_specs=[vmem] * 7,
        scratch_shapes=[
            pltpu.VMEM((rows, depth), jnp.float32),
            tile(6),
            tile(),
            tile(),
            pltpu.SemaphoreType.DMA((2,)),
        ],
        compiler_params=params,
        cost_estimate=cost(200 * cells, 18 * 4 * cells),
        name="velocity",
    )(
        in_hbm(lame_lambda),
        in_hbm(shear_modulus),
        receiver_cell,
        residual_amp,
        forward,
        adjoint,
        density_now,
    )

    def boundary(links, send_links, halos, velocity, name):
        velocity, *sends = pl.pallas_call(
            functools.partial(boundary_kernel, links, send_links),
            out_shape=[padded(6)] + shapes(send_links),
            in_specs=[vmem] * (len(links) + 3),
            out_specs=[vmem] * (1 + len(send_links)),
            input_output_aliases={len(links) + 2: 0},
            compiler_params=params,
            cost_estimate=cost(cells, 10 * 2 * tile_x * depth * 4),
            name=name,
        )(*halos, rim_added, buoyancy, velocity)
        return velocity, exchange(send_links, sends)

    later_y = links_y[::-1]
    velocity, velocity_halos_y = boundary(links_x, later_y, halos_x, velocity, "boundary_x")
    velocity, velocity_halos_x = boundary(links_y, links_x, halos_y, velocity, "boundary_y")
    halos = halos_y + halos_x
    later_links = later_y + links_x
    later_halos = halos_y[::-1] + halos_x
    velocity_halos = velocity_halos_y + velocity_halos_x

    out_shape = jax.ShapeDtypeStruct(forward.shape, jnp.float32)
    halves = [
        pltpu.VMEM((size, tile_y, depth), jnp.float32) for size in (tile_x // 2, -(-tile_x // 2))
    ]
    strain, low_part, high_part, _, forward_next, adjoint_next, *missing = pl.pallas_call(
        functools.partial(strain_kernel, links, width_y),
        out_shape=[tile(12), *halves, padded(6), out_shape, out_shape] + shapes(links),
        in_specs=[vmem] * count + [smem] * 2 + [vmem] * 5,
        out_specs=[vmem] * 4 + [hbm] * 2 + [vmem] * count,
        input_output_aliases={count + 5: 3},
        scratch_shapes=[tile(3), pltpu.SemaphoreType.DMA((6,))],
        compiler_params=params,
        cost_estimate=cost(200 * cells, 18 * 4 * cells),
        name="strain",
    )(*halos, *source, rim_added, buoyancy, accel, velocity, stress)
    pair = [(0, 1), (1, 0)]
    density_parts = low_part, high_part
    other_parts = [lax.ppermute(part, "shot", pair) for part in density_parts]

    missing = missing[:count_y][::-1] + missing[count_y:]
    strain, gradient, density_total = pl.pallas_call(
        functools.partial(gradient_kernel, later_links),
        out_shape=[tile(12), tile(2), tile()],
        in_specs=[vmem] * (3 * count + 8),
        out_specs=[vmem] * 3,
        input_output_aliases={3 * count + 7: 0},
        compiler_params=params,
        cost_estimate=cost(30 * cells, 2 * 4 * cells),
        name="gradient",
    )(
        *velocity_halos,
        *later_halos,
        *missing,
        stress,
        scaled_lame,
        scaled_shear,
        *density_parts,
        *other_parts,
        strain,
    )
    other = lax.ppermute(gradient, "shot", pair)

    chunk = 4 if tile_x % 4 == 0 else 1
    total_shape = jax.ShapeDtypeStruct((3, tile_x, tile_y, depth), jnp.float32)
    forward_next, adjoint_next, total = pl.pallas_call(
        functools.partial(output_kernel, chunk, width_y),
        out_shape=[out_shape, out_shape, total_shape],
        in_specs=[smem] * 2 + [vmem] * 5 + [hbm] * 2,
        out_specs=[hbm] * 3,
        input_output_aliases={7: 0, 8: 1},
        scratch_shapes=[tile(12), pltpu.SemaphoreType.DMA((1 + 2 * tile_x // chunk,))],
        compiler_params=params,
        cost_estimate=cost(60 * cells, 18 * 4 * cells),
        name="outputs",
    )(
        *source,
        strain,
        stress,
        scaled_lame,
        scaled_shear,
        density_total,
        forward_next,
        adjoint_next,
    )
    total = pl.pallas_call(
        sum_kernel,
        out_shape=total_shape,
        in_specs=[vmem] * 2 + [hbm],
        out_specs=hbm,
        input_output_aliases={2: 0},
        scratch_shapes=[tile(2), pltpu.SemaphoreType.DMA((2,))],
        compiler_params=params,
        cost_estimate=cost(2 * cells, 6 * 4 * cells),
        name="sum",
    )(gradient, other, total)
    return forward_next[None], adjoint_next[None], total


def solution(mesh):
    return jax.shard_map(
        body,
        mesh=mesh,
        in_specs=(
            P("shot", None, "tx", "ty", None),
            P("shot", None, "tx", "ty", None),
            P("tx", "ty", None),
            P("tx", "ty", None),
            P("tx", "ty", None),
            P("shot"),
            P("shot"),
            P("shot", None),
            P("shot", None),
        ),
        out_specs=(
            P("shot", None, "tx", "ty", None),
            P("shot", None, "tx", "ty", None),
            P(None, "tx", "ty", None),
        ),
        check_vma=False,
    )
```

```python
import functools

import jax
import jax.numpy as jnp
from jax import lax
from jax.experimental import pallas as pl
from jax.experimental.pallas import tpu as pltpu
from jax.sharding import PartitionSpec as P

near = 9.0 / 8.0
far = -1.0 / 24.0
time_step = 0.15

LAYERS = 2
ROWS = 8
SLOTS = 5

STRESS_ALONG = ((0, 3, 4), (1, 3, 5))
ACCEL_OF = ((0, 1, 2), (1, 0, 2))
VELOCITY_ALONG = ((0, 1, 2), (1, 0, 2))
STRAIN_OF = ((0, 3, 4), (1, 3, 5))

vmem = pl.BlockSpec(memory_space=pltpu.VMEM)
smem = pl.BlockSpec(memory_space=pltpu.SMEM)
hbm = pl.BlockSpec(memory_space=pltpu.HBM)
params = pltpu.CompilerParams(vmem_limit_bytes=24 * 1024 * 1024)


def links_of(sizes):
    along_x = (("tx", 0, 1), ("tx", 0, 0))
    along_y = (("ty", 1, 1), ("ty", 1, 0))
    return [[link for link in order if link[2] + 1 < sizes[link[0]]] for order in (along_x, along_y)]


def swap(value, axis, first):
    pairs = [(i, i + 1) for i in range(first, lax.axis_size(axis) - 1, 2)]
    return lax.ppermute(value, axis, pairs + [(j, i) for i, j in pairs])


def is_lower(axis, first):
    return lax.axis_index(axis) % 2 == first


def has_peer(axis, first):
    index = lax.axis_index(axis)
    partner = jnp.where(is_lower(axis, first), index + 1, index - 1)
    return (partner >= 0) & (partner < lax.axis_size(axis))


def by_role(link, act, upper, lower):
    lower_here = is_lower(link[0], link[2])
    pl.when(lower_here)(lambda: act(lower, True))
    pl.when(jnp.logical_not(lower_here))(lambda: act(upper, False))


SPARE = SLOTS - 1


def stress_plan(dim):
    n, a, b = STRESS_ALONG[dim]
    return ((n, 0), (n, 1), (a, 0), (b, 0)), ((n, -1), (a, -2), (a, -1), (b, -2), (b, -1))


def velocity_plan(dim):
    n, a, b = VELOCITY_ALONG[dim]
    return ((n, 0), (a, 0), (a, 1), (b, 0), (b, 1)), ((n, -2), (n, -1), (a, -1), (b, -1))


def early_pack_kernel(links, forward, adjoint, density, *refs):
    sends, (density_rows, sems) = refs[: len(links)], refs[len(links) :]
    tile = forward.shape[1:3]
    waits = []
    for row in range(2):
        copy = pltpu.make_async_copy(
            density.at[:, row, :], density_rows.at[row], sems.at[2 * SLOTS * len(links) + row]
        )
        copy.start()
        waits.append(copy)

    def layer(ref, dim, index):
        return ref.at[index] if dim == 0 else ref.at[:, index, :]

    for at, (link, send) in enumerate(zip(links, sends)):
        dim = link[1]

        def semaphore(wave, slot):
            return sems.at[(2 * at + wave) * SLOTS + slot]

        def start(plan, lower):
            for wave, fields in enumerate((forward, adjoint)):
                sources = [
                    layer(fields.at[3 + part], dim, index % tile[dim]) for part, index in plan
                ]
                if not lower:
                    sources.append(layer(density, dim, wave))
                for slot, source in enumerate(sources):
                    pltpu.make_async_copy(
                        source, send.at[wave, slot], semaphore(wave, slot)
                    ).start()

        by_role(link, start, *stress_plan(dim))
        for wave in range(2):
            for slot in range(SLOTS):
                waits.append(
                    pltpu.make_async_copy(
                        layer(density, dim, 0), send.at[wave, slot], semaphore(wave, slot)
                    )
                )
    for copy in waits:
        copy.wait()


def pack_kernel(links, forward, adjoint, density_rows, *sends):
    for link, send in zip(links, sends):
        dim = link[1]

        def put(plan, lower):
            for wave, fields in enumerate((forward, adjoint)):
                for slot, (part, index) in enumerate(plan):
                    send[wave, slot] = face(fields, 3 + part, dim, index, False)[...]
                if not lower:
                    send[wave, SPARE] = density_rows[wave]

        by_role(link, put, *stress_plan(dim))


def send_velocities(links, velocity, buoyancy, sends):
    for link, send in zip(links, sends):
        dim = link[1]

        def put(plan, lower):
            for wave in range(2):
                for slot, (part, index) in enumerate(plan):
                    send[wave, slot] = face(velocity, 3 * wave + part, dim, index, True)[...]
                if lower:
                    send[wave, SPARE] = light_face(buoyancy, dim, -1 - wave)

        by_role(link, put, *velocity_plan(dim))


def column_ids(tile_x, tile_y, width_y, lanes):
    x_start = lax.axis_index("tx") * tile_x
    y_start = lax.axis_index("ty") * tile_y

    def column(x, y):
        inside = (y >= 0) & (y < width_y)
        return jnp.where(inside, x * width_y + y, -1)

    def iota(shape, dim):
        return lax.broadcasted_iota(jnp.int32, shape, dim)

    shape = (tile_x, tile_y, lanes)
    tile = column(x_start + iota(shape, 0), y_start + iota(shape, 1))
    shape = (3, tile_y, lanes)
    layer = iota(shape, 0)
    along_x = column(
        x_start + jnp.where(layer == 0, -1, tile_x - 1 + layer), y_start + iota(shape, 1)
    )
    shape = (3, tile_x, lanes)
    layer = iota(shape, 0)
    along_y = column(
        x_start + iota(shape, 1), y_start + jnp.where(layer == 0, -1, tile_y - 1 + layer)
    )
    return jnp.concatenate([part.reshape(-1, lanes) for part in (tile, along_x, along_y)], axis=0)


def differ(zero, one, two, minus):
    return near * (one - zero) + far * (two - minus)


def along_x(ref, part, x, tile_y, upward):
    def at(offset):
        return ref[part, x + (LAYERS + offset), pl.ds(ROWS, tile_y), :]

    return differ(at(0), at(1), at(2), at(-1)) if upward else differ(at(-1), at(0), at(1), at(-2))


def along_y(ref, part, x, tile_y, upward):
    def at(offset):
        return ref[part, x + LAYERS, pl.ds(ROWS + offset, tile_y), :]

    return differ(at(0), at(1), at(2), at(-1)) if upward else differ(at(-1), at(0), at(1), at(-2))


def along_z(ref, part, x, tile_y, upward):
    value = ref[part, x + LAYERS, pl.ds(ROWS, tile_y), :]
    depth = value.shape[-1]
    lane = lax.broadcasted_iota(jnp.int32, value.shape, 1)

    def at(offset):
        if offset == 0:
            return value
        moved = pltpu.roll(value, (-offset) % depth, 1)
        inside = lane < depth - offset if offset > 0 else lane >= -offset
        return jnp.where(inside, moved, 0.0)

    return differ(at(0), at(1), at(2), at(-1)) if upward else differ(at(-1), at(0), at(1), at(-2))


def clear_rim(ref, parts_x, parts_y):
    _, layers, rows, depth = ref.shape
    tile_x, tile_y = layers - 2 * LAYERS, rows - 2 * ROWS
    for part in parts_x:
        for begin in (0, LAYERS + tile_x):
            ref[part, pl.ds(begin, LAYERS), pl.ds(ROWS, tile_y), :] = jnp.zeros(
                (LAYERS, tile_y, depth), jnp.float32
            )
    for part in parts_y:
        for begin in (0, ROWS + tile_y):
            ref[part, pl.ds(LAYERS, tile_x), pl.ds(begin, ROWS), :] = jnp.zeros(
                (tile_x, ROWS, depth), jnp.float32
            )


def receiver_sum(cells, amps, columns):
    depth, receivers = columns.shape[-1], cells.shape[-1]
    column = lax.div(cells, depth)
    level = cells - column * depth
    column_hot = jnp.concatenate(
        [
            (columns == column[:, begin : begin + depth]).astype(jnp.bfloat16)
            for begin in range(0, receivers, depth)
        ],
        axis=1,
    )
    levels = lax.broadcasted_iota(jnp.int32, (depth, receivers), 0)
    rest = jnp.where(levels == level, amps, 0.0)
    total = jnp.zeros(columns.shape, jnp.float32)
    for _ in range(3):
        part = rest.astype(jnp.bfloat16)
        rest = rest - part.astype(jnp.float32)
        total = total + lax.dot_general(
            column_hot,
            part,
            (((1,), (1,)), ((), ())),
            preferred_element_type=jnp.float32,
        )
    return total


def velocity_kernel(
    width_y,
    lame,
    shear,
    density,
    receiver_cell,
    residual_amp,
    forward,
    adjoint,
    stress,
    velocity,
    accel,
    rim_added,
    buoyancy,
    scaled_lame,
    scaled_shear,
    received,
    gained,
    lame_now,
    shear_now,
    density_now,
    sems,
):
    tile_x, tile_y, depth = density.shape
    copies = [
        pltpu.make_async_copy(lame, lame_now, sems.at[0]),
        pltpu.make_async_copy(shear, shear_now, sems.at[1]),
        pltpu.make_async_copy(density, density_now, sems.at[2]),
    ]
    for copy in copies:
        copy.start()
    cells = tile_x * tile_y
    middle = pl.ds(ROWS, tile_y)
    columns = column_ids(tile_x, tile_y, width_y, depth)
    received[...] = receiver_sum(receiver_cell[...], residual_amp[...], columns)
    for layer in range(3):
        rim_added[0, layer] = received[pl.ds(cells + layer * tile_y, tile_y), :]
        rim_added[1, layer] = received[pl.ds(cells + 3 * tile_y + layer * tile_x, tile_x), :]
    for wave in range(2):
        clear_rim(
            stress, *([6 * wave + part for part in STRESS_ALONG[dim]] for dim in range(2))
        )

    def fill(x, carry):
        extra = received[pl.ds(pl.multiple_of(x * tile_y, 8), tile_y), :]
        for wave, fields in enumerate((forward, adjoint)):
            for part in range(6):
                value = fields[3 + part, x]
                stress[6 * wave + part, x + LAYERS, middle, :] = (
                    value + extra if wave == 1 and part < 3 else value
                )
        return carry

    lax.fori_loop(0, tile_x, fill, 0, unroll=8)

    def layer(x, carry):
        for wave in range(2):
            xx, yy, zz, xy, xz, yz = range(6 * wave, 6 * wave + 6)
            values = (
                along_x(stress, xx, x, tile_y, True)
                + along_y(stress, xy, x, tile_y, False)
                + along_z(stress, xz, x, tile_y, False),
                along_x(stress, xy, x, tile_y, False)
                + along_y(stress, yy, x, tile_y, True)
                + along_z(stress, yz, x, tile_y, False),
                along_x(stress, xz, x, tile_y, False)
                + along_y(stress, yz, x, tile_y, False)
                + along_z(stress, zz, x, tile_y, True),
            )
            for part, value in enumerate(values):
                gained[3 * wave + part, x] = value
        return carry

    lax.fori_loop(0, tile_x, layer, 0, unroll=8)
    for copy in copies:
        copy.wait()

    def finish(x, carry):
        light = 1.0 / density_now[x]
        buoyancy[x] = light
        scaled_lame[x] = time_step * lame_now[x]
        scaled_shear[x] = time_step * shear_now[x]
        for wave, fields in enumerate((forward, adjoint)):
            for part in range(3):
                value = light * gained[3 * wave + part, x]
                if wave == 0:
                    accel[part, x] = value
                velocity[3 * wave + part, x + LAYERS, middle, :] = (
                    fields[part, x] + time_step * value
                )
        return carry

    lax.fori_loop(0, tile_x, finish, 0, unroll=8)


def stress_halo_terms(links, received, rim_added, waves, add):
    for link, halo in zip(links, received):
        dim = link[1]
        part_n, part_a, part_b = ACCEL_OF[dim]

        def normal(wave, slot, layer):
            value = halo[wave, slot]
            return value + rim_added[dim, layer] if wave == 1 else value

        def after():
            for wave in waves:
                n0, n1 = normal(wave, 0, 1), normal(wave, 1, 2)
                add(wave, part_n, dim, -1, near * n0 + far * n1)
                add(wave, part_n, dim, -2, far * n0)
                add(wave, part_a, dim, -1, far * halo[wave, 2])
                add(wave, part_b, dim, -1, far * halo[wave, 3])

        def before():
            for wave in waves:
                add(wave, part_n, dim, 0, -far * normal(wave, 0, 0))
                for part, slot in ((part_a, 1), (part_b, 3)):
                    outer, inner = halo[wave, slot], halo[wave, slot + 1]
                    add(wave, part, dim, 0, -near * inner - far * outer)
                    add(wave, part, dim, 1, -far * inner)

        real = has_peer(link[0], link[2])
        lower = is_lower(link[0], link[2])
        pl.when(real & lower)(after)
        pl.when(real & jnp.logical_not(lower))(before)


def source_gain(cell, part, x, y, z, width_y):
    depth = z.shape[-1]
    column = lax.div(cell, depth)
    source_x = lax.div(column, width_y)
    away = [source_x - x, column - source_x * width_y - y, cell - column * depth - z]
    along = away.pop(part)
    gain = jnp.where(along == 0, -near, 0.0)
    for offset, value in ((1, near), (2, far), (-1, -far)):
        gain = jnp.where(along == offset, value, gain)
    return jnp.where((away[0] == 0) & (away[1] == 0), gain, 0.0)


def start_of(tile_x, tile_y):
    return lax.axis_index("tx") * tile_x, lax.axis_index("ty") * tile_y


def velocity_halo_terms(links, received, stresses, stress, source, width_y, add):
    cell, amp = source
    layers, rows, depth = stress.shape[1:]
    tile = layers - 2 * LAYERS, rows - 2 * ROWS
    starts = start_of(*tile)
    for link, halo, stress_halo in zip(links, received, stresses):
        dim = link[1]
        part_n, part_a, part_b = STRAIN_OF[dim]
        shape = halo.shape[2:]
        cross = starts[1 - dim] + lax.broadcasted_iota(jnp.int32, shape, 0)
        level = lax.broadcasted_iota(jnp.int32, shape, 1)

        def own(wave, part, index):
            return face(stress, 6 * wave + STRESS_ALONG[dim][part], dim, index, True)[...]

        def whole(wave, slot, part, layer, light, terms):
            value = halo[wave, slot]
            if dim == 1:
                value += time_step * light * terms()
            if wave == 0:
                here = jnp.full(shape, starts[dim] + layer, jnp.int32)
                x, y = (here, cross) if dim == 0 else (cross, here)
                gain = source_gain(cell, VELOCITY_ALONG[dim][part], x, y, level, width_y)
                value += time_step * amp * light * gain
            return value

        def after():
            count = tile[dim]
            lights = [1.0 / stress_halo[layer, SPARE] for layer in range(2)]
            for wave in range(2):
                n = whole(wave, 0, 0, count, lights[0], lambda: -far * own(wave, 0, -1))
                add(wave, part_n, dim, -1, far * n)
                for part, name, slot in ((part_a, 1, 1), (part_b, 2, 3)):
                    inner = whole(
                        wave, slot, name, count, lights[0],
                        lambda: -near * own(wave, name, -1) - far * own(wave, name, -2),
                    )
                    outer = whole(
                        wave, slot + 1, name, count + 1, lights[1],
                        lambda: -far * own(wave, name, -1),
                    )
                    add(wave, part, dim, -1, near * inner + far * outer)
                    add(wave, part, dim, -2, far * inner)

        def before():
            lights = [halo[layer, SPARE] for layer in range(2)]
            for wave in range(2):
                outer = whole(wave, 0, 0, -2, lights[1], lambda: far * own(wave, 0, 0))
                inner = whole(
                    wave, 1, 0, -1, lights[0],
                    lambda: near * own(wave, 0, 0) + far * own(wave, 0, 1),
                )
                add(wave, part_n, dim, 0, -near * inner - far * outer)
                add(wave, part_n, dim, 1, -far * inner)
                for part, name, slot in ((part_a, 1, 2), (part_b, 2, 3)):
                    value = whole(
                        wave, slot, name, -1, lights[0], lambda: far * own(wave, name, 0)
                    )
                    add(wave, part, dim, 0, -far * value)

        real = has_peer(link[0], link[2])
        lower = is_lower(link[0], link[2])
        pl.when(real & lower)(after)
        pl.when(real & jnp.logical_not(lower))(before)


def face(ref, part, dim, index, padded):
    layers, rows, depth = ref.shape[1:]
    tile_x = layers - 2 * LAYERS if padded else layers
    tile_y = rows - 2 * ROWS if padded else rows
    if dim == 0:
        at = index % tile_x
        if padded:
            return ref.at[part, at + LAYERS, pl.ds(ROWS, tile_y), :]
        return ref.at[part, at]
    at = index % tile_y
    flat = ref.reshape(ref.shape[0], layers * rows, depth)
    begin = LAYERS * rows + ROWS + at if padded else at
    return flat.at[part, pl.ds(begin, tile_x, stride=rows), :]


def light_face(buoyancy, dim, index):
    layers, rows, depth = buoyancy.shape
    if dim == 0:
        return buoyancy[index % layers]
    return buoyancy.reshape(layers * rows, depth)[pl.ds(index % rows, layers, stride=rows), :]


def boundary_kernel(links, send_links, *refs):
    count = len(links)
    received = refs[:count]
    rim_added, buoyancy, _, velocity = refs[count : count + 4]
    sends = refs[count + 4 :]

    def add(wave, part, dim, index, term):
        target = face(velocity, 3 * wave + part, dim, index, True)
        target[...] += time_step * light_face(buoyancy, dim, index) * term

    stress_halo_terms(links, received, rim_added, (0, 1), add)
    send_velocities(send_links, velocity, buoyancy, sends)


def strain_kernel(links, width_y, *refs):
    count = len(links)
    received = refs[:count]
    source_cell, source_amp, rim_added, buoyancy, accel = refs[count : count + 5]
    strain, gradient, velocity = refs[count + 6 : count + 9]
    outputs, (accel_now, sems) = refs[count + 9 : count + 11], refs[count + 11 :]
    tile_x, tile_y, depth = buoyancy.shape
    middle = pl.ds(ROWS, tile_y)
    clear_rim(velocity, range(6), range(6))
    accel_now[...] = accel[...]

    def add(wave, part, dim, index, term):
        target = face(accel_now, part, dim, index, False)
        target[...] += light_face(buoyancy, dim, index) * term

    stress_halo_terms(links, received, rim_added, (0,), add)
    x_start, y_start = start_of(tile_x, tile_y)
    cell, amp = source_cell[0], source_amp[0]
    source_x = lax.div(cell, width_y * depth)
    y = y_start + lax.broadcasted_iota(jnp.int32, (tile_y, depth), 0)
    level = lax.broadcasted_iota(jnp.int32, (tile_y, depth), 1)
    for offset in (-2, -1, 0, 1):
        x = source_x + offset - x_start

        @pl.when((x >= 0) & (x < tile_x))
        def add_source():
            here = jnp.full((tile_y, depth), source_x + offset, jnp.int32)
            for part in range(3):
                gain = source_gain(cell, part, here, y, level, width_y)
                value = amp * buoyancy[x] * gain
                accel_now[part, x] += value
                velocity[part, x + LAYERS, middle, :] += time_step * value

    copies = [
        pltpu.make_async_copy(
            velocity.at[3 * wave + part, pl.ds(LAYERS, tile_x), middle, :],
            outputs[wave].at[part],
            sems.at[3 * wave + part],
        )
        for wave in range(2)
        for part in range(3)
    ]
    for copy in copies:
        copy.start()
    def layer(x, carry):
        for wave in range(2):
            vx, vy, vz = range(3 * wave, 3 * wave + 3)
            values = (
                along_x(velocity, vx, x, tile_y, False),
                along_y(velocity, vy, x, tile_y, False),
                along_z(velocity, vz, x, tile_y, False),
                along_y(velocity, vx, x, tile_y, True) + along_x(velocity, vy, x, tile_y, True),
                along_z(velocity, vx, x, tile_y, True) + along_x(velocity, vz, x, tile_y, True),
                along_z(velocity, vy, x, tile_y, True) + along_y(velocity, vz, x, tile_y, True),
            )
            for part, value in enumerate(values):
                strain[6 * wave + part, x] = value
        total = sum(
            accel_now[part, x] * velocity[3 + part, x + LAYERS, middle, :] for part in range(3)
        )
        gradient[2, x] = -time_step * total
        return carry

    lax.fori_loop(0, tile_x, layer, 0, unroll=4)
    for copy in copies:
        copy.wait()


def new_stress(strain, stress, scaled_lame, scaled_shear, wave, x, tile_y):
    lame, shear = scaled_lame[x], scaled_shear[x]
    strains = [strain[6 * wave + part, x] for part in range(6)]
    volume = lame * (strains[0] + strains[1] + strains[2])
    values = []
    for part in range(6):
        old = stress[6 * wave + part, x + LAYERS, pl.ds(ROWS, tile_y), :]
        if part < 3:
            values.append(old + (volume + 2.0 * shear * strains[part]))
        else:
            values.append(old + shear * strains[part])
    return strains, values


def gradient_kernel(links, width_y, *refs):
    count = len(links)
    received, stresses = refs[:count], refs[count : 2 * count]
    source_cell, source_amp, stress, scaled_lame, scaled_shear = refs[2 * count : 2 * count + 5]
    strain, gradient = refs[2 * count + 7 :]
    tile_x, tile_y, _ = scaled_lame.shape

    def add(wave, part, dim, index, term):
        target = face(strain, 6 * wave + part, dim, index, False)
        target[...] += term

    source = source_cell[0], source_amp[0]
    velocity_halo_terms(links, received, stresses, stress, source, width_y, add)

    def layer(x, carry):
        strains = [strain[part, x] for part in range(6)]
        _, values = new_stress(strain, stress, scaled_lame, scaled_shear, 1, x, tile_y)
        trace = strains[0] + strains[1] + strains[2]
        gradient[0, x] = -time_step * trace * (values[0] + values[1] + values[2])
        total = sum(left * right for left, right in zip(strains, values))
        gradient[1, x] = -time_step * total
        return carry

    lax.fori_loop(0, tile_x, layer, 0, unroll=4)


def output_kernel(
    chunk, width_y, source_cell, source_amp, strain, stress, scaled_lame, scaled_shear, *refs
):
    outputs, (values_now, sems) = refs[2:4], refs[4:]
    tile_x, tile_y, depth = scaled_lame.shape
    x_start, y_start = start_of(tile_x, tile_y)
    y = y_start + lax.broadcasted_iota(jnp.int32, (tile_y, depth), 0)
    level = lax.broadcasted_iota(jnp.int32, (tile_y, depth), 1)
    in_layer = y * depth + level - source_cell[0]
    copies = []
    for begin in range(0, tile_x, chunk):
        for wave in range(2):
            for x in range(begin, begin + chunk):
                _, values = new_stress(strain, stress, scaled_lame, scaled_shear, wave, x, tile_y)
                if wave == 0:
                    first = (x_start + x) * (width_y * depth)
                    added = jnp.where(in_layer == -first, source_amp[0], 0.0)
                    values[:3] = [value + added for value in values[:3]]
                for part in range(6):
                    values_now[6 * wave + part, x] = values[part]
            layers = pl.ds(begin, chunk)
            copy = pltpu.make_async_copy(
                values_now.at[pl.ds(6 * wave, 6), layers],
                outputs[wave].at[pl.ds(3, 6), layers],
                sems.at[len(copies)],
            )
            copy.start()
            copies.append(copy)
    for copy in copies:
        copy.wait()


def sum_kernel(mine, other, total, total_now, sems):
    copies = []
    for part in range(mine.shape[0]):
        total_now[part] = mine[part] + other[part]
        copy = pltpu.make_async_copy(total_now.at[part], total.at[part], sems.at[part])
        copy.start()
        copies.append(copy)
    for copy in copies:
        copy.wait()


def in_hbm(value):
    return pltpu.with_memory_space_constraint(value, pltpu.HBM)


def cost(flops, size):
    return pl.CostEstimate(flops=flops, bytes_accessed=size, transcendentals=0)


def body(
    forward_fields,
    adjoint_fields,
    lame_lambda,
    shear_modulus,
    density,
    source_cell,
    source_amp,
    receiver_cell,
    residual_amp,
):
    _, _, tile_x, tile_y, depth = forward_fields.shape
    forward = forward_fields.reshape(forward_fields.shape[1:])
    adjoint = adjoint_fields.reshape(adjoint_fields.shape[1:])
    sizes = {name: lax.axis_size(name) for name in ("tx", "ty")}
    width_y = tile_y * sizes["ty"]
    links_x, links_y = links_of(sizes)
    cells = tile_x * tile_y * depth

    def buffers(dim):
        return pltpu.VMEM((2, SLOTS, tile_y if dim == 0 else tile_x, depth), jnp.float32)

    def tile(*lead):
        return pltpu.VMEM((*lead, tile_x, tile_y, depth), jnp.float32)

    def padded(parts):
        return pltpu.VMEM(
            (parts, tile_x + 2 * LAYERS, tile_y + 2 * ROWS, depth), jnp.float32
        )

    def exchange(links, sends):
        return [swap(send, axis, first) for (axis, _, first), send in zip(links, sends)]

    def shapes(links):
        return [buffers(dim) for _, dim, _ in links]

    links = links_y + links_x
    count, count_x, count_y = len(links), len(links_x), len(links_y)
    rows = tile_x * tile_y + 3 * (tile_x + tile_y)
    source = source_cell, source_amp

    *sends, density_rows = pl.pallas_call(
        functools.partial(early_pack_kernel, links_x),
        out_shape=shapes(links_x) + [pltpu.VMEM((2, tile_x, depth), jnp.float32)],
        in_specs=[hbm] * 3,
        out_specs=[vmem] * (count_x + 1),
        scratch_shapes=[pltpu.SemaphoreType.DMA((2 + 2 * SLOTS * count_x,))],
        compiler_params=params,
        cost_estimate=cost(0, 4 * cells),
        name="early_pack",
    )(*(in_hbm(x) for x in (forward, adjoint, density)))
    halos_x = exchange(links_x, sends)
    halos_y = []
    if links_y:
        sends = pl.pallas_call(
            functools.partial(pack_kernel, links_y),
            out_shape=shapes(links_y),
            in_specs=[vmem] * 3,
            out_specs=[vmem] * count_y,
            compiler_params=params,
            cost_estimate=cost(0, 2 * 2 * SLOTS * count_y * tile_x * depth * 4),
            name="pack",
        )(forward, adjoint, density_rows)
        halos_y = exchange(links_y, sends)

    stress, velocity, accel, rim_added, buoyancy, scaled_lame, scaled_shear = pl.pallas_call(
        functools.partial(velocity_kernel, width_y),
        out_shape=[
            padded(12),
            padded(6),
            tile(3),
            pltpu.VMEM((2, 3, max(tile_x, tile_y), depth), jnp.float32),
            tile(),
            tile(),
            tile(),
        ],
        in_specs=[hbm] * 3 + [vmem] * 4,
        out_specs=[vmem] * 7,
        scratch_shapes=[
            pltpu.VMEM((rows, depth), jnp.float32),
            tile(6),
            tile(),
            tile(),
            tile(),
            pltpu.SemaphoreType.DMA((3,)),
        ],
        compiler_params=params,
        cost_estimate=cost(200 * cells, 18 * 4 * cells),
        name="velocity",
    )(
        *(in_hbm(x) for x in (lame_lambda, shear_modulus, density)),
        receiver_cell,
        residual_amp,
        forward,
        adjoint,
    )

    def boundary(links, send_links, halos, velocity, name):
        velocity, *sends = pl.pallas_call(
            functools.partial(boundary_kernel, links, send_links),
            out_shape=[padded(6)] + shapes(send_links),
            in_specs=[vmem] * (len(links) + 3),
            out_specs=[vmem] * (1 + len(send_links)),
            input_output_aliases={len(links) + 2: 0},
            compiler_params=params,
            cost_estimate=cost(cells, 10 * 2 * tile_x * depth * 4),
            name=name,
        )(*halos, rim_added, buoyancy, velocity)
        return velocity, exchange(send_links, sends)

    later_y = links_y[::-1]
    velocity, velocity_halos_y = boundary(links_x, later_y, halos_x, velocity, "boundary_x")
    velocity, velocity_halos_x = boundary(links_y, links_x, halos_y, velocity, "boundary_y")
    halos = halos_y + halos_x
    later_links = later_y + links_x
    later_halos = halos_y[::-1] + halos_x
    velocity_halos = velocity_halos_y + velocity_halos_x

    out_shape = jax.ShapeDtypeStruct(forward.shape, jnp.float32)
    strain, gradient, _, forward_next, adjoint_next = pl.pallas_call(
        functools.partial(strain_kernel, links, width_y),
        out_shape=[tile(12), tile(3), padded(6), out_shape, out_shape],
        in_specs=[vmem] * count + [smem] * 2 + [vmem] * 4,
        out_specs=[vmem] * 3 + [hbm] * 2,
        input_output_aliases={count + 5: 2},
        scratch_shapes=[tile(3), pltpu.SemaphoreType.DMA((6,))],
        compiler_params=params,
        cost_estimate=cost(200 * cells, 18 * 4 * cells),
        name="strain",
    )(*halos, *source, rim_added, buoyancy, accel, velocity)

    strain, gradient = pl.pallas_call(
        functools.partial(gradient_kernel, later_links, width_y),
        out_shape=[tile(12), tile(3)],
        in_specs=[vmem] * (2 * count) + [smem] * 2 + [vmem] * 5,
        out_specs=[vmem] * 2,
        input_output_aliases={2 * count + 5: 0, 2 * count + 6: 1},
        compiler_params=params,
        cost_estimate=cost(30 * cells, 2 * 4 * cells),
        name="gradient",
    )(*velocity_halos, *later_halos, *source, stress, scaled_lame, scaled_shear, strain, gradient)
    other = lax.ppermute(gradient, "shot", [(0, 1), (1, 0)])

    chunk = 4 if tile_x % 4 == 0 else 1
    forward_next, adjoint_next = pl.pallas_call(
        functools.partial(output_kernel, chunk, width_y),
        out_shape=[out_shape, out_shape],
        in_specs=[smem] * 2 + [vmem] * 4 + [hbm] * 2,
        out_specs=[hbm] * 2,
        input_output_aliases={6: 0, 7: 1},
        scratch_shapes=[tile(12), pltpu.SemaphoreType.DMA((2 * tile_x // chunk,))],
        compiler_params=params,
        cost_estimate=cost(60 * cells, 18 * 4 * cells),
        name="outputs",
    )(*source, strain, stress, scaled_lame, scaled_shear, forward_next, adjoint_next)
    total = pl.pallas_call(
        sum_kernel,
        out_shape=jax.ShapeDtypeStruct((3, tile_x, tile_y, depth), jnp.float32),
        in_specs=[vmem] * 2,
        out_specs=hbm,
        scratch_shapes=[tile(3), pltpu.SemaphoreType.DMA((3,))],
        compiler_params=params,
        cost_estimate=cost(3 * cells, 9 * 4 * cells),
        name="sum",
    )(gradient, other)
    return forward_next[None], adjoint_next[None], total


def solution(mesh):
    return jax.shard_map(
        body,
        mesh=mesh,
        in_specs=(
            P("shot", None, "tx", "ty", None),
            P("shot", None, "tx", "ty", None),
            P("tx", "ty", None),
            P("tx", "ty", None),
            P("tx", "ty", None),
            P("shot"),
            P("shot"),
            P("shot", None),
            P("shot", None),
        ),
        out_specs=(
            P("shot", None, "tx", "ty", None),
            P("shot", None, "tx", "ty", None),
            P(None, "tx", "ty", None),
        ),
        check_vma=False,
    )
```

```python
import functools

import jax
import jax.numpy as jnp
from jax import lax
from jax.experimental import pallas as pl
from jax.experimental.pallas import tpu as pltpu
from jax.sharding import PartitionSpec as P

near = 9.0 / 8.0
far = -1.0 / 24.0
time_step = 0.15

LAYERS = 2
ROWS = 8
SLOTS = 5

STRESS_ALONG = ((0, 3, 4), (1, 3, 5))
ACCEL_OF = ((0, 1, 2), (1, 0, 2))
VELOCITY_ALONG = ((0, 1, 2), (1, 0, 2))
STRAIN_OF = ((0, 3, 4), (1, 3, 5))

vmem = pl.BlockSpec(memory_space=pltpu.VMEM)
smem = pl.BlockSpec(memory_space=pltpu.SMEM)
hbm = pl.BlockSpec(memory_space=pltpu.HBM)
params = pltpu.CompilerParams(vmem_limit_bytes=24 * 1024 * 1024)


def links_of(sizes):
    along_x = (("tx", 0, 1), ("tx", 0, 0))
    along_y = (("ty", 1, 1), ("ty", 1, 0))
    return [[link for link in order if link[2] + 1 < sizes[link[0]]] for order in (along_x, along_y)]


def swap(value, axis, first):
    pairs = [(i, i + 1) for i in range(first, lax.axis_size(axis) - 1, 2)]
    return lax.ppermute(value, axis, pairs + [(j, i) for i, j in pairs])


def is_lower(axis, first):
    return lax.axis_index(axis) % 2 == first


def has_peer(axis, first):
    index = lax.axis_index(axis)
    partner = jnp.where(is_lower(axis, first), index + 1, index - 1)
    return (partner >= 0) & (partner < lax.axis_size(axis))


def by_role(link, act, upper, lower):
    lower_here = is_lower(link[0], link[2])
    pl.when(lower_here)(lambda: act(lower, True))
    pl.when(jnp.logical_not(lower_here))(lambda: act(upper, False))


SPARE = SLOTS - 1


def stress_plan(dim):
    n, a, b = STRESS_ALONG[dim]
    return ((n, 0), (n, 1), (a, 0), (b, 0)), ((n, -1), (a, -2), (a, -1), (b, -2), (b, -1))


def velocity_plan(dim):
    n, a, b = VELOCITY_ALONG[dim]
    return ((n, 0), (a, 0), (a, 1), (b, 0), (b, 1)), ((n, -2), (n, -1), (a, -1), (b, -1))


def early_pack_kernel(links, forward, adjoint, density, *refs):
    sends, (density_rows, sems) = refs[: len(links)], refs[len(links) :]
    tile = forward.shape[1:3]
    waits = []
    for row in range(2):
        copy = pltpu.make_async_copy(
            density.at[:, row, :], density_rows.at[row], sems.at[2 * SLOTS * len(links) + row]
        )
        copy.start()
        waits.append(copy)

    def layer(ref, dim, index):
        return ref.at[index] if dim == 0 else ref.at[:, index, :]

    for at, (link, send) in enumerate(zip(links, sends)):
        dim = link[1]

        def semaphore(wave, slot):
            return sems.at[(2 * at + wave) * SLOTS + slot]

        def start(plan, lower):
            for wave, fields in enumerate((forward, adjoint)):
                sources = [
                    layer(fields.at[3 + part], dim, index % tile[dim]) for part, index in plan
                ]
                if not lower:
                    sources.append(layer(density, dim, wave))
                for slot, source in enumerate(sources):
                    pltpu.make_async_copy(
                        source, send.at[wave, slot], semaphore(wave, slot)
                    ).start()

        by_role(link, start, *stress_plan(dim))
        for wave in range(2):
            for slot in range(SLOTS):
                waits.append(
                    pltpu.make_async_copy(
                        layer(density, dim, 0), send.at[wave, slot], semaphore(wave, slot)
                    )
                )
    for copy in waits:
        copy.wait()


def pack_kernel(links, forward, adjoint, density_rows, *sends):
    for link, send in zip(links, sends):
        dim = link[1]

        def put(plan, lower):
            for wave, fields in enumerate((forward, adjoint)):
                for slot, (part, index) in enumerate(plan):
                    send[wave, slot] = face(fields, 3 + part, dim, index, False)[...]
                if not lower:
                    send[wave, SPARE] = density_rows[wave]

        by_role(link, put, *stress_plan(dim))


def send_velocities(links, velocity, buoyancy, sends):
    for link, send in zip(links, sends):
        dim = link[1]

        def put(plan, lower):
            for wave in range(2):
                for slot, (part, index) in enumerate(plan):
                    send[wave, slot] = face(velocity, 3 * wave + part, dim, index, True)[...]
                if lower:
                    send[wave, SPARE] = light_face(buoyancy, dim, -1 - wave)

        by_role(link, put, *velocity_plan(dim))


def column_ids(tile_x, tile_y, width_y, lanes):
    x_start = lax.axis_index("tx") * tile_x
    y_start = lax.axis_index("ty") * tile_y

    def column(x, y):
        inside = (y >= 0) & (y < width_y)
        return jnp.where(inside, x * width_y + y, -1)

    def iota(shape, dim):
        return lax.broadcasted_iota(jnp.int32, shape, dim)

    shape = (tile_x, tile_y, lanes)
    tile = column(x_start + iota(shape, 0), y_start + iota(shape, 1))
    shape = (3, tile_y, lanes)
    layer = iota(shape, 0)
    along_x = column(
        x_start + jnp.where(layer == 0, -1, tile_x - 1 + layer), y_start + iota(shape, 1)
    )
    shape = (3, tile_x, lanes)
    layer = iota(shape, 0)
    along_y = column(
        x_start + iota(shape, 1), y_start + jnp.where(layer == 0, -1, tile_y - 1 + layer)
    )
    return jnp.concatenate([part.reshape(-1, lanes) for part in (tile, along_x, along_y)], axis=0)


def differ(zero, one, two, minus):
    return near * (one - zero) + far * (two - minus)


def along_x(ref, part, x, tile_y, upward):
    def at(offset):
        return ref[part, x + (LAYERS + offset), pl.ds(ROWS, tile_y), :]

    return differ(at(0), at(1), at(2), at(-1)) if upward else differ(at(-1), at(0), at(1), at(-2))


def along_y(ref, part, x, tile_y, upward):
    def at(offset):
        return ref[part, x + LAYERS, pl.ds(ROWS + offset, tile_y), :]

    return differ(at(0), at(1), at(2), at(-1)) if upward else differ(at(-1), at(0), at(1), at(-2))


def along_z(ref, part, x, tile_y, upward):
    value = ref[part, x + LAYERS, pl.ds(ROWS, tile_y), :]
    depth = value.shape[-1]
    lane = lax.broadcasted_iota(jnp.int32, value.shape, 1)

    def at(offset):
        if offset == 0:
            return value
        moved = pltpu.roll(value, (-offset) % depth, 1)
        inside = lane < depth - offset if offset > 0 else lane >= -offset
        return jnp.where(inside, moved, 0.0)

    return differ(at(0), at(1), at(2), at(-1)) if upward else differ(at(-1), at(0), at(1), at(-2))


def clear_rim(ref, parts_x, parts_y):
    _, layers, rows, depth = ref.shape
    tile_x, tile_y = layers - 2 * LAYERS, rows - 2 * ROWS
    for part in parts_x:
        for begin in (0, LAYERS + tile_x):
            ref[part, pl.ds(begin, LAYERS), pl.ds(ROWS, tile_y), :] = jnp.zeros(
                (LAYERS, tile_y, depth), jnp.float32
            )
    for part in parts_y:
        for begin in (0, ROWS + tile_y):
            ref[part, pl.ds(LAYERS, tile_x), pl.ds(begin, ROWS), :] = jnp.zeros(
                (tile_x, ROWS, depth), jnp.float32
            )


def receiver_sum(cells, amps, columns):
    depth, receivers = columns.shape[-1], cells.shape[-1]
    column = lax.div(cells, depth)
    level = cells - column * depth
    column_hot = jnp.concatenate(
        [
            (columns == column[:, begin : begin + depth]).astype(jnp.bfloat16)
            for begin in range(0, receivers, depth)
        ],
        axis=1,
    )
    levels = lax.broadcasted_iota(jnp.int32, (depth, receivers), 0)
    rest = jnp.where(levels == level, amps, 0.0)
    total = jnp.zeros(columns.shape, jnp.float32)
    for _ in range(3):
        part = rest.astype(jnp.bfloat16)
        rest = rest - part.astype(jnp.float32)
        total = total + lax.dot_general(
            column_hot,
            part,
            (((1,), (1,)), ((), ())),
            preferred_element_type=jnp.float32,
        )
    return total


def velocity_kernel(
    width_y,
    lame,
    shear,
    density,
    receiver_cell,
    residual_amp,
    forward,
    adjoint,
    stress,
    velocity,
    accel,
    rim_added,
    buoyancy,
    scaled_lame,
    scaled_shear,
    received,
    gained,
    lame_now,
    shear_now,
    density_now,
    sems,
):
    tile_x, tile_y, depth = density.shape
    copies = [
        pltpu.make_async_copy(lame, lame_now, sems.at[0]),
        pltpu.make_async_copy(shear, shear_now, sems.at[1]),
        pltpu.make_async_copy(density, density_now, sems.at[2]),
    ]
    for copy in copies:
        copy.start()
    cells = tile_x * tile_y
    middle = pl.ds(ROWS, tile_y)
    columns = column_ids(tile_x, tile_y, width_y, depth)
    received[...] = receiver_sum(receiver_cell[...], residual_amp[...], columns)
    for layer in range(3):
        rim_added[0, layer] = received[pl.ds(cells + layer * tile_y, tile_y), :]
        rim_added[1, layer] = received[pl.ds(cells + 3 * tile_y + layer * tile_x, tile_x), :]
    for wave in range(2):
        clear_rim(
            stress, *([6 * wave + part for part in STRESS_ALONG[dim]] for dim in range(2))
        )

    def fill(x, carry):
        extra = received[pl.ds(pl.multiple_of(x * tile_y, 8), tile_y), :]
        for wave, fields in enumerate((forward, adjoint)):
            for part in range(6):
                value = fields[3 + part, x]
                stress[6 * wave + part, x + LAYERS, middle, :] = (
                    value + extra if wave == 1 and part < 3 else value
                )
        return carry

    lax.fori_loop(0, tile_x, fill, 0, unroll=8)

    def layer(x, carry):
        for wave in range(2):
            xx, yy, zz, xy, xz, yz = range(6 * wave, 6 * wave + 6)
            values = (
                along_x(stress, xx, x, tile_y, True)
                + along_y(stress, xy, x, tile_y, False)
                + along_z(stress, xz, x, tile_y, False),
                along_x(stress, xy, x, tile_y, False)
                + along_y(stress, yy, x, tile_y, True)
                + along_z(stress, yz, x, tile_y, False),
                along_x(stress, xz, x, tile_y, False)
                + along_y(stress, yz, x, tile_y, False)
                + along_z(stress, zz, x, tile_y, True),
            )
            for part, value in enumerate(values):
                gained[3 * wave + part, x] = value
        return carry

    lax.fori_loop(0, tile_x, layer, 0, unroll=8)
    for copy in copies:
        copy.wait()

    def finish(x, carry):
        light = 1.0 / density_now[x]
        buoyancy[x] = light
        scaled_lame[x] = time_step * lame_now[x]
        scaled_shear[x] = time_step * shear_now[x]
        for wave, fields in enumerate((forward, adjoint)):
            for part in range(3):
                value = light * gained[3 * wave + part, x]
                if wave == 0:
                    accel[part, x] = value
                velocity[3 * wave + part, x + LAYERS, middle, :] = (
                    fields[part, x] + time_step * value
                )
        return carry

    lax.fori_loop(0, tile_x, finish, 0, unroll=8)


def stress_halo_terms(links, received, rim_added, waves, add):
    for link, halo in zip(links, received):
        dim = link[1]
        part_n, part_a, part_b = ACCEL_OF[dim]

        def normal(wave, slot, layer):
            value = halo[wave, slot]
            return value + rim_added[dim, layer] if wave == 1 else value

        def after():
            for wave in waves:
                n0, n1 = normal(wave, 0, 1), normal(wave, 1, 2)
                add(wave, part_n, dim, -1, near * n0 + far * n1)
                add(wave, part_n, dim, -2, far * n0)
                add(wave, part_a, dim, -1, far * halo[wave, 2])
                add(wave, part_b, dim, -1, far * halo[wave, 3])

        def before():
            for wave in waves:
                add(wave, part_n, dim, 0, -far * normal(wave, 0, 0))
                for part, slot in ((part_a, 1), (part_b, 3)):
                    outer, inner = halo[wave, slot], halo[wave, slot + 1]
                    add(wave, part, dim, 0, -near * inner - far * outer)
                    add(wave, part, dim, 1, -far * inner)

        real = has_peer(link[0], link[2])
        lower = is_lower(link[0], link[2])
        pl.when(real & lower)(after)
        pl.when(real & jnp.logical_not(lower))(before)


def source_gain(cell, part, x, y, z, width_y):
    depth = z.shape[-1]
    column = lax.div(cell, depth)
    source_x = lax.div(column, width_y)
    away = [source_x - x, column - source_x * width_y - y, cell - column * depth - z]
    along = away.pop(part)
    gain = jnp.where(along == 0, -near, 0.0)
    for offset, value in ((1, near), (2, far), (-1, -far)):
        gain = jnp.where(along == offset, value, gain)
    return jnp.where((away[0] == 0) & (away[1] == 0), gain, 0.0)


def start_of(tile_x, tile_y):
    return lax.axis_index("tx") * tile_x, lax.axis_index("ty") * tile_y


def missing_terms(links, stress, source, width_y, missing):
    cell, amp = source
    layers, rows, depth = stress.shape[1:]
    tile = layers - 2 * LAYERS, rows - 2 * ROWS
    starts = start_of(*tile)
    for link, out in zip(links, missing):
        dim = link[1]
        shape = out.shape[2:]
        cross = starts[1 - dim] + lax.broadcasted_iota(jnp.int32, shape, 0)
        level = lax.broadcasted_iota(jnp.int32, shape, 1)

        def own(wave, part, index):
            return face(stress, 6 * wave + STRESS_ALONG[dim][part], dim, index, True)[...]

        def put(slots):
            for wave in range(2):
                for slot, (part, layer, terms) in enumerate(slots):
                    value = terms(wave) if dim == 1 else jnp.zeros(shape, jnp.float32)
                    if wave == 0:
                        here = jnp.full(shape, starts[dim] + layer, jnp.int32)
                        x, y = (here, cross) if dim == 0 else (cross, here)
                        value += amp * source_gain(
                            cell, VELOCITY_ALONG[dim][part], x, y, level, width_y
                        )
                    out[wave, slot] = value

        def after():
            count = tile[dim]
            slots = [(0, count, lambda wave: -far * own(wave, 0, -1))]
            for part in (1, 2):
                slots += [
                    (
                        part,
                        count,
                        lambda wave, part=part: -near * own(wave, part, -1)
                        - far * own(wave, part, -2),
                    ),
                    (part, count + 1, lambda wave, part=part: -far * own(wave, part, -1)),
                ]
            put(slots)

        def before():
            put([
                (0, -2, lambda wave: far * own(wave, 0, 0)),
                (0, -1, lambda wave: near * own(wave, 0, 0) + far * own(wave, 0, 1)),
                (1, -1, lambda wave: far * own(wave, 1, 0)),
                (2, -1, lambda wave: far * own(wave, 2, 0)),
            ])

        lower = is_lower(link[0], link[2])
        pl.when(lower)(after)
        pl.when(jnp.logical_not(lower))(before)


def velocity_halo_terms(links, received, stresses, missing, add):
    for link, halo, stress_halo, lack in zip(links, received, stresses, missing):
        dim = link[1]
        part_n, part_a, part_b = STRAIN_OF[dim]

        def after():
            lights = [time_step / stress_halo[layer, SPARE] for layer in range(2)]
            for wave in range(2):

                def whole(slot, layer):
                    return halo[wave, slot] + lights[layer] * lack[wave, slot]

                add(wave, part_n, dim, -1, far * whole(0, 0))
                for part, slot in ((part_a, 1), (part_b, 3)):
                    inner, outer = whole(slot, 0), whole(slot + 1, 1)
                    add(wave, part, dim, -1, near * inner + far * outer)
                    add(wave, part, dim, -2, far * inner)

        def before():
            lights = [time_step * halo[layer, SPARE] for layer in range(2)]
            for wave in range(2):

                def whole(slot, layer):
                    return halo[wave, slot] + lights[layer] * lack[wave, slot]

                outer, inner = whole(0, 1), whole(1, 0)
                add(wave, part_n, dim, 0, -near * inner - far * outer)
                add(wave, part_n, dim, 1, -far * inner)
                add(wave, part_a, dim, 0, -far * whole(2, 0))
                add(wave, part_b, dim, 0, -far * whole(3, 0))

        real = has_peer(link[0], link[2])
        lower = is_lower(link[0], link[2])
        pl.when(real & lower)(after)
        pl.when(real & jnp.logical_not(lower))(before)


def face(ref, part, dim, index, padded):
    layers, rows, depth = ref.shape[1:]
    tile_x = layers - 2 * LAYERS if padded else layers
    tile_y = rows - 2 * ROWS if padded else rows
    if dim == 0:
        at = index % tile_x
        if padded:
            return ref.at[part, at + LAYERS, pl.ds(ROWS, tile_y), :]
        return ref.at[part, at]
    at = index % tile_y
    flat = ref.reshape(ref.shape[0], layers * rows, depth)
    begin = LAYERS * rows + ROWS + at if padded else at
    return flat.at[part, pl.ds(begin, tile_x, stride=rows), :]


def light_face(buoyancy, dim, index):
    layers, rows, depth = buoyancy.shape
    if dim == 0:
        return buoyancy[index % layers]
    return buoyancy.reshape(layers * rows, depth)[pl.ds(index % rows, layers, stride=rows), :]


def boundary_kernel(links, send_links, *refs):
    count = len(links)
    received = refs[:count]
    rim_added, buoyancy, _, velocity = refs[count : count + 4]
    sends = refs[count + 4 :]

    def add(wave, part, dim, index, term):
        target = face(velocity, 3 * wave + part, dim, index, True)
        target[...] += time_step * light_face(buoyancy, dim, index) * term

    stress_halo_terms(links, received, rim_added, (0, 1), add)
    send_velocities(send_links, velocity, buoyancy, sends)


def strain_kernel(links, width_y, *refs):
    count = len(links)
    received = refs[:count]
    source_cell, source_amp, rim_added, buoyancy, accel = refs[count : count + 5]
    stress = refs[count + 6]
    strain, gradient, velocity = refs[count + 7 : count + 10]
    outputs, missing = refs[count + 10 : count + 12], refs[count + 12 : 2 * count + 12]
    accel_now, sems = refs[2 * count + 12 :]
    tile_x, tile_y, depth = buoyancy.shape
    middle = pl.ds(ROWS, tile_y)
    clear_rim(velocity, range(6), range(6))
    accel_now[...] = accel[...]

    def add(wave, part, dim, index, term):
        target = face(accel_now, part, dim, index, False)
        target[...] += light_face(buoyancy, dim, index) * term

    stress_halo_terms(links, received, rim_added, (0,), add)
    x_start, y_start = start_of(tile_x, tile_y)
    cell, amp = source_cell[0], source_amp[0]
    source_x = lax.div(cell, width_y * depth)
    y = y_start + lax.broadcasted_iota(jnp.int32, (tile_y, depth), 0)
    level = lax.broadcasted_iota(jnp.int32, (tile_y, depth), 1)
    for offset in (-2, -1, 0, 1):
        x = source_x + offset - x_start

        @pl.when((x >= 0) & (x < tile_x))
        def add_source():
            here = jnp.full((tile_y, depth), source_x + offset, jnp.int32)
            for part in range(3):
                gain = source_gain(cell, part, here, y, level, width_y)
                value = amp * buoyancy[x] * gain
                accel_now[part, x] += value
                velocity[part, x + LAYERS, middle, :] += time_step * value

    copies = [
        pltpu.make_async_copy(
            velocity.at[3 * wave + part, pl.ds(LAYERS, tile_x), middle, :],
            outputs[wave].at[part],
            sems.at[3 * wave + part],
        )
        for wave in range(2)
        for part in range(3)
    ]
    for copy in copies:
        copy.start()
    def layer(x, carry):
        for wave in range(2):
            vx, vy, vz = range(3 * wave, 3 * wave + 3)
            values = (
                along_x(velocity, vx, x, tile_y, False),
                along_y(velocity, vy, x, tile_y, False),
                along_z(velocity, vz, x, tile_y, False),
                along_y(velocity, vx, x, tile_y, True) + along_x(velocity, vy, x, tile_y, True),
                along_z(velocity, vx, x, tile_y, True) + along_x(velocity, vz, x, tile_y, True),
                along_z(velocity, vy, x, tile_y, True) + along_y(velocity, vz, x, tile_y, True),
            )
            for part, value in enumerate(values):
                strain[6 * wave + part, x] = value
        total = sum(
            accel_now[part, x] * velocity[3 + part, x + LAYERS, middle, :] for part in range(3)
        )
        gradient[2, x] = -time_step * total
        return carry

    lax.fori_loop(0, tile_x, layer, 0, unroll=8)
    missing_terms(links, stress, (cell, amp), width_y, missing)
    for copy in copies:
        copy.wait()


def new_stress(strain, stress, scaled_lame, scaled_shear, wave, x, tile_y):
    lame, shear = scaled_lame[x], scaled_shear[x]
    strains = [strain[6 * wave + part, x] for part in range(6)]
    volume = lame * (strains[0] + strains[1] + strains[2])
    values = []
    for part in range(6):
        old = stress[6 * wave + part, x + LAYERS, pl.ds(ROWS, tile_y), :]
        if part < 3:
            values.append(old + (volume + 2.0 * shear * strains[part]))
        else:
            values.append(old + shear * strains[part])
    return strains, values


def gradient_kernel(links, *refs):
    count = len(links)
    received, stresses, missing = (refs[at : at + count] for at in range(0, 3 * count, count))
    stress, scaled_lame, scaled_shear, _, _, strain, gradient = refs[3 * count :]
    tile_x, tile_y, _ = scaled_lame.shape

    def add(wave, part, dim, index, term):
        target = face(strain, 6 * wave + part, dim, index, False)
        target[...] += term

    velocity_halo_terms(links, received, stresses, missing, add)

    def layer(x, carry):
        strains = [strain[part, x] for part in range(6)]
        _, values = new_stress(strain, stress, scaled_lame, scaled_shear, 1, x, tile_y)
        trace = strains[0] + strains[1] + strains[2]
        gradient[0, x] = -time_step * trace * (values[0] + values[1] + values[2])
        total = sum(left * right for left, right in zip(strains, values))
        gradient[1, x] = -time_step * total
        return carry

    lax.fori_loop(0, tile_x, layer, 0, unroll=8)


def output_kernel(
    chunk, width_y, source_cell, source_amp, strain, stress, scaled_lame, scaled_shear, *refs
):
    outputs, (values_now, sems) = refs[2:4], refs[4:]
    tile_x, tile_y, depth = scaled_lame.shape
    x_start, y_start = start_of(tile_x, tile_y)
    y = y_start + lax.broadcasted_iota(jnp.int32, (tile_y, depth), 0)
    level = lax.broadcasted_iota(jnp.int32, (tile_y, depth), 1)
    in_layer = y * depth + level - source_cell[0]
    copies = []
    for begin in range(0, tile_x, chunk):
        for wave in range(2):
            for x in range(begin, begin + chunk):
                _, values = new_stress(strain, stress, scaled_lame, scaled_shear, wave, x, tile_y)
                if wave == 0:
                    first = (x_start + x) * (width_y * depth)
                    added = jnp.where(in_layer == -first, source_amp[0], 0.0)
                    values[:3] = [value + added for value in values[:3]]
                for part in range(6):
                    values_now[6 * wave + part, x] = values[part]
            layers = pl.ds(begin, chunk)
            copy = pltpu.make_async_copy(
                values_now.at[pl.ds(6 * wave, 6), layers],
                outputs[wave].at[pl.ds(3, 6), layers],
                sems.at[len(copies)],
            )
            copy.start()
            copies.append(copy)
    for copy in copies:
        copy.wait()


def sum_kernel(chunk, mine, other, total, total_now, sems):
    copies = []
    for part in range(mine.shape[0]):
        for begin in range(0, mine.shape[1], chunk):
            layers = pl.ds(begin, chunk)
            total_now[part, layers] = mine[part, layers] + other[part, layers]
            copy = pltpu.make_async_copy(
                total_now.at[part, layers], total.at[part, layers], sems.at[len(copies)]
            )
            copy.start()
            copies.append(copy)
    for copy in copies:
        copy.wait()


def in_hbm(value):
    return pltpu.with_memory_space_constraint(value, pltpu.HBM)


def cost(flops, size):
    return pl.CostEstimate(flops=flops, bytes_accessed=size, transcendentals=0)


def body(
    forward_fields,
    adjoint_fields,
    lame_lambda,
    shear_modulus,
    density,
    source_cell,
    source_amp,
    receiver_cell,
    residual_amp,
):
    _, _, tile_x, tile_y, depth = forward_fields.shape
    forward = forward_fields.reshape(forward_fields.shape[1:])
    adjoint = adjoint_fields.reshape(adjoint_fields.shape[1:])
    sizes = {name: lax.axis_size(name) for name in ("tx", "ty")}
    width_y = tile_y * sizes["ty"]
    links_x, links_y = links_of(sizes)
    cells = tile_x * tile_y * depth

    def buffers(dim):
        return pltpu.VMEM((2, SLOTS, tile_y if dim == 0 else tile_x, depth), jnp.float32)

    def tile(*lead):
        return pltpu.VMEM((*lead, tile_x, tile_y, depth), jnp.float32)

    def padded(parts):
        return pltpu.VMEM(
            (parts, tile_x + 2 * LAYERS, tile_y + 2 * ROWS, depth), jnp.float32
        )

    def exchange(links, sends):
        return [swap(send, axis, first) for (axis, _, first), send in zip(links, sends)]

    def shapes(links):
        return [buffers(dim) for _, dim, _ in links]

    links = links_y + links_x
    count, count_x, count_y = len(links), len(links_x), len(links_y)
    rows = tile_x * tile_y + 3 * (tile_x + tile_y)
    source = source_cell, source_amp

    *sends, density_rows = pl.pallas_call(
        functools.partial(early_pack_kernel, links_x),
        out_shape=shapes(links_x) + [pltpu.VMEM((2, tile_x, depth), jnp.float32)],
        in_specs=[hbm] * 3,
        out_specs=[vmem] * (count_x + 1),
        scratch_shapes=[pltpu.SemaphoreType.DMA((2 + 2 * SLOTS * count_x,))],
        compiler_params=params,
        cost_estimate=cost(0, 4 * cells),
        name="early_pack",
    )(*(in_hbm(x) for x in (forward, adjoint, density)))
    halos_x = exchange(links_x, sends)
    halos_y = []
    if links_y:
        sends = pl.pallas_call(
            functools.partial(pack_kernel, links_y),
            out_shape=shapes(links_y),
            in_specs=[vmem] * 3,
            out_specs=[vmem] * count_y,
            compiler_params=params,
            cost_estimate=cost(0, 2 * 2 * SLOTS * count_y * tile_x * depth * 4),
            name="pack",
        )(forward, adjoint, density_rows)
        halos_y = exchange(links_y, sends)

    stress, velocity, accel, rim_added, buoyancy, scaled_lame, scaled_shear = pl.pallas_call(
        functools.partial(velocity_kernel, width_y),
        out_shape=[
            padded(12),
            padded(6),
            tile(3),
            pltpu.VMEM((2, 3, max(tile_x, tile_y), depth), jnp.float32),
            tile(),
            tile(),
            tile(),
        ],
        in_specs=[hbm] * 3 + [vmem] * 4,
        out_specs=[vmem] * 7,
        scratch_shapes=[
            pltpu.VMEM((rows, depth), jnp.float32),
            tile(6),
            tile(),
            tile(),
            tile(),
            pltpu.SemaphoreType.DMA((3,)),
        ],
        compiler_params=params,
        cost_estimate=cost(200 * cells, 18 * 4 * cells),
        name="velocity",
    )(
        *(in_hbm(x) for x in (lame_lambda, shear_modulus, density)),
        receiver_cell,
        residual_amp,
        forward,
        adjoint,
    )

    def boundary(links, send_links, halos, velocity, name):
        velocity, *sends = pl.pallas_call(
            functools.partial(boundary_kernel, links, send_links),
            out_shape=[padded(6)] + shapes(send_links),
            in_specs=[vmem] * (len(links) + 3),
            out_specs=[vmem] * (1 + len(send_links)),
            input_output_aliases={len(links) + 2: 0},
            compiler_params=params,
            cost_estimate=cost(cells, 10 * 2 * tile_x * depth * 4),
            name=name,
        )(*halos, rim_added, buoyancy, velocity)
        return velocity, exchange(send_links, sends)

    later_y = links_y[::-1]
    velocity, velocity_halos_y = boundary(links_x, later_y, halos_x, velocity, "boundary_x")
    velocity, velocity_halos_x = boundary(links_y, links_x, halos_y, velocity, "boundary_y")
    halos = halos_y + halos_x
    later_links = later_y + links_x
    later_halos = halos_y[::-1] + halos_x
    velocity_halos = velocity_halos_y + velocity_halos_x

    out_shape = jax.ShapeDtypeStruct(forward.shape, jnp.float32)
    strain, gradient, _, forward_next, adjoint_next, *missing = pl.pallas_call(
        functools.partial(strain_kernel, links, width_y),
        out_shape=[tile(12), tile(3), padded(6), out_shape, out_shape] + shapes(links),
        in_specs=[vmem] * count + [smem] * 2 + [vmem] * 5,
        out_specs=[vmem] * 3 + [hbm] * 2 + [vmem] * count,
        input_output_aliases={count + 5: 2},
        scratch_shapes=[tile(3), pltpu.SemaphoreType.DMA((6,))],
        compiler_params=params,
        cost_estimate=cost(200 * cells, 18 * 4 * cells),
        name="strain",
    )(*halos, *source, rim_added, buoyancy, accel, velocity, stress)
    missing = missing[:count_y][::-1] + missing[count_y:]

    strain, gradient = pl.pallas_call(
        functools.partial(gradient_kernel, later_links),
        out_shape=[tile(12), tile(3)],
        in_specs=[vmem] * (3 * count + 5),
        out_specs=[vmem] * 2,
        input_output_aliases={3 * count + 3: 0, 3 * count + 4: 1},
        compiler_params=params,
        cost_estimate=cost(30 * cells, 2 * 4 * cells),
        name="gradient",
    )(*velocity_halos, *later_halos, *missing, stress, scaled_lame, scaled_shear, strain, gradient)
    other = lax.ppermute(gradient, "shot", [(0, 1), (1, 0)])

    chunk = 4 if tile_x % 4 == 0 else 1
    forward_next, adjoint_next = pl.pallas_call(
        functools.partial(output_kernel, chunk, width_y),
        out_shape=[out_shape, out_shape],
        in_specs=[smem] * 2 + [vmem] * 4 + [hbm] * 2,
        out_specs=[hbm] * 2,
        input_output_aliases={6: 0, 7: 1},
        scratch_shapes=[tile(12), pltpu.SemaphoreType.DMA((2 * tile_x // chunk,))],
        compiler_params=params,
        cost_estimate=cost(60 * cells, 18 * 4 * cells),
        name="outputs",
    )(*source, strain, stress, scaled_lame, scaled_shear, forward_next, adjoint_next)
    total = pl.pallas_call(
        functools.partial(sum_kernel, chunk),
        out_shape=jax.ShapeDtypeStruct((3, tile_x, tile_y, depth), jnp.float32),
        in_specs=[vmem] * 2,
        out_specs=hbm,
        scratch_shapes=[tile(3), pltpu.SemaphoreType.DMA((3 * tile_x // chunk,))],
        compiler_params=params,
        cost_estimate=cost(3 * cells, 9 * 4 * cells),
        name="sum",
    )(gradient, other)
    return forward_next[None], adjoint_next[None], total


def solution(mesh):
    return jax.shard_map(
        body,
        mesh=mesh,
        in_specs=(
            P("shot", None, "tx", "ty", None),
            P("shot", None, "tx", "ty", None),
            P("tx", "ty", None),
            P("tx", "ty", None),
            P("tx", "ty", None),
            P("shot"),
            P("shot"),
            P("shot", None),
            P("shot", None),
        ),
        out_specs=(
            P("shot", None, "tx", "ty", None),
            P("shot", None, "tx", "ty", None),
            P(None, "tx", "ty", None),
        ),
        check_vma=False,
    )
```

```python
import functools

import jax
import jax.numpy as jnp
from jax import lax
from jax.experimental import pallas as pl
from jax.experimental.pallas import tpu as pltpu
from jax.sharding import PartitionSpec as P

near = 9.0 / 8.0
far = -1.0 / 24.0
time_step = 0.15

LAYERS = 2
ROWS = 8
SLOTS = 5

STRESS_ALONG = ((0, 3, 4), (1, 3, 5))
ACCEL_OF = ((0, 1, 2), (1, 0, 2))
VELOCITY_ALONG = ((0, 1, 2), (1, 0, 2))
STRAIN_OF = ((0, 3, 4), (1, 3, 5))

vmem = pl.BlockSpec(memory_space=pltpu.VMEM)
smem = pl.BlockSpec(memory_space=pltpu.SMEM)
hbm = pl.BlockSpec(memory_space=pltpu.HBM)
params = pltpu.CompilerParams(vmem_limit_bytes=24 * 1024 * 1024)


def links_of(sizes):
    along_x = (("tx", 0, 1), ("tx", 0, 0))
    along_y = (("ty", 1, 1), ("ty", 1, 0))
    return [[link for link in order if link[2] + 1 < sizes[link[0]]] for order in (along_x, along_y)]


def swap(value, axis, first):
    pairs = [(i, i + 1) for i in range(first, lax.axis_size(axis) - 1, 2)]
    return lax.ppermute(value, axis, pairs + [(j, i) for i, j in pairs])


def is_lower(axis, first):
    return lax.axis_index(axis) % 2 == first


def has_peer(axis, first):
    index = lax.axis_index(axis)
    partner = jnp.where(is_lower(axis, first), index + 1, index - 1)
    return (partner >= 0) & (partner < lax.axis_size(axis))


def by_role(link, act, upper, lower):
    lower_here = is_lower(link[0], link[2])
    pl.when(lower_here)(lambda: act(lower, True))
    pl.when(jnp.logical_not(lower_here))(lambda: act(upper, False))


SPARE = SLOTS - 1


def stress_plan(dim):
    n, a, b = STRESS_ALONG[dim]
    return ((n, 0), (n, 1), (a, 0), (b, 0)), ((n, -1), (a, -2), (a, -1), (b, -2), (b, -1))


def velocity_plan(dim):
    n, a, b = VELOCITY_ALONG[dim]
    return ((n, 0), (a, 0), (a, 1), (b, 0), (b, 1)), ((n, -2), (n, -1), (a, -1), (b, -1))


def early_pack_kernel(
    links, width_y, forward, adjoint, density, receiver_cell, residual_amp, *refs
):
    sends = refs[: len(links)]
    density_rows, received, stress, cells_now, amps_now, sems = refs[len(links) :]
    tile = forward.shape[1:3]
    small = [
        pltpu.make_async_copy(source, target, sems.at[2 * SLOTS * len(links) + 2 + at])
        for at, (source, target) in enumerate(
            ((receiver_cell, cells_now), (residual_amp, amps_now))
        )
    ]
    for copy in small:
        copy.start()
    waits = []
    for row in range(2):
        copy = pltpu.make_async_copy(
            density.at[:, row, :], density_rows.at[row], sems.at[2 * SLOTS * len(links) + row]
        )
        copy.start()
        waits.append(copy)

    def layer(ref, dim, index):
        return ref.at[index] if dim == 0 else ref.at[:, index, :]

    for at, (link, send) in enumerate(zip(links, sends)):
        dim = link[1]

        def semaphore(wave, slot):
            return sems.at[(2 * at + wave) * SLOTS + slot]

        def start(plan, lower):
            for wave, fields in enumerate((forward, adjoint)):
                sources = [
                    layer(fields.at[3 + part], dim, index % tile[dim]) for part, index in plan
                ]
                if not lower:
                    sources.append(layer(density, dim, wave))
                for slot, source in enumerate(sources):
                    pltpu.make_async_copy(
                        source, send.at[wave, slot], semaphore(wave, slot)
                    ).start()

        by_role(link, start, *stress_plan(dim))
        for wave in range(2):
            for slot in range(SLOTS):
                waits.append(
                    pltpu.make_async_copy(
                        layer(density, dim, 0), send.at[wave, slot], semaphore(wave, slot)
                    )
                )
    for wave in range(2):
        clear_rim(
            stress, *([6 * wave + part for part in STRESS_ALONG[dim]] for dim in range(2))
        )
    columns = column_ids(*tile, width_y, forward.shape[-1])
    for copy in small:
        copy.wait()
    received[...] = receiver_sum(cells_now[...], amps_now[...], columns)
    for copy in waits:
        copy.wait()


def pack_kernel(links, forward, adjoint, density_rows, *sends):
    for link, send in zip(links, sends):
        dim = link[1]

        def put(plan, lower):
            for wave, fields in enumerate((forward, adjoint)):
                for slot, (part, index) in enumerate(plan):
                    send[wave, slot] = face(fields, 3 + part, dim, index, False)[...]
                if not lower:
                    send[wave, SPARE] = density_rows[wave]

        by_role(link, put, *stress_plan(dim))


def send_velocities(links, velocity, buoyancy, sends):
    for link, send in zip(links, sends):
        dim = link[1]

        def put(plan, lower):
            for wave in range(2):
                for slot, (part, index) in enumerate(plan):
                    send[wave, slot] = face(velocity, 3 * wave + part, dim, index, True)[...]
                if lower:
                    send[wave, SPARE] = light_face(buoyancy, dim, -1 - wave)

        by_role(link, put, *velocity_plan(dim))


def column_ids(tile_x, tile_y, width_y, lanes):
    x_start = lax.axis_index("tx") * tile_x
    y_start = lax.axis_index("ty") * tile_y

    def column(x, y):
        inside = (y >= 0) & (y < width_y)
        return jnp.where(inside, x * width_y + y, -1)

    def iota(shape, dim):
        return lax.broadcasted_iota(jnp.int32, shape, dim)

    shape = (tile_x, tile_y, lanes)
    tile = column(x_start + iota(shape, 0), y_start + iota(shape, 1))
    shape = (3, tile_y, lanes)
    layer = iota(shape, 0)
    along_x = column(
        x_start + jnp.where(layer == 0, -1, tile_x - 1 + layer), y_start + iota(shape, 1)
    )
    shape = (3, tile_x, lanes)
    layer = iota(shape, 0)
    along_y = column(
        x_start + iota(shape, 1), y_start + jnp.where(layer == 0, -1, tile_y - 1 + layer)
    )
    return jnp.concatenate([part.reshape(-1, lanes) for part in (tile, along_x, along_y)], axis=0)


def differ(zero, one, two, minus):
    return near * (one - zero) + far * (two - minus)


def along_x(ref, part, x, tile_y, upward):
    def at(offset):
        return ref[part, x + (LAYERS + offset), pl.ds(ROWS, tile_y), :]

    return differ(at(0), at(1), at(2), at(-1)) if upward else differ(at(-1), at(0), at(1), at(-2))


def along_y(ref, part, x, tile_y, upward):
    def at(offset):
        return ref[part, x + LAYERS, pl.ds(ROWS + offset, tile_y), :]

    return differ(at(0), at(1), at(2), at(-1)) if upward else differ(at(-1), at(0), at(1), at(-2))


def along_z(ref, part, x, tile_y, upward):
    value = ref[part, x + LAYERS, pl.ds(ROWS, tile_y), :]
    depth = value.shape[-1]
    lane = lax.broadcasted_iota(jnp.int32, value.shape, 1)

    def at(offset):
        if offset == 0:
            return value
        moved = pltpu.roll(value, (-offset) % depth, 1)
        inside = lane < depth - offset if offset > 0 else lane >= -offset
        return jnp.where(inside, moved, 0.0)

    return differ(at(0), at(1), at(2), at(-1)) if upward else differ(at(-1), at(0), at(1), at(-2))


def clear_rim(ref, parts_x, parts_y):
    _, layers, rows, depth = ref.shape
    tile_x, tile_y = layers - 2 * LAYERS, rows - 2 * ROWS
    for part in parts_x:
        for begin in (0, LAYERS + tile_x):
            ref[part, pl.ds(begin, LAYERS), pl.ds(ROWS, tile_y), :] = jnp.zeros(
                (LAYERS, tile_y, depth), jnp.float32
            )
    for part in parts_y:
        for begin in (0, ROWS + tile_y):
            ref[part, pl.ds(LAYERS, tile_x), pl.ds(begin, ROWS), :] = jnp.zeros(
                (tile_x, ROWS, depth), jnp.float32
            )


def receiver_sum(cells, amps, columns):
    depth, receivers = columns.shape[-1], cells.shape[-1]
    column = lax.div(cells, depth)
    level = cells - column * depth
    column_hot = jnp.concatenate(
        [
            (columns == column[:, begin : begin + depth]).astype(jnp.bfloat16)
            for begin in range(0, receivers, depth)
        ],
        axis=1,
    )
    levels = lax.broadcasted_iota(jnp.int32, (depth, receivers), 0)
    rest = jnp.where(levels == level, amps, 0.0)
    total = jnp.zeros(columns.shape, jnp.float32)
    for _ in range(3):
        part = rest.astype(jnp.bfloat16)
        rest = rest - part.astype(jnp.float32)
        total = total + lax.dot_general(
            column_hot,
            part,
            (((1,), (1,)), ((), ())),
            preferred_element_type=jnp.float32,
        )
    return total


def velocity_kernel(
    lame,
    shear,
    density,
    received,
    forward,
    adjoint,
    _,
    stress,
    velocity,
    accel,
    rim_added,
    buoyancy,
    scaled_lame,
    scaled_shear,
    gained,
    lame_now,
    shear_now,
    density_now,
    sems,
):
    tile_x, tile_y, depth = density.shape
    copies = [
        pltpu.make_async_copy(lame, lame_now, sems.at[0]),
        pltpu.make_async_copy(shear, shear_now, sems.at[1]),
        pltpu.make_async_copy(density, density_now, sems.at[2]),
    ]
    for copy in copies:
        copy.start()
    cells = tile_x * tile_y
    middle = pl.ds(ROWS, tile_y)
    for layer in range(3):
        rim_added[0, layer] = received[pl.ds(cells + layer * tile_y, tile_y), :]
        rim_added[1, layer] = received[pl.ds(cells + 3 * tile_y + layer * tile_x, tile_x), :]

    def fill(x, carry):
        extra = received[pl.ds(pl.multiple_of(x * tile_y, 8), tile_y), :]
        for wave, fields in enumerate((forward, adjoint)):
            for part in range(6):
                value = fields[3 + part, x]
                stress[6 * wave + part, x + LAYERS, middle, :] = (
                    value + extra if wave == 1 and part < 3 else value
                )
        return carry

    lax.fori_loop(0, tile_x, fill, 0, unroll=8)

    def layer(x, carry):
        for wave in range(2):
            xx, yy, zz, xy, xz, yz = range(6 * wave, 6 * wave + 6)
            values = (
                along_x(stress, xx, x, tile_y, True)
                + along_y(stress, xy, x, tile_y, False)
                + along_z(stress, xz, x, tile_y, False),
                along_x(stress, xy, x, tile_y, False)
                + along_y(stress, yy, x, tile_y, True)
                + along_z(stress, yz, x, tile_y, False),
                along_x(stress, xz, x, tile_y, False)
                + along_y(stress, yz, x, tile_y, False)
                + along_z(stress, zz, x, tile_y, True),
            )
            for part, value in enumerate(values):
                gained[3 * wave + part, x] = value
        return carry

    lax.fori_loop(0, tile_x, layer, 0, unroll=8)
    for copy in copies:
        copy.wait()

    def finish(x, carry):
        light = 1.0 / density_now[x]
        buoyancy[x] = light
        scaled_lame[x] = time_step * lame_now[x]
        scaled_shear[x] = time_step * shear_now[x]
        for wave, fields in enumerate((forward, adjoint)):
            for part in range(3):
                value = light * gained[3 * wave + part, x]
                if wave == 0:
                    accel[part, x] = value
                velocity[3 * wave + part, x + LAYERS, middle, :] = (
                    fields[part, x] + time_step * value
                )
        return carry

    lax.fori_loop(0, tile_x, finish, 0, unroll=8)


def stress_halo_terms(links, received, rim_added, waves, add):
    for link, halo in zip(links, received):
        dim = link[1]
        part_n, part_a, part_b = ACCEL_OF[dim]

        def normal(wave, slot, layer):
            value = halo[wave, slot]
            return value + rim_added[dim, layer] if wave == 1 else value

        def after():
            for wave in waves:
                n0, n1 = normal(wave, 0, 1), normal(wave, 1, 2)
                add(wave, part_n, dim, -1, near * n0 + far * n1)
                add(wave, part_n, dim, -2, far * n0)
                add(wave, part_a, dim, -1, far * halo[wave, 2])
                add(wave, part_b, dim, -1, far * halo[wave, 3])

        def before():
            for wave in waves:
                add(wave, part_n, dim, 0, -far * normal(wave, 0, 0))
                for part, slot in ((part_a, 1), (part_b, 3)):
                    outer, inner = halo[wave, slot], halo[wave, slot + 1]
                    add(wave, part, dim, 0, -near * inner - far * outer)
                    add(wave, part, dim, 1, -far * inner)

        real = has_peer(link[0], link[2])
        lower = is_lower(link[0], link[2])
        pl.when(real & lower)(after)
        pl.when(real & jnp.logical_not(lower))(before)


def source_gain(cell, part, x, y, z, width_y):
    depth = z.shape[-1]
    column = lax.div(cell, depth)
    source_x = lax.div(column, width_y)
    away = [source_x - x, column - source_x * width_y - y, cell - column * depth - z]
    along = away.pop(part)
    gain = jnp.where(along == 0, -near, 0.0)
    for offset, value in ((1, near), (2, far), (-1, -far)):
        gain = jnp.where(along == offset, value, gain)
    return jnp.where((away[0] == 0) & (away[1] == 0), gain, 0.0)


def start_of(tile_x, tile_y):
    return lax.axis_index("tx") * tile_x, lax.axis_index("ty") * tile_y


def missing_terms(links, stress, source, width_y, missing):
    cell, amp = source
    layers, rows, depth = stress.shape[1:]
    tile = layers - 2 * LAYERS, rows - 2 * ROWS
    starts = start_of(*tile)
    for link, out in zip(links, missing):
        dim = link[1]
        shape = out.shape[2:]
        cross = starts[1 - dim] + lax.broadcasted_iota(jnp.int32, shape, 0)
        level = lax.broadcasted_iota(jnp.int32, shape, 1)

        def own(wave, part, index):
            return face(stress, 6 * wave + STRESS_ALONG[dim][part], dim, index, True)[...]

        def put(slots):
            for wave in range(2):
                for slot, (part, layer, terms) in enumerate(slots):
                    value = terms(wave) if dim == 1 else jnp.zeros(shape, jnp.float32)
                    if wave == 0:
                        here = jnp.full(shape, starts[dim] + layer, jnp.int32)
                        x, y = (here, cross) if dim == 0 else (cross, here)
                        value += amp * source_gain(
                            cell, VELOCITY_ALONG[dim][part], x, y, level, width_y
                        )
                    out[wave, slot] = value

        def after():
            count = tile[dim]
            slots = [(0, count, lambda wave: -far * own(wave, 0, -1))]
            for part in (1, 2):
                slots += [
                    (
                        part,
                        count,
                        lambda wave, part=part: -near * own(wave, part, -1)
                        - far * own(wave, part, -2),
                    ),
                    (part, count + 1, lambda wave, part=part: -far * own(wave, part, -1)),
                ]
            put(slots)

        def before():
            put([
                (0, -2, lambda wave: far * own(wave, 0, 0)),
                (0, -1, lambda wave: near * own(wave, 0, 0) + far * own(wave, 0, 1)),
                (1, -1, lambda wave: far * own(wave, 1, 0)),
                (2, -1, lambda wave: far * own(wave, 2, 0)),
            ])

        lower = is_lower(link[0], link[2])
        pl.when(lower)(after)
        pl.when(jnp.logical_not(lower))(before)


def velocity_halo_terms(links, received, stresses, missing, add):
    for link, halo, stress_halo, lack in zip(links, received, stresses, missing):
        dim = link[1]
        part_n, part_a, part_b = STRAIN_OF[dim]

        def after():
            lights = [time_step / stress_halo[layer, SPARE] for layer in range(2)]
            for wave in range(2):

                def whole(slot, layer):
                    return halo[wave, slot] + lights[layer] * lack[wave, slot]

                add(wave, part_n, dim, -1, far * whole(0, 0))
                for part, slot in ((part_a, 1), (part_b, 3)):
                    inner, outer = whole(slot, 0), whole(slot + 1, 1)
                    add(wave, part, dim, -1, near * inner + far * outer)
                    add(wave, part, dim, -2, far * inner)

        def before():
            lights = [time_step * halo[layer, SPARE] for layer in range(2)]
            for wave in range(2):

                def whole(slot, layer):
                    return halo[wave, slot] + lights[layer] * lack[wave, slot]

                outer, inner = whole(0, 1), whole(1, 0)
                add(wave, part_n, dim, 0, -near * inner - far * outer)
                add(wave, part_n, dim, 1, -far * inner)
                add(wave, part_a, dim, 0, -far * whole(2, 0))
                add(wave, part_b, dim, 0, -far * whole(3, 0))

        real = has_peer(link[0], link[2])
        lower = is_lower(link[0], link[2])
        pl.when(real & lower)(after)
        pl.when(real & jnp.logical_not(lower))(before)


def face(ref, part, dim, index, padded):
    layers, rows, depth = ref.shape[1:]
    tile_x = layers - 2 * LAYERS if padded else layers
    tile_y = rows - 2 * ROWS if padded else rows
    if dim == 0:
        at = index % tile_x
        if padded:
            return ref.at[part, at + LAYERS, pl.ds(ROWS, tile_y), :]
        return ref.at[part, at]
    at = index % tile_y
    flat = ref.reshape(ref.shape[0], layers * rows, depth)
    begin = LAYERS * rows + ROWS + at if padded else at
    return flat.at[part, pl.ds(begin, tile_x, stride=rows), :]


def light_face(buoyancy, dim, index):
    layers, rows, depth = buoyancy.shape
    if dim == 0:
        return buoyancy[index % layers]
    return buoyancy.reshape(layers * rows, depth)[pl.ds(index % rows, layers, stride=rows), :]


def boundary_kernel(links, send_links, *refs):
    count = len(links)
    received = refs[:count]
    rim_added, buoyancy, _, velocity = refs[count : count + 4]
    sends = refs[count + 4 :]

    def add(wave, part, dim, index, term):
        target = face(velocity, 3 * wave + part, dim, index, True)
        target[...] += time_step * light_face(buoyancy, dim, index) * term

    stress_halo_terms(links, received, rim_added, (0, 1), add)
    send_velocities(send_links, velocity, buoyancy, sends)


def strain_kernel(links, width_y, *refs):
    count = len(links)
    received = refs[:count]
    source_cell, source_amp, rim_added, buoyancy, accel = refs[count : count + 5]
    stress = refs[count + 6]
    strain, gradient, velocity = refs[count + 7 : count + 10]
    outputs, missing = refs[count + 10 : count + 12], refs[count + 12 : 2 * count + 12]
    accel_now, sems = refs[2 * count + 12 :]
    tile_x, tile_y, depth = buoyancy.shape
    middle = pl.ds(ROWS, tile_y)
    clear_rim(velocity, range(6), range(6))
    accel_now[...] = accel[...]

    def add(wave, part, dim, index, term):
        target = face(accel_now, part, dim, index, False)
        target[...] += light_face(buoyancy, dim, index) * term

    stress_halo_terms(links, received, rim_added, (0,), add)
    x_start, y_start = start_of(tile_x, tile_y)
    cell, amp = source_cell[0], source_amp[0]
    source_x = lax.div(cell, width_y * depth)
    y = y_start + lax.broadcasted_iota(jnp.int32, (tile_y, depth), 0)
    level = lax.broadcasted_iota(jnp.int32, (tile_y, depth), 1)
    for offset in (-2, -1, 0, 1):
        x = source_x + offset - x_start

        @pl.when((x >= 0) & (x < tile_x))
        def add_source():
            here = jnp.full((tile_y, depth), source_x + offset, jnp.int32)
            for part in range(3):
                gain = source_gain(cell, part, here, y, level, width_y)
                value = amp * buoyancy[x] * gain
                accel_now[part, x] += value
                velocity[part, x + LAYERS, middle, :] += time_step * value

    copies = [
        pltpu.make_async_copy(
            velocity.at[3 * wave + part, pl.ds(LAYERS, tile_x), middle, :],
            outputs[wave].at[part],
            sems.at[3 * wave + part],
        )
        for wave in range(2)
        for part in range(3)
    ]
    for copy in copies:
        copy.start()
    def layer(x, carry):
        for wave in range(2):
            vx, vy, vz = range(3 * wave, 3 * wave + 3)
            values = (
                along_x(velocity, vx, x, tile_y, False),
                along_y(velocity, vy, x, tile_y, False),
                along_z(velocity, vz, x, tile_y, False),
                along_y(velocity, vx, x, tile_y, True) + along_x(velocity, vy, x, tile_y, True),
                along_z(velocity, vx, x, tile_y, True) + along_x(velocity, vz, x, tile_y, True),
                along_z(velocity, vy, x, tile_y, True) + along_y(velocity, vz, x, tile_y, True),
            )
            for part, value in enumerate(values):
                strain[6 * wave + part, x] = value
        total = sum(
            accel_now[part, x] * velocity[3 + part, x + LAYERS, middle, :] for part in range(3)
        )
        gradient[2, x] = -time_step * total
        return carry

    lax.fori_loop(0, tile_x, layer, 0, unroll=8)
    missing_terms(links, stress, (cell, amp), width_y, missing)
    for copy in copies:
        copy.wait()


def new_stress(strain, stress, scaled_lame, scaled_shear, wave, x, tile_y):
    lame, shear = scaled_lame[x], scaled_shear[x]
    strains = [strain[6 * wave + part, x] for part in range(6)]
    volume = lame * (strains[0] + strains[1] + strains[2])
    values = []
    for part in range(6):
        old = stress[6 * wave + part, x + LAYERS, pl.ds(ROWS, tile_y), :]
        if part < 3:
            values.append(old + (volume + 2.0 * shear * strains[part]))
        else:
            values.append(old + shear * strains[part])
    return strains, values


def gradient_kernel(links, inner, *refs):
    count = len(links)
    received, stresses, missing = (refs[at : at + count] for at in range(0, 3 * count, count))
    stress, scaled_lame, scaled_shear, _, _, strain, gradient = refs[3 * count :]
    tile_x, tile_y, _ = scaled_lame.shape
    first, last = min(2, tile_x), max(2, tile_x - 2)

    def add(wave, part, dim, index, term):
        target = face(strain, 6 * wave + part, dim, index, False)
        target[...] += term

    velocity_halo_terms(links, received, stresses, missing, add)

    def layer(x, carry):
        strains = [strain[part, x] for part in range(6)]
        _, values = new_stress(strain, stress, scaled_lame, scaled_shear, 1, x, tile_y)
        trace = strains[0] + strains[1] + strains[2]
        gradient[0, x] = -time_step * trace * (values[0] + values[1] + values[2])
        total = sum(left * right for left, right in zip(strains, values))
        gradient[1, x] = -time_step * total
        return carry

    if inner:
        if last > first:
            lax.fori_loop(first, last, layer, 0, unroll=4)
    else:
        for x in (*range(first), *range(last, tile_x)):
            layer(x, 0)


def output_kernel(
    chunk, width_y, source_cell, source_amp, strain, stress, scaled_lame, scaled_shear, *refs
):
    outputs, (values_now, sems) = refs[2:4], refs[4:]
    tile_x, tile_y, depth = scaled_lame.shape
    x_start, y_start = start_of(tile_x, tile_y)
    y = y_start + lax.broadcasted_iota(jnp.int32, (tile_y, depth), 0)
    level = lax.broadcasted_iota(jnp.int32, (tile_y, depth), 1)
    in_layer = y * depth + level - source_cell[0]
    copies = []
    for begin in range(0, tile_x, chunk):
        for wave in range(2):
            for x in range(begin, begin + chunk):
                _, values = new_stress(strain, stress, scaled_lame, scaled_shear, wave, x, tile_y)
                if wave == 0:
                    first = (x_start + x) * (width_y * depth)
                    added = jnp.where(in_layer == -first, source_amp[0], 0.0)
                    values[:3] = [value + added for value in values[:3]]
                for part in range(6):
                    values_now[6 * wave + part, x] = values[part]
            layers = pl.ds(begin, chunk)
            copy = pltpu.make_async_copy(
                values_now.at[pl.ds(6 * wave, 6), layers],
                outputs[wave].at[pl.ds(3, 6), layers],
                sems.at[len(copies)],
            )
            copy.start()
            copies.append(copy)
    for copy in copies:
        copy.wait()


def sum_kernel(chunk, mine, other, total, total_now, sems):
    copies = []
    for part in range(mine.shape[0]):
        for begin in range(0, mine.shape[1], chunk):
            layers = pl.ds(begin, chunk)
            total_now[part, layers] = mine[part, layers] + other[part, layers]
            copy = pltpu.make_async_copy(
                total_now.at[part, layers], total.at[part, layers], sems.at[len(copies)]
            )
            copy.start()
            copies.append(copy)
    for copy in copies:
        copy.wait()


def in_hbm(value):
    return pltpu.with_memory_space_constraint(value, pltpu.HBM)


def cost(flops, size):
    return pl.CostEstimate(flops=flops, bytes_accessed=size, transcendentals=0)


def body(
    forward_fields,
    adjoint_fields,
    lame_lambda,
    shear_modulus,
    density,
    source_cell,
    source_amp,
    receiver_cell,
    residual_amp,
):
    _, _, tile_x, tile_y, depth = forward_fields.shape
    forward = forward_fields.reshape(forward_fields.shape[1:])
    adjoint = adjoint_fields.reshape(adjoint_fields.shape[1:])
    sizes = {name: lax.axis_size(name) for name in ("tx", "ty")}
    width_y = tile_y * sizes["ty"]
    links_x, links_y = links_of(sizes)
    cells = tile_x * tile_y * depth

    def buffers(dim):
        return pltpu.VMEM((2, SLOTS, tile_y if dim == 0 else tile_x, depth), jnp.float32)

    def tile(*lead):
        return pltpu.VMEM((*lead, tile_x, tile_y, depth), jnp.float32)

    def padded(parts):
        return pltpu.VMEM(
            (parts, tile_x + 2 * LAYERS, tile_y + 2 * ROWS, depth), jnp.float32
        )

    def exchange(links, sends):
        return [swap(send, axis, first) for (axis, _, first), send in zip(links, sends)]

    def shapes(links):
        return [buffers(dim) for _, dim, _ in links]

    links = links_y + links_x
    count, count_x, count_y = len(links), len(links_x), len(links_y)
    rows = tile_x * tile_y + 3 * (tile_x + tile_y)
    source = source_cell, source_amp

    receivers = receiver_cell.shape[-1]
    *sends, density_rows, received, stress = pl.pallas_call(
        functools.partial(early_pack_kernel, links_x, width_y),
        out_shape=shapes(links_x)
        + [
            pltpu.VMEM((2, tile_x, depth), jnp.float32),
            pltpu.VMEM((rows, depth), jnp.float32),
            padded(12),
        ],
        in_specs=[hbm] * 5,
        out_specs=[vmem] * (count_x + 3),
        scratch_shapes=[
            pltpu.VMEM((1, receivers), jnp.int32),
            pltpu.VMEM((1, receivers), jnp.float32),
            pltpu.SemaphoreType.DMA((4 + 2 * SLOTS * count_x,)),
        ],
        compiler_params=params,
        cost_estimate=cost(0, 4 * cells),
        name="early_pack",
    )(*(in_hbm(x) for x in (forward, adjoint, density, receiver_cell, residual_amp)))
    halos_x = exchange(links_x, sends)
    halos_y = []
    if links_y:
        sends = pl.pallas_call(
            functools.partial(pack_kernel, links_y),
            out_shape=shapes(links_y),
            in_specs=[vmem] * 3,
            out_specs=[vmem] * count_y,
            compiler_params=params,
            cost_estimate=cost(0, 2 * 2 * SLOTS * count_y * tile_x * depth * 4),
            name="pack",
        )(forward, adjoint, density_rows)
        halos_y = exchange(links_y, sends)

    stress, velocity, accel, rim_added, buoyancy, scaled_lame, scaled_shear = pl.pallas_call(
        velocity_kernel,
        out_shape=[
            padded(12),
            padded(6),
            tile(3),
            pltpu.VMEM((2, 3, max(tile_x, tile_y), depth), jnp.float32),
            tile(),
            tile(),
            tile(),
        ],
        in_specs=[hbm] * 3 + [vmem] * 4,
        out_specs=[vmem] * 7,
        input_output_aliases={6: 0},
        scratch_shapes=[
            tile(6),
            tile(),
            tile(),
            tile(),
            pltpu.SemaphoreType.DMA((3,)),
        ],
        compiler_params=params,
        cost_estimate=cost(200 * cells, 18 * 4 * cells),
        name="velocity",
    )(
        *(in_hbm(x) for x in (lame_lambda, shear_modulus, density)),
        received,
        forward,
        adjoint,
        stress,
    )

    def boundary(links, send_links, halos, velocity, name):
        velocity, *sends = pl.pallas_call(
            functools.partial(boundary_kernel, links, send_links),
            out_shape=[padded(6)] + shapes(send_links),
            in_specs=[vmem] * (len(links) + 3),
            out_specs=[vmem] * (1 + len(send_links)),
            input_output_aliases={len(links) + 2: 0},
            compiler_params=params,
            cost_estimate=cost(cells, 10 * 2 * tile_x * depth * 4),
            name=name,
        )(*halos, rim_added, buoyancy, velocity)
        return velocity, exchange(send_links, sends)

    later_y = links_y[::-1]
    velocity, velocity_halos_y = boundary(links_x, later_y, halos_x, velocity, "boundary_x")
    velocity, velocity_halos_x = boundary(links_y, links_x, halos_y, velocity, "boundary_y")
    halos = halos_y + halos_x

    out_shape = jax.ShapeDtypeStruct(forward.shape, jnp.float32)
    strain, gradient, _, forward_next, adjoint_next, *missing = pl.pallas_call(
        functools.partial(strain_kernel, links, width_y),
        out_shape=[tile(12), tile(3), padded(6), out_shape, out_shape] + shapes(links),
        in_specs=[vmem] * count + [smem] * 2 + [vmem] * 5,
        out_specs=[vmem] * 3 + [hbm] * 2 + [vmem] * count,
        input_output_aliases={count + 5: 2},
        scratch_shapes=[tile(3), pltpu.SemaphoreType.DMA((6,))],
        compiler_params=params,
        cost_estimate=cost(200 * cells, 18 * 4 * cells),
        name="strain",
    )(*halos, *source, rim_added, buoyancy, accel, velocity, stress)

    def gradients(links, inner, received, stresses, missing, strain, gradient, name):
        return pl.pallas_call(
            functools.partial(gradient_kernel, links, inner),
            out_shape=[tile(12), tile(3)],
            in_specs=[vmem] * (3 * len(links) + 5),
            out_specs=[vmem] * 2,
            input_output_aliases={3 * len(links) + 3: 0, 3 * len(links) + 4: 1},
            compiler_params=params,
            cost_estimate=cost(30 * cells, 2 * 4 * cells),
            name=name,
        )(*received, *stresses, *missing, stress, scaled_lame, scaled_shear, strain, gradient)

    strain, gradient = gradients(
        later_y,
        True,
        velocity_halos_y,
        halos_y[::-1],
        missing[:count_y][::-1],
        strain,
        gradient,
        "gradient_inner",
    )
    strain, gradient = gradients(
        links_x, False, velocity_halos_x, halos_x, missing[count_y:], strain, gradient, "gradient"
    )
    other = lax.ppermute(gradient, "shot", [(0, 1), (1, 0)])

    chunk = 4 if tile_x % 4 == 0 else 1
    forward_next, adjoint_next = pl.pallas_call(
        functools.partial(output_kernel, chunk, width_y),
        out_shape=[out_shape, out_shape],
        in_specs=[smem] * 2 + [vmem] * 4 + [hbm] * 2,
        out_specs=[hbm] * 2,
        input_output_aliases={6: 0, 7: 1},
        scratch_shapes=[tile(12), pltpu.SemaphoreType.DMA((2 * tile_x // chunk,))],
        compiler_params=params,
        cost_estimate=cost(60 * cells, 18 * 4 * cells),
        name="outputs",
    )(*source, strain, stress, scaled_lame, scaled_shear, forward_next, adjoint_next)
    total = pl.pallas_call(
        functools.partial(sum_kernel, tile_x),
        out_shape=jax.ShapeDtypeStruct((3, tile_x, tile_y, depth), jnp.float32),
        in_specs=[vmem] * 2,
        out_specs=hbm,
        scratch_shapes=[tile(3), pltpu.SemaphoreType.DMA((3,))],
        compiler_params=params,
        cost_estimate=cost(3 * cells, 9 * 4 * cells),
        name="sum",
    )(gradient, other)
    return forward_next[None], adjoint_next[None], total


def solution(mesh):
    return jax.shard_map(
        body,
        mesh=mesh,
        in_specs=(
            P("shot", None, "tx", "ty", None),
            P("shot", None, "tx", "ty", None),
            P("tx", "ty", None),
            P("tx", "ty", None),
            P("tx", "ty", None),
            P("shot"),
            P("shot"),
            P("shot", None),
            P("shot", None),
        ),
        out_specs=(
            P("shot", None, "tx", "ty", None),
            P("shot", None, "tx", "ty", None),
            P(None, "tx", "ty", None),
        ),
        check_vma=False,
    )
```

```python
import functools

import jax
import jax.numpy as jnp
from jax import lax
from jax.experimental import pallas as pl
from jax.experimental.pallas import tpu as pltpu
from jax.sharding import PartitionSpec as P

near = 9.0 / 8.0
far = -1.0 / 24.0
time_step = 0.15

LAYERS = 2
ROWS = 8
SLOTS = 5

STRESS_ALONG = ((0, 3, 4), (1, 3, 5))
ACCEL_OF = ((0, 1, 2), (1, 0, 2))
VELOCITY_ALONG = ((0, 1, 2), (1, 0, 2))
STRAIN_OF = ((0, 3, 4), (1, 3, 5))

vmem = pl.BlockSpec(memory_space=pltpu.VMEM)
smem = pl.BlockSpec(memory_space=pltpu.SMEM)
hbm = pl.BlockSpec(memory_space=pltpu.HBM)
params = pltpu.CompilerParams(vmem_limit_bytes=24 * 1024 * 1024)


def links_of(sizes):
    along_x = (("tx", 0, 1), ("tx", 0, 0))
    along_y = (("ty", 1, 1), ("ty", 1, 0))
    return [[link for link in order if link[2] + 1 < sizes[link[0]]] for order in (along_x, along_y)]


def swap(value, axis, first):
    pairs = [(i, i + 1) for i in range(first, lax.axis_size(axis) - 1, 2)]
    return lax.ppermute(value, axis, pairs + [(j, i) for i, j in pairs])


def is_lower(axis, first):
    return lax.axis_index(axis) % 2 == first


def has_peer(axis, first):
    index = lax.axis_index(axis)
    partner = jnp.where(is_lower(axis, first), index + 1, index - 1)
    return (partner >= 0) & (partner < lax.axis_size(axis))


def by_role(link, act, upper, lower):
    lower_here = is_lower(link[0], link[2])
    pl.when(lower_here)(lambda: act(lower, True))
    pl.when(jnp.logical_not(lower_here))(lambda: act(upper, False))


SPARE = SLOTS - 1


def stress_plan(dim):
    n, a, b = STRESS_ALONG[dim]
    return ((n, 0), (n, 1), (a, 0), (b, 0)), ((n, -1), (a, -2), (a, -1), (b, -2), (b, -1))


def velocity_plan(dim):
    n, a, b = VELOCITY_ALONG[dim]
    return ((n, 0), (a, 0), (a, 1), (b, 0), (b, 1)), ((n, -2), (n, -1), (a, -1), (b, -1))


def early_pack_kernel(links, forward, adjoint, density, *refs):
    sends, (density_rows, stress, sems) = refs[: len(links)], refs[len(links) :]
    tile = forward.shape[1:3]
    waits = []
    for row in range(2):
        copy = pltpu.make_async_copy(
            density.at[:, row, :], density_rows.at[row], sems.at[2 * SLOTS * len(links) + row]
        )
        copy.start()
        waits.append(copy)

    def layer(ref, dim, index):
        return ref.at[index] if dim == 0 else ref.at[:, index, :]

    for at, (link, send) in enumerate(zip(links, sends)):
        dim = link[1]

        def semaphore(wave, slot):
            return sems.at[(2 * at + wave) * SLOTS + slot]

        def start(plan, lower):
            for wave, fields in enumerate((forward, adjoint)):
                sources = [
                    layer(fields.at[3 + part], dim, index % tile[dim]) for part, index in plan
                ]
                if not lower:
                    sources.append(layer(density, dim, wave))
                for slot, source in enumerate(sources):
                    pltpu.make_async_copy(
                        source, send.at[wave, slot], semaphore(wave, slot)
                    ).start()

        by_role(link, start, *stress_plan(dim))
        for wave in range(2):
            for slot in range(SLOTS):
                waits.append(
                    pltpu.make_async_copy(
                        layer(density, dim, 0), send.at[wave, slot], semaphore(wave, slot)
                    )
                )
    for wave in range(2):
        clear_rim(
            stress, *([6 * wave + part for part in STRESS_ALONG[dim]] for dim in range(2))
        )
    for copy in waits:
        copy.wait()


def pack_kernel(links, forward, adjoint, density_rows, *sends):
    for link, send in zip(links, sends):
        dim = link[1]

        def put(plan, lower):
            for wave, fields in enumerate((forward, adjoint)):
                for slot, (part, index) in enumerate(plan):
                    send[wave, slot] = face(fields, 3 + part, dim, index, False)[...]
                if not lower:
                    send[wave, SPARE] = density_rows[wave]

        by_role(link, put, *stress_plan(dim))


def send_velocities(links, velocity, buoyancy, sends):
    for link, send in zip(links, sends):
        dim = link[1]

        def put(plan, lower):
            for wave in range(2):
                for slot, (part, index) in enumerate(plan):
                    send[wave, slot] = face(velocity, 3 * wave + part, dim, index, True)[...]
                if lower:
                    send[wave, SPARE] = light_face(buoyancy, dim, -1 - wave)

        by_role(link, put, *velocity_plan(dim))


def column_ids(tile_x, tile_y, width_y, lanes):
    x_start = lax.axis_index("tx") * tile_x
    y_start = lax.axis_index("ty") * tile_y

    def column(x, y):
        inside = (y >= 0) & (y < width_y)
        return jnp.where(inside, x * width_y + y, -1)

    def iota(shape, dim):
        return lax.broadcasted_iota(jnp.int32, shape, dim)

    shape = (tile_x, tile_y, lanes)
    tile = column(x_start + iota(shape, 0), y_start + iota(shape, 1))
    shape = (3, tile_y, lanes)
    layer = iota(shape, 0)
    along_x = column(
        x_start + jnp.where(layer == 0, -1, tile_x - 1 + layer), y_start + iota(shape, 1)
    )
    shape = (3, tile_x, lanes)
    layer = iota(shape, 0)
    along_y = column(
        x_start + iota(shape, 1), y_start + jnp.where(layer == 0, -1, tile_y - 1 + layer)
    )
    return jnp.concatenate([part.reshape(-1, lanes) for part in (tile, along_x, along_y)], axis=0)


def differ(zero, one, two, minus):
    return near * (one - zero) + far * (two - minus)


def along_x(ref, part, x, tile_y, upward):
    def at(offset):
        return ref[part, x + (LAYERS + offset), pl.ds(ROWS, tile_y), :]

    return differ(at(0), at(1), at(2), at(-1)) if upward else differ(at(-1), at(0), at(1), at(-2))


def along_y(ref, part, x, tile_y, upward):
    def at(offset):
        return ref[part, x + LAYERS, pl.ds(ROWS + offset, tile_y), :]

    return differ(at(0), at(1), at(2), at(-1)) if upward else differ(at(-1), at(0), at(1), at(-2))


def along_z(ref, part, x, tile_y, upward):
    value = ref[part, x + LAYERS, pl.ds(ROWS, tile_y), :]
    depth = value.shape[-1]
    lane = lax.broadcasted_iota(jnp.int32, value.shape, 1)

    def at(offset):
        if offset == 0:
            return value
        moved = pltpu.roll(value, (-offset) % depth, 1)
        inside = lane < depth - offset if offset > 0 else lane >= -offset
        return jnp.where(inside, moved, 0.0)

    return differ(at(0), at(1), at(2), at(-1)) if upward else differ(at(-1), at(0), at(1), at(-2))


def clear_rim(ref, parts_x, parts_y):
    _, layers, rows, depth = ref.shape
    tile_x, tile_y = layers - 2 * LAYERS, rows - 2 * ROWS
    for part in parts_x:
        for begin in (0, LAYERS + tile_x):
            ref[part, pl.ds(begin, LAYERS), pl.ds(ROWS, tile_y), :] = jnp.zeros(
                (LAYERS, tile_y, depth), jnp.float32
            )
    for part in parts_y:
        for begin in (0, ROWS + tile_y):
            ref[part, pl.ds(LAYERS, tile_x), pl.ds(begin, ROWS), :] = jnp.zeros(
                (tile_x, ROWS, depth), jnp.float32
            )


def receiver_sum(cells, amps, columns):
    depth, receivers = columns.shape[-1], cells.shape[-1]
    column = lax.div(cells, depth)
    level = cells - column * depth
    column_hot = jnp.concatenate(
        [
            (columns == column[:, begin : begin + depth]).astype(jnp.bfloat16)
            for begin in range(0, receivers, depth)
        ],
        axis=1,
    )
    levels = lax.broadcasted_iota(jnp.int32, (depth, receivers), 0)
    rest = jnp.where(levels == level, amps, 0.0)
    total = jnp.zeros(columns.shape, jnp.float32)
    for _ in range(3):
        part = rest.astype(jnp.bfloat16)
        rest = rest - part.astype(jnp.float32)
        total = total + lax.dot_general(
            column_hot,
            part,
            (((1,), (1,)), ((), ())),
            preferred_element_type=jnp.float32,
        )
    return total


def velocity_kernel(
    width_y,
    lame,
    shear,
    density,
    receiver_cell,
    residual_amp,
    forward,
    adjoint,
    _,
    stress,
    velocity,
    accel,
    rim_added,
    buoyancy,
    scaled_lame,
    scaled_shear,
    received,
    gained,
    lame_now,
    shear_now,
    density_now,
    sems,
):
    tile_x, tile_y, depth = density.shape
    copies = [
        pltpu.make_async_copy(lame, lame_now, sems.at[0]),
        pltpu.make_async_copy(shear, shear_now, sems.at[1]),
        pltpu.make_async_copy(density, density_now, sems.at[2]),
    ]
    for copy in copies:
        copy.start()
    cells = tile_x * tile_y
    middle = pl.ds(ROWS, tile_y)
    columns = column_ids(tile_x, tile_y, width_y, depth)
    received[...] = receiver_sum(receiver_cell[...], residual_amp[...], columns)
    for layer in range(3):
        rim_added[0, layer] = received[pl.ds(cells + layer * tile_y, tile_y), :]
        rim_added[1, layer] = received[pl.ds(cells + 3 * tile_y + layer * tile_x, tile_x), :]

    def fill(x, carry):
        extra = received[pl.ds(pl.multiple_of(x * tile_y, 8), tile_y), :]
        for wave, fields in enumerate((forward, adjoint)):
            for part in range(6):
                value = fields[3 + part, x]
                stress[6 * wave + part, x + LAYERS, middle, :] = (
                    value + extra if wave == 1 and part < 3 else value
                )
        return carry

    lax.fori_loop(0, tile_x, fill, 0, unroll=8)

    def layer(x, carry):
        for wave in range(2):
            xx, yy, zz, xy, xz, yz = range(6 * wave, 6 * wave + 6)
            values = (
                along_x(stress, xx, x, tile_y, True)
                + along_y(stress, xy, x, tile_y, False)
                + along_z(stress, xz, x, tile_y, False),
                along_x(stress, xy, x, tile_y, False)
                + along_y(stress, yy, x, tile_y, True)
                + along_z(stress, yz, x, tile_y, False),
                along_x(stress, xz, x, tile_y, False)
                + along_y(stress, yz, x, tile_y, False)
                + along_z(stress, zz, x, tile_y, True),
            )
            for part, value in enumerate(values):
                gained[3 * wave + part, x] = value
        return carry

    lax.fori_loop(0, tile_x, layer, 0, unroll=True)
    for copy in copies:
        copy.wait()

    def finish(x, carry):
        light = 1.0 / density_now[x]
        buoyancy[x] = light
        scaled_lame[x] = time_step * lame_now[x]
        scaled_shear[x] = time_step * shear_now[x]
        for wave, fields in enumerate((forward, adjoint)):
            for part in range(3):
                value = light * gained[3 * wave + part, x]
                if wave == 0:
                    accel[part, x] = value
                velocity[3 * wave + part, x + LAYERS, middle, :] = (
                    fields[part, x] + time_step * value
                )
        return carry

    lax.fori_loop(0, tile_x, finish, 0, unroll=8)


def stress_halo_terms(links, received, rim_added, waves, add):
    for link, halo in zip(links, received):
        dim = link[1]
        part_n, part_a, part_b = ACCEL_OF[dim]

        def normal(wave, slot, layer):
            value = halo[wave, slot]
            return value + rim_added[dim, layer] if wave == 1 else value

        def after():
            for wave in waves:
                n0, n1 = normal(wave, 0, 1), normal(wave, 1, 2)
                add(wave, part_n, dim, -1, near * n0 + far * n1)
                add(wave, part_n, dim, -2, far * n0)
                add(wave, part_a, dim, -1, far * halo[wave, 2])
                add(wave, part_b, dim, -1, far * halo[wave, 3])

        def before():
            for wave in waves:
                add(wave, part_n, dim, 0, -far * normal(wave, 0, 0))
                for part, slot in ((part_a, 1), (part_b, 3)):
                    outer, inner = halo[wave, slot], halo[wave, slot + 1]
                    add(wave, part, dim, 0, -near * inner - far * outer)
                    add(wave, part, dim, 1, -far * inner)

        real = has_peer(link[0], link[2])
        lower = is_lower(link[0], link[2])
        pl.when(real & lower)(after)
        pl.when(real & jnp.logical_not(lower))(before)


def source_gain(cell, part, x, y, z, width_y):
    depth = z.shape[-1]
    column = lax.div(cell, depth)
    source_x = lax.div(column, width_y)
    away = [source_x - x, column - source_x * width_y - y, cell - column * depth - z]
    along = away.pop(part)
    gain = jnp.where(along == 0, -near, 0.0)
    for offset, value in ((1, near), (2, far), (-1, -far)):
        gain = jnp.where(along == offset, value, gain)
    return jnp.where((away[0] == 0) & (away[1] == 0), gain, 0.0)


def start_of(tile_x, tile_y):
    return lax.axis_index("tx") * tile_x, lax.axis_index("ty") * tile_y


def missing_terms(links, stress, source, width_y, missing):
    cell, amp = source
    layers, rows, depth = stress.shape[1:]
    tile = layers - 2 * LAYERS, rows - 2 * ROWS
    starts = start_of(*tile)
    for link, out in zip(links, missing):
        dim = link[1]
        shape = out.shape[2:]
        cross = starts[1 - dim] + lax.broadcasted_iota(jnp.int32, shape, 0)
        level = lax.broadcasted_iota(jnp.int32, shape, 1)

        def own(wave, part, index):
            return face(stress, 6 * wave + STRESS_ALONG[dim][part], dim, index, True)[...]

        def put(slots):
            for wave in range(2):
                for slot, (part, layer, terms) in enumerate(slots):
                    value = terms(wave) if dim == 1 else jnp.zeros(shape, jnp.float32)
                    if wave == 0:
                        here = jnp.full(shape, starts[dim] + layer, jnp.int32)
                        x, y = (here, cross) if dim == 0 else (cross, here)
                        value += amp * source_gain(
                            cell, VELOCITY_ALONG[dim][part], x, y, level, width_y
                        )
                    out[wave, slot] = value

        def after():
            count = tile[dim]
            slots = [(0, count, lambda wave: -far * own(wave, 0, -1))]
            for part in (1, 2):
                slots += [
                    (
                        part,
                        count,
                        lambda wave, part=part: -near * own(wave, part, -1)
                        - far * own(wave, part, -2),
                    ),
                    (part, count + 1, lambda wave, part=part: -far * own(wave, part, -1)),
                ]
            put(slots)

        def before():
            put([
                (0, -2, lambda wave: far * own(wave, 0, 0)),
                (0, -1, lambda wave: near * own(wave, 0, 0) + far * own(wave, 0, 1)),
                (1, -1, lambda wave: far * own(wave, 1, 0)),
                (2, -1, lambda wave: far * own(wave, 2, 0)),
            ])

        lower = is_lower(link[0], link[2])
        pl.when(lower)(after)
        pl.when(jnp.logical_not(lower))(before)


def velocity_halo_terms(links, received, stresses, missing, add):
    for link, halo, stress_halo, lack in zip(links, received, stresses, missing):
        dim = link[1]
        part_n, part_a, part_b = STRAIN_OF[dim]

        def after():
            lights = [time_step / stress_halo[layer, SPARE] for layer in range(2)]
            for wave in range(2):

                def whole(slot, layer):
                    return halo[wave, slot] + lights[layer] * lack[wave, slot]

                add(wave, part_n, dim, -1, far * whole(0, 0))
                for part, slot in ((part_a, 1), (part_b, 3)):
                    inner, outer = whole(slot, 0), whole(slot + 1, 1)
                    add(wave, part, dim, -1, near * inner + far * outer)
                    add(wave, part, dim, -2, far * inner)

        def before():
            lights = [time_step * halo[layer, SPARE] for layer in range(2)]
            for wave in range(2):

                def whole(slot, layer):
                    return halo[wave, slot] + lights[layer] * lack[wave, slot]

                outer, inner = whole(0, 1), whole(1, 0)
                add(wave, part_n, dim, 0, -near * inner - far * outer)
                add(wave, part_n, dim, 1, -far * inner)
                add(wave, part_a, dim, 0, -far * whole(2, 0))
                add(wave, part_b, dim, 0, -far * whole(3, 0))

        real = has_peer(link[0], link[2])
        lower = is_lower(link[0], link[2])
        pl.when(real & lower)(after)
        pl.when(real & jnp.logical_not(lower))(before)


def face(ref, part, dim, index, padded):
    layers, rows, depth = ref.shape[1:]
    tile_x = layers - 2 * LAYERS if padded else layers
    tile_y = rows - 2 * ROWS if padded else rows
    if dim == 0:
        at = index % tile_x
        if padded:
            return ref.at[part, at + LAYERS, pl.ds(ROWS, tile_y), :]
        return ref.at[part, at]
    at = index % tile_y
    flat = ref.reshape(ref.shape[0], layers * rows, depth)
    begin = LAYERS * rows + ROWS + at if padded else at
    return flat.at[part, pl.ds(begin, tile_x, stride=rows), :]


def light_face(buoyancy, dim, index):
    layers, rows, depth = buoyancy.shape
    if dim == 0:
        return buoyancy[index % layers]
    return buoyancy.reshape(layers * rows, depth)[pl.ds(index % rows, layers, stride=rows), :]


def boundary_kernel(links, send_links, *refs):
    count = len(links)
    received = refs[:count]
    rim_added, buoyancy, _, velocity = refs[count : count + 4]
    sends = refs[count + 4 :]

    def add(wave, part, dim, index, term):
        target = face(velocity, 3 * wave + part, dim, index, True)
        target[...] += time_step * light_face(buoyancy, dim, index) * term

    stress_halo_terms(links, received, rim_added, (0, 1), add)
    send_velocities(send_links, velocity, buoyancy, sends)


def strain_kernel(links, width_y, *refs):
    count = len(links)
    received = refs[:count]
    source_cell, source_amp, rim_added, buoyancy, accel = refs[count : count + 5]
    stress = refs[count + 6]
    strain, gradient, velocity = refs[count + 7 : count + 10]
    outputs, missing = refs[count + 10 : count + 12], refs[count + 12 : 2 * count + 12]
    accel_now, sems = refs[2 * count + 12 :]
    tile_x, tile_y, depth = buoyancy.shape
    middle = pl.ds(ROWS, tile_y)
    clear_rim(velocity, range(6), range(6))
    accel_now[...] = accel[...]

    def add(wave, part, dim, index, term):
        target = face(accel_now, part, dim, index, False)
        target[...] += light_face(buoyancy, dim, index) * term

    stress_halo_terms(links, received, rim_added, (0,), add)
    x_start, y_start = start_of(tile_x, tile_y)
    cell, amp = source_cell[0], source_amp[0]
    source_x = lax.div(cell, width_y * depth)
    y = y_start + lax.broadcasted_iota(jnp.int32, (tile_y, depth), 0)
    level = lax.broadcasted_iota(jnp.int32, (tile_y, depth), 1)
    for offset in (-2, -1, 0, 1):
        x = source_x + offset - x_start

        @pl.when((x >= 0) & (x < tile_x))
        def add_source():
            here = jnp.full((tile_y, depth), source_x + offset, jnp.int32)
            for part in range(3):
                gain = source_gain(cell, part, here, y, level, width_y)
                value = amp * buoyancy[x] * gain
                accel_now[part, x] += value
                velocity[part, x + LAYERS, middle, :] += time_step * value

    copies = [
        pltpu.make_async_copy(
            velocity.at[3 * wave + part, pl.ds(LAYERS, tile_x), middle, :],
            outputs[wave].at[part],
            sems.at[3 * wave + part],
        )
        for wave in range(2)
        for part in range(3)
    ]
    for copy in copies:
        copy.start()
    def layer(x, carry):
        for wave in range(2):
            vx, vy, vz = range(3 * wave, 3 * wave + 3)
            values = (
                along_x(velocity, vx, x, tile_y, False),
                along_y(velocity, vy, x, tile_y, False),
                along_z(velocity, vz, x, tile_y, False),
                along_y(velocity, vx, x, tile_y, True) + along_x(velocity, vy, x, tile_y, True),
                along_z(velocity, vx, x, tile_y, True) + along_x(velocity, vz, x, tile_y, True),
                along_z(velocity, vy, x, tile_y, True) + along_y(velocity, vz, x, tile_y, True),
            )
            for part, value in enumerate(values):
                strain[6 * wave + part, x] = value
        total = sum(
            accel_now[part, x] * velocity[3 + part, x + LAYERS, middle, :] for part in range(3)
        )
        gradient[2, x] = -time_step * total
        return carry

    lax.fori_loop(0, tile_x, layer, 0, unroll=8)
    missing_terms(links, stress, (cell, amp), width_y, missing)
    for copy in copies:
        copy.wait()


def new_stress(strain, stress, scaled_lame, scaled_shear, wave, x, tile_y):
    lame, shear = scaled_lame[x], scaled_shear[x]
    strains = [strain[6 * wave + part, x] for part in range(6)]
    volume = lame * (strains[0] + strains[1] + strains[2])
    values = []
    for part in range(6):
        old = stress[6 * wave + part, x + LAYERS, pl.ds(ROWS, tile_y), :]
        if part < 3:
            values.append(old + (volume + 2.0 * shear * strains[part]))
        else:
            values.append(old + shear * strains[part])
    return strains, values


def gradient_kernel(links, inner, *refs):
    count = len(links)
    received, stresses, missing = (refs[at : at + count] for at in range(0, 3 * count, count))
    stress, scaled_lame, scaled_shear, _, _, strain, gradient = refs[3 * count :]
    tile_x, tile_y, _ = scaled_lame.shape
    first, last = min(2, tile_x), max(2, tile_x - 2)

    def add(wave, part, dim, index, term):
        target = face(strain, 6 * wave + part, dim, index, False)
        target[...] += term

    velocity_halo_terms(links, received, stresses, missing, add)

    def layer(x, carry):
        strains = [strain[part, x] for part in range(6)]
        _, values = new_stress(strain, stress, scaled_lame, scaled_shear, 1, x, tile_y)
        trace = strains[0] + strains[1] + strains[2]
        gradient[0, x] = -time_step * trace * (values[0] + values[1] + values[2])
        total = sum(left * right for left, right in zip(strains, values))
        gradient[1, x] = -time_step * total
        return carry

    if inner:
        if last > first:
            lax.fori_loop(first, last, layer, 0, unroll=4)
    else:
        for x in (*range(first), *range(last, tile_x)):
            layer(x, 0)


def output_kernel(
    chunk, width_y, source_cell, source_amp, strain, stress, scaled_lame, scaled_shear, *refs
):
    outputs, (values_now, sems) = refs[2:4], refs[4:]
    tile_x, tile_y, depth = scaled_lame.shape
    x_start, y_start = start_of(tile_x, tile_y)
    y = y_start + lax.broadcasted_iota(jnp.int32, (tile_y, depth), 0)
    level = lax.broadcasted_iota(jnp.int32, (tile_y, depth), 1)
    in_layer = y * depth + level - source_cell[0]
    copies = []
    for begin in range(0, tile_x, chunk):
        for wave in range(2):
            for x in range(begin, begin + chunk):
                _, values = new_stress(strain, stress, scaled_lame, scaled_shear, wave, x, tile_y)
                if wave == 0:
                    first = (x_start + x) * (width_y * depth)
                    added = jnp.where(in_layer == -first, source_amp[0], 0.0)
                    values[:3] = [value + added for value in values[:3]]
                for part in range(6):
                    values_now[6 * wave + part, x] = values[part]
            layers = pl.ds(begin, chunk)
            copy = pltpu.make_async_copy(
                values_now.at[pl.ds(6 * wave, 6), layers],
                outputs[wave].at[pl.ds(3, 6), layers],
                sems.at[len(copies)],
            )
            copy.start()
            copies.append(copy)
    for copy in copies:
        copy.wait()


def sum_kernel(chunk, mine, other, total, total_now, sems):
    copies = []
    for part in range(mine.shape[0]):
        for begin in range(0, mine.shape[1], chunk):
            layers = pl.ds(begin, chunk)
            total_now[part, layers] = mine[part, layers] + other[part, layers]
            copy = pltpu.make_async_copy(
                total_now.at[part, layers], total.at[part, layers], sems.at[len(copies)]
            )
            copy.start()
            copies.append(copy)
    for copy in copies:
        copy.wait()


def in_hbm(value):
    return pltpu.with_memory_space_constraint(value, pltpu.HBM)


def cost(flops, size):
    return pl.CostEstimate(flops=flops, bytes_accessed=size, transcendentals=0)


def body(
    forward_fields,
    adjoint_fields,
    lame_lambda,
    shear_modulus,
    density,
    source_cell,
    source_amp,
    receiver_cell,
    residual_amp,
):
    _, _, tile_x, tile_y, depth = forward_fields.shape
    forward = forward_fields.reshape(forward_fields.shape[1:])
    adjoint = adjoint_fields.reshape(adjoint_fields.shape[1:])
    sizes = {name: lax.axis_size(name) for name in ("tx", "ty")}
    width_y = tile_y * sizes["ty"]
    links_x, links_y = links_of(sizes)
    cells = tile_x * tile_y * depth

    def buffers(dim):
        return pltpu.VMEM((2, SLOTS, tile_y if dim == 0 else tile_x, depth), jnp.float32)

    def tile(*lead):
        return pltpu.VMEM((*lead, tile_x, tile_y, depth), jnp.float32)

    def padded(parts):
        return pltpu.VMEM(
            (parts, tile_x + 2 * LAYERS, tile_y + 2 * ROWS, depth), jnp.float32
        )

    def exchange(links, sends):
        return [swap(send, axis, first) for (axis, _, first), send in zip(links, sends)]

    def shapes(links):
        return [buffers(dim) for _, dim, _ in links]

    links = links_y + links_x
    count, count_x, count_y = len(links), len(links_x), len(links_y)
    rows = tile_x * tile_y + 3 * (tile_x + tile_y)
    source = source_cell, source_amp

    *sends, density_rows, stress = pl.pallas_call(
        functools.partial(early_pack_kernel, links_x),
        out_shape=shapes(links_x) + [pltpu.VMEM((2, tile_x, depth), jnp.float32), padded(12)],
        in_specs=[hbm] * 3,
        out_specs=[vmem] * (count_x + 2),
        scratch_shapes=[pltpu.SemaphoreType.DMA((2 + 2 * SLOTS * count_x,))],
        compiler_params=params,
        cost_estimate=cost(0, 4 * cells),
        name="early_pack",
    )(*(in_hbm(x) for x in (forward, adjoint, density)))
    halos_x = exchange(links_x, sends)
    halos_y = []
    if links_y:
        sends = pl.pallas_call(
            functools.partial(pack_kernel, links_y),
            out_shape=shapes(links_y),
            in_specs=[vmem] * 3,
            out_specs=[vmem] * count_y,
            compiler_params=params,
            cost_estimate=cost(0, 2 * 2 * SLOTS * count_y * tile_x * depth * 4),
            name="pack",
        )(forward, adjoint, density_rows)
        halos_y = exchange(links_y, sends)

    stress, velocity, accel, rim_added, buoyancy, scaled_lame, scaled_shear = pl.pallas_call(
        functools.partial(velocity_kernel, width_y),
        out_shape=[
            padded(12),
            padded(6),
            tile(3),
            pltpu.VMEM((2, 3, max(tile_x, tile_y), depth), jnp.float32),
            tile(),
            tile(),
            tile(),
        ],
        in_specs=[hbm] * 3 + [vmem] * 5,
        out_specs=[vmem] * 7,
        input_output_aliases={7: 0},
        scratch_shapes=[
            pltpu.VMEM((rows, depth), jnp.float32),
            tile(6),
            tile(),
            tile(),
            tile(),
            pltpu.SemaphoreType.DMA((3,)),
        ],
        compiler_params=params,
        cost_estimate=cost(200 * cells, 18 * 4 * cells),
        name="velocity",
    )(
        *(in_hbm(x) for x in (lame_lambda, shear_modulus, density)),
        receiver_cell,
        residual_amp,
        forward,
        adjoint,
        stress,
    )

    def boundary(links, send_links, halos, velocity, name):
        velocity, *sends = pl.pallas_call(
            functools.partial(boundary_kernel, links, send_links),
            out_shape=[padded(6)] + shapes(send_links),
            in_specs=[vmem] * (len(links) + 3),
            out_specs=[vmem] * (1 + len(send_links)),
            input_output_aliases={len(links) + 2: 0},
            compiler_params=params,
            cost_estimate=cost(cells, 10 * 2 * tile_x * depth * 4),
            name=name,
        )(*halos, rim_added, buoyancy, velocity)
        return velocity, exchange(send_links, sends)

    later_y = links_y[::-1]
    velocity, velocity_halos_y = boundary(links_x, later_y, halos_x, velocity, "boundary_x")
    velocity, velocity_halos_x = boundary(links_y, links_x, halos_y, velocity, "boundary_y")
    halos = halos_y + halos_x

    out_shape = jax.ShapeDtypeStruct(forward.shape, jnp.float32)
    strain, gradient, _, forward_next, adjoint_next, *missing = pl.pallas_call(
        functools.partial(strain_kernel, links, width_y),
        out_shape=[tile(12), tile(3), padded(6), out_shape, out_shape] + shapes(links),
        in_specs=[vmem] * count + [smem] * 2 + [vmem] * 5,
        out_specs=[vmem] * 3 + [hbm] * 2 + [vmem] * count,
        input_output_aliases={count + 5: 2},
        scratch_shapes=[tile(3), pltpu.SemaphoreType.DMA((6,))],
        compiler_params=params,
        cost_estimate=cost(200 * cells, 18 * 4 * cells),
        name="strain",
    )(*halos, *source, rim_added, buoyancy, accel, velocity, stress)

    def gradients(links, inner, received, stresses, missing, strain, gradient, name):
        return pl.pallas_call(
            functools.partial(gradient_kernel, links, inner),
            out_shape=[tile(12), tile(3)],
            in_specs=[vmem] * (3 * len(links) + 5),
            out_specs=[vmem] * 2,
            input_output_aliases={3 * len(links) + 3: 0, 3 * len(links) + 4: 1},
            compiler_params=params,
            cost_estimate=cost(30 * cells, 2 * 4 * cells),
            name=name,
        )(*received, *stresses, *missing, stress, scaled_lame, scaled_shear, strain, gradient)

    strain, gradient = gradients(
        later_y,
        True,
        velocity_halos_y,
        halos_y[::-1],
        missing[:count_y][::-1],
        strain,
        gradient,
        "gradient_inner",
    )
    strain, gradient = gradients(
        links_x, False, velocity_halos_x, halos_x, missing[count_y:], strain, gradient, "gradient"
    )
    other = lax.ppermute(gradient, "shot", [(0, 1), (1, 0)])

    chunk = 4 if tile_x % 4 == 0 else 1
    forward_next, adjoint_next = pl.pallas_call(
        functools.partial(output_kernel, chunk, width_y),
        out_shape=[out_shape, out_shape],
        in_specs=[smem] * 2 + [vmem] * 4 + [hbm] * 2,
        out_specs=[hbm] * 2,
        input_output_aliases={6: 0, 7: 1},
        scratch_shapes=[tile(12), pltpu.SemaphoreType.DMA((2 * tile_x // chunk,))],
        compiler_params=params,
        cost_estimate=cost(60 * cells, 18 * 4 * cells),
        name="outputs",
    )(*source, strain, stress, scaled_lame, scaled_shear, forward_next, adjoint_next)
    total = pl.pallas_call(
        functools.partial(sum_kernel, tile_x),
        out_shape=jax.ShapeDtypeStruct((3, tile_x, tile_y, depth), jnp.float32),
        in_specs=[vmem] * 2,
        out_specs=hbm,
        scratch_shapes=[tile(3), pltpu.SemaphoreType.DMA((3,))],
        compiler_params=params,
        cost_estimate=cost(3 * cells, 9 * 4 * cells),
        name="sum",
    )(gradient, other)
    return forward_next[None], adjoint_next[None], total


def solution(mesh):
    return jax.shard_map(
        body,
        mesh=mesh,
        in_specs=(
            P("shot", None, "tx", "ty", None),
            P("shot", None, "tx", "ty", None),
            P("tx", "ty", None),
            P("tx", "ty", None),
            P("tx", "ty", None),
            P("shot"),
            P("shot"),
            P("shot", None),
            P("shot", None),
        ),
        out_specs=(
            P("shot", None, "tx", "ty", None),
            P("shot", None, "tx", "ty", None),
            P(None, "tx", "ty", None),
        ),
        check_vma=False,
    )
```

```python
import functools

import jax
import jax.numpy as jnp
from jax import lax
from jax.experimental import pallas as pl
from jax.experimental.pallas import tpu as pltpu
from jax.sharding import PartitionSpec as P

near = 9.0 / 8.0
far = -1.0 / 24.0
time_step = 0.15

LAYERS = 2
ROWS = 8
SLOTS = 5

STRESS_ALONG = ((0, 3, 4), (1, 3, 5))
ACCEL_OF = ((0, 1, 2), (1, 0, 2))
VELOCITY_ALONG = ((0, 1, 2), (1, 0, 2))
STRAIN_OF = ((0, 3, 4), (1, 3, 5))

vmem = pl.BlockSpec(memory_space=pltpu.VMEM)
smem = pl.BlockSpec(memory_space=pltpu.SMEM)
hbm = pl.BlockSpec(memory_space=pltpu.HBM)
params = pltpu.CompilerParams(vmem_limit_bytes=24 * 1024 * 1024)


def links_of(sizes):
    along_x = (("tx", 0, 1), ("tx", 0, 0))
    along_y = (("ty", 1, 1), ("ty", 1, 0))
    return [[link for link in order if link[2] + 1 < sizes[link[0]]] for order in (along_x, along_y)]


def swap(value, axis, first):
    pairs = [(i, i + 1) for i in range(first, lax.axis_size(axis) - 1, 2)]
    return lax.ppermute(value, axis, pairs + [(j, i) for i, j in pairs])


def is_lower(axis, first):
    return lax.axis_index(axis) % 2 == first


def has_peer(axis, first):
    index = lax.axis_index(axis)
    partner = jnp.where(is_lower(axis, first), index + 1, index - 1)
    return (partner >= 0) & (partner < lax.axis_size(axis))


def by_role(link, act, upper, lower):
    lower_here = is_lower(link[0], link[2])
    pl.when(lower_here)(lambda: act(lower, True))
    pl.when(jnp.logical_not(lower_here))(lambda: act(upper, False))


SPARE = SLOTS - 1


def stress_plan(dim):
    n, a, b = STRESS_ALONG[dim]
    return ((n, 0), (n, 1), (a, 0), (b, 0)), ((n, -1), (a, -2), (a, -1), (b, -2), (b, -1))


def velocity_plan(dim):
    n, a, b = VELOCITY_ALONG[dim]
    return ((n, 0), (a, 0), (a, 1), (b, 0), (b, 1)), ((n, -2), (n, -1), (a, -1), (b, -1))


def early_pack_kernel(links, forward, adjoint, density, *refs):
    sends, (density_rows, stress, sems) = refs[: len(links)], refs[len(links) :]
    tile_x = forward.shape[1]
    waits = []
    for at, (link, send) in enumerate(zip(links, sends)):
        n, a, b = (3 + part for part in STRESS_ALONG[link[1]])

        def start(plan, lower):
            for wave, fields in enumerate((forward, adjoint)):
                first, last = pl.ds(0, 2), pl.ds(tile_x - 2, 2)
                if lower:
                    pieces = (
                        (fields.at[n, pl.ds(tile_x - 1, 1)], 0, 1),
                        (fields.at[a, last], 1, 2),
                        (fields.at[b, last], 3, 2),
                    )
                else:
                    pieces = (
                        (fields.at[n, first], 0, 2),
                        (fields.at[a, pl.ds(0, 1)], 2, 1),
                        (fields.at[b, pl.ds(0, 1)], 3, 1),
                        (density.at[pl.ds(wave, 1)], SPARE, 1),
                    )
                for source, slot, size in pieces:
                    pltpu.make_async_copy(
                        source, send.at[wave, pl.ds(slot, size)], sems.at[2 * at + wave]
                    ).start()

        by_role(link, start, *stress_plan(link[1]))
        for wave in range(2):
            waits.append(
                pltpu.make_async_copy(
                    forward.at[0, pl.ds(0, SLOTS)], send.at[wave], sems.at[2 * at + wave]
                )
            )
    for row in range(2):
        copy = pltpu.make_async_copy(
            density.at[:, row, :], density_rows.at[row], sems.at[2 * len(links) + row]
        )
        copy.start()
        waits.append(copy)
    for wave in range(2):
        clear_rim(
            stress, *([6 * wave + part for part in STRESS_ALONG[dim]] for dim in range(2))
        )
    for copy in waits:
        copy.wait()


def pack_kernel(links, forward, adjoint, density_rows, *sends):
    for link, send in zip(links, sends):
        dim = link[1]

        def put(plan, lower):
            for wave, fields in enumerate((forward, adjoint)):
                for slot, (part, index) in enumerate(plan):
                    send[wave, slot] = face(fields, 3 + part, dim, index, False)[...]
                if not lower:
                    send[wave, SPARE] = density_rows[wave]

        by_role(link, put, *stress_plan(dim))


def send_velocities(links, velocity, buoyancy, sends):
    for link, send in zip(links, sends):
        dim = link[1]

        def put(plan, lower):
            for wave in range(2):
                for slot, (part, index) in enumerate(plan):
                    send[wave, slot] = face(velocity, 3 * wave + part, dim, index, True)[...]
                if lower:
                    send[wave, SPARE] = light_face(buoyancy, dim, -1 - wave)

        by_role(link, put, *velocity_plan(dim))


def column_ids(tile_x, tile_y, width_y, lanes):
    x_start = lax.axis_index("tx") * tile_x
    y_start = lax.axis_index("ty") * tile_y

    def column(x, y):
        inside = (y >= 0) & (y < width_y)
        return jnp.where(inside, x * width_y + y, -1)

    def iota(shape, dim):
        return lax.broadcasted_iota(jnp.int32, shape, dim)

    shape = (tile_x, tile_y, lanes)
    tile = column(x_start + iota(shape, 0), y_start + iota(shape, 1))
    shape = (3, tile_y, lanes)
    layer = iota(shape, 0)
    along_x = column(
        x_start + jnp.where(layer == 0, -1, tile_x - 1 + layer), y_start + iota(shape, 1)
    )
    shape = (3, tile_x, lanes)
    layer = iota(shape, 0)
    along_y = column(
        x_start + iota(shape, 1), y_start + jnp.where(layer == 0, -1, tile_y - 1 + layer)
    )
    return jnp.concatenate([part.reshape(-1, lanes) for part in (tile, along_x, along_y)], axis=0)


def differ(zero, one, two, minus):
    return near * (one - zero) + far * (two - minus)


def along_x(ref, part, x, tile_y, upward):
    def at(offset):
        return ref[part, x + (LAYERS + offset), pl.ds(ROWS, tile_y), :]

    return differ(at(0), at(1), at(2), at(-1)) if upward else differ(at(-1), at(0), at(1), at(-2))


def along_y(ref, part, x, tile_y, upward):
    def at(offset):
        return ref[part, x + LAYERS, pl.ds(ROWS + offset, tile_y), :]

    return differ(at(0), at(1), at(2), at(-1)) if upward else differ(at(-1), at(0), at(1), at(-2))


def along_z(ref, part, x, tile_y, upward):
    value = ref[part, x + LAYERS, pl.ds(ROWS, tile_y), :]
    depth = value.shape[-1]
    lane = lax.broadcasted_iota(jnp.int32, value.shape, 1)

    def at(offset):
        if offset == 0:
            return value
        moved = pltpu.roll(value, (-offset) % depth, 1)
        inside = lane < depth - offset if offset > 0 else lane >= -offset
        return jnp.where(inside, moved, 0.0)

    return differ(at(0), at(1), at(2), at(-1)) if upward else differ(at(-1), at(0), at(1), at(-2))


def clear_rim(ref, parts_x, parts_y):
    _, layers, rows, depth = ref.shape
    tile_x, tile_y = layers - 2 * LAYERS, rows - 2 * ROWS
    for part in parts_x:
        for begin in (0, LAYERS + tile_x):
            ref[part, pl.ds(begin, LAYERS), pl.ds(ROWS, tile_y), :] = jnp.zeros(
                (LAYERS, tile_y, depth), jnp.float32
            )
    for part in parts_y:
        for begin in (0, ROWS + tile_y):
            ref[part, pl.ds(LAYERS, tile_x), pl.ds(begin, ROWS), :] = jnp.zeros(
                (tile_x, ROWS, depth), jnp.float32
            )


def receiver_sum(cells, amps, columns):
    depth, receivers = columns.shape[-1], cells.shape[-1]
    column = lax.div(cells, depth)
    level = cells - column * depth
    column_hot = jnp.concatenate(
        [
            (columns == column[:, begin : begin + depth]).astype(jnp.bfloat16)
            for begin in range(0, receivers, depth)
        ],
        axis=1,
    )
    levels = lax.broadcasted_iota(jnp.int32, (depth, receivers), 0)
    rest = jnp.where(levels == level, amps, 0.0)
    total = jnp.zeros(columns.shape, jnp.float32)
    for _ in range(3):
        part = rest.astype(jnp.bfloat16)
        rest = rest - part.astype(jnp.float32)
        total = total + lax.dot_general(
            column_hot,
            part,
            (((1,), (1,)), ((), ())),
            preferred_element_type=jnp.float32,
        )
    return total


def velocity_kernel(
    width_y,
    density,
    receiver_cell,
    residual_amp,
    forward,
    adjoint,
    _,
    stress,
    velocity,
    accel,
    rim_added,
    buoyancy,
    received,
    gained,
    density_now,
    sems,
):
    tile_x, tile_y, depth = density.shape
    copy = pltpu.make_async_copy(density, density_now, sems.at[0])
    copy.start()
    cells = tile_x * tile_y
    middle = pl.ds(ROWS, tile_y)
    columns = column_ids(tile_x, tile_y, width_y, depth)
    received[...] = receiver_sum(receiver_cell[...], residual_amp[...], columns)
    for layer in range(3):
        rim_added[0, layer] = received[pl.ds(cells + layer * tile_y, tile_y), :]
        rim_added[1, layer] = received[pl.ds(cells + 3 * tile_y + layer * tile_x, tile_x), :]

    def fill(x, carry):
        extra = received[pl.ds(pl.multiple_of(x * tile_y, 8), tile_y), :]
        for wave, fields in enumerate((forward, adjoint)):
            for part in range(6):
                value = fields[3 + part, x]
                stress[6 * wave + part, x + LAYERS, middle, :] = (
                    value + extra if wave == 1 and part < 3 else value
                )
        return carry

    lax.fori_loop(0, tile_x, fill, 0, unroll=8)

    def layer(x, carry):
        for wave in range(2):
            xx, yy, zz, xy, xz, yz = range(6 * wave, 6 * wave + 6)
            values = (
                along_x(stress, xx, x, tile_y, True)
                + along_y(stress, xy, x, tile_y, False)
                + along_z(stress, xz, x, tile_y, False),
                along_x(stress, xy, x, tile_y, False)
                + along_y(stress, yy, x, tile_y, True)
                + along_z(stress, yz, x, tile_y, False),
                along_x(stress, xz, x, tile_y, False)
                + along_y(stress, yz, x, tile_y, False)
                + along_z(stress, zz, x, tile_y, True),
            )
            for part, value in enumerate(values):
                gained[3 * wave + part, x] = value
        return carry

    lax.fori_loop(0, tile_x, layer, 0, unroll=True)
    copy.wait()

    def finish(x, carry):
        light = 1.0 / density_now[x]
        buoyancy[x] = light
        for wave, fields in enumerate((forward, adjoint)):
            for part in range(3):
                value = light * gained[3 * wave + part, x]
                if wave == 0:
                    accel[part, x] = value
                velocity[3 * wave + part, x + LAYERS, middle, :] = (
                    fields[part, x] + time_step * value
                )
        return carry

    lax.fori_loop(0, tile_x, finish, 0, unroll=8)


def stress_halo_terms(links, received, rim_added, waves, add):
    for link, halo in zip(links, received):
        dim = link[1]
        part_n, part_a, part_b = ACCEL_OF[dim]

        def normal(wave, slot, layer):
            value = halo[wave, slot]
            return value + rim_added[dim, layer] if wave == 1 else value

        def after():
            for wave in waves:
                n0, n1 = normal(wave, 0, 1), normal(wave, 1, 2)
                add(wave, part_n, dim, -1, near * n0 + far * n1)
                add(wave, part_n, dim, -2, far * n0)
                add(wave, part_a, dim, -1, far * halo[wave, 2])
                add(wave, part_b, dim, -1, far * halo[wave, 3])

        def before():
            for wave in waves:
                add(wave, part_n, dim, 0, -far * normal(wave, 0, 0))
                for part, slot in ((part_a, 1), (part_b, 3)):
                    outer, inner = halo[wave, slot], halo[wave, slot + 1]
                    add(wave, part, dim, 0, -near * inner - far * outer)
                    add(wave, part, dim, 1, -far * inner)

        real = has_peer(link[0], link[2])
        lower = is_lower(link[0], link[2])
        pl.when(real & lower)(after)
        pl.when(real & jnp.logical_not(lower))(before)


def source_gain(cell, part, x, y, z, width_y):
    depth = z.shape[-1]
    column = lax.div(cell, depth)
    source_x = lax.div(column, width_y)
    away = [source_x - x, column - source_x * width_y - y, cell - column * depth - z]
    along = away.pop(part)
    gain = jnp.where(along == 0, -near, 0.0)
    for offset, value in ((1, near), (2, far), (-1, -far)):
        gain = jnp.where(along == offset, value, gain)
    return jnp.where((away[0] == 0) & (away[1] == 0), gain, 0.0)


def start_of(tile_x, tile_y):
    return lax.axis_index("tx") * tile_x, lax.axis_index("ty") * tile_y


def missing_terms(links, stress, source, width_y, missing):
    cell, amp = source
    layers, rows, depth = stress.shape[1:]
    tile = layers - 2 * LAYERS, rows - 2 * ROWS
    starts = start_of(*tile)
    for link, out in zip(links, missing):
        dim = link[1]
        shape = out.shape[2:]
        cross = starts[1 - dim] + lax.broadcasted_iota(jnp.int32, shape, 0)
        level = lax.broadcasted_iota(jnp.int32, shape, 1)

        def own(wave, part, index):
            return face(stress, 6 * wave + STRESS_ALONG[dim][part], dim, index, True)[...]

        def put(slots):
            for wave in range(2):
                for slot, (part, layer, terms) in enumerate(slots):
                    value = terms(wave) if dim == 1 else jnp.zeros(shape, jnp.float32)
                    if wave == 0:
                        here = jnp.full(shape, starts[dim] + layer, jnp.int32)
                        x, y = (here, cross) if dim == 0 else (cross, here)
                        value += amp * source_gain(
                            cell, VELOCITY_ALONG[dim][part], x, y, level, width_y
                        )
                    out[wave, slot] = value

        def after():
            count = tile[dim]
            slots = [(0, count, lambda wave: -far * own(wave, 0, -1))]
            for part in (1, 2):
                slots += [
                    (
                        part,
                        count,
                        lambda wave, part=part: -near * own(wave, part, -1)
                        - far * own(wave, part, -2),
                    ),
                    (part, count + 1, lambda wave, part=part: -far * own(wave, part, -1)),
                ]
            put(slots)

        def before():
            put([
                (0, -2, lambda wave: far * own(wave, 0, 0)),
                (0, -1, lambda wave: near * own(wave, 0, 0) + far * own(wave, 0, 1)),
                (1, -1, lambda wave: far * own(wave, 1, 0)),
                (2, -1, lambda wave: far * own(wave, 2, 0)),
            ])

        lower = is_lower(link[0], link[2])
        pl.when(lower)(after)
        pl.when(jnp.logical_not(lower))(before)


def velocity_halo_terms(links, received, stresses, missing, add):
    for link, halo, stress_halo, lack in zip(links, received, stresses, missing):
        dim = link[1]
        part_n, part_a, part_b = STRAIN_OF[dim]

        def after():
            lights = [time_step / stress_halo[layer, SPARE] for layer in range(2)]
            for wave in range(2):

                def whole(slot, layer):
                    return halo[wave, slot] + lights[layer] * lack[wave, slot]

                add(wave, part_n, dim, -1, far * whole(0, 0))
                for part, slot in ((part_a, 1), (part_b, 3)):
                    inner, outer = whole(slot, 0), whole(slot + 1, 1)
                    add(wave, part, dim, -1, near * inner + far * outer)
                    add(wave, part, dim, -2, far * inner)

        def before():
            lights = [time_step * halo[layer, SPARE] for layer in range(2)]
            for wave in range(2):

                def whole(slot, layer):
                    return halo[wave, slot] + lights[layer] * lack[wave, slot]

                outer, inner = whole(0, 1), whole(1, 0)
                add(wave, part_n, dim, 0, -near * inner - far * outer)
                add(wave, part_n, dim, 1, -far * inner)
                add(wave, part_a, dim, 0, -far * whole(2, 0))
                add(wave, part_b, dim, 0, -far * whole(3, 0))

        real = has_peer(link[0], link[2])
        lower = is_lower(link[0], link[2])
        pl.when(real & lower)(after)
        pl.when(real & jnp.logical_not(lower))(before)


def face(ref, part, dim, index, padded):
    layers, rows, depth = ref.shape[1:]
    tile_x = layers - 2 * LAYERS if padded else layers
    tile_y = rows - 2 * ROWS if padded else rows
    if dim == 0:
        at = index % tile_x
        if padded:
            return ref.at[part, at + LAYERS, pl.ds(ROWS, tile_y), :]
        return ref.at[part, at]
    at = index % tile_y
    flat = ref.reshape(ref.shape[0], layers * rows, depth)
    begin = LAYERS * rows + ROWS + at if padded else at
    return flat.at[part, pl.ds(begin, tile_x, stride=rows), :]


def light_face(buoyancy, dim, index):
    layers, rows, depth = buoyancy.shape
    if dim == 0:
        return buoyancy[index % layers]
    return buoyancy.reshape(layers * rows, depth)[pl.ds(index % rows, layers, stride=rows), :]


def boundary_kernel(links, send_links, *refs):
    count = len(links)
    received = refs[:count]
    rim_added, buoyancy, _, velocity = refs[count : count + 4]
    sends = refs[count + 4 :]

    def add(wave, part, dim, index, term):
        target = face(velocity, 3 * wave + part, dim, index, True)
        target[...] += time_step * light_face(buoyancy, dim, index) * term

    stress_halo_terms(links, received, rim_added, (0, 1), add)
    send_velocities(send_links, velocity, buoyancy, sends)


def strain_kernel(links, width_y, *refs):
    count = len(links)
    received = refs[:count]
    source_cell, source_amp, rim_added, buoyancy, accel = refs[count : count + 5]
    stress, lame, shear = refs[count + 6 : count + 9]
    strain, gradient, velocity, scaled_lame, scaled_shear = refs[count + 9 : count + 14]
    outputs, missing = refs[count + 14 : count + 16], refs[count + 16 : 2 * count + 16]
    accel_now, lame_now, shear_now, sems = refs[2 * count + 16 :]
    fetches = [
        pltpu.make_async_copy(lame, lame_now, sems.at[6]),
        pltpu.make_async_copy(shear, shear_now, sems.at[7]),
    ]
    for copy in fetches:
        copy.start()
    tile_x, tile_y, depth = buoyancy.shape
    middle = pl.ds(ROWS, tile_y)
    clear_rim(velocity, range(6), range(6))
    accel_now[...] = accel[...]

    def add(wave, part, dim, index, term):
        target = face(accel_now, part, dim, index, False)
        target[...] += light_face(buoyancy, dim, index) * term

    stress_halo_terms(links, received, rim_added, (0,), add)
    x_start, y_start = start_of(tile_x, tile_y)
    cell, amp = source_cell[0], source_amp[0]
    source_x = lax.div(cell, width_y * depth)
    y = y_start + lax.broadcasted_iota(jnp.int32, (tile_y, depth), 0)
    level = lax.broadcasted_iota(jnp.int32, (tile_y, depth), 1)
    for offset in (-2, -1, 0, 1):
        x = source_x + offset - x_start

        @pl.when((x >= 0) & (x < tile_x))
        def add_source():
            here = jnp.full((tile_y, depth), source_x + offset, jnp.int32)
            for part in range(3):
                gain = source_gain(cell, part, here, y, level, width_y)
                value = amp * buoyancy[x] * gain
                accel_now[part, x] += value
                velocity[part, x + LAYERS, middle, :] += time_step * value

    copies = [
        pltpu.make_async_copy(
            velocity.at[3 * wave + part, pl.ds(LAYERS, tile_x), middle, :],
            outputs[wave].at[part],
            sems.at[3 * wave + part],
        )
        for wave in range(2)
        for part in range(3)
    ]
    for copy in copies:
        copy.start()
    def layer(x, carry):
        for wave in range(2):
            vx, vy, vz = range(3 * wave, 3 * wave + 3)
            values = (
                along_x(velocity, vx, x, tile_y, False),
                along_y(velocity, vy, x, tile_y, False),
                along_z(velocity, vz, x, tile_y, False),
                along_y(velocity, vx, x, tile_y, True) + along_x(velocity, vy, x, tile_y, True),
                along_z(velocity, vx, x, tile_y, True) + along_x(velocity, vz, x, tile_y, True),
                along_z(velocity, vy, x, tile_y, True) + along_y(velocity, vz, x, tile_y, True),
            )
            for part, value in enumerate(values):
                strain[6 * wave + part, x] = value
        total = sum(
            accel_now[part, x] * velocity[3 + part, x + LAYERS, middle, :] for part in range(3)
        )
        gradient[2, x] = -time_step * total
        return carry

    lax.fori_loop(0, tile_x, layer, 0, unroll=8)
    missing_terms(links, stress, (cell, amp), width_y, missing)
    for copy in fetches:
        copy.wait()
    scaled_lame[...] = time_step * lame_now[...]
    scaled_shear[...] = time_step * shear_now[...]
    for copy in copies:
        copy.wait()


def new_stress(strain, stress, scaled_lame, scaled_shear, wave, x, tile_y):
    lame, shear = scaled_lame[x], scaled_shear[x]
    strains = [strain[6 * wave + part, x] for part in range(6)]
    volume = lame * (strains[0] + strains[1] + strains[2])
    values = []
    for part in range(6):
        old = stress[6 * wave + part, x + LAYERS, pl.ds(ROWS, tile_y), :]
        if part < 3:
            values.append(old + (volume + 2.0 * shear * strains[part]))
        else:
            values.append(old + shear * strains[part])
    return strains, values


def gradient_kernel(links, inner, *refs):
    count = len(links)
    received, stresses, missing = (refs[at : at + count] for at in range(0, 3 * count, count))
    stress, scaled_lame, scaled_shear, _, _, strain, gradient = refs[3 * count :]
    tile_x, tile_y, _ = scaled_lame.shape
    first, last = min(2, tile_x), max(2, tile_x - 2)

    def add(wave, part, dim, index, term):
        target = face(strain, 6 * wave + part, dim, index, False)
        target[...] += term

    velocity_halo_terms(links, received, stresses, missing, add)

    def layer(x, carry):
        strains = [strain[part, x] for part in range(6)]
        _, values = new_stress(strain, stress, scaled_lame, scaled_shear, 1, x, tile_y)
        trace = strains[0] + strains[1] + strains[2]
        gradient[0, x] = -time_step * trace * (values[0] + values[1] + values[2])
        total = sum(left * right for left, right in zip(strains, values))
        gradient[1, x] = -time_step * total
        return carry

    if inner:
        if last > first:
            lax.fori_loop(first, last, layer, 0, unroll=4)
    else:
        for x in (*range(first), *range(last, tile_x)):
            layer(x, 0)


def output_kernel(
    chunk, width_y, source_cell, source_amp, strain, stress, scaled_lame, scaled_shear, *refs
):
    outputs, (values_now, sems) = refs[2:4], refs[4:]
    tile_x, tile_y, depth = scaled_lame.shape
    x_start, y_start = start_of(tile_x, tile_y)
    y = y_start + lax.broadcasted_iota(jnp.int32, (tile_y, depth), 0)
    level = lax.broadcasted_iota(jnp.int32, (tile_y, depth), 1)
    in_layer = y * depth + level - source_cell[0]
    copies = []
    for begin in range(0, tile_x, chunk):
        for wave in range(2):
            for x in range(begin, begin + chunk):
                _, values = new_stress(strain, stress, scaled_lame, scaled_shear, wave, x, tile_y)
                if wave == 0:
                    first = (x_start + x) * (width_y * depth)
                    added = jnp.where(in_layer == -first, source_amp[0], 0.0)
                    values[:3] = [value + added for value in values[:3]]
                for part in range(6):
                    values_now[6 * wave + part, x] = values[part]
            layers = pl.ds(begin, chunk)
            copy = pltpu.make_async_copy(
                values_now.at[pl.ds(6 * wave, 6), layers],
                outputs[wave].at[pl.ds(3, 6), layers],
                sems.at[len(copies)],
            )
            copy.start()
            copies.append(copy)
    for copy in copies:
        copy.wait()


def sum_kernel(chunk, mine, other, total, total_now, sems):
    copies = []
    for part in range(mine.shape[0]):
        for begin in range(0, mine.shape[1], chunk):
            layers = pl.ds(begin, chunk)
            total_now[part, layers] = mine[part, layers] + other[part, layers]
            copy = pltpu.make_async_copy(
                total_now.at[part, layers], total.at[part, layers], sems.at[len(copies)]
            )
            copy.start()
            copies.append(copy)
    for copy in copies:
        copy.wait()


def in_hbm(value):
    return pltpu.with_memory_space_constraint(value, pltpu.HBM)


def cost(flops, size):
    return pl.CostEstimate(flops=flops, bytes_accessed=size, transcendentals=0)


def body(
    forward_fields,
    adjoint_fields,
    lame_lambda,
    shear_modulus,
    density,
    source_cell,
    source_amp,
    receiver_cell,
    residual_amp,
):
    _, _, tile_x, tile_y, depth = forward_fields.shape
    forward = forward_fields.reshape(forward_fields.shape[1:])
    adjoint = adjoint_fields.reshape(adjoint_fields.shape[1:])
    sizes = {name: lax.axis_size(name) for name in ("tx", "ty")}
    width_y = tile_y * sizes["ty"]
    links_x, links_y = links_of(sizes)
    cells = tile_x * tile_y * depth

    def buffers(dim):
        return pltpu.VMEM((2, SLOTS, tile_y if dim == 0 else tile_x, depth), jnp.float32)

    def tile(*lead):
        return pltpu.VMEM((*lead, tile_x, tile_y, depth), jnp.float32)

    def padded(parts):
        return pltpu.VMEM(
            (parts, tile_x + 2 * LAYERS, tile_y + 2 * ROWS, depth), jnp.float32
        )

    def exchange(links, sends):
        return [swap(send, axis, first) for (axis, _, first), send in zip(links, sends)]

    def shapes(links):
        return [buffers(dim) for _, dim, _ in links]

    links = links_y + links_x
    count, count_x, count_y = len(links), len(links_x), len(links_y)
    rows = tile_x * tile_y + 3 * (tile_x + tile_y)
    source = source_cell, source_amp

    *sends, density_rows, stress = pl.pallas_call(
        functools.partial(early_pack_kernel, links_x),
        out_shape=shapes(links_x) + [pltpu.VMEM((2, tile_x, depth), jnp.float32), padded(12)],
        in_specs=[hbm] * 3,
        out_specs=[vmem] * (count_x + 2),
        scratch_shapes=[pltpu.SemaphoreType.DMA((2 + 2 * count_x,))],
        compiler_params=params,
        cost_estimate=cost(0, 4 * cells),
        name="early_pack",
    )(*(in_hbm(x) for x in (forward, adjoint, density)))
    halos_x = exchange(links_x, sends)
    halos_y = []
    if links_y:
        sends = pl.pallas_call(
            functools.partial(pack_kernel, links_y),
            out_shape=shapes(links_y),
            in_specs=[vmem] * 3,
            out_specs=[vmem] * count_y,
            compiler_params=params,
            cost_estimate=cost(0, 2 * 2 * SLOTS * count_y * tile_x * depth * 4),
            name="pack",
        )(forward, adjoint, density_rows)
        halos_y = exchange(links_y, sends)

    stress, velocity, accel, rim_added, buoyancy = pl.pallas_call(
        functools.partial(velocity_kernel, width_y),
        out_shape=[
            padded(12),
            padded(6),
            tile(3),
            pltpu.VMEM((2, 3, max(tile_x, tile_y), depth), jnp.float32),
            tile(),
        ],
        in_specs=[hbm] + [vmem] * 5,
        out_specs=[vmem] * 5,
        input_output_aliases={5: 0},
        scratch_shapes=[
            pltpu.VMEM((rows, depth), jnp.float32),
            tile(6),
            tile(),
            pltpu.SemaphoreType.DMA((1,)),
        ],
        compiler_params=params,
        cost_estimate=cost(200 * cells, 18 * 4 * cells),
        name="velocity",
    )(in_hbm(density), receiver_cell, residual_amp, forward, adjoint, stress)

    def boundary(links, send_links, halos, velocity, name):
        velocity, *sends = pl.pallas_call(
            functools.partial(boundary_kernel, links, send_links),
            out_shape=[padded(6)] + shapes(send_links),
            in_specs=[vmem] * (len(links) + 3),
            out_specs=[vmem] * (1 + len(send_links)),
            input_output_aliases={len(links) + 2: 0},
            compiler_params=params,
            cost_estimate=cost(cells, 10 * 2 * tile_x * depth * 4),
            name=name,
        )(*halos, rim_added, buoyancy, velocity)
        return velocity, exchange(send_links, sends)

    later_y = links_y[::-1]
    velocity, velocity_halos_y = boundary(links_x, later_y, halos_x, velocity, "boundary_x")
    velocity, velocity_halos_x = boundary(links_y, links_x, halos_y, velocity, "boundary_y")
    halos = halos_y + halos_x

    out_shape = jax.ShapeDtypeStruct(forward.shape, jnp.float32)
    strain, gradient, _, scaled_lame, scaled_shear, *rest = pl.pallas_call(
        functools.partial(strain_kernel, links, width_y),
        out_shape=[tile(12), tile(3), padded(6), tile(), tile(), out_shape, out_shape]
        + shapes(links),
        in_specs=[vmem] * count + [smem] * 2 + [vmem] * 5 + [hbm] * 2,
        out_specs=[vmem] * 5 + [hbm] * 2 + [vmem] * count,
        input_output_aliases={count + 5: 2},
        scratch_shapes=[tile(3), tile(), tile(), pltpu.SemaphoreType.DMA((8,))],
        compiler_params=params,
        cost_estimate=cost(200 * cells, 18 * 4 * cells),
        name="strain",
    )(
        *halos,
        *source,
        rim_added,
        buoyancy,
        accel,
        velocity,
        stress,
        in_hbm(lame_lambda),
        in_hbm(shear_modulus),
    )
    forward_next, adjoint_next, *missing = rest

    def gradients(links, inner, received, stresses, missing, strain, gradient, name):
        return pl.pallas_call(
            functools.partial(gradient_kernel, links, inner),
            out_shape=[tile(12), tile(3)],
            in_specs=[vmem] * (3 * len(links) + 5),
            out_specs=[vmem] * 2,
            input_output_aliases={3 * len(links) + 3: 0, 3 * len(links) + 4: 1},
            compiler_params=params,
            cost_estimate=cost(30 * cells, 2 * 4 * cells),
            name=name,
        )(*received, *stresses, *missing, stress, scaled_lame, scaled_shear, strain, gradient)

    strain, gradient = gradients(
        later_y,
        True,
        velocity_halos_y,
        halos_y[::-1],
        missing[:count_y][::-1],
        strain,
        gradient,
        "gradient_inner",
    )
    strain, gradient = gradients(
        links_x, False, velocity_halos_x, halos_x, missing[count_y:], strain, gradient, "gradient"
    )
    other = lax.ppermute(gradient, "shot", [(0, 1), (1, 0)])

    chunk = 4 if tile_x % 4 == 0 else 1
    forward_next, adjoint_next = pl.pallas_call(
        functools.partial(output_kernel, chunk, width_y),
        out_shape=[out_shape, out_shape],
        in_specs=[smem] * 2 + [vmem] * 4 + [hbm] * 2,
        out_specs=[hbm] * 2,
        input_output_aliases={6: 0, 7: 1},
        scratch_shapes=[tile(12), pltpu.SemaphoreType.DMA((2 * tile_x // chunk,))],
        compiler_params=params,
        cost_estimate=cost(60 * cells, 18 * 4 * cells),
        name="outputs",
    )(*source, strain, stress, scaled_lame, scaled_shear, forward_next, adjoint_next)
    total = pl.pallas_call(
        functools.partial(sum_kernel, tile_x),
        out_shape=jax.ShapeDtypeStruct((3, tile_x, tile_y, depth), jnp.float32),
        in_specs=[vmem] * 2,
        out_specs=hbm,
        scratch_shapes=[tile(3), pltpu.SemaphoreType.DMA((3,))],
        compiler_params=params,
        cost_estimate=cost(3 * cells, 9 * 4 * cells),
        name="sum",
    )(gradient, other)
    return forward_next[None], adjoint_next[None], total


def solution(mesh):
    return jax.shard_map(
        body,
        mesh=mesh,
        in_specs=(
            P("shot", None, "tx", "ty", None),
            P("shot", None, "tx", "ty", None),
            P("tx", "ty", None),
            P("tx", "ty", None),
            P("tx", "ty", None),
            P("shot"),
            P("shot"),
            P("shot", None),
            P("shot", None),
        ),
        out_specs=(
            P("shot", None, "tx", "ty", None),
            P("shot", None, "tx", "ty", None),
            P(None, "tx", "ty", None),
        ),
        check_vma=False,
    )
```

```python
import functools

import jax
import jax.numpy as jnp
from jax import lax
from jax.experimental import pallas as pl
from jax.experimental.pallas import tpu as pltpu
from jax.sharding import PartitionSpec as P

near = 9.0 / 8.0
far = -1.0 / 24.0
time_step = 0.15

LAYERS = 2
ROWS = 8
SLOTS = 5

STRESS_ALONG = ((0, 3, 4), (1, 3, 5))
ACCEL_OF = ((0, 1, 2), (1, 0, 2))
VELOCITY_ALONG = ((0, 1, 2), (1, 0, 2))
STRAIN_OF = ((0, 3, 4), (1, 3, 5))

vmem = pl.BlockSpec(memory_space=pltpu.VMEM)
smem = pl.BlockSpec(memory_space=pltpu.SMEM)
hbm = pl.BlockSpec(memory_space=pltpu.HBM)
params = pltpu.CompilerParams(vmem_limit_bytes=24 * 1024 * 1024)


def links_of(sizes):
    along_x = (("tx", 0, 1), ("tx", 0, 0))
    along_y = (("ty", 1, 1), ("ty", 1, 0))
    return [[link for link in order if link[2] + 1 < sizes[link[0]]] for order in (along_x, along_y)]


def swap(value, axis, first):
    pairs = [(i, i + 1) for i in range(first, lax.axis_size(axis) - 1, 2)]
    return lax.ppermute(value, axis, pairs + [(j, i) for i, j in pairs])


def is_lower(axis, first):
    return lax.axis_index(axis) % 2 == first


def has_peer(axis, first):
    index = lax.axis_index(axis)
    partner = jnp.where(is_lower(axis, first), index + 1, index - 1)
    return (partner >= 0) & (partner < lax.axis_size(axis))


def by_role(link, act, upper, lower):
    lower_here = is_lower(link[0], link[2])
    pl.when(lower_here)(lambda: act(lower, True))
    pl.when(jnp.logical_not(lower_here))(lambda: act(upper, False))


SPARE = SLOTS - 1


def stress_plan(dim):
    n, a, b = STRESS_ALONG[dim]
    return ((n, 0), (n, 1), (a, 0), (b, 0)), ((n, -1), (a, -2), (a, -1), (b, -2), (b, -1))


def velocity_plan(dim):
    n, a, b = VELOCITY_ALONG[dim]
    return ((n, 0), (a, 0), (a, 1), (b, 0), (b, 1)), ((n, -2), (n, -1), (a, -1), (b, -1))


def early_pack_kernel(links, forward, adjoint, density, *refs):
    sends, (density_rows, stress, sems) = refs[: len(links)], refs[len(links) :]
    tile_x = forward.shape[1]
    waits = []
    for at, (link, send) in enumerate(zip(links, sends)):
        n, a, b = (3 + part for part in STRESS_ALONG[link[1]])

        def start(plan, lower):
            for wave, fields in enumerate((forward, adjoint)):
                first, last = pl.ds(0, 2), pl.ds(tile_x - 2, 2)
                if lower:
                    pieces = (
                        (fields.at[n, pl.ds(tile_x - 1, 1)], 0, 1),
                        (fields.at[a, last], 1, 2),
                        (fields.at[b, last], 3, 2),
                    )
                else:
                    pieces = (
                        (fields.at[n, first], 0, 2),
                        (fields.at[a, pl.ds(0, 1)], 2, 1),
                        (fields.at[b, pl.ds(0, 1)], 3, 1),
                        (density.at[pl.ds(wave, 1)], SPARE, 1),
                    )
                for source, slot, size in pieces:
                    pltpu.make_async_copy(
                        source, send.at[wave, pl.ds(slot, size)], sems.at[2 * at + wave]
                    ).start()

        by_role(link, start, *stress_plan(link[1]))
        for wave in range(2):
            waits.append(
                pltpu.make_async_copy(
                    forward.at[0, pl.ds(0, SLOTS)], send.at[wave], sems.at[2 * at + wave]
                )
            )
    for row in range(2):
        copy = pltpu.make_async_copy(
            density.at[:, row, :], density_rows.at[row], sems.at[2 * len(links) + row]
        )
        copy.start()
        waits.append(copy)
    for wave in range(2):
        clear_rim(
            stress, *([6 * wave + part for part in STRESS_ALONG[dim]] for dim in range(2))
        )
    for copy in waits:
        copy.wait()


def pack_kernel(links, forward, adjoint, density_rows, *sends):
    for link, send in zip(links, sends):
        dim = link[1]

        def put(plan, lower):
            for wave, fields in enumerate((forward, adjoint)):
                for slot, (part, index) in enumerate(plan):
                    send[wave, slot] = face(fields, 3 + part, dim, index, False)[...]
                if not lower:
                    send[wave, SPARE] = density_rows[wave]

        by_role(link, put, *stress_plan(dim))


def send_velocities(links, velocity, buoyancy, sends):
    for link, send in zip(links, sends):
        dim = link[1]

        def put(plan, lower):
            for wave in range(2):
                for slot, (part, index) in enumerate(plan):
                    send[wave, slot] = face(velocity, 3 * wave + part, dim, index, True)[...]
                if lower:
                    send[wave, SPARE] = light_face(buoyancy, dim, -1 - wave)

        by_role(link, put, *velocity_plan(dim))


def column_ids(tile_x, tile_y, width_y, lanes):
    x_start = lax.axis_index("tx") * tile_x
    y_start = lax.axis_index("ty") * tile_y

    def column(x, y):
        inside = (y >= 0) & (y < width_y)
        return jnp.where(inside, x * width_y + y, -1)

    def iota(shape, dim):
        return lax.broadcasted_iota(jnp.int32, shape, dim)

    shape = (tile_x, tile_y, lanes)
    tile = column(x_start + iota(shape, 0), y_start + iota(shape, 1))
    shape = (3, tile_y, lanes)
    layer = iota(shape, 0)
    along_x = column(
        x_start + jnp.where(layer == 0, -1, tile_x - 1 + layer), y_start + iota(shape, 1)
    )
    shape = (3, tile_x, lanes)
    layer = iota(shape, 0)
    along_y = column(
        x_start + iota(shape, 1), y_start + jnp.where(layer == 0, -1, tile_y - 1 + layer)
    )
    return jnp.concatenate([part.reshape(-1, lanes) for part in (tile, along_x, along_y)], axis=0)


def differ(zero, one, two, minus):
    return near * (one - zero) + far * (two - minus)


def along_x(ref, part, x, tile_y, upward):
    def at(offset):
        return ref[part, x + (LAYERS + offset), pl.ds(ROWS, tile_y), :]

    return differ(at(0), at(1), at(2), at(-1)) if upward else differ(at(-1), at(0), at(1), at(-2))


def along_y(ref, part, x, tile_y, upward):
    def at(offset):
        return ref[part, x + LAYERS, pl.ds(ROWS + offset, tile_y), :]

    return differ(at(0), at(1), at(2), at(-1)) if upward else differ(at(-1), at(0), at(1), at(-2))


def along_z(ref, part, x, tile_y, upward):
    value = ref[part, x + LAYERS, pl.ds(ROWS, tile_y), :]
    depth = value.shape[-1]
    lane = lax.broadcasted_iota(jnp.int32, value.shape, 1)

    def at(offset):
        if offset == 0:
            return value
        moved = pltpu.roll(value, (-offset) % depth, 1)
        inside = lane < depth - offset if offset > 0 else lane >= -offset
        return jnp.where(inside, moved, 0.0)

    return differ(at(0), at(1), at(2), at(-1)) if upward else differ(at(-1), at(0), at(1), at(-2))


def clear_rim(ref, parts_x, parts_y):
    _, layers, rows, depth = ref.shape
    tile_x, tile_y = layers - 2 * LAYERS, rows - 2 * ROWS
    for part in parts_x:
        for begin in (0, LAYERS + tile_x):
            ref[part, pl.ds(begin, LAYERS), pl.ds(ROWS, tile_y), :] = jnp.zeros(
                (LAYERS, tile_y, depth), jnp.float32
            )
    for part in parts_y:
        for begin in (0, ROWS + tile_y):
            ref[part, pl.ds(LAYERS, tile_x), pl.ds(begin, ROWS), :] = jnp.zeros(
                (tile_x, ROWS, depth), jnp.float32
            )


def receiver_sum(cells, amps, columns):
    depth, receivers = columns.shape[-1], cells.shape[-1]
    column = lax.div(cells, depth)
    level = cells - column * depth
    column_hot = jnp.concatenate(
        [
            (columns == column[:, begin : begin + depth]).astype(jnp.bfloat16)
            for begin in range(0, receivers, depth)
        ],
        axis=1,
    )
    levels = lax.broadcasted_iota(jnp.int32, (depth, receivers), 0)
    rest = jnp.where(levels == level, amps, 0.0)
    total = jnp.zeros(columns.shape, jnp.float32)
    for _ in range(3):
        part = rest.astype(jnp.bfloat16)
        rest = rest - part.astype(jnp.float32)
        total = total + lax.dot_general(
            column_hot,
            part,
            (((1,), (1,)), ((), ())),
            preferred_element_type=jnp.float32,
        )
    return total


def velocity_kernel(
    width_y,
    density,
    receiver_cell,
    residual_amp,
    forward,
    adjoint,
    _,
    stress,
    velocity,
    accel,
    rim_added,
    buoyancy,
    received,
    gained,
    density_now,
    sems,
):
    tile_x, tile_y, depth = density.shape
    copy = pltpu.make_async_copy(density, density_now, sems.at[0])
    copy.start()
    cells = tile_x * tile_y
    middle = pl.ds(ROWS, tile_y)
    columns = column_ids(tile_x, tile_y, width_y, depth)
    received[...] = receiver_sum(receiver_cell[...], residual_amp[...], columns)
    for layer in range(3):
        rim_added[0, layer] = received[pl.ds(cells + layer * tile_y, tile_y), :]
        rim_added[1, layer] = received[pl.ds(cells + 3 * tile_y + layer * tile_x, tile_x), :]

    def fill(x, carry):
        extra = received[pl.ds(pl.multiple_of(x * tile_y, 8), tile_y), :]
        for wave, fields in enumerate((forward, adjoint)):
            for part in range(6):
                value = fields[3 + part, x]
                stress[6 * wave + part, x + LAYERS, middle, :] = (
                    value + extra if wave == 1 and part < 3 else value
                )
        return carry

    lax.fori_loop(0, tile_x, fill, 0, unroll=True)

    def layer(x, carry):
        for wave in range(2):
            xx, yy, zz, xy, xz, yz = range(6 * wave, 6 * wave + 6)
            values = (
                along_x(stress, xx, x, tile_y, True)
                + along_y(stress, xy, x, tile_y, False)
                + along_z(stress, xz, x, tile_y, False),
                along_x(stress, xy, x, tile_y, False)
                + along_y(stress, yy, x, tile_y, True)
                + along_z(stress, yz, x, tile_y, False),
                along_x(stress, xz, x, tile_y, False)
                + along_y(stress, yz, x, tile_y, False)
                + along_z(stress, zz, x, tile_y, True),
            )
            for part, value in enumerate(values):
                gained[3 * wave + part, x] = value
        return carry

    lax.fori_loop(0, tile_x, layer, 0, unroll=True)
    copy.wait()

    def finish(x, carry):
        light = 1.0 / density_now[x]
        buoyancy[x] = light
        for wave, fields in enumerate((forward, adjoint)):
            for part in range(3):
                value = light * gained[3 * wave + part, x]
                if wave == 0:
                    accel[part, x] = value
                velocity[3 * wave + part, x + LAYERS, middle, :] = (
                    fields[part, x] + time_step * value
                )
        return carry

    lax.fori_loop(0, tile_x, finish, 0, unroll=True)


def stress_halo_terms(links, received, rim_added, waves, add):
    for link, halo in zip(links, received):
        dim = link[1]
        part_n, part_a, part_b = ACCEL_OF[dim]

        def normal(wave, slot, layer):
            value = halo[wave, slot]
            return value + rim_added[dim, layer] if wave == 1 else value

        def after():
            for wave in waves:
                n0, n1 = normal(wave, 0, 1), normal(wave, 1, 2)
                add(wave, part_n, dim, -1, near * n0 + far * n1)
                add(wave, part_n, dim, -2, far * n0)
                add(wave, part_a, dim, -1, far * halo[wave, 2])
                add(wave, part_b, dim, -1, far * halo[wave, 3])

        def before():
            for wave in waves:
                add(wave, part_n, dim, 0, -far * normal(wave, 0, 0))
                for part, slot in ((part_a, 1), (part_b, 3)):
                    outer, inner = halo[wave, slot], halo[wave, slot + 1]
                    add(wave, part, dim, 0, -near * inner - far * outer)
                    add(wave, part, dim, 1, -far * inner)

        real = has_peer(link[0], link[2])
        lower = is_lower(link[0], link[2])
        pl.when(real & lower)(after)
        pl.when(real & jnp.logical_not(lower))(before)


def source_gain(cell, part, x, y, z, width_y):
    depth = z.shape[-1]
    column = lax.div(cell, depth)
    source_x = lax.div(column, width_y)
    away = [source_x - x, column - source_x * width_y - y, cell - column * depth - z]
    along = away.pop(part)
    gain = jnp.where(along == 0, -near, 0.0)
    for offset, value in ((1, near), (2, far), (-1, -far)):
        gain = jnp.where(along == offset, value, gain)
    return jnp.where((away[0] == 0) & (away[1] == 0), gain, 0.0)


def start_of(tile_x, tile_y):
    return lax.axis_index("tx") * tile_x, lax.axis_index("ty") * tile_y


def missing_terms(links, stress, source, width_y, missing):
    cell, amp = source
    layers, rows, depth = stress.shape[1:]
    tile = layers - 2 * LAYERS, rows - 2 * ROWS
    starts = start_of(*tile)
    for link, out in zip(links, missing):
        dim = link[1]
        shape = out.shape[2:]
        cross = starts[1 - dim] + lax.broadcasted_iota(jnp.int32, shape, 0)
        level = lax.broadcasted_iota(jnp.int32, shape, 1)

        def own(wave, part, index):
            return face(stress, 6 * wave + STRESS_ALONG[dim][part], dim, index, True)[...]

        def put(slots):
            for wave in range(2):
                for slot, (part, layer, terms) in enumerate(slots):
                    value = terms(wave) if dim == 1 else jnp.zeros(shape, jnp.float32)
                    if wave == 0:
                        here = jnp.full(shape, starts[dim] + layer, jnp.int32)
                        x, y = (here, cross) if dim == 0 else (cross, here)
                        value += amp * source_gain(
                            cell, VELOCITY_ALONG[dim][part], x, y, level, width_y
                        )
                    out[wave, slot] = value

        def after():
            count = tile[dim]
            slots = [(0, count, lambda wave: -far * own(wave, 0, -1))]
            for part in (1, 2):
                slots += [
                    (
                        part,
                        count,
                        lambda wave, part=part: -near * own(wave, part, -1)
                        - far * own(wave, part, -2),
                    ),
                    (part, count + 1, lambda wave, part=part: -far * own(wave, part, -1)),
                ]
            put(slots)

        def before():
            put([
                (0, -2, lambda wave: far * own(wave, 0, 0)),
                (0, -1, lambda wave: near * own(wave, 0, 0) + far * own(wave, 0, 1)),
                (1, -1, lambda wave: far * own(wave, 1, 0)),
                (2, -1, lambda wave: far * own(wave, 2, 0)),
            ])

        lower = is_lower(link[0], link[2])
        pl.when(lower)(after)
        pl.when(jnp.logical_not(lower))(before)


def velocity_halo_terms(links, received, stresses, missing, add):
    for link, halo, stress_halo, lack in zip(links, received, stresses, missing):
        dim = link[1]
        part_n, part_a, part_b = STRAIN_OF[dim]

        def after():
            lights = [time_step / stress_halo[layer, SPARE] for layer in range(2)]
            for wave in range(2):

                def whole(slot, layer):
                    return halo[wave, slot] + lights[layer] * lack[wave, slot]

                add(wave, part_n, dim, -1, far * whole(0, 0))
                for part, slot in ((part_a, 1), (part_b, 3)):
                    inner, outer = whole(slot, 0), whole(slot + 1, 1)
                    add(wave, part, dim, -1, near * inner + far * outer)
                    add(wave, part, dim, -2, far * inner)

        def before():
            lights = [time_step * halo[layer, SPARE] for layer in range(2)]
            for wave in range(2):

                def whole(slot, layer):
                    return halo[wave, slot] + lights[layer] * lack[wave, slot]

                outer, inner = whole(0, 1), whole(1, 0)
                add(wave, part_n, dim, 0, -near * inner - far * outer)
                add(wave, part_n, dim, 1, -far * inner)
                add(wave, part_a, dim, 0, -far * whole(2, 0))
                add(wave, part_b, dim, 0, -far * whole(3, 0))

        real = has_peer(link[0], link[2])
        lower = is_lower(link[0], link[2])
        pl.when(real & lower)(after)
        pl.when(real & jnp.logical_not(lower))(before)


def face(ref, part, dim, index, padded):
    layers, rows, depth = ref.shape[1:]
    tile_x = layers - 2 * LAYERS if padded else layers
    tile_y = rows - 2 * ROWS if padded else rows
    if dim == 0:
        at = index % tile_x
        if padded:
            return ref.at[part, at + LAYERS, pl.ds(ROWS, tile_y), :]
        return ref.at[part, at]
    at = index % tile_y
    flat = ref.reshape(ref.shape[0], layers * rows, depth)
    begin = LAYERS * rows + ROWS + at if padded else at
    return flat.at[part, pl.ds(begin, tile_x, stride=rows), :]


def light_face(buoyancy, dim, index):
    layers, rows, depth = buoyancy.shape
    if dim == 0:
        return buoyancy[index % layers]
    return buoyancy.reshape(layers * rows, depth)[pl.ds(index % rows, layers, stride=rows), :]


def boundary_kernel(links, send_links, *refs):
    count = len(links)
    received = refs[:count]
    rim_added, buoyancy, _, velocity = refs[count : count + 4]
    sends = refs[count + 4 :]

    def add(wave, part, dim, index, term):
        target = face(velocity, 3 * wave + part, dim, index, True)
        target[...] += time_step * light_face(buoyancy, dim, index) * term

    stress_halo_terms(links, received, rim_added, (0, 1), add)
    send_velocities(send_links, velocity, buoyancy, sends)


def strain_kernel(links, width_y, *refs):
    count = len(links)
    received = refs[:count]
    source_cell, source_amp, rim_added, buoyancy, accel = refs[count : count + 5]
    stress, lame, shear = refs[count + 6 : count + 9]
    strain, gradient, velocity, scaled_lame, scaled_shear = refs[count + 9 : count + 14]
    outputs, missing = refs[count + 14 : count + 16], refs[count + 16 : 2 * count + 16]
    accel_now, lame_now, shear_now, sems = refs[2 * count + 16 :]
    fetches = [
        pltpu.make_async_copy(lame, lame_now, sems.at[6]),
        pltpu.make_async_copy(shear, shear_now, sems.at[7]),
    ]
    for copy in fetches:
        copy.start()
    tile_x, tile_y, depth = buoyancy.shape
    middle = pl.ds(ROWS, tile_y)
    clear_rim(velocity, range(6), range(6))
    accel_now[...] = accel[...]

    def add(wave, part, dim, index, term):
        target = face(accel_now, part, dim, index, False)
        target[...] += light_face(buoyancy, dim, index) * term

    stress_halo_terms(links, received, rim_added, (0,), add)
    x_start, y_start = start_of(tile_x, tile_y)
    cell, amp = source_cell[0], source_amp[0]
    source_x = lax.div(cell, width_y * depth)
    y = y_start + lax.broadcasted_iota(jnp.int32, (tile_y, depth), 0)
    level = lax.broadcasted_iota(jnp.int32, (tile_y, depth), 1)
    for offset in (-2, -1, 0, 1):
        x = source_x + offset - x_start

        @pl.when((x >= 0) & (x < tile_x))
        def add_source():
            here = jnp.full((tile_y, depth), source_x + offset, jnp.int32)
            for part in range(3):
                gain = source_gain(cell, part, here, y, level, width_y)
                value = amp * buoyancy[x] * gain
                accel_now[part, x] += value
                velocity[part, x + LAYERS, middle, :] += time_step * value

    copies = [
        pltpu.make_async_copy(
            velocity.at[3 * wave + part, pl.ds(LAYERS, tile_x), middle, :],
            outputs[wave].at[part],
            sems.at[3 * wave + part],
        )
        for wave in range(2)
        for part in range(3)
    ]
    for copy in copies:
        copy.start()
    def layer(x, carry):
        for wave in range(2):
            vx, vy, vz = range(3 * wave, 3 * wave + 3)
            values = (
                along_x(velocity, vx, x, tile_y, False),
                along_y(velocity, vy, x, tile_y, False),
                along_z(velocity, vz, x, tile_y, False),
                along_y(velocity, vx, x, tile_y, True) + along_x(velocity, vy, x, tile_y, True),
                along_z(velocity, vx, x, tile_y, True) + along_x(velocity, vz, x, tile_y, True),
                along_z(velocity, vy, x, tile_y, True) + along_y(velocity, vz, x, tile_y, True),
            )
            for part, value in enumerate(values):
                strain[6 * wave + part, x] = value
        total = sum(
            accel_now[part, x] * velocity[3 + part, x + LAYERS, middle, :] for part in range(3)
        )
        gradient[2, x] = -time_step * total
        return carry

    lax.fori_loop(0, tile_x, layer, 0, unroll=8)
    missing_terms(links, stress, (cell, amp), width_y, missing)
    for copy in fetches:
        copy.wait()
    scaled_lame[...] = time_step * lame_now[...]
    scaled_shear[...] = time_step * shear_now[...]
    for copy in copies:
        copy.wait()


def new_stress(strain, stress, scaled_lame, scaled_shear, wave, x, tile_y):
    lame, shear = scaled_lame[x], scaled_shear[x]
    strains = [strain[6 * wave + part, x] for part in range(6)]
    volume = lame * (strains[0] + strains[1] + strains[2])
    values = []
    for part in range(6):
        old = stress[6 * wave + part, x + LAYERS, pl.ds(ROWS, tile_y), :]
        if part < 3:
            values.append(old + (volume + 2.0 * shear * strains[part]))
        else:
            values.append(old + shear * strains[part])
    return strains, values


def gradient_kernel(links, inner, *refs):
    count = len(links)
    received, stresses, missing = (refs[at : at + count] for at in range(0, 3 * count, count))
    stress, scaled_lame, scaled_shear, _, _, strain, gradient = refs[3 * count :]
    tile_x, tile_y, _ = scaled_lame.shape
    first, last = min(2, tile_x), max(2, tile_x - 2)

    def add(wave, part, dim, index, term):
        target = face(strain, 6 * wave + part, dim, index, False)
        target[...] += term

    velocity_halo_terms(links, received, stresses, missing, add)

    def layer(x, carry):
        strains = [strain[part, x] for part in range(6)]
        _, values = new_stress(strain, stress, scaled_lame, scaled_shear, 1, x, tile_y)
        trace = strains[0] + strains[1] + strains[2]
        gradient[0, x] = -time_step * trace * (values[0] + values[1] + values[2])
        total = sum(left * right for left, right in zip(strains, values))
        gradient[1, x] = -time_step * total
        return carry

    if inner:
        if last > first:
            lax.fori_loop(first, last, layer, 0, unroll=4)
    else:
        for x in (*range(first), *range(last, tile_x)):
            layer(x, 0)


def output_kernel(
    chunk, width_y, source_cell, source_amp, strain, stress, scaled_lame, scaled_shear, *refs
):
    outputs, (values_now, sems) = refs[2:4], refs[4:]
    tile_x, tile_y, depth = scaled_lame.shape
    x_start, y_start = start_of(tile_x, tile_y)
    y = y_start + lax.broadcasted_iota(jnp.int32, (tile_y, depth), 0)
    level = lax.broadcasted_iota(jnp.int32, (tile_y, depth), 1)
    in_layer = y * depth + level - source_cell[0]
    copies = []
    for begin in range(0, tile_x, chunk):
        for wave in range(2):
            for x in range(begin, begin + chunk):
                _, values = new_stress(strain, stress, scaled_lame, scaled_shear, wave, x, tile_y)
                if wave == 0:
                    first = (x_start + x) * (width_y * depth)
                    added = jnp.where(in_layer == -first, source_amp[0], 0.0)
                    values[:3] = [value + added for value in values[:3]]
                for part in range(6):
                    values_now[6 * wave + part, x] = values[part]
            layers = pl.ds(begin, chunk)
            copy = pltpu.make_async_copy(
                values_now.at[pl.ds(6 * wave, 6), layers],
                outputs[wave].at[pl.ds(3, 6), layers],
                sems.at[len(copies)],
            )
            copy.start()
            copies.append(copy)
    for copy in copies:
        copy.wait()


def sum_kernel(chunk, mine, other, total, total_now, sems):
    copies = []
    for part in range(mine.shape[0]):
        for begin in range(0, mine.shape[1], chunk):
            layers = pl.ds(begin, chunk)
            total_now[part, layers] = mine[part, layers] + other[part, layers]
            copy = pltpu.make_async_copy(
                total_now.at[part, layers], total.at[part, layers], sems.at[len(copies)]
            )
            copy.start()
            copies.append(copy)
    for copy in copies:
        copy.wait()


def in_hbm(value):
    return pltpu.with_memory_space_constraint(value, pltpu.HBM)


def cost(flops, size):
    return pl.CostEstimate(flops=flops, bytes_accessed=size, transcendentals=0)


def body(
    forward_fields,
    adjoint_fields,
    lame_lambda,
    shear_modulus,
    density,
    source_cell,
    source_amp,
    receiver_cell,
    residual_amp,
):
    _, _, tile_x, tile_y, depth = forward_fields.shape
    forward = forward_fields.reshape(forward_fields.shape[1:])
    adjoint = adjoint_fields.reshape(adjoint_fields.shape[1:])
    sizes = {name: lax.axis_size(name) for name in ("tx", "ty")}
    width_y = tile_y * sizes["ty"]
    links_x, links_y = links_of(sizes)
    cells = tile_x * tile_y * depth

    def buffers(dim):
        return pltpu.VMEM((2, SLOTS, tile_y if dim == 0 else tile_x, depth), jnp.float32)

    def tile(*lead):
        return pltpu.VMEM((*lead, tile_x, tile_y, depth), jnp.float32)

    def padded(parts):
        return pltpu.VMEM(
            (parts, tile_x + 2 * LAYERS, tile_y + 2 * ROWS, depth), jnp.float32
        )

    def exchange(links, sends):
        return [swap(send, axis, first) for (axis, _, first), send in zip(links, sends)]

    def shapes(links):
        return [buffers(dim) for _, dim, _ in links]

    links = links_y + links_x
    count, count_x, count_y = len(links), len(links_x), len(links_y)
    rows = tile_x * tile_y + 3 * (tile_x + tile_y)
    source = source_cell, source_amp

    *sends, density_rows, stress = pl.pallas_call(
        functools.partial(early_pack_kernel, links_x),
        out_shape=shapes(links_x) + [pltpu.VMEM((2, tile_x, depth), jnp.float32), padded(12)],
        in_specs=[hbm] * 3,
        out_specs=[vmem] * (count_x + 2),
        scratch_shapes=[pltpu.SemaphoreType.DMA((2 + 2 * count_x,))],
        compiler_params=params,
        cost_estimate=cost(0, 4 * cells),
        name="early_pack",
    )(*(in_hbm(x) for x in (forward, adjoint, density)))
    halos_x = exchange(links_x, sends)
    halos_y = []
    if links_y:
        sends = pl.pallas_call(
            functools.partial(pack_kernel, links_y),
            out_shape=shapes(links_y),
            in_specs=[vmem] * 3,
            out_specs=[vmem] * count_y,
            compiler_params=params,
            cost_estimate=cost(0, 2 * 2 * SLOTS * count_y * tile_x * depth * 4),
            name="pack",
        )(forward, adjoint, density_rows)
        halos_y = exchange(links_y, sends)

    stress, velocity, accel, rim_added, buoyancy = pl.pallas_call(
        functools.partial(velocity_kernel, width_y),
        out_shape=[
            padded(12),
            padded(6),
            tile(3),
            pltpu.VMEM((2, 3, max(tile_x, tile_y), depth), jnp.float32),
            tile(),
        ],
        in_specs=[hbm] + [vmem] * 5,
        out_specs=[vmem] * 5,
        input_output_aliases={5: 0},
        scratch_shapes=[
            pltpu.VMEM((rows, depth), jnp.float32),
            tile(6),
            tile(),
            pltpu.SemaphoreType.DMA((1,)),
        ],
        compiler_params=params,
        cost_estimate=cost(200 * cells, 18 * 4 * cells),
        name="velocity",
    )(in_hbm(density), receiver_cell, residual_amp, forward, adjoint, stress)

    def boundary(links, send_links, halos, velocity, name):
        velocity, *sends = pl.pallas_call(
            functools.partial(boundary_kernel, links, send_links),
            out_shape=[padded(6)] + shapes(send_links),
            in_specs=[vmem] * (len(links) + 3),
            out_specs=[vmem] * (1 + len(send_links)),
            input_output_aliases={len(links) + 2: 0},
            compiler_params=params,
            cost_estimate=cost(cells, 10 * 2 * tile_x * depth * 4),
            name=name,
        )(*halos, rim_added, buoyancy, velocity)
        return velocity, exchange(send_links, sends)

    later_y = links_y[::-1]
    velocity, velocity_halos_y = boundary(links_x, later_y, halos_x, velocity, "boundary_x")
    velocity, velocity_halos_x = boundary(links_y, links_x, halos_y, velocity, "boundary_y")
    halos = halos_y + halos_x

    out_shape = jax.ShapeDtypeStruct(forward.shape, jnp.float32)
    strain, gradient, _, scaled_lame, scaled_shear, *rest = pl.pallas_call(
        functools.partial(strain_kernel, links, width_y),
        out_shape=[tile(12), tile(3), padded(6), tile(), tile(), out_shape, out_shape]
        + shapes(links),
        in_specs=[vmem] * count + [smem] * 2 + [vmem] * 5 + [hbm] * 2,
        out_specs=[vmem] * 5 + [hbm] * 2 + [vmem] * count,
        input_output_aliases={count + 5: 2},
        scratch_shapes=[tile(3), tile(), tile(), pltpu.SemaphoreType.DMA((8,))],
        compiler_params=params,
        cost_estimate=cost(200 * cells, 18 * 4 * cells),
        name="strain",
    )(
        *halos,
        *source,
        rim_added,
        buoyancy,
        accel,
        velocity,
        stress,
        in_hbm(lame_lambda),
        in_hbm(shear_modulus),
    )
    forward_next, adjoint_next, *missing = rest

    def gradients(links, inner, received, stresses, missing, strain, gradient, name):
        return pl.pallas_call(
            functools.partial(gradient_kernel, links, inner),
            out_shape=[tile(12), tile(3)],
            in_specs=[vmem] * (3 * len(links) + 5),
            out_specs=[vmem] * 2,
            input_output_aliases={3 * len(links) + 3: 0, 3 * len(links) + 4: 1},
            compiler_params=params,
            cost_estimate=cost(30 * cells, 2 * 4 * cells),
            name=name,
        )(*received, *stresses, *missing, stress, scaled_lame, scaled_shear, strain, gradient)

    strain, gradient = gradients(
        later_y,
        True,
        velocity_halos_y,
        halos_y[::-1],
        missing[:count_y][::-1],
        strain,
        gradient,
        "gradient_inner",
    )
    strain, gradient = gradients(
        links_x, False, velocity_halos_x, halos_x, missing[count_y:], strain, gradient, "gradient"
    )
    other = lax.ppermute(gradient, "shot", [(0, 1), (1, 0)])

    chunk = 4 if tile_x % 4 == 0 else 1
    forward_next, adjoint_next = pl.pallas_call(
        functools.partial(output_kernel, chunk, width_y),
        out_shape=[out_shape, out_shape],
        in_specs=[smem] * 2 + [vmem] * 4 + [hbm] * 2,
        out_specs=[hbm] * 2,
        input_output_aliases={6: 0, 7: 1},
        scratch_shapes=[tile(12), pltpu.SemaphoreType.DMA((2 * tile_x // chunk,))],
        compiler_params=params,
        cost_estimate=cost(60 * cells, 18 * 4 * cells),
        name="outputs",
    )(*source, strain, stress, scaled_lame, scaled_shear, forward_next, adjoint_next)
    total = pl.pallas_call(
        functools.partial(sum_kernel, tile_x),
        out_shape=jax.ShapeDtypeStruct((3, tile_x, tile_y, depth), jnp.float32),
        in_specs=[vmem] * 2,
        out_specs=hbm,
        scratch_shapes=[tile(3), pltpu.SemaphoreType.DMA((3,))],
        compiler_params=params,
        cost_estimate=cost(3 * cells, 9 * 4 * cells),
        name="sum",
    )(gradient, other)
    return forward_next[None], adjoint_next[None], total


def solution(mesh):
    return jax.shard_map(
        body,
        mesh=mesh,
        in_specs=(
            P("shot", None, "tx", "ty", None),
            P("shot", None, "tx", "ty", None),
            P("tx", "ty", None),
            P("tx", "ty", None),
            P("tx", "ty", None),
            P("shot"),
            P("shot"),
            P("shot", None),
            P("shot", None),
        ),
        out_specs=(
            P("shot", None, "tx", "ty", None),
            P("shot", None, "tx", "ty", None),
            P(None, "tx", "ty", None),
        ),
        check_vma=False,
    )
```
